32 devices in a mesh: groups: 2 (over y), tensor: 4 (over z), dp: 2 (over x), pipe: 2 (over core).
Axes of the slice: x: 2, y: 2, z: 4, core: 2. Of those that a mesh axis runs over, the one named last changes fastest.
Arguments:
- tokens: bfloat16 [6144, 8192], P(('groups', 'dp', 'pipe'), 'tensor'), parts along dimension 0, may hold values from -6 to 6
- base_weight: bfloat16 [8192, 2048], P(None, 'tensor'), may hold values from -0.0625 to 0.0625
- adapter_a: bfloat16 [8, 64, 8192], P(('groups', 'dp'), None, 'tensor'), parts along dimension 0, may hold values from -0.0625 to 0.0625
- adapter_b: bfloat16 [8, 64, 2048], P(('groups', 'dp'), None, 'tensor'), parts along dimension 0, may hold values from -0.75 to 0.75
- cotangent: bfloat16 [6144, 2048], P(('groups', 'dp', 'pipe'), 'tensor'), parts along dimension 0, may hold values from -0.059814453 to 0.059814453
- block_tenant_index: int32 [48], P(('groups', 'dp', 'pipe')), parts along dimension 0, may hold values from 0 to 3
- block_fill: int32 [8, 6], P(('groups', 'dp', 'pipe')), parts along dimension 0, may hold values from 1 to 128, 512 in all within a row
Outputs:
- projection_output: bfloat16 [6144, 2048], P(('groups', 'dp', 'pipe'), 'tensor'), parts along dimension 0
- down_adapter_gradient: float32 [8, 64, 8192], P(('groups', 'dp'), None, 'tensor'), parts along dimension 0
- up_adapter_gradient: float32 [8, 64, 2048], P(('groups', 'dp'), None, 'tensor'), parts along dimension 0
The draws below stay inside these ranges and needn't reach their ends.
There are 2 independent parts, one for each index of `groups`. The reference program is written for one: setup_inputs(seed, part) draws one part's arguments, and reference() takes and returns one part's arrays. A program takes and returns all parts, laid end to end along the dimension named above; an argument that names none is the same for every part. Nothing has to cross between parts.
Inputs may be any that keep to these rules, and one draw needn't show every extreme that they name: `block_fill`: the 6 numbers of one line sum to exactly 512.
All inputs are finite; a program needn't handle non-finite values.
Results may differ from the reference program's by a relative error of at most 0.015.
Values may be sent and summed in bfloat16 or wider, within the bound.
No kernel may reach another device: no remote copies, remote signals or barrier semaphores. Data moves between devices by JAX's collectives and lax.ppermute only.
A program may use at most 128 MiB of HBM per device.

```python
import math
import jax
import jax.numpy as jnp
import numpy as np
from jax import lax

D = 8192
E = 2048
RANK = 64
BLOCK = 128
BLK_DEV = 6
LIVE_DEV = 512
TENANT_COUNT = 4
BLOCKS = 24
TOKENS = 3072
N_TENSOR = 4
N_DP = 2
N_PIPE = 2


def plant(array, key, smallest, largest):
    shape = array.shape
    index_at = [jax.random.randint(jax.random.fold_in(key, axis), (), 0, shape[axis]) for axis in range(len(shape))]
    array = array.at[tuple(index_at)].set(smallest)
    longest = shape.index(max(shape))
    index_at[longest] = (index_at[longest] + 1) % shape[longest]
    return array.at[tuple(index_at)].set(largest)


def level_of(stream_key, extent, pieces, least, largest):
    factor_of, own = 1.0, jax.random.fold_in(stream_key, 6)
    for axis_at, shards_of in pieces:
        heights = jnp.exp(jax.random.uniform(jax.random.fold_in(own, axis_at), (shards_of,), jnp.float32, least / len(pieces), largest / len(pieces)))
        factor_of = factor_of * jnp.repeat(heights, extent[axis_at] // shards_of).reshape([-1 if axis == axis_at else 1 for axis in range(len(extent))])
    return factor_of


def rank_table(count, skew):
    weights = [(1 << 20) // math.isqrt(standing ** skew) + 1 for standing in range(1, count + 1)]
    spread = 1 + sum(weights) // (1 << 30)
    return np.cumsum(np.array([max(1, weight // spread) for weight in weights]))


def ranked(stream_key, shape, amount, slope):
    listing = rank_table(amount, slope)
    ticket = jax.random.randint(jax.random.fold_in(stream_key, 1), shape, 0, int(listing[amount - 1]))
    grade = jnp.searchsorted(jnp.asarray(listing, jnp.int32), ticket, side="right")
    return jax.random.permutation(jax.random.fold_in(stream_key, 2), amount)[grade].astype(jnp.int32)


def split_up(amount, total, most, skew):
    loads = [(1 << 20) // math.isqrt(grade ** skew) + 1 for grade in range(2, amount + 1)]
    rest, counts = total - most - (amount - 1), [1] * (amount - 1)
    while rest > 0:
        candidates = [i for i in range(amount - 1) if counts[i] < most]
        pool, budget = sum([loads[i] for i in candidates]), rest
        for i in candidates:
            more = min(most - counts[i], max(1, budget * loads[i] // pool), rest)
            counts[i] = counts[i] + more
            rest = rest - more
    return np.array([most] + counts)


def ragged_sizes(stream_key, amount, total, bound, lean):
    if amount == 2:
        one = jax.random.randint(stream_key, (), max(1, total - bound), min(bound, total - 1) + 1)
        return jnp.stack([one, total - one])
    sizes = jnp.asarray(split_up(amount, total, bound, lean), jnp.int32)
    couples = (amount - 1) // 2
    donor, receiver = sizes[1:1 + 2 * couples:2], sizes[2:2 + 2 * couples:2]
    slack = jnp.minimum(donor - 1, bound - receiver)
    moved = jax.random.randint(jax.random.fold_in(stream_key, 1), (couples,), 0, 1 << 20) % (slack + 1)
    sizes = sizes.at[1:1 + 2 * couples:2].set(donor - moved).at[2:2 + 2 * couples:2].set(receiver + moved)
    return sizes[jax.random.permutation(jax.random.fold_in(stream_key, 2), amount)]


def centred(stream_key, shape, scale, limit, shards=(), kind=jnp.bfloat16):
    result = jax.random.normal(stream_key, shape, jnp.float32) * scale
    if len(shards) > 0:
        result = level_of(stream_key, shape, shards, -0.22, 0.18) * result
    return jnp.clip(result, min=-limit, max=limit).astype(kind)


def setup_inputs(seed: int = 0, part: int = 0) -> dict:
    key_of = jax.random.split(jax.random.key(seed), 8)
    part_splits = jax.random.split(jax.random.fold_in(key_of[7], part), 8)
    return {
        "tokens": centred(part_splits[0], (TOKENS, D), 1.0, 6.0, ((0, 4), (1, 4))),
        "base_weight": centred(key_of[1], (D, E), D ** -0.5, 0.0625, ((1, 4),)),
        "adapter_a": centred(part_splits[2], (TENANT_COUNT, RANK, D), D ** -0.5, 0.0625, ((0, 2), (2, 4))),
        "adapter_b": centred(part_splits[3], (TENANT_COUNT, RANK, E), RANK ** -0.5, 0.75, ((0, 2), (2, 4))),
        "cotangent": centred(part_splits[4], (TOKENS, E), 0.01, 0.059814453, ((0, 4), (1, 4))),
        "block_tenant_index": plant(ranked(part_splits[5], (BLOCKS,), TENANT_COUNT, 2), jax.random.fold_in(part_splits[5], 3), 0, TENANT_COUNT - 1).astype(jnp.int32),
        "block_fill": jax.vmap(lambda own: ragged_sizes(own, BLK_DEV, LIVE_DEV, BLOCK, 0))(jax.random.split(part_splits[6], (N_DP * N_PIPE))).reshape((N_DP * N_PIPE, BLK_DEV)).astype(jnp.int32),
    }


ADAPTER_SCALE = 2.0


def reference(tokens, base_weight, adapter_a, adapter_b, cotangent, block_tenant_index, block_fill):
    row_blocks = block_tenant_index.shape[0]
    block_row_length = tokens.shape[0] // row_blocks
    fill_rows = block_fill.reshape(-1)
    active_row_mask = (jnp.arange(block_row_length, dtype=jnp.int32)[None, :] < fill_rows[:, None])[:, :, None]
    tok_blocks = tokens.reshape(row_blocks, block_row_length, -1).astype(jnp.float32)
    cot_blocks = cotangent.reshape(row_blocks, block_row_length, -1).astype(jnp.float32)
    chosen_down = adapter_a[block_tenant_index].astype(jnp.float32)
    chosen_up = adapter_b[block_tenant_index].astype(jnp.float32)
    low_in = jnp.einsum("bnd,brd->bnr", tok_blocks, chosen_down)
    low_in = jnp.where(active_row_mask, low_in, 0.0).astype(jnp.bfloat16)
    low_grad = jnp.einsum("bne,bre->bnr", cot_blocks, chosen_up)
    low_grad = jnp.where(active_row_mask, low_grad, 0.0).astype(jnp.bfloat16)
    slice_width = tokens.shape[1] // N_TENSOR

    def add_slice(total, index):
        offset = (index * slice_width).astype(jnp.int32)
        tok_slice = lax.dynamic_slice_in_dim(tokens, offset, slice_width, 1)
        weight_slice = lax.dynamic_slice_in_dim(base_weight, offset, slice_width, 0)
        part = jnp.dot(tok_slice, weight_slice, preferred_element_type=jnp.float32)
        part = lax.optimization_barrier(part.astype(jnp.bfloat16)).astype(jnp.float32)
        return total + part, None

    start = jnp.zeros((tokens.shape[0], base_weight.shape[1]), jnp.float32)
    base_output, _ = lax.scan(add_slice, start, jnp.arange(N_TENSOR, dtype=jnp.int32))
    base_output = base_output.reshape(row_blocks, block_row_length, -1)
    low_rank_output = jnp.einsum("bnr,bre->bne", low_in.astype(jnp.float32), chosen_up)
    projection_output = jnp.where(active_row_mask, base_output + ADAPTER_SCALE * low_rank_output, 0.0).astype(jnp.bfloat16)
    projection_output = projection_output.reshape(tokens.shape[0], -1)
    block_down_weight = jnp.einsum("bnr,bnd->brd", low_grad.astype(jnp.float32), tok_blocks)
    block_up_weight = jnp.einsum("bnr,bne->bre", low_in.astype(jnp.float32), cot_blocks)
    down_adapter_gradient = ADAPTER_SCALE * jax.ops.segment_sum(block_down_weight, block_tenant_index, num_segments=TENANT_COUNT)
    up_adapter_gradient = ADAPTER_SCALE * jax.ops.segment_sum(block_up_weight, block_tenant_index, num_segments=TENANT_COUNT)
    return projection_output, down_adapter_gradient, up_adapter_gradient
```

```python
import functools

import jax
import jax.numpy as jnp
from jax import lax
from jax.sharding import PartitionSpec as P

ADAPTER_SCALE = 2.0
LIVE_ROWS = 512
BF16 = jnp.bfloat16
F32 = jnp.float32


def dot(a, b, contract):
    return lax.dot_general(a, b, ((contract[0:1], contract[1:2]), ((), ())), preferred_element_type=F32)


def shift(x, name, count, step):
    return lax.ppermute(x, name, [(i, (i + step) % count) for i in range(count)])


def flip(x, names, count, mask):
    return lax.ppermute(x, names, [(i, i ^ mask) for i in range(count)])


def gather_xy(piece, planes):
    return [piece] + [flip(piece, ("groups", "dp"), planes, m) for m in range(1, planes)]


def body(sizes, tokens, base_weight, adapter_a, adapter_b, cotangent, block_tenant_index, block_fill):
    n_t, n_dp, n_pipe = sizes["tensor"], sizes["dp"], sizes["pipe"]
    planes = sizes["groups"] * n_dp
    rows, feat = tokens.shape
    cols = base_weight.shape[1]
    half = cols // n_pipe
    blocks = block_tenant_index.shape[0]
    block = rows // blocks
    rank = adapter_a.shape[1]
    tenants = adapter_a.shape[0] * n_dp
    me_t, me_pipe = lax.axis_index("tensor"), lax.axis_index("pipe")
    q = lax.axis_index("groups") * n_dp + lax.axis_index("dp")
    part_rows = feat // planes

    received = []
    for s in range(1, n_t):
        k = (me_t + s) % n_t
        share = lax.dynamic_slice(base_weight, (k * feat + q * part_rows, me_pipe * half), (part_rows, half))
        received.append(shift(share, "tensor", n_t, s))

    all_a = lax.all_gather(adapter_a, "dp", axis=0, tiled=True).reshape(tenants * rank, feat)
    all_b = lax.all_gather(adapter_b, "dp", axis=0, tiled=True).reshape(tenants * rank, cols)

    fill = block_fill.reshape(-1)
    ends = jnp.cumsum(fill)
    starts = ends - fill
    inside = jnp.arange(block, dtype=jnp.int32)
    place = jnp.where(inside[None, :] < fill[:, None], starts[:, None] + inside[None, :], -1).reshape(rows)
    packed = jnp.arange(LIVE_ROWS, dtype=jnp.int32)
    pick = (packed[:, None] == place[None, :]).astype(BF16)
    tenant_of = jnp.sum(
        jnp.where((packed[:, None] >= starts[None, :]) & (packed[:, None] < ends[None, :]), block_tenant_index[None, :], 0),
        axis=1,
    )
    own = tenant_of[:, None] == jnp.arange(tenants * rank, dtype=jnp.int32)[None, :] // rank

    x = dot(pick, tokens, (1, 0)).astype(BF16)
    c = dot(pick, cotangent, (1, 0)).astype(BF16)
    x_other = flip(x, "pipe", n_pipe, 1)

    def fold(v):
        return jnp.sum(jnp.where(own, v, 0.0).reshape(LIVE_ROWS, tenants, rank), axis=1)

    low = jnp.concatenate([fold(dot(x, all_a, (1, 1))), fold(dot(c, all_b, (1, 1)))], axis=1).astype(BF16)
    low_sum = low.astype(F32)
    for s in range(1, n_t):
        low_sum = low_sum + shift(low, "tensor", n_t, s).astype(F32)
    low_sum = low_sum.astype(BF16)

    def spread(v):
        return jnp.where(own, jnp.concatenate([v] * tenants, axis=1), jnp.zeros((), BF16))

    low_in, low_grad = spread(low_sum[:, :rank]), spread(low_sum[:, rank:])
    down = (ADAPTER_SCALE * dot(low_grad, x, (0, 0))).astype(BF16)
    up = (ADAPTER_SCALE * dot(low_in, c, (0, 0))).astype(BF16)
    both = jnp.concatenate([down, up], axis=1).reshape(n_dp, tenants // n_dp * rank, feat + cols)
    me_dp = lax.axis_index("dp")
    mine = lax.dynamic_index_in_dim(both, me_dp, 0, keepdims=False).astype(F32)
    for s in range(1, n_dp):
        sent = lax.dynamic_index_in_dim(both, (me_dp + s) % n_dp, 0, keepdims=False)
        mine = mine + shift(sent, "dp", n_dp, s).astype(F32)
    mine = mine + flip(mine.astype(BF16), "pipe", n_pipe, 1).astype(F32)
    down_out = mine[:, :feat].reshape(tenants // n_dp, rank, feat)
    up_out = mine[:, feat:].reshape(tenants // n_dp, rank, cols)

    def columns_of(v):
        return [lax.dynamic_slice_in_dim(v, (q ^ m) * part_rows, part_rows, 1) for m in range(planes)]

    x_parts, other_parts = columns_of(x), columns_of(x_other)
    own_half = jnp.zeros((LIVE_ROWS, half), F32)
    other_half = jnp.zeros((LIVE_ROWS, half), F32)
    for s in range(1, n_t):
        panel = gather_xy(received[s - 1], planes)
        y = sum(dot(a, w, (1, 0)) for a, w in zip(x_parts, panel)).astype(BF16)
        y_other = sum(dot(a, w, (1, 0)) for a, w in zip(other_parts, panel)).astype(BF16)
        own_half = own_half + shift(y, "tensor", n_t, -s).astype(F32)
        pairs = [
            (i * n_pipe + p, ((i - s) % n_t) * n_pipe + (p ^ 1)) for i in range(n_t) for p in range(n_pipe)
        ]
        other_half = other_half + lax.ppermute(y_other, ("tensor", "pipe"), pairs).astype(F32)
    weight = lax.dynamic_slice_in_dim(base_weight, me_t * feat, feat, 0)
    base = dot(x, weight, (1, 0)).astype(BF16).astype(F32)
    first = me_pipe == 0
    base = base + jnp.concatenate(
        [jnp.where(first, own_half, other_half), jnp.where(first, other_half, own_half)], axis=1
    )
    out = (base + ADAPTER_SCALE * dot(low_in, all_b, (1, 0))).astype(BF16)
    out = dot(pick, out, (0, 0)).astype(BF16)
    return out, down_out, up_out


def solution(mesh):
    placed = (
        P(("groups", "dp", "pipe"), "tensor"),
        P(None, "tensor"),
        P(("groups", "dp"), None, "tensor"),
        P(("groups", "dp"), None, "tensor"),
        P(("groups", "dp", "pipe"), "tensor"),
        P(("groups", "dp", "pipe")),
        P(("groups", "dp", "pipe"), None),
    )
    return jax.shard_map(
        functools.partial(body, dict(mesh.shape)),
        mesh=mesh,
        in_specs=placed,
        out_specs=(
            P(("groups", "dp", "pipe"), "tensor"),
            P(("groups", "dp"), None, "tensor"),
            P(("groups", "dp"), None, "tensor"),
        ),
        check_vma=False,
    )
```

```python
import functools

import jax
import jax.numpy as jnp
from jax import lax
from jax.experimental import pallas as pl
from jax.experimental.pallas import tpu as pltpu
from jax.sharding import PartitionSpec as P

ADAPTER_SCALE = 2.0
LIVE = 512
BF16 = jnp.bfloat16
F32 = jnp.float32
I32 = jnp.int32
MIB = 1 << 20
SMEM = pl.BlockSpec(memory_space=pltpu.SMEM)
VMEM = pl.BlockSpec(memory_space=pltpu.VMEM)


def shaped(shape, dtype):
    return jax.ShapeDtypeStruct(shape, dtype)


def dot(a, b, contract=(1, 0)):
    return lax.dot_general(a, b, ((contract[0:1], contract[1:2]), ((), ())), preferred_element_type=F32)


def shift(x, name, count, step):
    return lax.ppermute(x, name, [(i, (i + step) % count) for i in range(count)])


def flip(x, names, count, mask):
    return lax.ppermute(x, names, [(i, i ^ mask) for i in range(count)])


def params(mib):
    return pltpu.CompilerParams(vmem_limit_bytes=mib * MIB)


def cost(flops, bytes_accessed):
    return pl.CostEstimate(flops=flops, bytes_accessed=bytes_accessed, transcendentals=0)


def starts_of(fill_ref, blocks):
    starts, at = [], jnp.int32(0)
    for b in range(blocks):
        starts.append(at)
        at = at + fill_ref[0, b]
    return starts


def tenant_lanes(fill_ref, tenant_ref, blocks, lanes):
    row = lax.broadcasted_iota(I32, (LIVE, lanes), 0)
    tenant = jnp.zeros((LIVE, lanes), I32)
    for b, start in enumerate(starts_of(fill_ref, blocks)):
        tenant = jnp.where(row >= start, tenant_ref[b], tenant)
    return tenant


def pack_kernel(blocks, block, fill_ref, tok_ref, cot_ref, x_ref, c_ref, pick):
    @pl.when(pl.program_id(0) == 0)
    def _():
        row = lax.broadcasted_iota(I32, (LIVE, block), 0)
        col = lax.broadcasted_iota(I32, (LIVE, block), 1)
        for b, start in enumerate(starts_of(fill_ref, blocks)):
            hit = (row == col + start) & (col < fill_ref[0, b])
            pick[:, b * block : (b + 1) * block] = jnp.where(hit, 1.0, 0.0).astype(BF16)
        c_ref[...] = dot(pick[...], cot_ref[...]).astype(BF16)

    x_ref[...] = dot(pick[...], tok_ref[...]).astype(BF16)


def pack(fill, tokens, cotangent, blocks):
    rows, feat = tokens.shape
    cols = cotangent.shape[1]
    steps = 4 if feat % 512 == 0 else 1
    wide = feat // steps
    return pl.pallas_call(
        functools.partial(pack_kernel, blocks, rows // blocks),
        grid=(steps,),
        in_specs=[SMEM, pl.BlockSpec((rows, wide), lambda i: (0, i)), pl.BlockSpec((rows, cols), lambda i: (0, 0))],
        out_specs=[pl.BlockSpec((LIVE, wide), lambda i: (0, i)), pl.BlockSpec((LIVE, cols), lambda i: (0, 0))],
        out_shape=[shaped((LIVE, feat), BF16), shaped((LIVE, cols), BF16)],
        scratch_shapes=[pltpu.VMEM((LIVE, rows), BF16)],
        compiler_params=params(24),
        cost_estimate=cost(2 * LIVE * rows * (feat + cols), 2 * (LIVE + rows) * (feat + cols)),
        name="pack",
    )(fill, tokens, cotangent)


def owner_mask(tenant, lane, owner, rank):
    return tenant == 2 * owner + (lane >= rank).astype(I32)


def low_kernel(n_dp, rank, blocks, dp_ref, fill_ref, tenant_ref, x_ref, c_ref, *refs):
    a_refs, b_refs, out_ref = refs[:n_dp], refs[n_dp : 2 * n_dp], refs[2 * n_dp]
    lanes = 2 * rank
    tenant = tenant_lanes(fill_ref, tenant_ref, blocks, lanes)
    lane = lax.broadcasted_iota(I32, (LIVE, lanes), 1)
    low_in = jnp.zeros((LIVE, lanes), F32)
    low_grad = jnp.zeros((LIVE, lanes), F32)
    for s in range(n_dp):
        mask = owner_mask(tenant, lane, (dp_ref[0] + n_dp - s) % n_dp, rank)
        low_in = low_in + jnp.where(mask, dot(x_ref[...], a_refs[s][...], (1, 1)), 0.0)
        low_grad = low_grad + jnp.where(mask, dot(c_ref[...], b_refs[s][...], (1, 1)), 0.0)
    low_in = low_in + pltpu.roll(low_in, rank, 1)
    low_grad = low_grad + pltpu.roll(low_grad, rank, 1)
    out_ref[...] = jnp.where(lane < rank, low_in, low_grad).astype(BF16)


def low_part(dp, fill, tenant, x, c, a_list, b_list, blocks, rank):
    n_dp = len(a_list)
    width = x.shape[1] + c.shape[1]
    return pl.pallas_call(
        functools.partial(low_kernel, n_dp, rank, blocks),
        in_specs=[SMEM] * 3 + [VMEM] * (2 + 2 * n_dp),
        out_specs=VMEM,
        out_shape=shaped((LIVE, 2 * rank), BF16),
        compiler_params=params(24),
        cost_estimate=cost(4 * LIVE * rank * n_dp * width, 2 * LIVE * width + 4 * rank * n_dp * width),
        name="low_part",
    )(dp, fill, tenant, x, c, *a_list, *b_list)


def doubled(low, lane, rank):
    turned = pltpu.roll(low, rank, 1)
    return jnp.where(lane < rank, low, turned), jnp.where(lane < rank, turned, low)


def grad_kernel(n_dp, n_t, rank, blocks, dp_ref, fill_ref, tenant_ref, x_ref, c_ref, *refs):
    lows, low_ref, own_ref, sends = refs[:n_t], refs[n_t], refs[n_t + 1], refs[n_t + 2 :]
    lanes = 2 * rank
    feat = x_ref.shape[1]
    total = lows[0][...].astype(F32)
    for ref in lows[1:]:
        total = total + ref[...].astype(F32)
    low_ref[...] = total.astype(BF16)
    total = total.astype(BF16).astype(F32)
    tenant = tenant_lanes(fill_ref, tenant_ref, blocks, lanes)
    lane = lax.broadcasted_iota(I32, (LIVE, lanes), 1)
    low_in, low_grad = doubled(total, lane, rank)
    for s in range(n_dp):
        mask = owner_mask(tenant, lane, (dp_ref[0] + s) % n_dp, rank)
        target = own_ref if s == 0 else sends[s - 1]
        grad_t = jnp.transpose(jnp.where(mask, ADAPTER_SCALE * low_grad, 0.0)).astype(BF16)
        in_t = jnp.transpose(jnp.where(mask, ADAPTER_SCALE * low_in, 0.0)).astype(BF16)
        target[:, :feat] = dot(grad_t, x_ref[...]).astype(target.dtype)
        target[:, feat:] = dot(in_t, c_ref[...]).astype(target.dtype)


def grads(dp, fill, tenant, x, c, lows, n_dp, blocks, rank):
    n_t = len(lows)
    width = x.shape[1] + c.shape[1]
    return pl.pallas_call(
        functools.partial(grad_kernel, n_dp, n_t, rank, blocks),
        in_specs=[SMEM] * 3 + [VMEM] * (2 + n_t),
        out_specs=[VMEM] * (1 + n_dp),
        out_shape=[shaped((LIVE, 2 * rank), BF16), shaped((2 * rank, width), F32)]
        + [shaped((2 * rank, width), BF16)] * (n_dp - 1),
        compiler_params=params(32),
        cost_estimate=cost(4 * LIVE * rank * n_dp * width, 2 * LIVE * width + 4 * rank * n_dp * width),
        name="grads",
    )(dp, fill, tenant, x, c, *lows)


def panel_kernel(count, place_ref, *refs):
    xs, others = refs[:count], refs[count : 2 * count]
    pieces, y_ref, y_other_ref = refs[2 * count : 3 * count], refs[3 * count], refs[3 * count + 1]
    for part, out in ((xs, y_ref), (others, y_other_ref)):
        total = dot(part[0][...], pieces[0][...])
        for a, w in zip(part[1:], pieces[1:]):
            total = total + dot(a[...], w[...])
        out[...] = total.astype(BF16)


def panel_product(place, x, x_other, pieces):
    count = len(pieces)
    deep, half = pieces[0].shape
    x_specs = [pl.BlockSpec((LIVE, deep), functools.partial(lambda m, i, place: (0, place[0] ^ m), m)) for m in range(count)]
    whole = lambda i, place: (0, 0)
    return pl.pallas_call(
        functools.partial(panel_kernel, count),
        grid_spec=pltpu.PrefetchScalarGridSpec(
            num_scalar_prefetch=1,
            grid=(1,),
            in_specs=x_specs * 2 + [pl.BlockSpec((deep, half), whole)] * count,
            out_specs=[pl.BlockSpec((LIVE, half), whole)] * 2,
        ),
        out_shape=[shaped((LIVE, half), BF16)] * 2,
        compiler_params=params(24),
        cost_estimate=cost(4 * LIVE * count * deep * half, 4 * LIVE * count * deep + 2 * count * deep * half),
        name="panel",
    )(place, *([x] * count), *([x_other] * count), *pieces)


def base_kernel(n_dp, rank, blocks, at_ref, dp_ref, fill_ref, tenant_ref, x_ref, w_ref, low_ref, *refs):
    b_refs, out_ref = refs[:n_dp], refs[n_dp]
    lanes = 2 * rank
    tenant = tenant_lanes(fill_ref, tenant_ref, blocks, lanes)
    lane = lax.broadcasted_iota(I32, (LIVE, lanes), 1)
    low_in, _ = doubled(low_ref[...].astype(F32), lane, rank)
    total = dot(x_ref[...], w_ref[...])
    for s in range(n_dp):
        mask = owner_mask(tenant, lane, (dp_ref[0] + n_dp - s) % n_dp, rank)
        total = total + dot(jnp.where(mask, ADAPTER_SCALE * low_in, 0.0).astype(BF16), b_refs[s][...])
    out_ref[...] = total


def base_product(at, dp, fill, tenant, x, base_weight, low, b_list, blocks, rank):
    n_dp = len(b_list)
    feat, cols = x.shape[1], base_weight.shape[1]
    whole = lambda i, at: (0, 0)
    return pl.pallas_call(
        functools.partial(base_kernel, n_dp, rank, blocks),
        grid_spec=pltpu.PrefetchScalarGridSpec(
            num_scalar_prefetch=1,
            grid=(1,),
            in_specs=[SMEM] * 3
            + [pl.BlockSpec((LIVE, feat), whole), pl.BlockSpec((feat, cols), lambda i, at: (at[0], 0)), pl.BlockSpec((LIVE, 2 * rank), whole)]
            + [pl.BlockSpec((2 * rank, cols), whole)] * n_dp,
            out_specs=pl.BlockSpec((LIVE, cols), whole),
        ),
        out_shape=shaped((LIVE, cols), F32),
        compiler_params=params(24),
        cost_estimate=cost(2 * LIVE * feat * cols, 2 * feat * (LIVE + cols) + 4 * LIVE * cols),
        name="base",
    )(at, dp, fill, tenant, x, base_weight, low, *b_list)


def out_kernel(count, blocks, block, core_ref, fill_ref, base_ref, *refs):
    owns, others, out_ref, held = refs[:count], refs[count : 2 * count], refs[2 * count], refs[2 * count + 1]
    half = owns[0].shape[1]

    def total(parts):
        value = parts[0][...].astype(F32)
        for part in parts[1:]:
            value = value + part[...].astype(F32)
        return value

    own, other = total(owns), total(others)
    first = core_ref[0] == 0
    held[:, :half] = (base_ref[:, :half] + jnp.where(first, own, other)).astype(BF16)
    held[:, half:] = (base_ref[:, half:] + jnp.where(first, other, own)).astype(BF16)
    row = lax.broadcasted_iota(I32, (block, LIVE), 0)
    col = lax.broadcasted_iota(I32, (block, LIVE), 1)
    for b, start in enumerate(starts_of(fill_ref, blocks)):
        hit = (col == row + start) & (row < fill_ref[0, b])
        pick = jnp.where(hit, 1.0, 0.0).astype(BF16)
        out_ref[b * block : (b + 1) * block, :] = dot(pick, held[...]).astype(BF16)


def finish(core, fill, base, owns, others, rows, blocks):
    cols = base.shape[1]
    count = len(owns)
    return pl.pallas_call(
        functools.partial(out_kernel, count, blocks, rows // blocks),
        in_specs=[SMEM] * 2 + [VMEM] * (1 + 2 * count),
        out_specs=VMEM,
        out_shape=shaped((rows, cols), BF16),
        scratch_shapes=[pltpu.VMEM((LIVE, cols), BF16)],
        compiler_params=params(24),
        cost_estimate=cost(2 * LIVE * rows * cols, 4 * LIVE * cols + 2 * LIVE * cols * count + 2 * rows * cols),
        name="finish",
    )(core, fill, base, *owns, *others)


def body(sizes, tokens, base_weight, adapter_a, adapter_b, cotangent, block_tenant_index, block_fill):
    n_t, n_dp, n_pipe = sizes["tensor"], sizes["dp"], sizes["pipe"]
    planes = sizes["groups"] * n_dp
    rows, feat = tokens.shape
    cols = base_weight.shape[1]
    half = cols // n_pipe
    blocks = block_tenant_index.shape[0]
    pair, rank = adapter_a.shape[:2]
    me_t, me_pipe, me_dp = lax.axis_index("tensor"), lax.axis_index("pipe"), lax.axis_index("dp")
    q = lax.axis_index("groups") * n_dp + me_dp
    part_rows = feat // planes
    scalar = lambda v: v.astype(I32).reshape(1)
    dp, core, at, place = scalar(me_dp), scalar(me_pipe), scalar(me_t), scalar(q)

    received = []
    for s in range(1, n_t):
        k = (me_t + s) % n_t
        share = lax.dynamic_slice(base_weight, (k * feat + q * part_rows, me_pipe * half), (part_rows, half))
        received.append(shift(share, "tensor", n_t, s))

    own_a, own_b = adapter_a.reshape(pair * rank, feat), adapter_b.reshape(pair * rank, cols)
    a_list = [own_a] + [shift(own_a, "dp", n_dp, s) for s in range(1, n_dp)]
    b_list = [own_b] + [shift(own_b, "dp", n_dp, s) for s in range(1, n_dp)]

    x, c = pack(block_fill, tokens, cotangent, blocks)
    x_other = flip(x, "pipe", n_pipe, 1)

    low = low_part(dp, block_fill, block_tenant_index, x, c, a_list, b_list, blocks, rank)
    lows = [low] + [shift(low, "tensor", n_t, s) for s in range(1, n_t)]
    low_sum, mine, *sends = grads(dp, block_fill, block_tenant_index, x, c, lows, n_dp, blocks, rank)
    for s in range(1, n_dp):
        mine = mine + shift(sends[s - 1], "dp", n_dp, s).astype(F32)
    mine = mine + flip(mine.astype(BF16), "pipe", n_pipe, 1).astype(F32)
    down_out = mine[:, :feat].reshape(pair, rank, feat)
    up_out = mine[:, feat:].reshape(pair, rank, cols)

    owns, others = [], []
    for s in range(1, n_t):
        if planes == 4:
            pieces = [received[s - 1]] + [flip(received[s - 1], ("groups", "dp"), planes, m) for m in range(1, planes)]
            y, y_other = panel_product(place, x, x_other, pieces)
        else:
            panel = lax.all_gather(received[s - 1], ("groups", "dp"), axis=0, tiled=True)
            y, y_other = panel_product(jnp.zeros_like(place), x, x_other, [panel])
        pairs = [
            (i * n_pipe + p, ((i - s) % n_t) * n_pipe + (p ^ 1)) for i in range(n_t) for p in range(n_pipe)
        ]
        owns.append(shift(y, "tensor", n_t, -s))
        others.append(lax.ppermute(y_other, ("tensor", "pipe"), pairs))
    base = base_product(at, dp, block_fill, block_tenant_index, x, base_weight, low_sum, b_list, blocks, rank)
    out = finish(core, block_fill, base, owns, others, rows, blocks)
    return out, down_out, up_out


def solution(mesh):
    placed = (
        P(("groups", "dp", "pipe"), "tensor"),
        P(None, "tensor"),
        P(("groups", "dp"), None, "tensor"),
        P(("groups", "dp"), None, "tensor"),
        P(("groups", "dp", "pipe"), "tensor"),
        P(("groups", "dp", "pipe")),
        P(("groups", "dp", "pipe"), None),
    )
    return jax.shard_map(
        functools.partial(body, dict(mesh.shape)),
        mesh=mesh,
        in_specs=placed,
        out_specs=(
            P(("groups", "dp", "pipe"), "tensor"),
            P(("groups", "dp"), None, "tensor"),
            P(("groups", "dp"), None, "tensor"),
        ),
        check_vma=False,
    )
```

```python
import functools

import jax
import jax.numpy as jnp
from jax import lax
from jax.experimental import pallas as pl
from jax.experimental.pallas import tpu as pltpu
from jax.sharding import PartitionSpec as P

ADAPTER_SCALE = 2.0
LIVE = 512
BF16 = jnp.bfloat16
F32 = jnp.float32
I32 = jnp.int32
MIB = 1 << 20
SMEM = pl.BlockSpec(memory_space=pltpu.SMEM)
VMEM = pl.BlockSpec(memory_space=pltpu.VMEM)


def shaped(shape, dtype):
    return jax.ShapeDtypeStruct(shape, dtype)


def dot(a, b, contract=(1, 0)):
    return lax.dot_general(a, b, ((contract[0:1], contract[1:2]), ((), ())), preferred_element_type=F32)


def shift(x, name, count, step):
    return lax.ppermute(x, name, [(i, (i + step) % count) for i in range(count)])


def flip(x, names, count, mask):
    return lax.ppermute(x, names, [(i, i ^ mask) for i in range(count)])


def params(mib):
    return pltpu.CompilerParams(vmem_limit_bytes=mib * MIB)


def cost(flops, bytes_accessed):
    return pl.CostEstimate(flops=1, bytes_accessed=1, transcendentals=0)


def after(x, *others):
    return lax.optimization_barrier((x, *others))[0]


def starts_of(fill_ref, blocks):
    starts, at = [], jnp.int32(0)
    for b in range(blocks):
        starts.append(at)
        at = at + fill_ref[0, b]
    return starts


def tenant_lanes(fill_ref, tenant_ref, blocks, lanes):
    row = lax.broadcasted_iota(I32, (LIVE, lanes), 0)
    tenant = jnp.zeros((LIVE, lanes), I32)
    for b, start in enumerate(starts_of(fill_ref, blocks)):
        tenant = jnp.where(row >= start, tenant_ref[b], tenant)
    return tenant


def shares_kernel(count, at_ref, w_ref, a_ref, b_ref, *refs):
    outs, both, sems = refs[:count], refs[count], refs[count + 1]
    deep, half = outs[0].shape
    feat = a_ref.shape[1]
    col = pl.multiple_of(at_ref[count], 128)
    copies = []
    for s in range(count):
        source = w_ref.at[pl.ds(pl.multiple_of(at_ref[s], 16), deep), pl.ds(col, half)]
        copies.append(pltpu.make_async_copy(source, outs[s], sems.at[s]))
    copies.append(pltpu.make_async_copy(a_ref, both.at[:, :feat], sems.at[count]))
    copies.append(pltpu.make_async_copy(b_ref, both.at[:, feat:], sems.at[count + 1]))
    for copy in copies:
        copy.start()
    for copy in copies:
        copy.wait()


def shares_of(rows_at, col_at, base_weight, a, b, deep, half):
    if half % 128 or deep % 16:
        blocks = [lax.dynamic_slice(base_weight, (row, col_at), (deep, half)) for row in rows_at]
        return blocks, jnp.concatenate([a, b], axis=1)
    count = len(rows_at)
    shapes = [shaped((deep, half), BF16)] * count + [shaped((a.shape[0], a.shape[1] + b.shape[1]), BF16)]
    *blocks, both = pl.pallas_call(
        functools.partial(shares_kernel, count),
        in_specs=[SMEM] + [pl.BlockSpec(memory_space=pl.ANY)] * 3,
        out_specs=[VMEM] * (count + 1),
        out_shape=shapes,
        scratch_shapes=[pltpu.SemaphoreType.DMA((count + 2,))],
        compiler_params=params(8),
        cost_estimate=cost(0, 4 * (count * deep * half + shapes[-1].size)),
        name="shares",
    )(jnp.stack([*rows_at, col_at]).astype(I32), base_weight, a, b)
    return blocks, both


def pack_kernel(blocks, block, fill_ref, tok_ref, cot_ref, x_ref, c_ref, pick):
    @pl.when(pl.program_id(0) == 0)
    def _():
        row = lax.broadcasted_iota(I32, (LIVE, block), 0)
        col = lax.broadcasted_iota(I32, (LIVE, block), 1)
        for b, start in enumerate(starts_of(fill_ref, blocks)):
            hit = (row == col + start) & (col < fill_ref[0, b])
            pick[:, b * block : (b + 1) * block] = jnp.where(hit, 1.0, 0.0).astype(BF16)
        c_ref[...] = dot(pick[...], cot_ref[...]).astype(BF16)

    x_ref[...] = dot(pick[...], tok_ref[...]).astype(BF16)


def pack(fill, tokens, cotangent, blocks):
    rows, feat = tokens.shape
    cols = cotangent.shape[1]
    steps = 4 if feat % 512 == 0 else 1
    wide = feat // steps
    return pl.pallas_call(
        functools.partial(pack_kernel, blocks, rows // blocks),
        grid=(steps,),
        in_specs=[SMEM, pl.BlockSpec((rows, wide), lambda i: (0, i)), pl.BlockSpec((rows, cols), lambda i: (0, 0))],
        out_specs=[pl.BlockSpec((LIVE, wide), lambda i: (0, i)), pl.BlockSpec((LIVE, cols), lambda i: (0, 0))],
        out_shape=[shaped((LIVE, feat), BF16), shaped((LIVE, cols), BF16)],
        scratch_shapes=[pltpu.VMEM((LIVE, rows), BF16)],
        compiler_params=params(24),
        cost_estimate=cost(2 * LIVE * rows * (feat + cols), 2 * (LIVE + rows) * (feat + cols)),
        name="pack",
    )(fill, tokens, cotangent)


def owner_mask(tenant, lane, owner, rank):
    return tenant == 2 * owner + (lane >= rank).astype(I32)


def low_kernel(n_dp, rank, blocks, dp_ref, fill_ref, tenant_ref, x_ref, c_ref, *refs):
    ab_refs, out_ref = refs[:n_dp], refs[n_dp]
    feat = x_ref.shape[1]
    lanes = 2 * rank
    tenant = tenant_lanes(fill_ref, tenant_ref, blocks, lanes)
    lane = lax.broadcasted_iota(I32, (LIVE, lanes), 1)
    low_in = jnp.zeros((LIVE, lanes), F32)
    low_grad = jnp.zeros((LIVE, lanes), F32)
    for s in range(n_dp):
        mask = owner_mask(tenant, lane, (dp_ref[0] + n_dp - s) % n_dp, rank)
        low_in = low_in + jnp.where(mask, dot(x_ref[...], ab_refs[s][:, :feat], (1, 1)), 0.0)
        low_grad = low_grad + jnp.where(mask, dot(c_ref[...], ab_refs[s][:, feat:], (1, 1)), 0.0)
    low_in = low_in + pltpu.roll(low_in, rank, 1)
    low_grad = low_grad + pltpu.roll(low_grad, rank, 1)
    out_ref[...] = jnp.where(lane < rank, low_in, low_grad).astype(BF16)


def low_part(dp, fill, tenant, x, c, ab_list, blocks, rank):
    n_dp = len(ab_list)
    width = x.shape[1] + c.shape[1]
    return pl.pallas_call(
        functools.partial(low_kernel, n_dp, rank, blocks),
        in_specs=[SMEM] * 3 + [VMEM] * (2 + n_dp),
        out_specs=VMEM,
        out_shape=shaped((LIVE, 2 * rank), BF16),
        compiler_params=params(24),
        cost_estimate=cost(4 * LIVE * rank * n_dp * width, 2 * LIVE * width + 4 * rank * n_dp * width),
        name="low_part",
    )(dp, fill, tenant, x, c, *ab_list)


def doubled(low, lane, rank):
    turned = pltpu.roll(low, rank, 1)
    return jnp.where(lane < rank, low, turned), jnp.where(lane < rank, turned, low)


def grad_kernel(n_dp, n_t, rank, blocks, dp_ref, fill_ref, tenant_ref, x_ref, c_ref, *refs):
    lows, low_ref, own_ref, sends = refs[:n_t], refs[n_t], refs[n_t + 1], refs[n_t + 2 :]
    lanes = 2 * rank
    feat = x_ref.shape[1]
    total = lows[0][...].astype(F32)
    for ref in lows[1:]:
        total = total + ref[...].astype(F32)
    low_ref[...] = total.astype(BF16)
    total = total.astype(BF16).astype(F32)
    tenant = tenant_lanes(fill_ref, tenant_ref, blocks, lanes)
    lane = lax.broadcasted_iota(I32, (LIVE, lanes), 1)
    low_in, low_grad = doubled(total, lane, rank)
    for s in range(n_dp):
        mask = owner_mask(tenant, lane, (dp_ref[0] + s) % n_dp, rank)
        target = own_ref if s == 0 else sends[s - 1]
        grad_t = jnp.transpose(jnp.where(mask, ADAPTER_SCALE * low_grad, 0.0)).astype(BF16)
        in_t = jnp.transpose(jnp.where(mask, ADAPTER_SCALE * low_in, 0.0)).astype(BF16)
        target[:, :feat] = dot(grad_t, x_ref[...]).astype(target.dtype)
        target[:, feat:] = dot(in_t, c_ref[...]).astype(target.dtype)


def grads(dp, fill, tenant, x, c, lows, n_dp, blocks, rank):
    n_t = len(lows)
    width = x.shape[1] + c.shape[1]
    return pl.pallas_call(
        functools.partial(grad_kernel, n_dp, n_t, rank, blocks),
        in_specs=[SMEM] * 3 + [VMEM] * (2 + n_t),
        out_specs=[VMEM] * (1 + n_dp),
        out_shape=[shaped((LIVE, 2 * rank), BF16), shaped((2 * rank, width), F32)]
        + [shaped((2 * rank, width), BF16)] * (n_dp - 1),
        compiler_params=params(32),
        cost_estimate=cost(4 * LIVE * rank * n_dp * width, 2 * LIVE * width + 4 * rank * n_dp * width),
        name="grads",
    )(dp, fill, tenant, x, c, *lows)


def panel_kernel(order, sources, place_ref, *refs):
    pieces, outs = refs[sources:-sources], refs[-sources:]
    for source, out in zip(refs[:sources], outs):
        total, at = None, 0
        deep = source.shape[1] // len(order)
        for piece in pieces:
            for i in range(piece.shape[0] // deep):
                col = pl.multiple_of((place_ref[0] ^ order[at]) * deep, min(deep, 128))
                term = dot(source[:, pl.ds(col, deep)], piece[i * deep : (i + 1) * deep, :])
                total = term if total is None else total + term
                at += 1
        out[...] = total.astype(BF16)


def panel_product(order, place, sources, pieces):
    feat, half = sources[0].shape[1], pieces[0].shape[1]
    count = len(sources)
    return pl.pallas_call(
        functools.partial(panel_kernel, order, count),
        in_specs=[SMEM] + [VMEM] * (count + len(pieces)),
        out_specs=[VMEM] * count,
        out_shape=[shaped((LIVE, half), BF16)] * count,
        compiler_params=params(24),
        cost_estimate=cost(2 * count * LIVE * feat * half, 2 * count * LIVE * feat + 2 * feat * half),
        name="panel",
    )(place, *sources, *pieces)


def settle_kernel(own_ref, got_ref, down_ref, up_ref):
    pair, rank, feat = down_ref.shape
    for t in range(pair):
        total = own_ref[t * rank : (t + 1) * rank, :] + got_ref[t * rank : (t + 1) * rank, :].astype(F32)
        down_ref[t], up_ref[t] = total[:, :feat], total[:, feat:]


def settle(own, got, pair, feat):
    rank, width = own.shape[0] // pair, own.shape[1]
    return pl.pallas_call(
        settle_kernel,
        in_specs=[VMEM] * 2,
        out_specs=[VMEM] * 2,
        out_shape=[shaped((pair, rank, feat), F32), shaped((pair, rank, width - feat), F32)],
        compiler_params=params(16),
        cost_estimate=cost(own.size, 10 * own.size),
        name="settle",
    )(own, got)


def base_kernel(n_dp, rank, blocks, at_ref, dp_ref, fill_ref, tenant_ref, x_ref, w_ref, low_ref, *refs):
    ab_refs, out_ref = refs[:n_dp], refs[n_dp]
    lanes = 2 * rank
    tenant = tenant_lanes(fill_ref, tenant_ref, blocks, lanes)
    lane = lax.broadcasted_iota(I32, (LIVE, lanes), 1)
    low_in, _ = doubled(low_ref[...].astype(F32), lane, rank)
    total = dot(x_ref[...], w_ref[...])
    for s in range(n_dp):
        mask = owner_mask(tenant, lane, (dp_ref[0] + n_dp - s) % n_dp, rank)
        total = total + dot(jnp.where(mask, ADAPTER_SCALE * low_in, 0.0).astype(BF16), ab_refs[s][...])
    out_ref[...] = total


def base_product(at, dp, fill, tenant, x, base_weight, low, ab_list, blocks, rank):
    n_dp = len(ab_list)
    feat, cols = x.shape[1], base_weight.shape[1]
    whole = lambda i, at: (0, 0)
    return pl.pallas_call(
        functools.partial(base_kernel, n_dp, rank, blocks),
        grid_spec=pltpu.PrefetchScalarGridSpec(
            num_scalar_prefetch=1,
            grid=(1,),
            in_specs=[SMEM] * 3
            + [pl.BlockSpec((LIVE, feat), whole), pl.BlockSpec((feat, cols), lambda i, at: (at[0], 0)), pl.BlockSpec((LIVE, 2 * rank), whole)]
            + [pl.BlockSpec((2 * rank, cols), lambda i, at: (0, feat // cols))] * n_dp,
            out_specs=pl.BlockSpec((LIVE, cols), whole),
        ),
        out_shape=shaped((LIVE, cols), F32),
        compiler_params=params(24),
        cost_estimate=cost(2 * LIVE * feat * cols, 2 * feat * (LIVE + cols) + 4 * LIVE * cols),
        name="base",
    )(at, dp, fill, tenant, x, base_weight, low, *ab_list)


def out_kernel(count, blocks, block, core_ref, fill_ref, base_ref, *refs):
    owns, others, out_ref, held = refs[:count], refs[count : 2 * count], refs[2 * count], refs[2 * count + 1]
    half = owns[0].shape[1]

    def total(parts):
        value = parts[0][...].astype(F32)
        for part in parts[1:]:
            value = value + part[...].astype(F32)
        return value

    own, other = total(owns), total(others)
    first = core_ref[0] == 0
    held[:, :half] = (base_ref[:, :half] + jnp.where(first, own, other)).astype(BF16)
    held[:, half:] = (base_ref[:, half:] + jnp.where(first, other, own)).astype(BF16)
    row = lax.broadcasted_iota(I32, (block, LIVE), 0)
    col = lax.broadcasted_iota(I32, (block, LIVE), 1)
    for b, start in enumerate(starts_of(fill_ref, blocks)):
        hit = (col == row + start) & (row < fill_ref[0, b])
        pick = jnp.where(hit, 1.0, 0.0).astype(BF16)
        out_ref[b * block : (b + 1) * block, :] = dot(pick, held[...]).astype(BF16)


def finish(core, fill, base, owns, others, rows, blocks):
    cols = base.shape[1]
    count = len(owns)
    return pl.pallas_call(
        functools.partial(out_kernel, count, blocks, rows // blocks),
        in_specs=[SMEM] * 2 + [VMEM] * (1 + 2 * count),
        out_specs=VMEM,
        out_shape=shaped((rows, cols), BF16),
        scratch_shapes=[pltpu.VMEM((LIVE, cols), BF16)],
        compiler_params=params(24),
        cost_estimate=cost(2 * LIVE * rows * cols, 4 * LIVE * cols + 2 * LIVE * cols * count + 2 * rows * cols),
        name="finish",
    )(core, fill, base, *owns, *others)


def body(sizes, tokens, base_weight, adapter_a, adapter_b, cotangent, block_tenant_index, block_fill):
    n_t, n_dp, n_pipe = sizes["tensor"], sizes["dp"], sizes["pipe"]
    planes = sizes["groups"] * n_dp
    rows, feat = tokens.shape
    cols = base_weight.shape[1]
    half = cols // n_pipe
    blocks = block_tenant_index.shape[0]
    pair, rank = adapter_a.shape[:2]
    me_t, me_pipe, me_dp = lax.axis_index("tensor"), lax.axis_index("pipe"), lax.axis_index("dp")
    q = lax.axis_index("groups") * n_dp + me_dp
    part_rows = feat // planes
    scalar = lambda v: v.astype(I32).reshape(1)
    dp, core, at, place = scalar(me_dp), scalar(me_pipe), scalar(me_t), scalar(q)

    steps = list(range(1, n_t))
    own_a, own_b = adapter_a.reshape(pair * rank, feat), adapter_b.reshape(pair * rank, cols)
    rows_at = [(me_t + s) % n_t * feat + q * part_rows for s in steps]
    blocks_w, own_ab = shares_of(rows_at, me_pipe * half, base_weight, own_a, own_b, part_rows, half)
    shares = dict(zip(steps, blocks_w))
    lead = n_t // 2
    received = {lead: shift(shares[lead], "tensor", n_t, lead)}
    ab_list = [own_ab] + [shift(own_ab, "dp", n_dp, s) for s in range(1, n_dp)]

    fill = after(block_fill, shares[lead])
    x, c = pack(fill, tokens, cotangent, blocks)
    rest = [s for s in steps if s != lead][::-1]
    for s in rest:
        received[s] = shift(shares[s], "tensor", n_t, s)

    def gathered(piece, first, low=None):
        if planes != 4:
            return [lax.all_gather(piece, ("groups", "dp"), axis=0, tiled=True)], [0]
        if first is None:
            near = [flip(piece, ("groups", "dp"), planes, m) for m in (1, 2)]
            return [piece, *near, flip(after(piece, received[rest[0]]), ("groups", "dp"), planes, 3)], [0, 1, 2, 3]
        stack = jnp.concatenate([piece, flip(piece, ("groups", "dp"), planes, first)], axis=0)
        stack = after(stack, low)
        return [stack, flip(stack, ("groups", "dp"), planes, 3 - first)], [0, first, 3 - first, 3]

    def send_back(s, y, y_other):
        pairs = [(i * n_pipe + p, ((i - s) % n_t) * n_pipe + (p ^ 1)) for i in range(n_t) for p in range(n_pipe)]
        return shift(y, "tensor", n_t, -s), lax.ppermute(y_other, ("tensor", "pipe"), pairs)

    low = low_part(dp, block_fill, block_tenant_index, x, c, ab_list, blocks, rank)
    panel_at = place if planes == 4 else jnp.zeros_like(place)
    pieces, order = gathered(received[lead], None)
    x_other = flip(after(x, received[lead]), "pipe", n_pipe, 1)
    pieces = [after(pieces[0], *[received[s] for s in rest]), *pieces[1:]]
    (y,) = panel_product(order, panel_at, [x], pieces)
    received.update((s, after(received[s], y)) for s in rest)
    (y_other,) = panel_product(order, panel_at, [x_other], pieces)
    owns, others = zip(send_back(lead, y, y_other))

    low = after(low, x_other, y, *[received[s] for s in rest])
    mask = 1
    while 2 * mask < n_t:
        low = (low.astype(F32) + flip(low, "tensor", n_t, mask).astype(F32)).astype(BF16)
        mask *= 2
    final_low = after(low, owns[0], y_other)
    lows = [final_low] + ([flip(final_low, "tensor", n_t, mask)] if n_t > 1 else [])

    last = []
    for i, s in enumerate(rest):
        pieces, order = gathered(received[s], 1 + i % 2, low)
        last += pieces
        y, y_other = panel_product(order, panel_at, [x, x_other], pieces)
        if i > 0:
            y, y_other = lax.optimization_barrier((y, y_other, owns[0], others[0]))[:2]
        own, other = send_back(s, y, y_other)
        owns, others = [*owns, own], [*others, other]

    low_sum, mine, *sends = grads(dp, block_fill, block_tenant_index, x, c, lows, n_dp, blocks, rank)
    for s in range(1, n_dp):
        mine = mine + after(shift(after(sends[s - 1], *last), "dp", n_dp, s), y).astype(F32)
    down_out, up_out = settle(mine, flip(mine.astype(BF16), "pipe", n_pipe, 1), pair, feat)

    base = base_product(at, dp, block_fill, block_tenant_index, x, base_weight, low_sum, ab_list, blocks, rank)
    out = finish(core, block_fill, base, owns, others, rows, blocks)
    return out, down_out, up_out


def solution(mesh):
    placed = (
        P(("groups", "dp", "pipe"), "tensor"),
        P(None, "tensor"),
        P(("groups", "dp"), None, "tensor"),
        P(("groups", "dp"), None, "tensor"),
        P(("groups", "dp", "pipe"), "tensor"),
        P(("groups", "dp", "pipe")),
        P(("groups", "dp", "pipe"), None),
    )
    return jax.shard_map(
        functools.partial(body, dict(mesh.shape)),
        mesh=mesh,
        in_specs=placed,
        out_specs=(
            P(("groups", "dp", "pipe"), "tensor"),
            P(("groups", "dp"), None, "tensor"),
            P(("groups", "dp"), None, "tensor"),
        ),
        check_vma=False,
    )
```

```python
import functools

import jax
import jax.numpy as jnp
from jax import lax
from jax.experimental import pallas as pl
from jax.experimental.pallas import tpu as pltpu
from jax.sharding import PartitionSpec as P

ADAPTER_SCALE = 2.0
LIVE = 512
BF16 = jnp.bfloat16
F32 = jnp.float32
I32 = jnp.int32
MIB = 1 << 20
SMEM = pl.BlockSpec(memory_space=pltpu.SMEM)
VMEM = pl.BlockSpec(memory_space=pltpu.VMEM)


def shaped(shape, dtype):
    return jax.ShapeDtypeStruct(shape, dtype)


def dot(a, b, contract=(1, 0)):
    return lax.dot_general(a, b, ((contract[0:1], contract[1:2]), ((), ())), preferred_element_type=F32)


def shift(x, name, count, step):
    return lax.ppermute(x, name, [(i, (i + step) % count) for i in range(count)])


def flip(x, names, count, mask):
    return lax.ppermute(x, names, [(i, i ^ mask) for i in range(count)])


def params(mib):
    return pltpu.CompilerParams(vmem_limit_bytes=mib * MIB)


def cost(flops, bytes_accessed):
    return pl.CostEstimate(flops=1, bytes_accessed=1, transcendentals=0)


def after(x, *others):
    return lax.optimization_barrier((x, *others))[0]


def starts_of(fill_ref, blocks):
    starts, at = [], jnp.int32(0)
    for b in range(blocks):
        starts.append(at)
        at = at + fill_ref[0, b]
    return starts


def tenant_lanes(fill_ref, tenant_ref, blocks, lanes):
    row = lax.broadcasted_iota(I32, (LIVE, lanes), 0)
    tenant = jnp.zeros((LIVE, lanes), I32)
    for b, start in enumerate(starts_of(fill_ref, blocks)):
        tenant = jnp.where(row >= start, tenant_ref[b], tenant)
    return tenant


def shares_kernel(count, at_ref, w_ref, a_ref, b_ref, *refs):
    outs, both, sems = refs[:count], refs[count], refs[count + 1]
    deep, half = outs[0].shape
    feat = a_ref.shape[1]
    col = pl.multiple_of(at_ref[count], 128)
    copies = []
    for s in range(count):
        source = w_ref.at[pl.ds(pl.multiple_of(at_ref[s], 16), deep), pl.ds(col, half)]
        copies.append(pltpu.make_async_copy(source, outs[s], sems.at[s]))
    copies.append(pltpu.make_async_copy(a_ref, both.at[:, :feat], sems.at[count]))
    copies.append(pltpu.make_async_copy(b_ref, both.at[:, feat:], sems.at[count + 1]))
    for copy in copies:
        copy.start()
    for copy in copies:
        copy.wait()


def shares_of(rows_at, col_at, base_weight, a, b, deep, half):
    if half % 128 or deep % 16:
        blocks = [lax.dynamic_slice(base_weight, (row, col_at), (deep, half)) for row in rows_at]
        return blocks, jnp.concatenate([a, b], axis=1)
    count = len(rows_at)
    shapes = [shaped((deep, half), BF16)] * count + [shaped((a.shape[0], a.shape[1] + b.shape[1]), BF16)]
    *blocks, both = pl.pallas_call(
        functools.partial(shares_kernel, count),
        in_specs=[SMEM] + [pl.BlockSpec(memory_space=pl.ANY)] * 3,
        out_specs=[VMEM] * (count + 1),
        out_shape=shapes,
        scratch_shapes=[pltpu.SemaphoreType.DMA((count + 2,))],
        compiler_params=params(56),
        cost_estimate=cost(0, 4 * (count * deep * half + shapes[-1].size)),
        name="shares",
    )(jnp.stack([*rows_at, col_at]).astype(I32), base_weight, a, b)
    return blocks, both


def pack_kernel(blocks, block, fill_ref, tok_ref, cot_ref, x_ref, c_ref, pick):
    @pl.when(pl.program_id(0) == 0)
    def _():
        row = lax.broadcasted_iota(I32, (LIVE, block), 0)
        col = lax.broadcasted_iota(I32, (LIVE, block), 1)
        for b, start in enumerate(starts_of(fill_ref, blocks)):
            hit = (row == col + start) & (col < fill_ref[0, b])
            pick[:, b * block : (b + 1) * block] = jnp.where(hit, 1.0, 0.0).astype(BF16)
        c_ref[...] = dot(pick[...], cot_ref[...]).astype(BF16)

    x_ref[...] = dot(pick[...], tok_ref[...]).astype(BF16)


def pack(fill, tokens, cotangent, blocks):
    rows, feat = tokens.shape
    cols = cotangent.shape[1]
    steps = 4 if feat % 512 == 0 else 1
    wide = feat // steps
    return pl.pallas_call(
        functools.partial(pack_kernel, blocks, rows // blocks),
        grid=(steps,),
        in_specs=[SMEM, pl.BlockSpec((rows, wide), lambda i: (0, i)), pl.BlockSpec((rows, cols), lambda i: (0, 0))],
        out_specs=[pl.BlockSpec((LIVE, wide), lambda i: (0, i)), pl.BlockSpec((LIVE, cols), lambda i: (0, 0))],
        out_shape=[shaped((LIVE, feat), BF16), shaped((LIVE, cols), BF16)],
        scratch_shapes=[pltpu.VMEM((LIVE, rows), BF16)],
        compiler_params=params(24),
        cost_estimate=cost(2 * LIVE * rows * (feat + cols), 2 * (LIVE + rows) * (feat + cols)),
        name="pack",
    )(fill, tokens, cotangent)


def owner_mask(tenant, lane, owner, rank):
    return tenant == 2 * owner + (lane >= rank).astype(I32)


def low_kernel(n_dp, rank, blocks, dp_ref, fill_ref, tenant_ref, x_ref, c_ref, *refs):
    ab_refs, out_ref = refs[:n_dp], refs[n_dp]
    feat = x_ref.shape[1]
    lanes = 2 * rank
    tenant = tenant_lanes(fill_ref, tenant_ref, blocks, lanes)
    lane = lax.broadcasted_iota(I32, (LIVE, lanes), 1)
    low_in = jnp.zeros((LIVE, lanes), F32)
    low_grad = jnp.zeros((LIVE, lanes), F32)
    for s in range(n_dp):
        mask = owner_mask(tenant, lane, (dp_ref[0] + n_dp - s) % n_dp, rank)
        low_in = low_in + jnp.where(mask, dot(x_ref[...], ab_refs[s][:, :feat], (1, 1)), 0.0)
        low_grad = low_grad + jnp.where(mask, dot(c_ref[...], ab_refs[s][:, feat:], (1, 1)), 0.0)
    low_in = low_in + pltpu.roll(low_in, rank, 1)
    low_grad = low_grad + pltpu.roll(low_grad, rank, 1)
    out_ref[...] = jnp.where(lane < rank, low_in, low_grad).astype(BF16)


def low_part(dp, fill, tenant, x, c, ab_list, blocks, rank):
    n_dp = len(ab_list)
    width = x.shape[1] + c.shape[1]
    return pl.pallas_call(
        functools.partial(low_kernel, n_dp, rank, blocks),
        in_specs=[SMEM] * 3 + [VMEM] * (2 + n_dp),
        out_specs=VMEM,
        out_shape=shaped((LIVE, 2 * rank), BF16),
        compiler_params=params(24),
        cost_estimate=cost(4 * LIVE * rank * n_dp * width, 2 * LIVE * width + 4 * rank * n_dp * width),
        name="low_part",
    )(dp, fill, tenant, x, c, *ab_list)


def doubled(low, lane, rank):
    turned = pltpu.roll(low, rank, 1)
    return jnp.where(lane < rank, low, turned), jnp.where(lane < rank, turned, low)


def grad_kernel(n_dp, n_t, rank, blocks, dp_ref, fill_ref, tenant_ref, x_ref, c_ref, *refs):
    lows, low_ref, own_ref, sends = refs[:n_t], refs[n_t], refs[n_t + 1], refs[n_t + 2 :]
    lanes = 2 * rank
    feat = x_ref.shape[1]
    total = lows[0][...].astype(F32)
    for ref in lows[1:]:
        total = total + ref[...].astype(F32)
    low_ref[...] = total.astype(BF16)
    total = total.astype(BF16).astype(F32)
    tenant = tenant_lanes(fill_ref, tenant_ref, blocks, lanes)
    lane = lax.broadcasted_iota(I32, (LIVE, lanes), 1)
    low_in, low_grad = doubled(total, lane, rank)
    for s in range(n_dp):
        mask = owner_mask(tenant, lane, (dp_ref[0] + s) % n_dp, rank)
        target = own_ref if s == 0 else sends[s - 1]
        grad_t = jnp.transpose(jnp.where(mask, ADAPTER_SCALE * low_grad, 0.0)).astype(BF16)
        in_t = jnp.transpose(jnp.where(mask, ADAPTER_SCALE * low_in, 0.0)).astype(BF16)
        target[:, :feat] = dot(grad_t, x_ref[...]).astype(target.dtype)
        target[:, feat:] = dot(in_t, c_ref[...]).astype(target.dtype)


def grads(dp, fill, tenant, x, c, lows, n_dp, blocks, rank):
    n_t = len(lows)
    width = x.shape[1] + c.shape[1]
    return pl.pallas_call(
        functools.partial(grad_kernel, n_dp, n_t, rank, blocks),
        in_specs=[SMEM] * 3 + [VMEM] * (2 + n_t),
        out_specs=[VMEM] * (1 + n_dp),
        out_shape=[shaped((LIVE, 2 * rank), BF16), shaped((2 * rank, width), F32)]
        + [shaped((2 * rank, width), BF16)] * (n_dp - 1),
        compiler_params=params(32),
        cost_estimate=cost(4 * LIVE * rank * n_dp * width, 2 * LIVE * width + 4 * rank * n_dp * width),
        name="grads",
    )(dp, fill, tenant, x, c, *lows)


def panel_kernel(order, sources, place_ref, *refs):
    pieces, outs = refs[sources:-sources], refs[-sources:]
    for source, out in zip(refs[:sources], outs):
        total, at = None, 0
        deep = source.shape[1] // len(order)
        for piece in pieces:
            for i in range(piece.shape[0] // deep):
                col = pl.multiple_of((place_ref[0] ^ order[at]) * deep, min(deep, 128))
                term = dot(source[:, pl.ds(col, deep)], piece[i * deep : (i + 1) * deep, :])
                total = term if total is None else total + term
                at += 1
        out[...] = total.astype(BF16)


def panel_product(order, place, sources, pieces):
    feat, half = sources[0].shape[1], pieces[0].shape[1]
    count = len(sources)
    return pl.pallas_call(
        functools.partial(panel_kernel, order, count),
        in_specs=[SMEM] + [VMEM] * (count + len(pieces)),
        out_specs=[VMEM] * count,
        out_shape=[shaped((LIVE, half), BF16)] * count,
        compiler_params=params(24),
        cost_estimate=cost(2 * count * LIVE * feat * half, 2 * count * LIVE * feat + 2 * feat * half),
        name="panel",
    )(place, *sources, *pieces)


def settle_kernel(own_ref, got_ref, down_ref, up_ref):
    pair, rank, feat = down_ref.shape
    for t in range(pair):
        total = own_ref[t * rank : (t + 1) * rank, :] + got_ref[t * rank : (t + 1) * rank, :].astype(F32)
        down_ref[t], up_ref[t] = total[:, :feat], total[:, feat:]


def settle(own, got, pair, feat):
    rank, width = own.shape[0] // pair, own.shape[1]
    return pl.pallas_call(
        settle_kernel,
        in_specs=[VMEM] * 2,
        out_specs=[VMEM] * 2,
        out_shape=[shaped((pair, rank, feat), F32), shaped((pair, rank, width - feat), F32)],
        compiler_params=params(16),
        cost_estimate=cost(own.size, 10 * own.size),
        name="settle",
    )(own, got)


def base_kernel(n_dp, rank, blocks, at_ref, dp_ref, fill_ref, tenant_ref, x_ref, w_ref, low_ref, *refs):
    ab_refs, out_ref = refs[:n_dp], refs[n_dp]
    lanes = 2 * rank
    tenant = tenant_lanes(fill_ref, tenant_ref, blocks, lanes)
    lane = lax.broadcasted_iota(I32, (LIVE, lanes), 1)
    low_in, _ = doubled(low_ref[...].astype(F32), lane, rank)
    total = dot(x_ref[...], w_ref[...])
    for s in range(n_dp):
        mask = owner_mask(tenant, lane, (dp_ref[0] + n_dp - s) % n_dp, rank)
        total = total + dot(jnp.where(mask, ADAPTER_SCALE * low_in, 0.0).astype(BF16), ab_refs[s][...])
    out_ref[...] = total


def base_product(at, dp, fill, tenant, x, base_weight, low, ab_list, blocks, rank):
    n_dp = len(ab_list)
    feat, cols = x.shape[1], base_weight.shape[1]
    whole = lambda i, at: (0, 0)
    return pl.pallas_call(
        functools.partial(base_kernel, n_dp, rank, blocks),
        grid_spec=pltpu.PrefetchScalarGridSpec(
            num_scalar_prefetch=1,
            grid=(1,),
            in_specs=[SMEM] * 3
            + [pl.BlockSpec((LIVE, feat), whole), pl.BlockSpec((feat, cols), lambda i, at: (at[0], 0)), pl.BlockSpec((LIVE, 2 * rank), whole)]
            + [pl.BlockSpec((2 * rank, cols), lambda i, at: (0, feat // cols))] * n_dp,
            out_specs=pl.BlockSpec((LIVE, cols), whole),
        ),
        out_shape=shaped((LIVE, cols), F32),
        compiler_params=params(24),
        cost_estimate=cost(2 * LIVE * feat * cols, 2 * feat * (LIVE + cols) + 4 * LIVE * cols),
        name="base",
    )(at, dp, fill, tenant, x, base_weight, low, *ab_list)


def out_kernel(count, blocks, block, core_ref, fill_ref, base_ref, *refs):
    owns, others, out_ref, held = refs[:count], refs[count : 2 * count], refs[2 * count], refs[2 * count + 1]
    half = owns[0].shape[1]

    def total(parts):
        value = parts[0][...].astype(F32)
        for part in parts[1:]:
            value = value + part[...].astype(F32)
        return value

    own, other = total(owns), total(others)
    first = core_ref[0] == 0
    held[:, :half] = (base_ref[:, :half] + jnp.where(first, own, other)).astype(BF16)
    held[:, half:] = (base_ref[:, half:] + jnp.where(first, other, own)).astype(BF16)
    row = lax.broadcasted_iota(I32, (block, LIVE), 0)
    col = lax.broadcasted_iota(I32, (block, LIVE), 1)
    for b, start in enumerate(starts_of(fill_ref, blocks)):
        hit = (col == row + start) & (row < fill_ref[0, b])
        pick = jnp.where(hit, 1.0, 0.0).astype(BF16)
        out_ref[b * block : (b + 1) * block, :] = dot(pick, held[...]).astype(BF16)


def finish(core, fill, base, owns, others, rows, blocks):
    cols = base.shape[1]
    count = len(owns)
    return pl.pallas_call(
        functools.partial(out_kernel, count, blocks, rows // blocks),
        in_specs=[SMEM] * 2 + [VMEM] * (1 + 2 * count),
        out_specs=VMEM,
        out_shape=shaped((rows, cols), BF16),
        scratch_shapes=[pltpu.VMEM((LIVE, cols), BF16)],
        compiler_params=params(24),
        cost_estimate=cost(2 * LIVE * rows * cols, 4 * LIVE * cols + 2 * LIVE * cols * count + 2 * rows * cols),
        name="finish",
    )(core, fill, base, *owns, *others)


def body(sizes, tokens, base_weight, adapter_a, adapter_b, cotangent, block_tenant_index, block_fill):
    n_t, n_dp, n_pipe = sizes["tensor"], sizes["dp"], sizes["pipe"]
    planes = sizes["groups"] * n_dp
    rows, feat = tokens.shape
    cols = base_weight.shape[1]
    half = cols // n_pipe
    blocks = block_tenant_index.shape[0]
    pair, rank = adapter_a.shape[:2]
    me_t, me_pipe, me_dp = lax.axis_index("tensor"), lax.axis_index("pipe"), lax.axis_index("dp")
    q = lax.axis_index("groups") * n_dp + me_dp
    part_rows = feat // planes
    scalar = lambda v: v.astype(I32).reshape(1)
    dp, core, at, place = scalar(me_dp), scalar(me_pipe), scalar(me_t), scalar(q)

    steps = list(range(1, n_t))
    own_a, own_b = adapter_a.reshape(pair * rank, feat), adapter_b.reshape(pair * rank, cols)
    rows_at = [(me_t + s) % n_t * feat + q * part_rows for s in steps]
    blocks_w, own_ab = shares_of(rows_at, me_pipe * half, base_weight, own_a, own_b, part_rows, half)
    shares = dict(zip(steps, blocks_w))
    lead = n_t // 2
    received = {lead: shift(shares[lead], "tensor", n_t, lead)}
    ab_list = [own_ab] + [shift(own_ab, "dp", n_dp, s) for s in range(1, n_dp)]

    fill = after(block_fill, shares[lead])
    x, c = pack(fill, tokens, cotangent, blocks)
    rest = [s for s in steps if s != lead][::-1]
    for s in rest:
        received[s] = shift(shares[s], "tensor", n_t, s)

    def gathered(piece, first):
        if planes != 4:
            return [lax.all_gather(piece, ("groups", "dp"), axis=0, tiled=True)], [0]
        if first is None:
            return [piece] + [flip(piece, ("groups", "dp"), planes, m) for m in range(1, 4)], [0, 1, 2, 3]
        stack = jnp.concatenate([piece, flip(piece, ("groups", "dp"), planes, first)], axis=0)
        return [stack, flip(stack, ("groups", "dp"), planes, 3 - first)], [0, first, 3 - first, 3]

    def send_back(s, y, y_other):
        pairs = [(i * n_pipe + p, ((i - s) % n_t) * n_pipe + (p ^ 1)) for i in range(n_t) for p in range(n_pipe)]
        return shift(y, "tensor", n_t, -s), lax.ppermute(y_other, ("tensor", "pipe"), pairs)

    low = low_part(dp, block_fill, block_tenant_index, x, c, ab_list, blocks, rank)
    panel_at = place if planes == 4 else jnp.zeros_like(place)
    pieces, order = gathered(received[lead], None)
    x_other = flip(after(x, *pieces, *received.values(), *ab_list[1:]), "pipe", n_pipe, 1)
    (y,) = panel_product(order, panel_at, [x], pieces)
    received.update((s, after(received[s], y)) for s in rest)
    (y_other,) = panel_product(order, panel_at, [x_other], pieces)
    owns, others = zip(send_back(lead, y, y_other))

    low = after(low, owns[0], y_other)
    mask = 1
    while 2 * mask < n_t:
        low = (low.astype(F32) + flip(low, "tensor", n_t, mask).astype(F32)).astype(BF16)
        mask *= 2
    lows = [low] + ([flip(low, "tensor", n_t, mask)] if n_t > 1 else [])

    last = []
    for i, s in enumerate(rest):
        pieces, order = gathered(received[s], 1 + i % 2)
        y, y_other = panel_product(order, panel_at, [x, x_other], pieces)
        last += [y, y_other]
        own, other = send_back(s, y, y_other)
        owns, others = [*owns, own], [*others, other]

    low_sum, mine, *sends = grads(dp, block_fill, block_tenant_index, x, c, lows, n_dp, blocks, rank)
    for s in range(1, n_dp):
        mine = mine + shift(after(sends[s - 1], *last, others[0]), "dp", n_dp, s).astype(F32)
    down_out, up_out = settle(mine, flip(after(mine.astype(BF16), *owns[1:], others[1]), "pipe", n_pipe, 1), pair, feat)

    base = base_product(at, dp, block_fill, block_tenant_index, x, base_weight, low_sum, ab_list, blocks, rank)
    out = finish(core, block_fill, base, owns, others, rows, blocks)
    return out, down_out, up_out


def solution(mesh):
    placed = (
        P(("groups", "dp", "pipe"), "tensor"),
        P(None, "tensor"),
        P(("groups", "dp"), None, "tensor"),
        P(("groups", "dp"), None, "tensor"),
        P(("groups", "dp", "pipe"), "tensor"),
        P(("groups", "dp", "pipe")),
        P(("groups", "dp", "pipe"), None),
    )
    return jax.shard_map(
        functools.partial(body, dict(mesh.shape)),
        mesh=mesh,
        in_specs=placed,
        out_specs=(
            P(("groups", "dp", "pipe"), "tensor"),
            P(("groups", "dp"), None, "tensor"),
            P(("groups", "dp"), None, "tensor"),
        ),
        check_vma=False,
    )
```

```python
import functools

import jax
import jax.numpy as jnp
from jax import lax
from jax.experimental import pallas as pl
from jax.experimental.pallas import tpu as pltpu
from jax.sharding import PartitionSpec as P

ADAPTER_SCALE = 2.0
LIVE = 512
BF16 = jnp.bfloat16
F32 = jnp.float32
I32 = jnp.int32
MIB = 1 << 20
SMEM = pl.BlockSpec(memory_space=pltpu.SMEM)
VMEM = pl.BlockSpec(memory_space=pltpu.VMEM)


def shaped(shape, dtype):
    return jax.ShapeDtypeStruct(shape, dtype)


def dot(a, b, contract=(1, 0)):
    return lax.dot_general(a, b, ((contract[0:1], contract[1:2]), ((), ())), preferred_element_type=F32)


def shift(x, name, count, step):
    return lax.ppermute(x, name, [(i, (i + step) % count) for i in range(count)])


def flip(x, names, count, mask):
    return lax.ppermute(x, names, [(i, i ^ mask) for i in range(count)])


def params(mib):
    return pltpu.CompilerParams(vmem_limit_bytes=mib * MIB)


def cost(flops, bytes_accessed):
    return pl.CostEstimate(flops=1, bytes_accessed=1, transcendentals=0)


def after(x, *others):
    return lax.optimization_barrier((x, *others))[0]


def starts_of(fill_ref, blocks):
    starts, at = [], jnp.int32(0)
    for b in range(blocks):
        starts.append(at)
        at = at + fill_ref[0, b]
    return starts


def tenant_lanes(fill_ref, tenant_ref, blocks, lanes):
    row = lax.broadcasted_iota(I32, (LIVE, lanes), 0)
    tenant = jnp.zeros((LIVE, lanes), I32)
    for b, start in enumerate(starts_of(fill_ref, blocks)):
        tenant = jnp.where(row >= start, tenant_ref[b], tenant)
    return tenant


def pack_kernel(blocks, block, fill_ref, tok_ref, cot_ref, x_ref, c_ref, pick):
    @pl.when(pl.program_id(0) == 0)
    def _():
        row = lax.broadcasted_iota(I32, (LIVE, block), 0)
        col = lax.broadcasted_iota(I32, (LIVE, block), 1)
        for b, start in enumerate(starts_of(fill_ref, blocks)):
            hit = (row == col + start) & (col < fill_ref[0, b])
            pick[:, b * block : (b + 1) * block] = jnp.where(hit, 1.0, 0.0).astype(BF16)
        c_ref[...] = dot(pick[...], cot_ref[...]).astype(BF16)

    x_ref[...] = dot(pick[...], tok_ref[...]).astype(BF16)


def pack(fill, tokens, cotangent, blocks):
    rows, feat = tokens.shape
    cols = cotangent.shape[1]
    steps = 4 if feat % 512 == 0 else 1
    wide = feat // steps
    return pl.pallas_call(
        functools.partial(pack_kernel, blocks, rows // blocks),
        grid=(steps,),
        in_specs=[SMEM, pl.BlockSpec((rows, wide), lambda i: (0, i)), pl.BlockSpec((rows, cols), lambda i: (0, 0))],
        out_specs=[pl.BlockSpec((LIVE, wide), lambda i: (0, i)), pl.BlockSpec((LIVE, cols), lambda i: (0, 0))],
        out_shape=[shaped((LIVE, feat), BF16), shaped((LIVE, cols), BF16)],
        scratch_shapes=[pltpu.VMEM((LIVE, rows), BF16)],
        compiler_params=params(24),
        cost_estimate=cost(2 * LIVE * rows * (feat + cols), 2 * (LIVE + rows) * (feat + cols)),
        name="pack",
    )(fill, tokens, cotangent)


def owner_mask(tenant, lane, owner, rank):
    return tenant == 2 * owner + (lane >= rank).astype(I32)


def low_kernel(n_dp, rank, blocks, dp_ref, fill_ref, tenant_ref, x_ref, c_ref, *refs):
    ab_refs, out_ref = refs[:n_dp], refs[n_dp]
    feat = x_ref.shape[1]
    lanes = 2 * rank
    tenant = tenant_lanes(fill_ref, tenant_ref, blocks, lanes)
    lane = lax.broadcasted_iota(I32, (LIVE, lanes), 1)
    low_in = jnp.zeros((LIVE, lanes), F32)
    low_grad = jnp.zeros((LIVE, lanes), F32)
    for s in range(n_dp):
        mask = owner_mask(tenant, lane, (dp_ref[0] + n_dp - s) % n_dp, rank)
        low_in = low_in + jnp.where(mask, dot(x_ref[...], ab_refs[s][:, :feat], (1, 1)), 0.0)
        low_grad = low_grad + jnp.where(mask, dot(c_ref[...], ab_refs[s][:, feat:], (1, 1)), 0.0)
    low_in = low_in + pltpu.roll(low_in, rank, 1)
    low_grad = low_grad + pltpu.roll(low_grad, rank, 1)
    out_ref[...] = jnp.where(lane < rank, low_in, low_grad).astype(BF16)


def low_part(dp, fill, tenant, x, c, ab_list, blocks, rank):
    n_dp = len(ab_list)
    width = x.shape[1] + c.shape[1]
    return pl.pallas_call(
        functools.partial(low_kernel, n_dp, rank, blocks),
        in_specs=[SMEM] * 3 + [VMEM] * (2 + n_dp),
        out_specs=VMEM,
        out_shape=shaped((LIVE, 2 * rank), BF16),
        compiler_params=params(24),
        cost_estimate=cost(4 * LIVE * rank * n_dp * width, 2 * LIVE * width + 4 * rank * n_dp * width),
        name="low_part",
    )(dp, fill, tenant, x, c, *ab_list)


def doubled(low, lane, rank):
    turned = pltpu.roll(low, rank, 1)
    return jnp.where(lane < rank, low, turned), jnp.where(lane < rank, turned, low)


def grad_kernel(n_dp, n_t, rank, blocks, dp_ref, fill_ref, tenant_ref, x_ref, c_ref, *refs):
    lows, low_ref, out_ref = refs[:n_t], refs[n_t], refs[n_t + 1]
    lanes = 2 * rank
    feat = x_ref.shape[1]
    total = lows[0][...].astype(F32)
    for ref in lows[1:]:
        total = total + ref[...].astype(F32)
    low_ref[...] = total.astype(BF16)
    total = total.astype(BF16).astype(F32)
    tenant = tenant_lanes(fill_ref, tenant_ref, blocks, lanes)
    lane = lax.broadcasted_iota(I32, (LIVE, lanes), 1)
    low_in, low_grad = doubled(total, lane, rank)
    for s in range(n_dp):
        mask = owner_mask(tenant, lane, (dp_ref[0] + s) % n_dp, rank)
        grad_t = jnp.transpose(jnp.where(mask, ADAPTER_SCALE * low_grad, 0.0)).astype(BF16)
        in_t = jnp.transpose(jnp.where(mask, ADAPTER_SCALE * low_in, 0.0)).astype(BF16)
        out_ref[s * lanes : (s + 1) * lanes, :feat] = dot(grad_t, x_ref[...]).astype(BF16)
        out_ref[s * lanes : (s + 1) * lanes, feat:] = dot(in_t, c_ref[...]).astype(BF16)


def grads(dp, fill, tenant, x, c, lows, n_dp, blocks, rank):
    n_t = len(lows)
    width = x.shape[1] + c.shape[1]
    return pl.pallas_call(
        functools.partial(grad_kernel, n_dp, n_t, rank, blocks),
        in_specs=[SMEM] * 3 + [VMEM] * (2 + n_t),
        out_specs=[VMEM] * 2,
        out_shape=[shaped((LIVE, 2 * rank), BF16), shaped((n_dp * 2 * rank, width), BF16)],
        compiler_params=params(32),
        cost_estimate=cost(4 * LIVE * rank * n_dp * width, 2 * LIVE * width + 4 * rank * n_dp * width),
        name="grads",
    )(dp, fill, tenant, x, c, *lows)


def panel_kernel(order, count, split, place_ref, x_ref, other_ref, *refs):
    pieces, refs = refs[:count], refs[count:]
    half = refs[-1].shape[1]
    panels = pieces[0].shape[1] // half
    if split:
        adds, outs = refs[:-2], [refs[-2:]]
    else:
        adds, outs = refs[:-panels], [(ref.at[:LIVE, :], ref.at[LIVE:, :]) for ref in refs[-panels:]]
    deep = x_ref.shape[1] // len(order)
    for n, source in enumerate((x_ref, other_ref)):
        total = None
        for piece, m in zip(pieces, order):
            col = pl.multiple_of((place_ref[0] ^ m) * deep, min(deep, 128))
            term = dot(source[:, pl.ds(col, deep)], piece[...])
            total = term if total is None else total + term
        for i, out in enumerate(outs):
            value = total[:, i * half : (i + 1) * half]
            if i < len(adds):
                value = value + adds[i][n * LIVE : (n + 1) * LIVE, :].astype(F32)
            out[n][...] = value.astype(BF16)


def panel_product(order, place, x, x_other, pieces, half, adds=(), split=False):
    feat, wide = x.shape[1], pieces[0].shape[1]
    shapes = [shaped((LIVE, half), BF16)] * 2 if split else [shaped((2 * LIVE, half), BF16)] * (wide // half)
    return pl.pallas_call(
        functools.partial(panel_kernel, order, len(pieces), split),
        in_specs=[SMEM] + [VMEM] * (2 + len(pieces) + len(adds)),
        out_specs=[VMEM] * len(shapes),
        out_shape=shapes,
        compiler_params=params(24),
        cost_estimate=cost(4 * LIVE * feat * wide, 4 * LIVE * feat + 2 * feat * wide),
        name="panel",
    )(place, x, x_other, *pieces, *adds)


def settle_kernel(own_ref, got_ref, down_ref, up_ref):
    pair, rank, feat = down_ref.shape
    for t in range(pair):
        total = own_ref[t * rank : (t + 1) * rank, :] + got_ref[t * rank : (t + 1) * rank, :].astype(F32)
        down_ref[t], up_ref[t] = total[:, :feat], total[:, feat:]


def settle(own, got, pair, feat):
    rank, width = own.shape[0] // pair, own.shape[1]
    return pl.pallas_call(
        settle_kernel,
        in_specs=[VMEM] * 2,
        out_specs=[VMEM] * 2,
        out_shape=[shaped((pair, rank, feat), F32), shaped((pair, rank, width - feat), F32)],
        compiler_params=params(16),
        cost_estimate=cost(own.size, 10 * own.size),
        name="settle",
    )(own, got)


def base_kernel(n_dp, rank, blocks, at_ref, dp_ref, fill_ref, tenant_ref, x_ref, w_ref, low_ref, *refs):
    ab_refs, out_ref = refs[:n_dp], refs[n_dp]
    lanes = 2 * rank
    tenant = tenant_lanes(fill_ref, tenant_ref, blocks, lanes)
    lane = lax.broadcasted_iota(I32, (LIVE, lanes), 1)
    low_in, _ = doubled(low_ref[...].astype(F32), lane, rank)
    total = dot(x_ref[...], w_ref[...])
    for s in range(n_dp):
        mask = owner_mask(tenant, lane, (dp_ref[0] + n_dp - s) % n_dp, rank)
        total = total + dot(jnp.where(mask, ADAPTER_SCALE * low_in, 0.0).astype(BF16), ab_refs[s][...])
    out_ref[...] = total


def base_product(at, dp, fill, tenant, x, base_weight, low, ab_list, blocks, rank):
    n_dp = len(ab_list)
    feat, cols = x.shape[1], base_weight.shape[1]
    whole = lambda i, at: (0, 0)
    return pl.pallas_call(
        functools.partial(base_kernel, n_dp, rank, blocks),
        grid_spec=pltpu.PrefetchScalarGridSpec(
            num_scalar_prefetch=1,
            grid=(1,),
            in_specs=[SMEM] * 3
            + [pl.BlockSpec((LIVE, feat), whole), pl.BlockSpec((feat, cols), lambda i, at: (at[0], 0)), pl.BlockSpec((LIVE, 2 * rank), whole)]
            + [pl.BlockSpec((2 * rank, cols), lambda i, at: (0, feat // cols))] * n_dp,
            out_specs=pl.BlockSpec((LIVE, cols), whole),
        ),
        out_shape=shaped((LIVE, cols), F32),
        compiler_params=params(24),
        cost_estimate=cost(2 * LIVE * feat * cols, 2 * feat * (LIVE + cols) + 4 * LIVE * cols),
        name="base",
    )(at, dp, fill, tenant, x, base_weight, low, *ab_list)


def swap_kernel(*refs):
    ins, out_ref = refs[:-1], refs[-1]
    total = ins[0][LIVE:, :].astype(F32)
    for ref in ins[1:]:
        total = total + ref[LIVE:, :].astype(F32)
    out_ref[...] = total.astype(BF16)


def other_rows(parts):
    half = parts[0].shape[1]
    return pl.pallas_call(
        swap_kernel,
        in_specs=[VMEM] * len(parts),
        out_specs=VMEM,
        out_shape=shaped((LIVE, half), BF16),
        compiler_params=params(24),
        cost_estimate=cost(LIVE * half, 2 * LIVE * half * len(parts)),
        name="other_rows",
    )(*parts)


def out_kernel(count, blocks, block, core_ref, fill_ref, base_ref, *refs):
    parts, rest, out_ref, held = refs[:count], refs[count:-2], refs[-2], refs[-1]
    half = rest[0].shape[1]
    own = parts[0][:LIVE, :].astype(F32)
    for part in parts[1:]:
        own = own + part[:LIVE, :].astype(F32)
    other = rest[0][...].astype(F32)
    for part in rest[1:]:
        other = other + part[...].astype(F32)
    first = core_ref[0] == 0
    held[:, :half] = (base_ref[:, :half] + jnp.where(first, own, other)).astype(BF16)
    held[:, half:] = (base_ref[:, half:] + jnp.where(first, other, own)).astype(BF16)
    row = lax.broadcasted_iota(I32, (block, LIVE), 0)
    col = lax.broadcasted_iota(I32, (block, LIVE), 1)
    for b, start in enumerate(starts_of(fill_ref, blocks)):
        hit = (col == row + start) & (row < fill_ref[0, b])
        pick = jnp.where(hit, 1.0, 0.0).astype(BF16)
        out_ref[b * block : (b + 1) * block, :] = dot(pick, held[...]).astype(BF16)


def finish(core, fill, base, parts, others, rows, blocks):
    cols = base.shape[1]
    count = len(parts)
    return pl.pallas_call(
        functools.partial(out_kernel, count, blocks, rows // blocks),
        in_specs=[SMEM] * 2 + [VMEM] * (1 + count + len(others)),
        out_specs=VMEM,
        out_shape=shaped((rows, cols), BF16),
        scratch_shapes=[pltpu.VMEM((LIVE, cols), BF16)],
        compiler_params=params(24),
        cost_estimate=cost(2 * LIVE * rows * cols, 4 * LIVE * cols + 2 * LIVE * cols * count + 2 * rows * cols),
        name="finish",
    )(core, fill, base, *parts, *others)


def body(sizes, tokens, base_weight, adapter_a, adapter_b, cotangent, block_tenant_index, block_fill):
    n_t, n_dp, n_pipe = sizes["tensor"], sizes["dp"], sizes["pipe"]
    planes = sizes["groups"] * n_dp
    rows, feat = tokens.shape
    cols = base_weight.shape[1]
    half = cols // n_pipe
    blocks = block_tenant_index.shape[0]
    pair, rank = adapter_a.shape[:2]
    me_t, me_pipe, me_dp = lax.axis_index("tensor"), lax.axis_index("pipe"), lax.axis_index("dp")
    q = lax.axis_index("groups") * n_dp + me_dp
    part_rows = feat // planes
    scalar = lambda v: v.astype(I32).reshape(1)
    dp, core, at, place = scalar(me_dp), scalar(me_pipe), scalar(me_t), scalar(q)

    own_a, own_b = adapter_a.reshape(pair * rank, feat), adapter_b.reshape(pair * rank, cols)
    own_ab = jnp.concatenate([own_a, own_b], axis=1)
    ab_list = [own_ab] + [shift(own_ab, "dp", n_dp, s) for s in range(1, n_dp)]
    panel_at = place if planes == 4 else jnp.zeros_like(place)

    def share(k):
        return lax.dynamic_slice(base_weight, (k * feat + q * part_rows, me_pipe * half), (part_rows, half))

    def gathered(piece):
        if planes != 4:
            return [lax.all_gather(piece, ("groups", "dp"), axis=0, tiled=True)], [0]
        return [piece] + [flip(piece, ("groups", "dp"), planes, m) for m in range(1, 4)], [0, 1, 2, 3]

    def low_sums(low):
        mask = 1
        while 2 * mask < n_t:
            low = (low.astype(F32) + flip(low, "tensor", n_t, mask).astype(F32)).astype(BF16)
            mask *= 2
        return [low] + ([flip(low, "tensor", n_t, mask)] if n_t > 1 else [])

    def gradients(x, c, lows):
        low_sum, grad = grads(dp, block_fill, block_tenant_index, x, c, lows, n_dp, blocks, rank)
        grad = grad.astype(F32) + flip(grad, "pipe", n_pipe, 1).astype(F32)
        mine, *sends = jnp.split(grad, n_dp, axis=0)
        return low_sum, mine, [send.astype(BF16) for send in sends]

    if n_t == 4:
        share_3 = share(me_t ^ 3)
        weight = {3: flip(share_3, "tensor", n_t, 3), 1: flip(share(me_t ^ 1), "tensor", n_t, 1)}
        weight[2] = flip(after(share(me_t ^ 2), weight[3]), "tensor", n_t, 2)
        x, c = pack(after(block_fill, share_3), tokens, cotangent, blocks)
        x_other = flip(after(x, weight[3], weight[1], *ab_list[1:]), "pipe", n_pipe, 1)
        low = low_part(dp, block_fill, block_tenant_index, x, c, ab_list, blocks, rank)
        low = (low.astype(F32) + flip(low, "tensor", n_t, 1).astype(F32)).astype(BF16)
        pieces, order = gathered(weight[3])
        pieces[0] = after(pieces[0], weight[1], weight[2], low)
        (y,) = panel_product(order, panel_at, x, x_other, pieces, half)
        add = flip(y, "tensor", n_t, 1)
        pieces, order = gathered(after(weight[2], y))
        (y_2,) = panel_product(order, panel_at, x, x_other, pieces, half, adds=[add])
        low_sum, mine, sends = gradients(x, c, [after(low, y_2), flip(after(low, y), "tensor", n_t, 2)])
        pieces, order = gathered(after(weight[1], *pieces))
        y_1, y_1_other = panel_product(order, panel_at, x, x_other, pieces, half, split=True)
        parts = [flip(y_2, "tensor", n_t, 2)]
        others = [flip(other_rows(parts), "pipe", n_pipe, 1)]
        parts.append(flip(y_1, "tensor", n_t, 1))
        others.append(flip(y_1_other, ("tensor", "pipe"), n_t * n_pipe, n_pipe + 1))
    else:
        x, c = pack(block_fill, tokens, cotangent, blocks)
        x_other = flip(x, "pipe", n_pipe, 1)
        low = low_part(dp, block_fill, block_tenant_index, x, c, ab_list, blocks, rank)
        low_sum, mine, sends = gradients(x, c, low_sums(low))
        steps = range(1, n_t)
        weights = [shift(share((me_t + s) % n_t), "tensor", n_t, s) for s in steps]
        pieces, order = gathered(jnp.concatenate(weights, axis=1))
        ys = panel_product(order, panel_at, x, x_other, pieces, half)
        parts = [shift(y, "tensor", n_t, -s) for s, y in zip(steps, ys)]
        others = [flip(other_rows(parts), "pipe", n_pipe, 1)]
    sends = [after(send, *pieces) for send in sends]
    got = [shift(send, "dp", n_dp, s + 1) for s, send in enumerate(sends)]
    for recv in got[:-1]:
        mine = mine + recv.astype(F32)
    down_out, up_out = settle(mine, got[-1], pair, feat)

    base = base_product(at, dp, block_fill, block_tenant_index, x, base_weight, low_sum, ab_list, blocks, rank)
    out = finish(core, block_fill, base, parts, others, rows, blocks)
    return out, down_out, up_out


def solution(mesh):
    placed = (
        P(("groups", "dp", "pipe"), "tensor"),
        P(None, "tensor"),
        P(("groups", "dp"), None, "tensor"),
        P(("groups", "dp"), None, "tensor"),
        P(("groups", "dp", "pipe"), "tensor"),
        P(("groups", "dp", "pipe")),
        P(("groups", "dp", "pipe"), None),
    )
    return jax.shard_map(
        functools.partial(body, dict(mesh.shape)),
        mesh=mesh,
        in_specs=placed,
        out_specs=(
            P(("groups", "dp", "pipe"), "tensor"),
            P(("groups", "dp"), None, "tensor"),
            P(("groups", "dp"), None, "tensor"),
        ),
        check_vma=False,
    )
```

```python
import functools

import jax
import jax.numpy as jnp
from jax import lax
from jax.experimental import pallas as pl
from jax.experimental.pallas import tpu as pltpu
from jax.sharding import PartitionSpec as P

ADAPTER_SCALE = 2.0
LIVE = 512
BF16 = jnp.bfloat16
F32 = jnp.float32
I32 = jnp.int32
MIB = 1 << 20
SMEM = pl.BlockSpec(memory_space=pltpu.SMEM)
VMEM = pl.BlockSpec(memory_space=pltpu.VMEM)


def shaped(shape, dtype):
    return jax.ShapeDtypeStruct(shape, dtype)


def dot(a, b, contract=(1, 0)):
    return lax.dot_general(a, b, ((contract[0:1], contract[1:2]), ((), ())), preferred_element_type=F32)


def shift(x, name, count, step):
    return lax.ppermute(x, name, [(i, (i + step) % count) for i in range(count)])


def flip(x, names, count, mask):
    return lax.ppermute(x, names, [(i, i ^ mask) for i in range(count)])


def params(mib):
    return pltpu.CompilerParams(vmem_limit_bytes=mib * MIB)


def cost(flops, bytes_accessed):
    return pl.CostEstimate(flops=1, bytes_accessed=1, transcendentals=0)


def after(x, *others):
    return lax.optimization_barrier((x, *others))[0]


def starts_of(fill_ref, blocks):
    starts, at = [], jnp.int32(0)
    for b in range(blocks):
        starts.append(at)
        at = at + fill_ref[0, b]
    return starts


def tenant_lanes(fill_ref, tenant_ref, blocks, lanes):
    row = lax.broadcasted_iota(I32, (LIVE, lanes), 0)
    tenant = jnp.zeros((LIVE, lanes), I32)
    for b, start in enumerate(starts_of(fill_ref, blocks)):
        tenant = jnp.where(row >= start, tenant_ref[b], tenant)
    return tenant


def pack_kernel(blocks, block, fill_ref, tenant_ref, tok_ref, cot_ref, out_ref, pick):
    feat, cols = tok_ref.shape[1], cot_ref.shape[1]
    row = lax.broadcasted_iota(I32, (LIVE, block), 0)
    col = lax.broadcasted_iota(I32, (LIVE, block), 1)
    for b, start in enumerate(starts_of(fill_ref, blocks)):
        hit = (row == col + start) & (col < fill_ref[0, b])
        pick[:, b * block : (b + 1) * block] = jnp.where(hit, 1.0, 0.0).astype(BF16)
    wide = min(feat, 512)
    for at in range(0, feat, wide):
        out_ref[:, at : at + wide] = dot(pick[...], tok_ref[:, at : at + wide]).astype(BF16)
    out_ref[:, feat : feat + cols] = dot(pick[...], cot_ref[...]).astype(BF16)
    lanes = out_ref.shape[1] - feat - cols
    out_ref[:, feat + cols :] = tenant_lanes(fill_ref, tenant_ref, blocks, lanes).astype(F32).astype(BF16)


def pack(fill, tenant, tokens, cotangent, blocks, lanes):
    rows, feat = tokens.shape
    cols = cotangent.shape[1]
    return pl.pallas_call(
        functools.partial(pack_kernel, blocks, rows // blocks),
        in_specs=[SMEM] * 2 + [VMEM] * 2,
        out_specs=VMEM,
        out_shape=shaped((LIVE, feat + cols + lanes), BF16),
        scratch_shapes=[pltpu.VMEM((LIVE, rows), BF16)],
        compiler_params=params(24),
        cost_estimate=cost(2 * LIVE * rows * (feat + cols), 2 * (LIVE + rows) * (feat + cols)),
        name="pack",
    )(fill, tenant, tokens, cotangent)


def owner_mask(tenant, lane, owner, rank):
    return tenant == 2 * owner + (lane >= rank).astype(I32)


def low_kernel(n_dp, rank, blocks, dp_ref, fill_ref, tenant_ref, x_ref, *refs):
    a_refs, b_refs, out_ref = refs[:n_dp], refs[n_dp : 2 * n_dp], refs[2 * n_dp]
    lanes, feat, cols = 2 * rank, a_refs[0].shape[1], b_refs[0].shape[1]
    tenant = tenant_lanes(fill_ref, tenant_ref, blocks, lanes)
    lane = lax.broadcasted_iota(I32, (LIVE, lanes), 1)
    low_in = jnp.zeros((LIVE, lanes), F32)
    low_grad = jnp.zeros((LIVE, lanes), F32)
    for s in range(n_dp):
        mask = owner_mask(tenant, lane, (dp_ref[0] + n_dp - s) % n_dp, rank)
        low_in = low_in + jnp.where(mask, dot(x_ref[:, :feat], a_refs[s][...], (1, 1)), 0.0)
        low_grad = low_grad + jnp.where(mask, dot(x_ref[:, feat : feat + cols], b_refs[s][...], (1, 1)), 0.0)
    low_in = low_in + pltpu.roll(low_in, rank, 1)
    low_grad = low_grad + pltpu.roll(low_grad, rank, 1)
    out_ref[...] = jnp.where(lane < rank, low_in, low_grad).astype(BF16)


def low_part(dp, fill, tenant, x, a_list, b_list, blocks, rank):
    n_dp = len(a_list)
    width = x.shape[1]
    return pl.pallas_call(
        functools.partial(low_kernel, n_dp, rank, blocks),
        in_specs=[SMEM] * 3 + [VMEM] * (1 + 2 * n_dp),
        out_specs=VMEM,
        out_shape=shaped((LIVE, 2 * rank), BF16),
        compiler_params=params(24),
        cost_estimate=cost(4 * LIVE * rank * n_dp * width, 2 * LIVE * width + 4 * rank * n_dp * width),
        name="low_part",
    )(dp, fill, tenant, x, *a_list, *b_list)


def doubled(low, lane, rank):
    turned = pltpu.roll(low, rank, 1)
    return jnp.where(lane < rank, low, turned), jnp.where(lane < rank, turned, low)


def grad_kernel(n_dp, rank, feat, cols, dp_ref, core_ref, own_ref, other_ref, low_ref, low_other_ref, *outs):
    lanes = 2 * rank
    lane = lax.broadcasted_iota(I32, (LIVE, lanes), 1)
    for s in range(0, n_dp, 2):
        first, second = (dp_ref[0] + s) % n_dp, (dp_ref[0] + s + 1) % n_dp
        wanted = (2 * jnp.where(lane < rank, first, second) + core_ref[0]).astype(F32)
        down, up = None, None
        for source, ref in ((own_ref, low_ref), (other_ref, low_other_ref)):
            low_in, low_grad = doubled(ref[...].astype(F32), lane, rank)
            mask = source[:, feat + cols :].astype(F32) == wanted
            grad_t = jnp.transpose(jnp.where(mask, ADAPTER_SCALE * low_grad, 0.0)).astype(BF16)
            in_t = jnp.transpose(jnp.where(mask, ADAPTER_SCALE * low_in, 0.0)).astype(BF16)
            down_term = dot(grad_t, source[:, :feat])
            up_term = dot(in_t, source[:, feat : feat + cols])
            down, up = (down_term, up_term) if down is None else (down + down_term, up + up_term)
        for i in range(2):
            out = outs[s + i]
            out[:, :feat] = down[i * rank : (i + 1) * rank, :].astype(out.dtype)
            out[:, feat:] = up[i * rank : (i + 1) * rank, :].astype(out.dtype)


def grads(dp, core, x, x_other, low, low_other, n_dp, rank, feat, cols):
    width = feat + cols
    return pl.pallas_call(
        functools.partial(grad_kernel, n_dp, rank, feat, cols),
        in_specs=[SMEM] * 2 + [VMEM] * 4,
        out_specs=[VMEM] * n_dp,
        out_shape=[shaped((rank, width), F32)] + [shaped((rank, width), BF16)] * (n_dp - 1),
        compiler_params=params(32),
        cost_estimate=cost(4 * LIVE * rank * n_dp * width, 4 * LIVE * width + 4 * rank * n_dp * width),
        name="grads",
    )(dp, core, x, x_other, low, low_other)


def panel_kernel(order, count, place_ref, x_ref, other_ref, *refs):
    pieces, refs = refs[:count], refs[count:]
    half = refs[-1].shape[1]
    panels = pieces[0].shape[1] // half
    adds, outs = refs[:-panels], refs[-panels:]
    deep = pieces[0].shape[0]
    for n, source in enumerate((x_ref, other_ref)):
        total = None
        for piece, m in zip(pieces, order):
            col = pl.multiple_of((place_ref[0] ^ m) * deep, min(deep, 128))
            term = dot(source[:, pl.ds(col, deep)], piece[...])
            total = term if total is None else total + term
        for i, out in enumerate(outs):
            value = total[:, i * half : (i + 1) * half]
            if i < len(adds):
                value = value + adds[i][n * LIVE : (n + 1) * LIVE, :].astype(F32)
            out[n * LIVE : (n + 1) * LIVE, :] = value.astype(BF16)


def panel_product(order, place, x, x_other, pieces, half, adds=()):
    feat, wide = len(pieces) * pieces[0].shape[0], pieces[0].shape[1]
    shapes = [shaped((2 * LIVE, half), BF16)] * (wide // half)
    return pl.pallas_call(
        functools.partial(panel_kernel, order, len(pieces)),
        in_specs=[SMEM] + [VMEM] * (2 + len(pieces) + len(adds)),
        out_specs=[VMEM] * len(shapes),
        out_shape=shapes,
        compiler_params=params(24),
        cost_estimate=cost(4 * LIVE * feat * wide, 4 * LIVE * feat + 2 * feat * wide),
        name="panel",
    )(place, x, x_other, *pieces, *adds)


def settle_kernel(core_ref, own_ref, got_ref, down_ref, up_ref):
    feat = down_ref.shape[2]
    own, got = own_ref[...].astype(F32), got_ref[...].astype(F32)
    first = core_ref[0] == 0
    down_ref[0], up_ref[0] = jnp.where(first, own, got)[:, :feat], jnp.where(first, own, got)[:, feat:]
    down_ref[1], up_ref[1] = jnp.where(first, got, own)[:, :feat], jnp.where(first, got, own)[:, feat:]


def settle(core, own, got, feat):
    rank, width = own.shape
    return pl.pallas_call(
        settle_kernel,
        in_specs=[SMEM] + [VMEM] * 2,
        out_specs=[VMEM] * 2,
        out_shape=[shaped((2, rank, feat), F32), shaped((2, rank, width - feat), F32)],
        compiler_params=params(16),
        cost_estimate=cost(own.size, 12 * own.size),
        name="settle",
    )(core, own, got)


def base_kernel(n_dp, rank, blocks, at_ref, dp_ref, fill_ref, tenant_ref, x_ref, w_ref, low_ref, *refs):
    b_refs, out_ref = refs[:n_dp], refs[n_dp]
    lanes = 2 * rank
    tenant = tenant_lanes(fill_ref, tenant_ref, blocks, lanes)
    lane = lax.broadcasted_iota(I32, (LIVE, lanes), 1)
    low_in, _ = doubled(low_ref[...].astype(F32), lane, rank)
    total = dot(x_ref[...], w_ref[...])
    for s in range(n_dp):
        mask = owner_mask(tenant, lane, (dp_ref[0] + n_dp - s) % n_dp, rank)
        total = total + dot(jnp.where(mask, ADAPTER_SCALE * low_in, 0.0).astype(BF16), b_refs[s][...])
    out_ref[...] = total


def base_product(at, dp, fill, tenant, x, base_weight, low, b_list, feat, blocks, rank):
    n_dp = len(b_list)
    cols = base_weight.shape[1]
    whole = lambda i, at: (0, 0)
    return pl.pallas_call(
        functools.partial(base_kernel, n_dp, rank, blocks),
        grid_spec=pltpu.PrefetchScalarGridSpec(
            num_scalar_prefetch=1,
            grid=(1,),
            in_specs=[SMEM] * 3
            + [pl.BlockSpec((LIVE, feat), whole), pl.BlockSpec((feat, cols), lambda i, at: (at[0], 0)), pl.BlockSpec((LIVE, 2 * rank), whole)]
            + [pl.BlockSpec((2 * rank, cols), whole)] * n_dp,
            out_specs=pl.BlockSpec((LIVE, cols), whole),
        ),
        out_shape=shaped((LIVE, cols), F32),
        compiler_params=params(24),
        cost_estimate=cost(2 * LIVE * feat * cols, 2 * feat * (LIVE + cols) + 4 * LIVE * cols),
        name="base",
    )(at, dp, fill, tenant, x, base_weight, low, *b_list)


def swap_kernel(*refs):
    ins, out_ref = refs[:-1], refs[-1]
    total = ins[0][LIVE:, :].astype(F32)
    for ref in ins[1:]:
        total = total + ref[LIVE:, :].astype(F32)
    out_ref[...] = total


def other_rows(parts):
    half = parts[0].shape[1]
    return pl.pallas_call(
        swap_kernel,
        in_specs=[VMEM] * len(parts),
        out_specs=VMEM,
        out_shape=shaped((LIVE, half), F32),
        compiler_params=params(24),
        cost_estimate=cost(LIVE * half, 2 * LIVE * half * len(parts)),
        name="other_rows",
    )(*parts)


def out_kernel(count, blocks, block, core_ref, fill_ref, base_ref, *refs):
    parts, rest, out_ref, held = refs[:count], refs[count:-2], refs[-2], refs[-1]
    half = rest[0].shape[1]
    own = parts[0][:LIVE, :].astype(F32)
    for part in parts[1:]:
        own = own + part[:LIVE, :].astype(F32)
    other = rest[0][...].astype(F32)
    for part in rest[1:]:
        other = other + part[...].astype(F32)
    first = core_ref[0] == 0
    held[:, :half] = (base_ref[:, :half] + jnp.where(first, own, other)).astype(BF16)
    held[:, half:] = (base_ref[:, half:] + jnp.where(first, other, own)).astype(BF16)
    row = lax.broadcasted_iota(I32, (block, LIVE), 0)
    col = lax.broadcasted_iota(I32, (block, LIVE), 1)
    for b, start in enumerate(starts_of(fill_ref, blocks)):
        hit = (col == row + start) & (row < fill_ref[0, b])
        pick = jnp.where(hit, 1.0, 0.0).astype(BF16)
        out_ref[b * block : (b + 1) * block, :] = dot(pick, held[...]).astype(BF16)


def finish(core, fill, base, parts, others, rows, blocks):
    cols = base.shape[1]
    count = len(parts)
    return pl.pallas_call(
        functools.partial(out_kernel, count, blocks, rows // blocks),
        in_specs=[SMEM] * 2 + [VMEM] * (1 + count + len(others)),
        out_specs=VMEM,
        out_shape=shaped((rows, cols), BF16),
        scratch_shapes=[pltpu.VMEM((LIVE, cols), BF16)],
        compiler_params=params(24),
        cost_estimate=cost(2 * LIVE * rows * cols, 4 * LIVE * cols + 2 * LIVE * cols * count + 2 * rows * cols),
        name="finish",
    )(core, fill, base, *parts, *others)


def body(sizes, tokens, base_weight, adapter_a, adapter_b, cotangent, block_tenant_index, block_fill):
    n_t, n_dp, n_pipe = sizes["tensor"], sizes["dp"], sizes["pipe"]
    planes = sizes["groups"] * n_dp
    rows, feat = tokens.shape
    cols = base_weight.shape[1]
    half = cols // n_pipe
    blocks = block_tenant_index.shape[0]
    pair, rank = adapter_a.shape[:2]
    me_t, me_pipe, me_dp = lax.axis_index("tensor"), lax.axis_index("pipe"), lax.axis_index("dp")
    q = lax.axis_index("groups") * n_dp + me_dp
    part_rows = feat // planes
    scalar = lambda v: v.astype(I32).reshape(1)
    dp, core, at, place = scalar(me_dp), scalar(me_pipe), scalar(me_t), scalar(q)

    own_a, own_b = adapter_a.reshape(pair * rank, feat), adapter_b.reshape(pair * rank, cols)
    a_list = [own_a] + [shift(own_a, "dp", n_dp, s) for s in range(1, n_dp)]
    b_list = [own_b] + [shift(own_b, "dp", n_dp, s) for s in range(1, n_dp)]
    panel_at = place if planes == 4 else jnp.zeros_like(place)

    def share(k):
        return lax.dynamic_slice(base_weight, (k * feat + q * part_rows, me_pipe * half), (part_rows, half))

    def gathered(piece):
        if planes != 4:
            return [lax.all_gather(piece, ("groups", "dp"), axis=0, tiled=True)], [0]
        return [piece] + [flip(piece, ("groups", "dp"), planes, m) for m in range(1, 4)], [0, 1, 2, 3]

    def add_flipped(low, mask, *before):
        return (low.astype(F32) + flip(after(low, *before), "tensor", n_t, mask).astype(F32)).astype(BF16)

    if n_t == 4:
        share_3 = share(me_t ^ 3)
        weight = {3: flip(share_3, "tensor", n_t, 3), 1: flip(share(me_t ^ 1), "tensor", n_t, 1)}
        weight[2] = flip(after(share(me_t ^ 2), weight[3]), "tensor", n_t, 2)
        x = pack(after(block_fill, share_3), block_tenant_index, tokens, cotangent, blocks, 2 * rank)
        x_other = flip(after(x, weight[3], weight[1], *a_list[1:], *b_list[1:]), "pipe", n_pipe, 1)
        pieces, order = gathered(weight[3])
        pieces[0] = after(pieces[0], weight[1], weight[2])
        (y,) = panel_product(order, panel_at, x, x_other, pieces, half)
        add = flip(y, "tensor", n_t, 1)
        low = low_part(after(dp, y), block_fill, block_tenant_index, x, a_list, b_list, blocks, rank)
        low = add_flipped(low, 1)
        pieces, order = gathered(after(weight[2], y))
        (y_2,) = panel_product(order, panel_at, x, x_other, pieces, half, adds=[add])
        low = add_flipped(low, 2)
        pieces, order = gathered(after(weight[1], add, *pieces))
        (y_1,) = panel_product(order, panel_at, x, x_other, pieces, half)
        parts = [flip(y_2, "tensor", n_t, 2), flip(y_1, "tensor", n_t, 1)]
    else:
        x = pack(block_fill, block_tenant_index, tokens, cotangent, blocks, 2 * rank)
        x_other = flip(x, "pipe", n_pipe, 1)
        low = low_part(dp, block_fill, block_tenant_index, x, a_list, b_list, blocks, rank)
        mask = 1
        while mask < n_t:
            low, mask = add_flipped(low, mask), 2 * mask
        steps = range(1, n_t)
        weights = [shift(share((me_t + s) % n_t), "tensor", n_t, s) for s in steps]
        pieces, order = gathered(jnp.concatenate(weights, axis=1))
        ys = panel_product(order, panel_at, x, x_other, pieces, half)
        parts = [shift(y, "tensor", n_t, -s) for s, y in zip(steps, ys)]
    others = [flip(other_rows(parts), "pipe", n_pipe, 1)]

    low_other = flip(low, "pipe", n_pipe, 1)
    mine, *sends = grads(dp, core, x, x_other, low, low_other, n_dp, rank, feat, cols)
    for s, send in enumerate(sends):
        mine = mine + shift(after(send, *pieces), "dp", n_dp, s + 1).astype(F32)
    mine = mine.astype(BF16)
    down_out, up_out = settle(core, mine, flip(mine, "pipe", n_pipe, 1), feat)

    base = base_product(at, dp, block_fill, block_tenant_index, x, base_weight, low, b_list, feat, blocks, rank)
    out = finish(core, block_fill, base, parts, others, rows, blocks)
    return out, down_out, up_out


def solution(mesh):
    placed = (
        P(("groups", "dp", "pipe"), "tensor"),
        P(None, "tensor"),
        P(("groups", "dp"), None, "tensor"),
        P(("groups", "dp"), None, "tensor"),
        P(("groups", "dp", "pipe"), "tensor"),
        P(("groups", "dp", "pipe")),
        P(("groups", "dp", "pipe"), None),
    )
    return jax.shard_map(
        functools.partial(body, dict(mesh.shape)),
        mesh=mesh,
        in_specs=placed,
        out_specs=(
            P(("groups", "dp", "pipe"), "tensor"),
            P(("groups", "dp"), None, "tensor"),
            P(("groups", "dp"), None, "tensor"),
        ),
        check_vma=False,
    )
```

```python
import functools

import jax
import jax.numpy as jnp
from jax import lax
from jax.experimental import pallas as pl
from jax.experimental.pallas import tpu as pltpu
from jax.sharding import PartitionSpec as P

ADAPTER_SCALE = 2.0
LIVE = 512
BF16 = jnp.bfloat16
F32 = jnp.float32
I32 = jnp.int32
MIB = 1 << 20
SMEM = pl.BlockSpec(memory_space=pltpu.SMEM)
VMEM = pl.BlockSpec(memory_space=pltpu.VMEM)


def shaped(shape, dtype):
    return jax.ShapeDtypeStruct(shape, dtype)


def dot(a, b, contract=(1, 0)):
    return lax.dot_general(a, b, ((contract[0:1], contract[1:2]), ((), ())), preferred_element_type=F32)


def shift(x, name, count, step):
    return lax.ppermute(x, name, [(i, (i + step) % count) for i in range(count)])


def flip(x, names, count, mask):
    return lax.ppermute(x, names, [(i, i ^ mask) for i in range(count)])


def params(mib):
    return pltpu.CompilerParams(vmem_limit_bytes=mib * MIB)


def cost(flops, bytes_accessed):
    return pl.CostEstimate(flops=1, bytes_accessed=1, transcendentals=0)


def after(x, *others):
    return lax.optimization_barrier((x, *others))[0]


def starts_of(fill_ref, blocks):
    starts, at = [], jnp.int32(0)
    for b in range(blocks):
        starts.append(at)
        at = at + fill_ref[0, b]
    return starts


def tenant_lanes(fill_ref, tenant_ref, blocks, lanes):
    row = lax.broadcasted_iota(I32, (LIVE, lanes), 0)
    tenant = jnp.zeros((LIVE, lanes), I32)
    for b, start in enumerate(starts_of(fill_ref, blocks)):
        tenant = jnp.where(row >= start, tenant_ref[b], tenant)
    return tenant


def pack_kernel(blocks, block, fill_ref, tenant_ref, tok_ref, cot_ref, out_ref, pick):
    feat, cols = tok_ref.shape[1], cot_ref.shape[1]
    row = lax.broadcasted_iota(I32, (LIVE, block), 0)
    col = lax.broadcasted_iota(I32, (LIVE, block), 1)
    for b, start in enumerate(starts_of(fill_ref, blocks)):
        hit = (row == col + start) & (col < fill_ref[0, b])
        pick[:, b * block : (b + 1) * block] = jnp.where(hit, 1.0, 0.0).astype(BF16)
    wide = min(feat, 512)
    for at in range(0, feat, wide):
        out_ref[:, at : at + wide] = dot(pick[...], tok_ref[:, at : at + wide]).astype(BF16)
    out_ref[:, feat : feat + cols] = dot(pick[...], cot_ref[...]).astype(BF16)
    lanes = out_ref.shape[1] - feat - cols
    out_ref[:, feat + cols :] = tenant_lanes(fill_ref, tenant_ref, blocks, lanes).astype(F32).astype(BF16)


def pack(fill, tenant, tokens, cotangent, blocks, lanes):
    rows, feat = tokens.shape
    cols = cotangent.shape[1]
    return pl.pallas_call(
        functools.partial(pack_kernel, blocks, rows // blocks),
        in_specs=[SMEM] * 2 + [VMEM] * 2,
        out_specs=VMEM,
        out_shape=shaped((LIVE, feat + cols + lanes), BF16),
        scratch_shapes=[pltpu.VMEM((LIVE, rows), BF16)],
        compiler_params=params(56),
        cost_estimate=cost(2 * LIVE * rows * (feat + cols), 2 * (LIVE + rows) * (feat + cols)),
        name="pack",
    )(fill, tenant, tokens, cotangent)


def owner_mask(tenant, lane, owner, rank):
    return tenant == 2 * owner + (lane >= rank).astype(I32)


def low_kernel(n_dp, rank, blocks, dp_ref, fill_ref, tenant_ref, x_ref, *refs):
    a_refs, b_refs, out_ref = refs[:n_dp], refs[n_dp : 2 * n_dp], refs[2 * n_dp]
    lanes, feat, cols = 2 * rank, a_refs[0].shape[1], b_refs[0].shape[1]
    tenant = tenant_lanes(fill_ref, tenant_ref, blocks, lanes)
    lane = lax.broadcasted_iota(I32, (LIVE, lanes), 1)
    low_in = jnp.zeros((LIVE, lanes), F32)
    low_grad = jnp.zeros((LIVE, lanes), F32)
    for s in range(n_dp):
        mask = owner_mask(tenant, lane, (dp_ref[0] + n_dp - s) % n_dp, rank)
        low_in = low_in + jnp.where(mask, dot(x_ref[:, :feat], a_refs[s][...], (1, 1)), 0.0)
        low_grad = low_grad + jnp.where(mask, dot(x_ref[:, feat : feat + cols], b_refs[s][...], (1, 1)), 0.0)
    low_in = low_in + pltpu.roll(low_in, rank, 1)
    low_grad = low_grad + pltpu.roll(low_grad, rank, 1)
    out_ref[...] = jnp.where(lane < rank, low_in, low_grad).astype(BF16)


def low_part(dp, fill, tenant, x, a_list, b_list, blocks, rank):
    n_dp = len(a_list)
    width = x.shape[1]
    return pl.pallas_call(
        functools.partial(low_kernel, n_dp, rank, blocks),
        in_specs=[SMEM] * 3 + [VMEM] * (1 + 2 * n_dp),
        out_specs=VMEM,
        out_shape=shaped((LIVE, 2 * rank), BF16),
        compiler_params=params(24),
        cost_estimate=cost(4 * LIVE * rank * n_dp * width, 2 * LIVE * width + 4 * rank * n_dp * width),
        name="low_part",
    )(dp, fill, tenant, x, *a_list, *b_list)


def doubled(low, lane, rank):
    turned = pltpu.roll(low, rank, 1)
    return jnp.where(lane < rank, low, turned), jnp.where(lane < rank, turned, low)


def grad_kernel(n_dp, rank, feat, cols, dp_ref, core_ref, own_ref, other_ref, low_ref, low_other_ref, *outs):
    lanes = 2 * rank
    lane = lax.broadcasted_iota(I32, (LIVE, lanes), 1)
    for s in range(0, n_dp, 2):
        first, second = (dp_ref[0] + s) % n_dp, (dp_ref[0] + s + 1) % n_dp
        wanted = (2 * jnp.where(lane < rank, first, second) + core_ref[0]).astype(F32)
        down, up = None, None
        for source, ref in ((own_ref, low_ref), (other_ref, low_other_ref)):
            low_in, low_grad = doubled(ref[...].astype(F32), lane, rank)
            mask = source[:, feat + cols :].astype(F32) == wanted
            grad_t = jnp.transpose(jnp.where(mask, ADAPTER_SCALE * low_grad, 0.0)).astype(BF16)
            in_t = jnp.transpose(jnp.where(mask, ADAPTER_SCALE * low_in, 0.0)).astype(BF16)
            down_term = dot(grad_t, source[:, :feat])
            up_term = dot(in_t, source[:, feat : feat + cols])
            down, up = (down_term, up_term) if down is None else (down + down_term, up + up_term)
        for i in range(2):
            out = outs[s + i]
            out[:, :feat] = down[i * rank : (i + 1) * rank, :].astype(out.dtype)
            out[:, feat:] = up[i * rank : (i + 1) * rank, :].astype(out.dtype)


def grads(dp, core, x, x_other, low, low_other, n_dp, rank, feat, cols):
    width = feat + cols
    return pl.pallas_call(
        functools.partial(grad_kernel, n_dp, rank, feat, cols),
        in_specs=[SMEM] * 2 + [VMEM] * 4,
        out_specs=[VMEM] * n_dp,
        out_shape=[shaped((rank, width), F32)] + [shaped((rank, width), BF16)] * (n_dp - 1),
        compiler_params=params(32),
        cost_estimate=cost(4 * LIVE * rank * n_dp * width, 4 * LIVE * width + 4 * rank * n_dp * width),
        name="grads",
    )(dp, core, x, x_other, low, low_other)


def panel_kernel(order, count, place_ref, x_ref, other_ref, *refs):
    pieces, refs = refs[:count], refs[count:]
    half = refs[-1].shape[1]
    panels = pieces[0].shape[1] // half
    adds, outs = refs[:-panels], refs[-panels:]
    deep = pieces[0].shape[0]
    for n, source in enumerate((x_ref, other_ref)):
        total = None
        for piece, m in zip(pieces, order):
            col = pl.multiple_of((place_ref[0] ^ m) * deep, min(deep, 128))
            term = dot(source[:, pl.ds(col, deep)], piece[...])
            total = term if total is None else total + term
        for i, out in enumerate(outs):
            value = total[:, i * half : (i + 1) * half]
            if i < len(adds):
                value = value + adds[i][n * LIVE : (n + 1) * LIVE, :].astype(F32)
            out[n * LIVE : (n + 1) * LIVE, :] = value.astype(BF16)


def panel_product(order, place, x, x_other, pieces, half, adds=()):
    feat, wide = len(pieces) * pieces[0].shape[0], pieces[0].shape[1]
    shapes = [shaped((2 * LIVE, half), BF16)] * (wide // half)
    return pl.pallas_call(
        functools.partial(panel_kernel, order, len(pieces)),
        in_specs=[SMEM] + [VMEM] * (2 + len(pieces) + len(adds)),
        out_specs=[VMEM] * len(shapes),
        out_shape=shapes,
        compiler_params=params(24),
        cost_estimate=cost(4 * LIVE * feat * wide, 4 * LIVE * feat + 2 * feat * wide),
        name="panel",
    )(place, x, x_other, *pieces, *adds)


def settle_kernel(core_ref, own_ref, got_ref, down_ref, up_ref):
    feat = down_ref.shape[2]
    own, got = own_ref[...].astype(F32), got_ref[...].astype(F32)
    first = core_ref[0] == 0
    down_ref[0], up_ref[0] = jnp.where(first, own, got)[:, :feat], jnp.where(first, own, got)[:, feat:]
    down_ref[1], up_ref[1] = jnp.where(first, got, own)[:, :feat], jnp.where(first, got, own)[:, feat:]


def settle(core, own, got, feat):
    rank, width = own.shape
    return pl.pallas_call(
        settle_kernel,
        in_specs=[SMEM] + [VMEM] * 2,
        out_specs=[VMEM] * 2,
        out_shape=[shaped((2, rank, feat), F32), shaped((2, rank, width - feat), F32)],
        compiler_params=params(16),
        cost_estimate=cost(own.size, 12 * own.size),
        name="settle",
    )(core, own, got)


def base_kernel(n_dp, rank, blocks, at_ref, dp_ref, fill_ref, tenant_ref, x_ref, w_ref, low_ref, *refs):
    b_refs, out_ref = refs[:n_dp], refs[n_dp]
    lanes = 2 * rank
    tenant = tenant_lanes(fill_ref, tenant_ref, blocks, lanes)
    lane = lax.broadcasted_iota(I32, (LIVE, lanes), 1)
    low_in, _ = doubled(low_ref[...].astype(F32), lane, rank)
    total = dot(x_ref[...], w_ref[...])
    for s in range(n_dp):
        mask = owner_mask(tenant, lane, (dp_ref[0] + n_dp - s) % n_dp, rank)
        total = total + dot(jnp.where(mask, ADAPTER_SCALE * low_in, 0.0).astype(BF16), b_refs[s][...])
    out_ref[...] = total


def base_product(at, dp, fill, tenant, x, base_weight, low, b_list, feat, blocks, rank):
    n_dp = len(b_list)
    cols = base_weight.shape[1]
    whole = lambda i, at: (0, 0)
    return pl.pallas_call(
        functools.partial(base_kernel, n_dp, rank, blocks),
        grid_spec=pltpu.PrefetchScalarGridSpec(
            num_scalar_prefetch=1,
            grid=(1,),
            in_specs=[SMEM] * 3
            + [pl.BlockSpec((LIVE, feat), whole), pl.BlockSpec((feat, cols), lambda i, at: (at[0], 0)), pl.BlockSpec((LIVE, 2 * rank), whole)]
            + [pl.BlockSpec((2 * rank, cols), whole)] * n_dp,
            out_specs=pl.BlockSpec((LIVE, cols), whole),
        ),
        out_shape=shaped((LIVE, cols), F32),
        compiler_params=params(24),
        cost_estimate=cost(2 * LIVE * feat * cols, 2 * feat * (LIVE + cols) + 4 * LIVE * cols),
        name="base",
    )(at, dp, fill, tenant, x, base_weight, low, *b_list)


def swap_kernel(*refs):
    ins, out_ref = refs[:-1], refs[-1]
    total = ins[0][LIVE:, :].astype(F32)
    for ref in ins[1:]:
        total = total + ref[LIVE:, :].astype(F32)
    out_ref[...] = total


def other_rows(parts):
    half = parts[0].shape[1]
    return pl.pallas_call(
        swap_kernel,
        in_specs=[VMEM] * len(parts),
        out_specs=VMEM,
        out_shape=shaped((LIVE, half), F32),
        compiler_params=params(24),
        cost_estimate=cost(LIVE * half, 2 * LIVE * half * len(parts)),
        name="other_rows",
    )(*parts)


def out_kernel(count, blocks, block, core_ref, fill_ref, base_ref, *refs):
    parts, rest, out_ref, held = refs[:count], refs[count:-2], refs[-2], refs[-1]
    half = rest[0].shape[1]
    own = parts[0][:LIVE, :].astype(F32)
    for part in parts[1:]:
        own = own + part[:LIVE, :].astype(F32)
    other = rest[0][...].astype(F32)
    for part in rest[1:]:
        other = other + part[...].astype(F32)
    first = core_ref[0] == 0
    held[:, :half] = (base_ref[:, :half] + jnp.where(first, own, other)).astype(BF16)
    held[:, half:] = (base_ref[:, half:] + jnp.where(first, other, own)).astype(BF16)
    row = lax.broadcasted_iota(I32, (block, LIVE), 0)
    col = lax.broadcasted_iota(I32, (block, LIVE), 1)
    for b, start in enumerate(starts_of(fill_ref, blocks)):
        hit = (col == row + start) & (row < fill_ref[0, b])
        pick = jnp.where(hit, 1.0, 0.0).astype(BF16)
        out_ref[b * block : (b + 1) * block, :] = dot(pick, held[...]).astype(BF16)


def finish(core, fill, base, parts, others, rows, blocks):
    cols = base.shape[1]
    count = len(parts)
    return pl.pallas_call(
        functools.partial(out_kernel, count, blocks, rows // blocks),
        in_specs=[SMEM] * 2 + [VMEM] * (1 + count + len(others)),
        out_specs=VMEM,
        out_shape=shaped((rows, cols), BF16),
        scratch_shapes=[pltpu.VMEM((LIVE, cols), BF16)],
        compiler_params=params(24),
        cost_estimate=cost(2 * LIVE * rows * cols, 4 * LIVE * cols + 2 * LIVE * cols * count + 2 * rows * cols),
        name="finish",
    )(core, fill, base, *parts, *others)


def body(sizes, tokens, base_weight, adapter_a, adapter_b, cotangent, block_tenant_index, block_fill):
    n_t, n_dp, n_pipe = sizes["tensor"], sizes["dp"], sizes["pipe"]
    planes = sizes["groups"] * n_dp
    rows, feat = tokens.shape
    cols = base_weight.shape[1]
    half = cols // n_pipe
    blocks = block_tenant_index.shape[0]
    pair, rank = adapter_a.shape[:2]
    me_t, me_pipe, me_dp = lax.axis_index("tensor"), lax.axis_index("pipe"), lax.axis_index("dp")
    q = lax.axis_index("groups") * n_dp + me_dp
    part_rows = feat // planes
    scalar = lambda v: v.astype(I32).reshape(1)
    dp, core, at, place = scalar(me_dp), scalar(me_pipe), scalar(me_t), scalar(q)

    own_a, own_b = adapter_a.reshape(pair * rank, feat), adapter_b.reshape(pair * rank, cols)
    a_list = [own_a] + [shift(own_a, "dp", n_dp, s) for s in range(1, n_dp)]
    b_list = [own_b] + [shift(own_b, "dp", n_dp, s) for s in range(1, n_dp)]
    panel_at = place if planes == 4 else jnp.zeros_like(place)

    def share(k):
        return lax.dynamic_slice(base_weight, (k * feat + q * part_rows, me_pipe * half), (part_rows, half))

    def gathered(piece):
        if planes != 4:
            return [lax.all_gather(piece, ("groups", "dp"), axis=0, tiled=True)], [0]
        return [piece] + [flip(piece, ("groups", "dp"), planes, m) for m in range(1, 4)], [0, 1, 2, 3]

    def add_flipped(low, mask, *before):
        return (low.astype(F32) + flip(after(low, *before), "tensor", n_t, mask).astype(F32)).astype(BF16)

    if n_t == 4:
        share_1 = share(me_t ^ 1)
        weight = {1: flip(share_1, "tensor", n_t, 1)}
        weight[3] = flip(after(share(me_t ^ 3), weight[1]), "tensor", n_t, 3)
        weight[2] = flip(after(share(me_t ^ 2), weight[3]), "tensor", n_t, 2)
        x = pack(after(block_fill, share_1), block_tenant_index, tokens, cotangent, blocks, 2 * rank)
        x_other = flip(after(x, weight[1], *a_list[1:], *b_list[1:]), "pipe", n_pipe, 1)
        pieces, order = gathered(weight[1])
        low = low_part(dp, block_fill, block_tenant_index, x, a_list, b_list, blocks, rank)
        pieces[0] = after(pieces[0], weight[3], low)
        (y_1,) = panel_product(order, panel_at, x, x_other, pieces, half)
        part_1 = flip(y_1, "tensor", n_t, 1)
        pieces, order = gathered(after(weight[3], y_1))
        pieces[0] = after(pieces[0], weight[2])
        (y,) = panel_product(order, panel_at, x, x_other, pieces, half)
        add = flip(y, "tensor", n_t, 1)
        low = add_flipped(add_flipped(low, 1, y), 2, part_1)
        pieces, order = gathered(after(weight[2], y))
        (y_2,) = panel_product(order, panel_at, x, x_other, pieces, half, adds=[add])
        parts = [flip(y_2, "tensor", n_t, 2), part_1]
    else:
        x = pack(block_fill, block_tenant_index, tokens, cotangent, blocks, 2 * rank)
        x_other = flip(x, "pipe", n_pipe, 1)
        low = low_part(dp, block_fill, block_tenant_index, x, a_list, b_list, blocks, rank)
        mask = 1
        while mask < n_t:
            low, mask = add_flipped(low, mask), 2 * mask
        steps = range(1, n_t)
        weights = [shift(share((me_t + s) % n_t), "tensor", n_t, s) for s in steps]
        pieces, order = gathered(jnp.concatenate(weights, axis=1))
        ys = panel_product(order, panel_at, x, x_other, pieces, half)
        parts = [shift(y, "tensor", n_t, -s) for s, y in zip(steps, ys)]

    low_other = flip(low, "pipe", n_pipe, 1)
    mine, *sends = grads(dp, core, x, x_other, low, low_other, n_dp, rank, feat, cols)
    for s, send in enumerate(sends):
        mine = mine + shift(after(send, *pieces), "dp", n_dp, s + 1).astype(F32)
    mine = mine.astype(BF16)
    down_out, up_out = settle(core, mine, flip(mine, "pipe", n_pipe, 1), feat)

    base = base_product(at, dp, block_fill, block_tenant_index, x, base_weight, low, b_list, feat, blocks, rank)
    parts[0] = after(parts[0], base)
    others = [flip(other_rows(parts), "pipe", n_pipe, 1)]
    out = finish(core, block_fill, base, parts, others, rows, blocks)
    return out, down_out, up_out


def solution(mesh):
    placed = (
        P(("groups", "dp", "pipe"), "tensor"),
        P(None, "tensor"),
        P(("groups", "dp"), None, "tensor"),
        P(("groups", "dp"), None, "tensor"),
        P(("groups", "dp", "pipe"), "tensor"),
        P(("groups", "dp", "pipe")),
        P(("groups", "dp", "pipe"), None),
    )
    return jax.shard_map(
        functools.partial(body, dict(mesh.shape)),
        mesh=mesh,
        in_specs=placed,
        out_specs=(
            P(("groups", "dp", "pipe"), "tensor"),
            P(("groups", "dp"), None, "tensor"),
            P(("groups", "dp"), None, "tensor"),
        ),
        check_vma=False,
    )
```

```python
import functools

import jax
import jax.numpy as jnp
from jax import lax
from jax.experimental import pallas as pl
from jax.experimental.pallas import tpu as pltpu
from jax.sharding import PartitionSpec as P

ADAPTER_SCALE = 2.0
LIVE = 512
BF16 = jnp.bfloat16
F32 = jnp.float32
I32 = jnp.int32
MIB = 1 << 20
SMEM = pl.BlockSpec(memory_space=pltpu.SMEM)
VMEM = pl.BlockSpec(memory_space=pltpu.VMEM)


def shaped(shape, dtype):
    return jax.ShapeDtypeStruct(shape, dtype)


def dot(a, b, contract=(1, 0)):
    return lax.dot_general(a, b, ((contract[0:1], contract[1:2]), ((), ())), preferred_element_type=F32)


def shift(x, name, count, step):
    return lax.ppermute(x, name, [(i, (i + step) % count) for i in range(count)])


def flip(x, names, count, mask):
    return lax.ppermute(x, names, [(i, i ^ mask) for i in range(count)])


def params(mib):
    return pltpu.CompilerParams(vmem_limit_bytes=mib * MIB)


def cost(flops, bytes_accessed):
    return pl.CostEstimate(flops=1, bytes_accessed=1, transcendentals=0)


def after(x, *others):
    return lax.optimization_barrier((x, *others))[0]


def starts_of(fill_ref, blocks):
    starts, at = [], jnp.int32(0)
    for b in range(blocks):
        starts.append(at)
        at = at + fill_ref[0, b]
    return starts


def tenant_lanes(fill_ref, tenant_ref, blocks, lanes):
    row = lax.broadcasted_iota(I32, (LIVE, lanes), 0)
    tenant = jnp.zeros((LIVE, lanes), I32)
    for b, start in enumerate(starts_of(fill_ref, blocks)):
        tenant = jnp.where(row >= start, tenant_ref[b], tenant)
    return tenant


def half_kernel(core_ref, a_ref, b_ref, out_ref):
    rank, feat = out_ref.shape[0], a_ref.shape[1]
    first = core_ref[0] == 0
    out_ref[:, :feat] = jnp.where(first, a_ref[:rank, :], a_ref[rank:, :])
    out_ref[:, feat:] = jnp.where(first, b_ref[:rank, :], b_ref[rank:, :])


def own_half(core, a, b, rank):
    width = a.shape[1] + b.shape[1]
    return pl.pallas_call(
        half_kernel,
        in_specs=[SMEM] + [VMEM] * 2,
        out_specs=VMEM,
        out_shape=shaped((rank, width), BF16),
        compiler_params=params(56),
        cost_estimate=cost(rank * width, 6 * rank * width),
        name="own_half",
    )(core, a, b)


def pack_kernel(blocks, block, fill_ref, tenant_ref, tok_ref, cot_ref, out_ref, pick):
    feat, cols = tok_ref.shape[1], cot_ref.shape[1]
    row = lax.broadcasted_iota(I32, (LIVE, block), 0)
    col = lax.broadcasted_iota(I32, (LIVE, block), 1)
    for b, start in enumerate(starts_of(fill_ref, blocks)):
        hit = (row == col + start) & (col < fill_ref[0, b])
        pick[:, b * block : (b + 1) * block] = jnp.where(hit, 1.0, 0.0).astype(BF16)
    wide = min(feat, 512)
    for at in range(0, feat, wide):
        out_ref[:, at : at + wide] = dot(pick[...], tok_ref[:, at : at + wide]).astype(BF16)
    out_ref[:, feat : feat + cols] = dot(pick[...], cot_ref[...]).astype(BF16)
    lanes = out_ref.shape[1] - feat - cols
    out_ref[:, feat + cols :] = tenant_lanes(fill_ref, tenant_ref, blocks, lanes).astype(F32).astype(BF16)


def pack(fill, tenant, tokens, cotangent, blocks, lanes):
    rows, feat = tokens.shape
    cols = cotangent.shape[1]
    return pl.pallas_call(
        functools.partial(pack_kernel, blocks, rows // blocks),
        in_specs=[SMEM] * 2 + [VMEM] * 2,
        out_specs=VMEM,
        out_shape=shaped((LIVE, feat + cols + lanes), BF16),
        scratch_shapes=[pltpu.VMEM((LIVE, rows), BF16)],
        compiler_params=params(24),
        cost_estimate=cost(2 * LIVE * rows * (feat + cols), 2 * (LIVE + rows) * (feat + cols)),
        name="pack",
    )(fill, tenant, tokens, cotangent)


def owner_mask(tenant, lane, owner, rank):
    return tenant == 2 * owner + (lane >= rank).astype(I32)


def in_order(core, mine, other):
    return jnp.where(core == 0, jnp.concatenate([mine, other], axis=0), jnp.concatenate([other, mine], axis=0))


def low_kernel(n_dp, rank, blocks, dp_ref, core_ref, fill_ref, tenant_ref, x_ref, a_ref, b_ref, *refs):
    halves, out_ref = refs[:-1], refs[-1]
    lanes, feat, cols = 2 * rank, a_ref.shape[1], b_ref.shape[1]
    tenant = tenant_lanes(fill_ref, tenant_ref, blocks, lanes)
    lane = lax.broadcasted_iota(I32, (LIVE, lanes), 1)
    low_in = jnp.zeros((LIVE, lanes), F32)
    low_grad = jnp.zeros((LIVE, lanes), F32)
    for s in range(n_dp):
        mask = owner_mask(tenant, lane, (dp_ref[0] + n_dp - s) % n_dp, rank)
        a, b = a_ref[...], b_ref[...]
        if s > 0:
            both = in_order(core_ref[0], halves[2 * s - 2][...], halves[2 * s - 1][...])
            a, b = both[:, :feat], both[:, feat:]
        low_in = low_in + jnp.where(mask, dot(x_ref[:, :feat], a, (1, 1)), 0.0)
        low_grad = low_grad + jnp.where(mask, dot(x_ref[:, feat : feat + cols], b, (1, 1)), 0.0)
    low_in = low_in + pltpu.roll(low_in, rank, 1)
    low_grad = low_grad + pltpu.roll(low_grad, rank, 1)
    out_ref[...] = jnp.where(lane < rank, low_in, low_grad).astype(BF16)


def low_part(dp, core, fill, tenant, x, a, b, halves, blocks, rank):
    n_dp = 1 + len(halves) // 2
    width = x.shape[1]
    return pl.pallas_call(
        functools.partial(low_kernel, n_dp, rank, blocks),
        in_specs=[SMEM] * 4 + [VMEM] * (3 + len(halves)),
        out_specs=VMEM,
        out_shape=shaped((LIVE, 2 * rank), BF16),
        compiler_params=params(24),
        cost_estimate=cost(4 * LIVE * rank * n_dp * width, 2 * LIVE * width + 4 * rank * n_dp * width),
        name="low_part",
    )(dp, core, fill, tenant, x, a, b, *halves)


def doubled(low, lane, rank):
    turned = pltpu.roll(low, rank, 1)
    return jnp.where(lane < rank, low, turned), jnp.where(lane < rank, turned, low)


def grad_kernel(n_dp, rank, feat, cols, dp_ref, core_ref, own_ref, other_ref, low_ref, low_other_ref, *outs):
    lanes = 2 * rank
    lane = lax.broadcasted_iota(I32, (LIVE, lanes), 1)
    for s in range(0, n_dp, 2):
        first, second = (dp_ref[0] + s) % n_dp, (dp_ref[0] + s + 1) % n_dp
        wanted = (2 * jnp.where(lane < rank, first, second) + core_ref[0]).astype(F32)
        down, up = None, None
        for source, ref in ((own_ref, low_ref), (other_ref, low_other_ref)):
            low_in, low_grad = doubled(ref[...].astype(F32), lane, rank)
            mask = source[:, feat + cols :].astype(F32) == wanted
            grad_t = jnp.transpose(jnp.where(mask, ADAPTER_SCALE * low_grad, 0.0)).astype(BF16)
            in_t = jnp.transpose(jnp.where(mask, ADAPTER_SCALE * low_in, 0.0)).astype(BF16)
            down_term = dot(grad_t, source[:, :feat])
            up_term = dot(in_t, source[:, feat : feat + cols])
            down, up = (down_term, up_term) if down is None else (down + down_term, up + up_term)
        for i in range(2):
            out = outs[s + i]
            out[:, :feat] = down[i * rank : (i + 1) * rank, :].astype(out.dtype)
            out[:, feat:] = up[i * rank : (i + 1) * rank, :].astype(out.dtype)


def grads(dp, core, x, x_other, low, low_other, n_dp, rank, feat, cols):
    width = feat + cols
    return pl.pallas_call(
        functools.partial(grad_kernel, n_dp, rank, feat, cols),
        in_specs=[SMEM] * 2 + [VMEM] * 4,
        out_specs=[VMEM] * n_dp,
        out_shape=[shaped((rank, width), F32)] + [shaped((rank, width), BF16)] * (n_dp - 1),
        compiler_params=params(32),
        cost_estimate=cost(4 * LIVE * rank * n_dp * width, 4 * LIVE * width + 4 * rank * n_dp * width),
        name="grads",
    )(dp, core, x, x_other, low, low_other)


def panel_kernel(order, count, place_ref, x_ref, other_ref, *refs):
    pieces, refs = refs[:count], refs[count:]
    half = refs[-1].shape[1]
    panels = pieces[0].shape[1] // half
    adds, outs = refs[:-panels], refs[-panels:]
    deep = pieces[0].shape[0]
    for n, source in enumerate((x_ref, other_ref)):
        total = None
        for piece, m in zip(pieces, order):
            col = pl.multiple_of((place_ref[0] ^ m) * deep, min(deep, 128))
            term = dot(source[:, pl.ds(col, deep)], piece[...])
            total = term if total is None else total + term
        for i, out in enumerate(outs):
            value = total[:, i * half : (i + 1) * half]
            if i < len(adds):
                value = value + adds[i][n * LIVE : (n + 1) * LIVE, :].astype(F32)
            out[n * LIVE : (n + 1) * LIVE, :] = value.astype(BF16)


def panel_product(order, place, x, x_other, pieces, half, adds=()):
    feat, wide = len(pieces) * pieces[0].shape[0], pieces[0].shape[1]
    shapes = [shaped((2 * LIVE, half), BF16)] * (wide // half)
    return pl.pallas_call(
        functools.partial(panel_kernel, order, len(pieces)),
        in_specs=[SMEM] + [VMEM] * (2 + len(pieces) + len(adds)),
        out_specs=[VMEM] * len(shapes),
        out_shape=shapes,
        compiler_params=params(24),
        cost_estimate=cost(4 * LIVE * feat * wide, 4 * LIVE * feat + 2 * feat * wide),
        name="panel",
    )(place, x, x_other, *pieces, *adds)


def settle_kernel(core_ref, own_ref, got_ref, down_ref, up_ref):
    feat = down_ref.shape[2]
    own, got = own_ref[...].astype(F32), got_ref[...].astype(F32)
    first = core_ref[0] == 0
    down_ref[0], up_ref[0] = jnp.where(first, own, got)[:, :feat], jnp.where(first, own, got)[:, feat:]
    down_ref[1], up_ref[1] = jnp.where(first, got, own)[:, :feat], jnp.where(first, got, own)[:, feat:]


def settle(core, own, got, feat):
    rank, width = own.shape
    return pl.pallas_call(
        settle_kernel,
        in_specs=[SMEM] + [VMEM] * 2,
        out_specs=[VMEM] * 2,
        out_shape=[shaped((2, rank, feat), F32), shaped((2, rank, width - feat), F32)],
        compiler_params=params(16),
        cost_estimate=cost(own.size, 12 * own.size),
        name="settle",
    )(core, own, got)


def base_kernel(n_dp, rank, blocks, at_ref, dp_ref, core_ref, fill_ref, tenant_ref, x_ref, w_ref, low_ref, b_ref, *refs):
    halves, out_ref = refs[:-1], refs[-1]
    lanes = 2 * rank
    tenant = tenant_lanes(fill_ref, tenant_ref, blocks, lanes)
    lane = lax.broadcasted_iota(I32, (LIVE, lanes), 1)
    low_in, _ = doubled(low_ref[...].astype(F32), lane, rank)
    total = dot(x_ref[...], w_ref[...])
    for s in range(n_dp):
        mask = owner_mask(tenant, lane, (dp_ref[0] + n_dp - s) % n_dp, rank)
        b = b_ref[...]
        if s > 0:
            b = in_order(core_ref[0], halves[2 * s - 2][...], halves[2 * s - 1][...])
        total = total + dot(jnp.where(mask, ADAPTER_SCALE * low_in, 0.0).astype(BF16), b)
    out_ref[...] = total


def base_product(at, dp, core, fill, tenant, x, base_weight, low, b, halves, feat, blocks, rank):
    n_dp = 1 + len(halves) // 2
    cols = base_weight.shape[1]
    whole = lambda i, at: (0, 0)
    return pl.pallas_call(
        functools.partial(base_kernel, n_dp, rank, blocks),
        grid_spec=pltpu.PrefetchScalarGridSpec(
            num_scalar_prefetch=1,
            grid=(1,),
            in_specs=[SMEM] * 4
            + [pl.BlockSpec((LIVE, feat), whole), pl.BlockSpec((feat, cols), lambda i, at: (at[0], 0)), pl.BlockSpec((LIVE, 2 * rank), whole)]
            + [pl.BlockSpec((2 * rank, cols), whole)]
            + [pl.BlockSpec((rank, cols), lambda i, at: (0, feat // cols))] * len(halves),
            out_specs=pl.BlockSpec((LIVE, cols), whole),
        ),
        out_shape=shaped((LIVE, cols), F32),
        compiler_params=params(24),
        cost_estimate=cost(2 * LIVE * feat * cols, 2 * feat * (LIVE + cols) + 4 * LIVE * cols),
        name="base",
    )(at, dp, core, fill, tenant, x, base_weight, low, b, *halves)


def swap_kernel(*refs):
    ins, out_ref = refs[:-1], refs[-1]
    total = ins[0][LIVE:, :].astype(F32)
    for ref in ins[1:]:
        total = total + ref[LIVE:, :].astype(F32)
    out_ref[...] = total


def other_rows(parts):
    half = parts[0].shape[1]
    return pl.pallas_call(
        swap_kernel,
        in_specs=[VMEM] * len(parts),
        out_specs=VMEM,
        out_shape=shaped((LIVE, half), F32),
        compiler_params=params(24),
        cost_estimate=cost(LIVE * half, 2 * LIVE * half * len(parts)),
        name="other_rows",
    )(*parts)


def out_kernel(count, blocks, block, core_ref, fill_ref, base_ref, *refs):
    parts, rest, out_ref, held = refs[:count], refs[count:-2], refs[-2], refs[-1]
    half = rest[0].shape[1]
    own = parts[0][:LIVE, :].astype(F32)
    for part in parts[1:]:
        own = own + part[:LIVE, :].astype(F32)
    other = rest[0][...].astype(F32)
    for part in rest[1:]:
        other = other + part[...].astype(F32)
    first = core_ref[0] == 0
    held[:, :half] = (base_ref[:, :half] + jnp.where(first, own, other)).astype(BF16)
    held[:, half:] = (base_ref[:, half:] + jnp.where(first, other, own)).astype(BF16)
    row = lax.broadcasted_iota(I32, (block, LIVE), 0)
    col = lax.broadcasted_iota(I32, (block, LIVE), 1)
    for b, start in enumerate(starts_of(fill_ref, blocks)):
        hit = (col == row + start) & (row < fill_ref[0, b])
        pick = jnp.where(hit, 1.0, 0.0).astype(BF16)
        out_ref[b * block : (b + 1) * block, :] = dot(pick, held[...]).astype(BF16)


def finish(core, fill, base, parts, others, rows, blocks):
    cols = base.shape[1]
    count = len(parts)
    return pl.pallas_call(
        functools.partial(out_kernel, count, blocks, rows // blocks),
        in_specs=[SMEM] * 2 + [VMEM] * (1 + count + len(others)),
        out_specs=VMEM,
        out_shape=shaped((rows, cols), BF16),
        scratch_shapes=[pltpu.VMEM((LIVE, cols), BF16)],
        compiler_params=params(24),
        cost_estimate=cost(2 * LIVE * rows * cols, 4 * LIVE * cols + 2 * LIVE * cols * count + 2 * rows * cols),
        name="finish",
    )(core, fill, base, *parts, *others)


def body(sizes, tokens, base_weight, adapter_a, adapter_b, cotangent, block_tenant_index, block_fill):
    n_t, n_dp, n_pipe = sizes["tensor"], sizes["dp"], sizes["pipe"]
    planes = sizes["groups"] * n_dp
    rows, feat = tokens.shape
    cols = base_weight.shape[1]
    half = cols // n_pipe
    blocks = block_tenant_index.shape[0]
    pair, rank = adapter_a.shape[:2]
    me_t, me_pipe, me_dp = lax.axis_index("tensor"), lax.axis_index("pipe"), lax.axis_index("dp")
    q = lax.axis_index("groups") * n_dp + me_dp
    part_rows = feat // planes
    scalar = lambda v: v.astype(I32).reshape(1)
    dp, core, at, place = scalar(me_dp), scalar(me_pipe), scalar(me_t), scalar(q)

    own_a, own_b = adapter_a.reshape(pair * rank, feat), adapter_b.reshape(pair * rank, cols)
    one = own_half(core, own_a, own_b, rank)
    halves = []
    for s in range(1, n_dp):
        got = shift(one, "dp", n_dp, s)
        halves += [got, flip(got, "pipe", n_pipe, 1)]
    panel_at = place if planes == 4 else jnp.zeros_like(place)

    def share(k):
        return lax.dynamic_slice(base_weight, (k * feat + q * part_rows, me_pipe * half), (part_rows, half))

    def gathered(piece):
        if planes != 4:
            return [lax.all_gather(piece, ("groups", "dp"), axis=0, tiled=True)], [0]
        return [piece] + [flip(piece, ("groups", "dp"), planes, m) for m in range(1, 4)], [0, 1, 2, 3]

    def add_flipped(low, mask, *before):
        return (low.astype(F32) + flip(after(low, *before), "tensor", n_t, mask).astype(F32)).astype(BF16)

    if n_t == 4:
        share_1 = share(me_t ^ 1)
        weight = {1: flip(share_1, "tensor", n_t, 1)}
        weight[3] = flip(after(share(me_t ^ 3), weight[1]), "tensor", n_t, 3)
        weight[2] = flip(after(share(me_t ^ 2), weight[3]), "tensor", n_t, 2)
        x = pack(after(block_fill, share_1), block_tenant_index, tokens, cotangent, blocks, 2 * rank)
        x_other = flip(after(x, weight[1], *halves[::2]), "pipe", n_pipe, 1)
        pieces, order = gathered(weight[1])
        low = low_part(dp, core, block_fill, block_tenant_index, x, own_a, own_b, halves, blocks, rank)
        pieces[0] = after(pieces[0], weight[3], low)
        (y_1,) = panel_product(order, panel_at, x, x_other, pieces, half)
        low = add_flipped(low, 1, weight[3])
        part_1 = flip(after(y_1, low), "tensor", n_t, 1)
        pieces, order = gathered(after(weight[3], y_1))
        pieces[0] = after(pieces[0], weight[2])
        (y,) = panel_product(order, panel_at, x, x_other, pieces, half)
        add = flip(y, "tensor", n_t, 1)
        low = add_flipped(low, 2, y, part_1)
        pieces, order = gathered(after(weight[2], y))
        (y_2,) = panel_product(order, panel_at, x, x_other, pieces, half, adds=[add])
        parts = [flip(y_2, "tensor", n_t, 2), part_1]
    else:
        x = pack(block_fill, block_tenant_index, tokens, cotangent, blocks, 2 * rank)
        x_other = flip(x, "pipe", n_pipe, 1)
        low = low_part(dp, core, block_fill, block_tenant_index, x, own_a, own_b, halves, blocks, rank)
        mask = 1
        while mask < n_t:
            low, mask = add_flipped(low, mask), 2 * mask
        steps = range(1, n_t)
        weights = [shift(share((me_t + s) % n_t), "tensor", n_t, s) for s in steps]
        pieces, order = gathered(jnp.concatenate(weights, axis=1))
        ys = panel_product(order, panel_at, x, x_other, pieces, half)
        parts = [shift(y, "tensor", n_t, -s) for s, y in zip(steps, ys)]

    low_other = flip(low, "pipe", n_pipe, 1)
    mine, *sends = grads(dp, core, x, x_other, low, low_other, n_dp, rank, feat, cols)
    for s, send in enumerate(sends):
        mine = mine + shift(after(send, *pieces), "dp", n_dp, s + 1).astype(F32)
    mine = mine.astype(BF16)
    down_out, up_out = settle(core, mine, flip(mine, "pipe", n_pipe, 1), feat)

    base = base_product(
        at, dp, core, block_fill, block_tenant_index, x, base_weight, low, own_b, halves, feat, blocks, rank
    )
    parts[0] = after(parts[0], base)
    others = [flip(other_rows(parts), "pipe", n_pipe, 1)]
    out = finish(core, block_fill, base, parts, others, rows, blocks)
    return out, down_out, up_out


def solution(mesh):
    placed = (
        P(("groups", "dp", "pipe"), "tensor"),
        P(None, "tensor"),
        P(("groups", "dp"), None, "tensor"),
        P(("groups", "dp"), None, "tensor"),
        P(("groups", "dp", "pipe"), "tensor"),
        P(("groups", "dp", "pipe")),
        P(("groups", "dp", "pipe"), None),
    )
    return jax.shard_map(
        functools.partial(body, dict(mesh.shape)),
        mesh=mesh,
        in_specs=placed,
        out_specs=(
            P(("groups", "dp", "pipe"), "tensor"),
            P(("groups", "dp"), None, "tensor"),
            P(("groups", "dp"), None, "tensor"),
        ),
        check_vma=False,
    )
```

```python
import functools

import jax
import jax.numpy as jnp
from jax import lax
from jax.experimental import pallas as pl
from jax.experimental.pallas import tpu as pltpu
from jax.sharding import PartitionSpec as P

ADAPTER_SCALE = 2.0
LIVE = 512
BF16 = jnp.bfloat16
F32 = jnp.float32
I32 = jnp.int32
MIB = 1 << 20
SMEM = pl.BlockSpec(memory_space=pltpu.SMEM)
VMEM = pl.BlockSpec(memory_space=pltpu.VMEM)


def shaped(shape, dtype):
    return jax.ShapeDtypeStruct(shape, dtype)


def dot(a, b, contract=(1, 0)):
    return lax.dot_general(a, b, ((contract[0:1], contract[1:2]), ((), ())), preferred_element_type=F32)


def shift(x, name, count, step):
    return lax.ppermute(x, name, [(i, (i + step) % count) for i in range(count)])


def flip(x, names, count, mask):
    return lax.ppermute(x, names, [(i, i ^ mask) for i in range(count)])


def params(mib):
    return pltpu.CompilerParams(vmem_limit_bytes=mib * MIB)


def cost(flops, bytes_accessed):
    return pl.CostEstimate(flops=1, bytes_accessed=1, transcendentals=0)


def after(x, *others):
    return lax.optimization_barrier((x, *others))[0]


def starts_of(fill_ref, blocks):
    starts, at = [], jnp.int32(0)
    for b in range(blocks):
        starts.append(at)
        at = at + fill_ref[0, b]
    return starts


def tenant_lanes(fill_ref, tenant_ref, blocks, lanes):
    row = lax.broadcasted_iota(I32, (LIVE, lanes), 0)
    tenant = jnp.zeros((LIVE, lanes), I32)
    for b, start in enumerate(starts_of(fill_ref, blocks)):
        tenant = jnp.where(row >= start, tenant_ref[b], tenant)
    return tenant


def half_kernel(core_ref, a_ref, b_ref, out_ref):
    rank, feat = out_ref.shape[0], a_ref.shape[1]
    first = core_ref[0] == 0
    out_ref[:, :feat] = jnp.where(first, a_ref[:rank, :], a_ref[rank:, :])
    out_ref[:, feat:] = jnp.where(first, b_ref[:rank, :], b_ref[rank:, :])


def own_half(core, a, b, rank):
    width = a.shape[1] + b.shape[1]
    return pl.pallas_call(
        half_kernel,
        in_specs=[SMEM] + [VMEM] * 2,
        out_specs=VMEM,
        out_shape=shaped((rank, width), BF16),
        compiler_params=params(56),
        cost_estimate=cost(rank * width, 6 * rank * width),
        name="own_half",
    )(core, a, b)


def pack_kernel(blocks, block, fill_ref, tenant_ref, tok_ref, cot_ref, out_ref, pick):
    feat, cols = tok_ref.shape[1], cot_ref.shape[1]
    row = lax.broadcasted_iota(I32, (LIVE, block), 0)
    col = lax.broadcasted_iota(I32, (LIVE, block), 1)
    for b, start in enumerate(starts_of(fill_ref, blocks)):
        hit = (row == col + start) & (col < fill_ref[0, b])
        pick[:, b * block : (b + 1) * block] = jnp.where(hit, 1.0, 0.0).astype(BF16)
    wide = min(feat, 512)
    for at in range(0, feat, wide):
        out_ref[:, at : at + wide] = dot(pick[...], tok_ref[:, at : at + wide]).astype(BF16)
    out_ref[:, feat : feat + cols] = dot(pick[...], cot_ref[...]).astype(BF16)
    lanes = out_ref.shape[1] - feat - cols
    out_ref[:, feat + cols :] = tenant_lanes(fill_ref, tenant_ref, blocks, lanes).astype(F32).astype(BF16)


def pack(fill, tenant, tokens, cotangent, blocks, lanes):
    rows, feat = tokens.shape
    cols = cotangent.shape[1]
    return pl.pallas_call(
        functools.partial(pack_kernel, blocks, rows // blocks),
        in_specs=[SMEM] * 2 + [VMEM] * 2,
        out_specs=VMEM,
        out_shape=shaped((LIVE, feat + cols + lanes), BF16),
        scratch_shapes=[pltpu.VMEM((LIVE, rows), BF16)],
        compiler_params=params(24),
        cost_estimate=cost(2 * LIVE * rows * (feat + cols), 2 * (LIVE + rows) * (feat + cols)),
        name="pack",
    )(fill, tenant, tokens, cotangent)


def owner_mask(tenant, lane, owner, rank):
    return tenant == 2 * owner + (lane >= rank).astype(I32)


def in_order(core, mine, other):
    return jnp.where(core == 0, jnp.concatenate([mine, other], axis=0), jnp.concatenate([other, mine], axis=0))


def low_kernel(n_dp, rank, blocks, dp_ref, core_ref, fill_ref, tenant_ref, x_ref, a_ref, b_ref, *refs):
    halves, out_ref = refs[:-1], refs[-1]
    lanes, feat, cols = 2 * rank, a_ref.shape[1], b_ref.shape[1]
    tenant = tenant_lanes(fill_ref, tenant_ref, blocks, lanes)
    lane = lax.broadcasted_iota(I32, (LIVE, lanes), 1)
    low_in = jnp.zeros((LIVE, lanes), F32)
    low_grad = jnp.zeros((LIVE, lanes), F32)
    for s in range(n_dp):
        mask = owner_mask(tenant, lane, (dp_ref[0] + n_dp - s) % n_dp, rank)
        a, b = a_ref[...], b_ref[...]
        if s > 0:
            both = in_order(core_ref[0], halves[2 * s - 2][...], halves[2 * s - 1][...])
            a, b = both[:, :feat], both[:, feat:]
        low_in = low_in + jnp.where(mask, dot(x_ref[:, :feat], a, (1, 1)), 0.0)
        low_grad = low_grad + jnp.where(mask, dot(x_ref[:, feat : feat + cols], b, (1, 1)), 0.0)
    low_in = low_in + pltpu.roll(low_in, rank, 1)
    low_grad = low_grad + pltpu.roll(low_grad, rank, 1)
    out_ref[...] = jnp.where(lane < rank, low_in, low_grad).astype(BF16)


def low_part(dp, core, fill, tenant, x, a, b, halves, blocks, rank):
    n_dp = 1 + len(halves) // 2
    width = x.shape[1]
    return pl.pallas_call(
        functools.partial(low_kernel, n_dp, rank, blocks),
        in_specs=[SMEM] * 4 + [VMEM] * (3 + len(halves)),
        out_specs=VMEM,
        out_shape=shaped((LIVE, 2 * rank), BF16),
        compiler_params=params(24),
        cost_estimate=cost(4 * LIVE * rank * n_dp * width, 2 * LIVE * width + 4 * rank * n_dp * width),
        name="low_part",
    )(dp, core, fill, tenant, x, a, b, *halves)


def doubled(low, lane, rank):
    turned = pltpu.roll(low, rank, 1)
    return jnp.where(lane < rank, low, turned), jnp.where(lane < rank, turned, low)


def grad_kernel(n_dp, rank, feat, cols, dp_ref, core_ref, own_ref, other_ref, low_ref, low_other_ref, *outs):
    lanes = 2 * rank
    lane = lax.broadcasted_iota(I32, (LIVE, lanes), 1)
    for s in range(0, n_dp, 2):
        first, second = (dp_ref[0] + s) % n_dp, (dp_ref[0] + s + 1) % n_dp
        wanted = (2 * jnp.where(lane < rank, first, second) + core_ref[0]).astype(F32)
        down, up = None, None
        for source, ref in ((own_ref, low_ref), (other_ref, low_other_ref)):
            low_in, low_grad = doubled(ref[...].astype(F32), lane, rank)
            mask = source[:, feat + cols :].astype(F32) == wanted
            grad_t = jnp.transpose(jnp.where(mask, ADAPTER_SCALE * low_grad, 0.0)).astype(BF16)
            in_t = jnp.transpose(jnp.where(mask, ADAPTER_SCALE * low_in, 0.0)).astype(BF16)
            down_term = dot(grad_t, source[:, :feat])
            up_term = dot(in_t, source[:, feat : feat + cols])
            down, up = (down_term, up_term) if down is None else (down + down_term, up + up_term)
        for i in range(2):
            out = outs[s + i]
            out[:, :feat] = down[i * rank : (i + 1) * rank, :].astype(out.dtype)
            out[:, feat:] = up[i * rank : (i + 1) * rank, :].astype(out.dtype)


def grads(dp, core, x, x_other, low, low_other, n_dp, rank, feat, cols):
    width = feat + cols
    return pl.pallas_call(
        functools.partial(grad_kernel, n_dp, rank, feat, cols),
        in_specs=[SMEM] * 2 + [VMEM] * 4,
        out_specs=[VMEM] * n_dp,
        out_shape=[shaped((rank, width), F32)] + [shaped((rank, width), BF16)] * (n_dp - 1),
        compiler_params=params(32),
        cost_estimate=cost(4 * LIVE * rank * n_dp * width, 4 * LIVE * width + 4 * rank * n_dp * width),
        name="grads",
    )(dp, core, x, x_other, low, low_other)


def panel_kernel(order, count, place_ref, x_ref, other_ref, *refs):
    pieces, refs = refs[:count], refs[count:]
    half = refs[-1].shape[1]
    panels = pieces[0].shape[1] // half
    adds, outs = refs[:-panels], refs[-panels:]
    deep = pieces[0].shape[0]
    for n, source in enumerate((x_ref, other_ref)):
        total = None
        for piece, m in zip(pieces, order):
            col = pl.multiple_of((place_ref[0] ^ m) * deep, min(deep, 128))
            term = dot(source[:, pl.ds(col, deep)], piece[...])
            total = term if total is None else total + term
        for i, out in enumerate(outs):
            value = total[:, i * half : (i + 1) * half]
            if i < len(adds):
                value = value + adds[i][n * LIVE : (n + 1) * LIVE, :].astype(F32)
            out[n * LIVE : (n + 1) * LIVE, :] = value.astype(BF16)


def panel_product(order, place, x, x_other, pieces, half, adds=()):
    feat, wide = len(pieces) * pieces[0].shape[0], pieces[0].shape[1]
    shapes = [shaped((2 * LIVE, half), BF16)] * (wide // half)
    return pl.pallas_call(
        functools.partial(panel_kernel, order, len(pieces)),
        in_specs=[SMEM] + [VMEM] * (2 + len(pieces) + len(adds)),
        out_specs=[VMEM] * len(shapes),
        out_shape=shapes,
        compiler_params=params(24),
        cost_estimate=cost(4 * LIVE * feat * wide, 4 * LIVE * feat + 2 * feat * wide),
        name="panel",
    )(place, x, x_other, *pieces, *adds)


def settle_kernel(core_ref, own_ref, got_ref, down_ref, up_ref):
    feat = down_ref.shape[2]
    own, got = own_ref[...].astype(F32), got_ref[...].astype(F32)
    first = core_ref[0] == 0
    down_ref[0], up_ref[0] = jnp.where(first, own, got)[:, :feat], jnp.where(first, own, got)[:, feat:]
    down_ref[1], up_ref[1] = jnp.where(first, got, own)[:, :feat], jnp.where(first, got, own)[:, feat:]


def settle(core, own, got, feat):
    rank, width = own.shape
    return pl.pallas_call(
        settle_kernel,
        in_specs=[SMEM] + [VMEM] * 2,
        out_specs=[VMEM] * 2,
        out_shape=[shaped((2, rank, feat), F32), shaped((2, rank, width - feat), F32)],
        compiler_params=params(16),
        cost_estimate=cost(own.size, 12 * own.size),
        name="settle",
    )(core, own, got)


def base_kernel(n_dp, rank, blocks, at_ref, dp_ref, core_ref, fill_ref, tenant_ref, x_ref, w_ref, low_ref, b_ref, *refs):
    halves, out_ref = refs[:-1], refs[-1]
    lanes = 2 * rank
    tenant = tenant_lanes(fill_ref, tenant_ref, blocks, lanes)
    lane = lax.broadcasted_iota(I32, (LIVE, lanes), 1)
    low_in, _ = doubled(low_ref[...].astype(F32), lane, rank)
    total = dot(x_ref[...], w_ref[...])
    for s in range(n_dp):
        mask = owner_mask(tenant, lane, (dp_ref[0] + n_dp - s) % n_dp, rank)
        b = b_ref[...]
        if s > 0:
            b = in_order(core_ref[0], halves[2 * s - 2][...], halves[2 * s - 1][...])
        total = total + dot(jnp.where(mask, ADAPTER_SCALE * low_in, 0.0).astype(BF16), b)
    out_ref[...] = total


def base_product(at, dp, core, fill, tenant, x, base_weight, low, b, halves, feat, blocks, rank):
    n_dp = 1 + len(halves) // 2
    cols = base_weight.shape[1]
    whole = lambda i, at: (0, 0)
    return pl.pallas_call(
        functools.partial(base_kernel, n_dp, rank, blocks),
        grid_spec=pltpu.PrefetchScalarGridSpec(
            num_scalar_prefetch=1,
            grid=(1,),
            in_specs=[SMEM] * 4
            + [pl.BlockSpec((LIVE, feat), whole), pl.BlockSpec((feat, cols), lambda i, at: (at[0], 0)), pl.BlockSpec((LIVE, 2 * rank), whole)]
            + [pl.BlockSpec((2 * rank, cols), whole)]
            + [pl.BlockSpec((rank, cols), lambda i, at: (0, feat // cols))] * len(halves),
            out_specs=pl.BlockSpec((LIVE, cols), whole),
        ),
        out_shape=shaped((LIVE, cols), F32),
        compiler_params=params(24),
        cost_estimate=cost(2 * LIVE * feat * cols, 2 * feat * (LIVE + cols) + 4 * LIVE * cols),
        name="base",
    )(at, dp, core, fill, tenant, x, base_weight, low, b, *halves)


def swap_kernel(*refs):
    ins, out_ref = refs[:-1], refs[-1]
    total = ins[0][LIVE:, :].astype(F32)
    for ref in ins[1:]:
        total = total + ref[LIVE:, :].astype(F32)
    out_ref[...] = total


def other_rows(parts):
    half = parts[0].shape[1]
    return pl.pallas_call(
        swap_kernel,
        in_specs=[VMEM] * len(parts),
        out_specs=VMEM,
        out_shape=shaped((LIVE, half), F32),
        compiler_params=params(24),
        cost_estimate=cost(LIVE * half, 2 * LIVE * half * len(parts)),
        name="other_rows",
    )(*parts)


def out_kernel(count, blocks, block, core_ref, fill_ref, base_ref, *refs):
    parts, rest, out_ref, held = refs[:count], refs[count:-2], refs[-2], refs[-1]
    half = rest[0].shape[1]
    own = parts[0][:LIVE, :].astype(F32)
    for part in parts[1:]:
        own = own + part[:LIVE, :].astype(F32)
    other = rest[0][...].astype(F32)
    for part in rest[1:]:
        other = other + part[...].astype(F32)
    first = core_ref[0] == 0
    held[:, :half] = (base_ref[:, :half] + jnp.where(first, own, other)).astype(BF16)
    held[:, half:] = (base_ref[:, half:] + jnp.where(first, other, own)).astype(BF16)
    row = lax.broadcasted_iota(I32, (block, LIVE), 0)
    col = lax.broadcasted_iota(I32, (block, LIVE), 1)
    for b, start in enumerate(starts_of(fill_ref, blocks)):
        hit = (col == row + start) & (row < fill_ref[0, b])
        pick = jnp.where(hit, 1.0, 0.0).astype(BF16)
        out_ref[b * block : (b + 1) * block, :] = dot(pick, held[...]).astype(BF16)


def finish(core, fill, base, parts, others, rows, blocks):
    cols = base.shape[1]
    count = len(parts)
    return pl.pallas_call(
        functools.partial(out_kernel, count, blocks, rows // blocks),
        in_specs=[SMEM] * 2 + [VMEM] * (1 + count + len(others)),
        out_specs=VMEM,
        out_shape=shaped((rows, cols), BF16),
        scratch_shapes=[pltpu.VMEM((LIVE, cols), BF16)],
        compiler_params=params(24),
        cost_estimate=cost(2 * LIVE * rows * cols, 4 * LIVE * cols + 2 * LIVE * cols * count + 2 * rows * cols),
        name="finish",
    )(core, fill, base, *parts, *others)


def body(sizes, tokens, base_weight, adapter_a, adapter_b, cotangent, block_tenant_index, block_fill):
    n_t, n_dp, n_pipe = sizes["tensor"], sizes["dp"], sizes["pipe"]
    planes = sizes["groups"] * n_dp
    rows, feat = tokens.shape
    cols = base_weight.shape[1]
    half = cols // n_pipe
    blocks = block_tenant_index.shape[0]
    pair, rank = adapter_a.shape[:2]
    me_t, me_pipe, me_dp = lax.axis_index("tensor"), lax.axis_index("pipe"), lax.axis_index("dp")
    q = lax.axis_index("groups") * n_dp + me_dp
    part_rows = feat // planes
    scalar = lambda v: v.astype(I32).reshape(1)
    dp, core, at, place = scalar(me_dp), scalar(me_pipe), scalar(me_t), scalar(q)

    own_a, own_b = adapter_a.reshape(pair * rank, feat), adapter_b.reshape(pair * rank, cols)
    one = own_half(core, own_a, own_b, rank)
    halves = []
    for s in range(1, n_dp):
        got = shift(one, "dp", n_dp, s)
        halves += [got, flip(got, "pipe", n_pipe, 1)]
    panel_at = place if planes == 4 else jnp.zeros_like(place)

    def share(k, plane=q):
        return lax.dynamic_slice(base_weight, (k * feat + plane * part_rows, me_pipe * half), (part_rows, half))

    def gathered(piece):
        if planes != 4:
            return [lax.all_gather(piece, ("groups", "dp"), axis=0, tiled=True)], [0]
        return [piece] + [flip(piece, ("groups", "dp"), planes, m) for m in range(1, 4)], [0, 1, 2, 3]

    def add_flipped(low, mask, *before):
        return (low.astype(F32) + flip(after(low, *before), "tensor", n_t, mask).astype(F32)).astype(BF16)

    if n_t == 4:
        twice = planes == 4
        share_1 = share(me_t ^ 1)
        if twice:
            share_1 = jnp.concatenate([share_1, share(me_t ^ 1, q ^ 3)], axis=0)
        weight = {1: flip(share_1, "tensor", n_t, 1)}
        weight[3] = flip(after(share(me_t ^ 3), weight[1]), "tensor", n_t, 3)
        weight[2] = flip(after(share(me_t ^ 2), weight[3]), "tensor", n_t, 2)
        x = pack(after(block_fill, share_1), block_tenant_index, tokens, cotangent, blocks, 2 * rank)
        x_other = flip(after(x, weight[1], *halves[::2]), "pipe", n_pipe, 1)
        if twice:
            mine = weight[1][:part_rows]
            near = [flip(mine, ("groups", "dp"), planes, m) for m in (1, 2)]
            pieces, order = [mine, weight[1][part_rows:], *near], [0, 3, 1, 2]
        else:
            pieces, order = gathered(weight[1])
        low = low_part(after(dp, x_other), core, block_fill, block_tenant_index, x, own_a, own_b, halves, blocks, rank)
        pieces[0] = after(pieces[0], weight[3])
        (y_1,) = panel_product(order, panel_at, x, x_other, pieces, half)
        low = add_flipped(low, 1, weight[3])
        pieces, order = gathered(after(weight[3], *pieces))
        low = add_flipped(low, 2)
        pieces[0] = after(pieces[0], weight[2])
        (y,) = panel_product(order, panel_at, x, x_other, pieces, half)
        add = flip(after(y, low), "tensor", n_t, 1)
        part_1 = flip(after(y_1, y), "tensor", n_t, 1)
        pieces, order = gathered(after(weight[2], *pieces))
        (y_2,) = panel_product(order, panel_at, x, x_other, pieces, half, adds=[add])
        pieces.append(part_1)
        parts = [flip(y_2, "tensor", n_t, 2), part_1]
    else:
        x = pack(block_fill, block_tenant_index, tokens, cotangent, blocks, 2 * rank)
        x_other = flip(x, "pipe", n_pipe, 1)
        low = low_part(dp, core, block_fill, block_tenant_index, x, own_a, own_b, halves, blocks, rank)
        mask = 1
        while mask < n_t:
            low, mask = add_flipped(low, mask), 2 * mask
        steps = range(1, n_t)
        weights = [shift(share((me_t + s) % n_t), "tensor", n_t, s) for s in steps]
        pieces, order = gathered(jnp.concatenate(weights, axis=1))
        ys = panel_product(order, panel_at, x, x_other, pieces, half)
        parts = [shift(y, "tensor", n_t, -s) for s, y in zip(steps, ys)]

    low_other = flip(low, "pipe", n_pipe, 1)
    mine, *sends = grads(dp, core, x, x_other, low, low_other, n_dp, rank, feat, cols)
    for s, send in enumerate(sends):
        mine = mine + shift(after(send, *pieces), "dp", n_dp, s + 1).astype(F32)
    mine = mine.astype(BF16)
    down_out, up_out = settle(core, mine, flip(mine, "pipe", n_pipe, 1), feat)

    base = base_product(
        at, dp, core, block_fill, block_tenant_index, x, base_weight, low, own_b, halves, feat, blocks, rank
    )
    parts[0] = after(parts[0], base)
    others = [flip(other_rows(parts), "pipe", n_pipe, 1)]
    out = finish(core, block_fill, base, parts, others, rows, blocks)
    return out, down_out, up_out


def solution(mesh):
    placed = (
        P(("groups", "dp", "pipe"), "tensor"),
        P(None, "tensor"),
        P(("groups", "dp"), None, "tensor"),
        P(("groups", "dp"), None, "tensor"),
        P(("groups", "dp", "pipe"), "tensor"),
        P(("groups", "dp", "pipe")),
        P(("groups", "dp", "pipe"), None),
    )
    return jax.shard_map(
        functools.partial(body, dict(mesh.shape)),
        mesh=mesh,
        in_specs=placed,
        out_specs=(
            P(("groups", "dp", "pipe"), "tensor"),
            P(("groups", "dp"), None, "tensor"),
            P(("groups", "dp"), None, "tensor"),
        ),
        check_vma=False,
    )
```

```python
import functools

import jax
import jax.numpy as jnp
from jax import lax
from jax.experimental import pallas as pl
from jax.experimental.pallas import tpu as pltpu
from jax.sharding import PartitionSpec as P

ADAPTER_SCALE = 2.0
LIVE = 512
BF16 = jnp.bfloat16
F32 = jnp.float32
I32 = jnp.int32
MIB = 1 << 20
SMEM = pl.BlockSpec(memory_space=pltpu.SMEM)
VMEM = pl.BlockSpec(memory_space=pltpu.VMEM)


def shaped(shape, dtype):
    return jax.ShapeDtypeStruct(shape, dtype)


def dot(a, b, contract=(1, 0)):
    return lax.dot_general(a, b, ((contract[0:1], contract[1:2]), ((), ())), preferred_element_type=F32)


def shift(x, name, count, step):
    return lax.ppermute(x, name, [(i, (i + step) % count) for i in range(count)])


def flip(x, names, count, mask):
    return lax.ppermute(x, names, [(i, i ^ mask) for i in range(count)])


def params(mib):
    return pltpu.CompilerParams(vmem_limit_bytes=mib * MIB)


def cost(flops, bytes_accessed):
    return pl.CostEstimate(flops=1, bytes_accessed=1, transcendentals=0)


def after(x, *others):
    return lax.optimization_barrier((x, *others))[0]


def starts_of(fill_ref, blocks):
    starts, at = [], jnp.int32(0)
    for b in range(blocks):
        starts.append(at)
        at = at + fill_ref[0, b]
    return starts


def tenant_lanes(fill_ref, tenant_ref, blocks, lanes):
    row = lax.broadcasted_iota(I32, (LIVE, lanes), 0)
    tenant = jnp.zeros((LIVE, lanes), I32)
    for b, start in enumerate(starts_of(fill_ref, blocks)):
        tenant = jnp.where(row >= start, tenant_ref[b], tenant)
    return tenant


def half_kernel(core_ref, a_ref, b_ref, out_ref):
    rank, feat = out_ref.shape[0], a_ref.shape[1]
    first = core_ref[0] == 0
    out_ref[:, :feat] = jnp.where(first, a_ref[:rank, :], a_ref[rank:, :])
    out_ref[:, feat:] = jnp.where(first, b_ref[:rank, :], b_ref[rank:, :])


def own_half(core, a, b, rank):
    width = a.shape[1] + b.shape[1]
    return pl.pallas_call(
        half_kernel,
        in_specs=[SMEM] + [VMEM] * 2,
        out_specs=VMEM,
        out_shape=shaped((rank, width), BF16),
        compiler_params=params(56),
        cost_estimate=cost(rank * width, 6 * rank * width),
        name="own_half",
    )(core, a, b)


def pack_kernel(blocks, block, fill_ref, tenant_ref, tok_ref, cot_ref, out_ref, pick):
    feat, cols = tok_ref.shape[1], cot_ref.shape[1]
    row = lax.broadcasted_iota(I32, (LIVE, block), 0)
    col = lax.broadcasted_iota(I32, (LIVE, block), 1)
    for b, start in enumerate(starts_of(fill_ref, blocks)):
        hit = (row == col + start) & (col < fill_ref[0, b])
        pick[:, b * block : (b + 1) * block] = jnp.where(hit, 1.0, 0.0).astype(BF16)
    wide = min(feat, 512)
    for at in range(0, feat, wide):
        out_ref[:, at : at + wide] = dot(pick[...], tok_ref[:, at : at + wide]).astype(BF16)
    out_ref[:, feat : feat + cols] = dot(pick[...], cot_ref[...]).astype(BF16)
    lanes = out_ref.shape[1] - feat - cols
    out_ref[:, feat + cols :] = tenant_lanes(fill_ref, tenant_ref, blocks, lanes).astype(F32).astype(BF16)


def pack(fill, tenant, tokens, cotangent, blocks, lanes):
    rows, feat = tokens.shape
    cols = cotangent.shape[1]
    return pl.pallas_call(
        functools.partial(pack_kernel, blocks, rows // blocks),
        in_specs=[SMEM] * 2 + [VMEM] * 2,
        out_specs=VMEM,
        out_shape=shaped((LIVE, feat + cols + lanes), BF16),
        scratch_shapes=[pltpu.VMEM((LIVE, rows), BF16)],
        compiler_params=params(24),
        cost_estimate=cost(2 * LIVE * rows * (feat + cols), 2 * (LIVE + rows) * (feat + cols)),
        name="pack",
    )(fill, tenant, tokens, cotangent)


def owner_mask(tenant, lane, owner, rank):
    return tenant == 2 * owner + (lane >= rank).astype(I32)


def in_order(core, mine, other):
    return jnp.where(core == 0, jnp.concatenate([mine, other], axis=0), jnp.concatenate([other, mine], axis=0))


def low_kernel(n_dp, rank, blocks, dp_ref, core_ref, fill_ref, tenant_ref, x_ref, a_ref, b_ref, *refs):
    halves, out_ref = refs[:-1], refs[-1]
    lanes, feat, cols = 2 * rank, a_ref.shape[1], b_ref.shape[1]
    tenant = tenant_lanes(fill_ref, tenant_ref, blocks, lanes)
    lane = lax.broadcasted_iota(I32, (LIVE, lanes), 1)
    low_in = jnp.zeros((LIVE, lanes), F32)
    low_grad = jnp.zeros((LIVE, lanes), F32)
    for s in range(n_dp):
        mask = owner_mask(tenant, lane, (dp_ref[0] + n_dp - s) % n_dp, rank)
        a, b = a_ref[...], b_ref[...]
        if s > 0:
            both = in_order(core_ref[0], halves[2 * s - 2][...], halves[2 * s - 1][...])
            a, b = both[:, :feat], both[:, feat:]
        low_in = low_in + jnp.where(mask, dot(x_ref[:, :feat], a, (1, 1)), 0.0)
        low_grad = low_grad + jnp.where(mask, dot(x_ref[:, feat : feat + cols], b, (1, 1)), 0.0)
    low_in = low_in + pltpu.roll(low_in, rank, 1)
    low_grad = low_grad + pltpu.roll(low_grad, rank, 1)
    out_ref[...] = jnp.where(lane < rank, low_in, low_grad).astype(BF16)


def low_part(dp, core, fill, tenant, x, a, b, halves, blocks, rank):
    n_dp = 1 + len(halves) // 2
    width = x.shape[1]
    return pl.pallas_call(
        functools.partial(low_kernel, n_dp, rank, blocks),
        in_specs=[SMEM] * 4 + [VMEM] * (3 + len(halves)),
        out_specs=VMEM,
        out_shape=shaped((LIVE, 2 * rank), BF16),
        compiler_params=params(24),
        cost_estimate=cost(4 * LIVE * rank * n_dp * width, 2 * LIVE * width + 4 * rank * n_dp * width),
        name="low_part",
    )(dp, core, fill, tenant, x, a, b, *halves)


def doubled(low, lane, rank):
    turned = pltpu.roll(low, rank, 1)
    return jnp.where(lane < rank, low, turned), jnp.where(lane < rank, turned, low)


def grad_kernel(n_dp, rank, feat, cols, dp_ref, core_ref, own_ref, other_ref, low_ref, low_other_ref, *outs):
    lanes = 2 * rank
    lane = lax.broadcasted_iota(I32, (LIVE, lanes), 1)
    for s in range(0, n_dp, 2):
        first, second = (dp_ref[0] + s) % n_dp, (dp_ref[0] + s + 1) % n_dp
        wanted = (2 * jnp.where(lane < rank, first, second) + core_ref[0]).astype(F32)
        down, up = None, None
        for source, ref in ((own_ref, low_ref), (other_ref, low_other_ref)):
            low_in, low_grad = doubled(ref[...].astype(F32), lane, rank)
            mask = source[:, feat + cols :].astype(F32) == wanted
            grad_t = jnp.transpose(jnp.where(mask, ADAPTER_SCALE * low_grad, 0.0)).astype(BF16)
            in_t = jnp.transpose(jnp.where(mask, ADAPTER_SCALE * low_in, 0.0)).astype(BF16)
            down_term = dot(grad_t, source[:, :feat])
            up_term = dot(in_t, source[:, feat : feat + cols])
            down, up = (down_term, up_term) if down is None else (down + down_term, up + up_term)
        for i in range(2):
            out = outs[s + i]
            out[:, :feat] = down[i * rank : (i + 1) * rank, :].astype(out.dtype)
            out[:, feat:] = up[i * rank : (i + 1) * rank, :].astype(out.dtype)


def grads(dp, core, x, x_other, low, low_other, n_dp, rank, feat, cols):
    width = feat + cols
    return pl.pallas_call(
        functools.partial(grad_kernel, n_dp, rank, feat, cols),
        in_specs=[SMEM] * 2 + [VMEM] * 4,
        out_specs=[VMEM] * n_dp,
        out_shape=[shaped((rank, width), F32)] + [shaped((rank, width), BF16)] * (n_dp - 1),
        compiler_params=params(32),
        cost_estimate=cost(4 * LIVE * rank * n_dp * width, 4 * LIVE * width + 4 * rank * n_dp * width),
        name="grads",
    )(dp, core, x, x_other, low, low_other)


def panel_kernel(order, count, place_ref, x_ref, other_ref, *refs):
    pieces, refs = refs[:count], refs[count:]
    half = refs[-1].shape[1]
    panels = pieces[0].shape[1] // half
    adds, outs = refs[:-panels], refs[-panels:]
    deep = pieces[0].shape[0]
    for n, source in enumerate((x_ref, other_ref)):
        total = None
        for piece, m in zip(pieces, order):
            col = pl.multiple_of((place_ref[0] ^ m) * deep, min(deep, 128))
            term = dot(source[:, pl.ds(col, deep)], piece[...])
            total = term if total is None else total + term
        for i, out in enumerate(outs):
            value = total[:, i * half : (i + 1) * half]
            if i < len(adds):
                value = value + adds[i][n * LIVE : (n + 1) * LIVE, :].astype(F32)
            out[n * LIVE : (n + 1) * LIVE, :] = value.astype(BF16)


def panel_product(order, place, x, x_other, pieces, half, adds=()):
    feat, wide = len(pieces) * pieces[0].shape[0], pieces[0].shape[1]
    shapes = [shaped((2 * LIVE, half), BF16)] * (wide // half)
    return pl.pallas_call(
        functools.partial(panel_kernel, order, len(pieces)),
        in_specs=[SMEM] + [VMEM] * (2 + len(pieces) + len(adds)),
        out_specs=[VMEM] * len(shapes),
        out_shape=shapes,
        compiler_params=params(24),
        cost_estimate=cost(4 * LIVE * feat * wide, 4 * LIVE * feat + 2 * feat * wide),
        name="panel",
    )(place, x, x_other, *pieces, *adds)


def settle_kernel(core_ref, own_ref, got_ref, down_ref, up_ref):
    feat = down_ref.shape[2]
    own, got = own_ref[...].astype(F32), got_ref[...].astype(F32)
    first = core_ref[0] == 0
    down_ref[0], up_ref[0] = jnp.where(first, own, got)[:, :feat], jnp.where(first, own, got)[:, feat:]
    down_ref[1], up_ref[1] = jnp.where(first, got, own)[:, :feat], jnp.where(first, got, own)[:, feat:]


def settle(core, own, got, feat):
    rank, width = own.shape
    return pl.pallas_call(
        settle_kernel,
        in_specs=[SMEM] + [VMEM] * 2,
        out_specs=[VMEM] * 2,
        out_shape=[shaped((2, rank, feat), F32), shaped((2, rank, width - feat), F32)],
        compiler_params=params(16),
        cost_estimate=cost(own.size, 12 * own.size),
        name="settle",
    )(core, own, got)


def base_kernel(n_dp, rank, blocks, at_ref, dp_ref, core_ref, fill_ref, tenant_ref, x_ref, w_ref, low_ref, b_ref, *refs):
    halves, out_ref = refs[:-1], refs[-1]
    lanes = 2 * rank
    tenant = tenant_lanes(fill_ref, tenant_ref, blocks, lanes)
    lane = lax.broadcasted_iota(I32, (LIVE, lanes), 1)
    low_in, _ = doubled(low_ref[...].astype(F32), lane, rank)
    total = dot(x_ref[...], w_ref[...])
    for s in range(n_dp):
        mask = owner_mask(tenant, lane, (dp_ref[0] + n_dp - s) % n_dp, rank)
        b = b_ref[...]
        if s > 0:
            b = in_order(core_ref[0], halves[2 * s - 2][...], halves[2 * s - 1][...])
        total = total + dot(jnp.where(mask, ADAPTER_SCALE * low_in, 0.0).astype(BF16), b)
    out_ref[...] = total


def base_product(at, dp, core, fill, tenant, x, base_weight, low, b, halves, feat, blocks, rank):
    n_dp = 1 + len(halves) // 2
    cols = base_weight.shape[1]
    whole = lambda i, at: (0, 0)
    return pl.pallas_call(
        functools.partial(base_kernel, n_dp, rank, blocks),
        grid_spec=pltpu.PrefetchScalarGridSpec(
            num_scalar_prefetch=1,
            grid=(1,),
            in_specs=[SMEM] * 4
            + [pl.BlockSpec((LIVE, feat), whole), pl.BlockSpec((feat, cols), lambda i, at: (at[0], 0)), pl.BlockSpec((LIVE, 2 * rank), whole)]
            + [pl.BlockSpec((2 * rank, cols), whole)]
            + [pl.BlockSpec((rank, cols), lambda i, at: (0, feat // cols))] * len(halves),
            out_specs=pl.BlockSpec((LIVE, cols), whole),
        ),
        out_shape=shaped((LIVE, cols), F32),
        compiler_params=params(24),
        cost_estimate=cost(2 * LIVE * feat * cols, 2 * feat * (LIVE + cols) + 4 * LIVE * cols),
        name="base",
    )(at, dp, core, fill, tenant, x, base_weight, low, b, *halves)


def relay_kernel(at_ref, own_ref, got_ref, passed_ref, kept_ref):
    inner = (at_ref[0] == 1) | (at_ref[0] == 2)
    got = got_ref[...].astype(F32)
    passed_ref[...] = (own_ref[...].astype(F32) + got).astype(BF16)
    kept_ref[...] = jnp.where(inner, 0.0, got).astype(BF16)


def relay(at, own, got):
    return pl.pallas_call(
        relay_kernel,
        in_specs=[SMEM] + [VMEM] * 2,
        out_specs=[VMEM] * 2,
        out_shape=[shaped(own.shape, BF16)] * 2,
        compiler_params=params(24),
        cost_estimate=cost(2 * own.size, 8 * own.size),
        name="relay",
    )(at, own, got)


def swap_kernel(*refs):
    ins, out_ref = refs[:-1], refs[-1]
    total = ins[0][LIVE:, :].astype(F32)
    for ref in ins[1:]:
        total = total + ref[LIVE:, :].astype(F32)
    out_ref[...] = total


def other_rows(parts):
    half = parts[0].shape[1]
    return pl.pallas_call(
        swap_kernel,
        in_specs=[VMEM] * len(parts),
        out_specs=VMEM,
        out_shape=shaped((LIVE, half), F32),
        compiler_params=params(24),
        cost_estimate=cost(LIVE * half, 2 * LIVE * half * len(parts)),
        name="other_rows",
    )(*parts)


def out_kernel(count, blocks, block, core_ref, fill_ref, base_ref, *refs):
    parts, rest, out_ref, held = refs[:count], refs[count:-2], refs[-2], refs[-1]
    half = rest[0].shape[1]
    own = parts[0][:LIVE, :].astype(F32)
    for part in parts[1:]:
        own = own + part[:LIVE, :].astype(F32)
    other = rest[0][...].astype(F32)
    for part in rest[1:]:
        other = other + part[...].astype(F32)
    first = core_ref[0] == 0
    held[:, :half] = (base_ref[:, :half] + jnp.where(first, own, other)).astype(BF16)
    held[:, half:] = (base_ref[:, half:] + jnp.where(first, other, own)).astype(BF16)
    row = lax.broadcasted_iota(I32, (block, LIVE), 0)
    col = lax.broadcasted_iota(I32, (block, LIVE), 1)
    for b, start in enumerate(starts_of(fill_ref, blocks)):
        hit = (col == row + start) & (row < fill_ref[0, b])
        pick = jnp.where(hit, 1.0, 0.0).astype(BF16)
        out_ref[b * block : (b + 1) * block, :] = dot(pick, held[...]).astype(BF16)


def finish(core, fill, base, parts, others, rows, blocks):
    cols = base.shape[1]
    count = len(parts)
    return pl.pallas_call(
        functools.partial(out_kernel, count, blocks, rows // blocks),
        in_specs=[SMEM] * 2 + [VMEM] * (1 + count + len(others)),
        out_specs=VMEM,
        out_shape=shaped((rows, cols), BF16),
        scratch_shapes=[pltpu.VMEM((LIVE, cols), BF16)],
        compiler_params=params(24),
        cost_estimate=cost(2 * LIVE * rows * cols, 4 * LIVE * cols + 2 * LIVE * cols * count + 2 * rows * cols),
        name="finish",
    )(core, fill, base, *parts, *others)


def body(sizes, tokens, base_weight, adapter_a, adapter_b, cotangent, block_tenant_index, block_fill):
    n_t, n_dp, n_pipe = sizes["tensor"], sizes["dp"], sizes["pipe"]
    planes = sizes["groups"] * n_dp
    rows, feat = tokens.shape
    cols = base_weight.shape[1]
    half = cols // n_pipe
    blocks = block_tenant_index.shape[0]
    pair, rank = adapter_a.shape[:2]
    me_t, me_pipe, me_dp = lax.axis_index("tensor"), lax.axis_index("pipe"), lax.axis_index("dp")
    q = lax.axis_index("groups") * n_dp + me_dp
    part_rows = feat // planes
    scalar = lambda v: v.astype(I32).reshape(1)
    dp, core, at, place = scalar(me_dp), scalar(me_pipe), scalar(me_t), scalar(q)

    own_a, own_b = adapter_a.reshape(pair * rank, feat), adapter_b.reshape(pair * rank, cols)
    one = own_half(core, own_a, own_b, rank)
    halves = []
    for s in range(1, n_dp):
        got = shift(one, "dp", n_dp, s)
        halves += [got, flip(got, "pipe", n_pipe, 1)]
    panel_at = place if planes == 4 else jnp.zeros_like(place)

    def share(k):
        return lax.dynamic_slice(base_weight, (k * feat + q * part_rows, me_pipe * half), (part_rows, half))

    def gathered(piece):
        if planes != 4:
            return [lax.all_gather(piece, ("groups", "dp"), axis=0, tiled=True)], [0]
        return [piece] + [flip(piece, ("groups", "dp"), planes, m) for m in range(1, 4)], [0, 1, 2, 3]

    def add_flipped(low, mask, *before):
        return (low.astype(F32) + flip(after(low, *before), "tensor", n_t, mask).astype(F32)).astype(BF16)

    if n_t == 4:
        share_3 = share(me_t ^ 3)
        weight = {3: flip(share_3, "tensor", n_t, 3)}
        weight[2] = flip(after(share(me_t ^ 2), weight[3]), "tensor", n_t, 2)
        weight[1] = flip(after(share(me_t ^ 1), weight[2]), "tensor", n_t, 1)
        x = pack(after(block_fill, share_3), block_tenant_index, tokens, cotangent, blocks, 2 * rank)
        x_other = flip(after(x, weight[3], *halves[::2]), "pipe", n_pipe, 1)
        pieces, order = gathered(weight[3])
        low = low_part(after(dp, x_other), core, block_fill, block_tenant_index, x, own_a, own_b, halves, blocks, rank)
        pieces[0] = after(pieces[0], weight[2], low)
        (y_3,) = panel_product(order, panel_at, x, x_other, pieces, half)
        low = add_flipped(low, 1, weight[2])
        far = lax.ppermute(after(y_3, low), "tensor", [(0, 1), (3, 2)])
        pieces, order = gathered(after(weight[2], *pieces))
        pieces[0] = after(pieces[0], weight[1])
        (y_2,) = panel_product(order, panel_at, x, x_other, pieces, half, adds=[far])
        low = add_flipped(low, 2)
        near = lax.ppermute(after(y_2, low), "tensor", [(0, 1), (3, 2), (1, 3), (2, 0)])
        pieces, order = gathered(after(weight[1], *pieces))
        (y_1,) = panel_product(order, panel_at, x, x_other, pieces, half)
        part_1 = flip(y_1, "tensor", n_t, 1)
        passed, kept = relay(at, y_3, near)
        parts = [lax.ppermute(passed, "tensor", [(1, 2), (2, 1)]), part_1, kept]
    else:
        x = pack(block_fill, block_tenant_index, tokens, cotangent, blocks, 2 * rank)
        x_other = flip(x, "pipe", n_pipe, 1)
        low = low_part(dp, core, block_fill, block_tenant_index, x, own_a, own_b, halves, blocks, rank)
        mask = 1
        while mask < n_t:
            low, mask = add_flipped(low, mask), 2 * mask
        steps = range(1, n_t)
        weights = [shift(share((me_t + s) % n_t), "tensor", n_t, s) for s in steps]
        pieces, order = gathered(jnp.concatenate(weights, axis=1))
        ys = panel_product(order, panel_at, x, x_other, pieces, half)
        parts = [shift(y, "tensor", n_t, -s) for s, y in zip(steps, ys)]

    low_other = flip(low, "pipe", n_pipe, 1)
    mine, *sends = grads(dp, core, x, x_other, low, low_other, n_dp, rank, feat, cols)
    for s, send in enumerate(sends):
        mine = mine + shift(after(send, *pieces), "dp", n_dp, s + 1).astype(F32)
    mine = mine.astype(BF16)
    down_out, up_out = settle(core, mine, flip(mine, "pipe", n_pipe, 1), feat)

    base = base_product(
        at, dp, core, block_fill, block_tenant_index, x, base_weight, low, own_b, halves, feat, blocks, rank
    )
    parts[0] = after(parts[0], base)
    others = [flip(other_rows(parts), "pipe", n_pipe, 1)]
    out = finish(core, block_fill, base, parts, others, rows, blocks)
    return out, down_out, up_out


def solution(mesh):
    placed = (
        P(("groups", "dp", "pipe"), "tensor"),
        P(None, "tensor"),
        P(("groups", "dp"), None, "tensor"),
        P(("groups", "dp"), None, "tensor"),
        P(("groups", "dp", "pipe"), "tensor"),
        P(("groups", "dp", "pipe")),
        P(("groups", "dp", "pipe"), None),
    )
    return jax.shard_map(
        functools.partial(body, dict(mesh.shape)),
        mesh=mesh,
        in_specs=placed,
        out_specs=(
            P(("groups", "dp", "pipe"), "tensor"),
            P(("groups", "dp"), None, "tensor"),
            P(("groups", "dp"), None, "tensor"),
        ),
        check_vma=False,
    )
```

```python
import functools

import jax
import jax.numpy as jnp
from jax import lax
from jax.experimental import pallas as pl
from jax.experimental.pallas import tpu as pltpu
from jax.sharding import PartitionSpec as P

ADAPTER_SCALE = 2.0
LIVE = 512
BF16 = jnp.bfloat16
F32 = jnp.float32
I32 = jnp.int32
MIB = 1 << 20
SMEM = pl.BlockSpec(memory_space=pltpu.SMEM)
VMEM = pl.BlockSpec(memory_space=pltpu.VMEM)


def shaped(shape, dtype):
    return jax.ShapeDtypeStruct(shape, dtype)


def dot(a, b, contract=(1, 0)):
    return lax.dot_general(a, b, ((contract[0:1], contract[1:2]), ((), ())), preferred_element_type=F32)


def shift(x, name, count, step):
    return lax.ppermute(x, name, [(i, (i + step) % count) for i in range(count)])


def flip(x, names, count, mask):
    return lax.ppermute(x, names, [(i, i ^ mask) for i in range(count)])


def params(mib):
    return pltpu.CompilerParams(vmem_limit_bytes=mib * MIB)


def cost(flops, bytes_accessed):
    return pl.CostEstimate(flops=1, bytes_accessed=1, transcendentals=0)


def after(x, *others):
    return lax.optimization_barrier((x, *others))[0]


def starts_of(fill_ref, blocks):
    starts, at = [], jnp.int32(0)
    for b in range(blocks):
        starts.append(at)
        at = at + fill_ref[0, b]
    return starts


def tenant_lanes(fill_ref, tenant_ref, blocks, lanes):
    row = lax.broadcasted_iota(I32, (LIVE, lanes), 0)
    tenant = jnp.zeros((LIVE, lanes), I32)
    for b, start in enumerate(starts_of(fill_ref, blocks)):
        tenant = jnp.where(row >= start, tenant_ref[b], tenant)
    return tenant


def half_kernel(core_ref, a_ref, b_ref, *outs):
    rank, feat, rows = a_ref.shape[0] // 2, a_ref.shape[1], outs[0].shape[0]
    first = core_ref[0] == 0
    for n, out in enumerate(outs):
        one, other = slice(n * rows, (n + 1) * rows), slice(rank + n * rows, rank + (n + 1) * rows)
        out[:, :feat] = jnp.where(first, a_ref[one, :], a_ref[other, :])
        out[:, feat:] = jnp.where(first, b_ref[one, :], b_ref[other, :])


def own_half(core, a, b, rank):
    width = a.shape[1] + b.shape[1]
    return pl.pallas_call(
        half_kernel,
        in_specs=[SMEM] + [VMEM] * 2,
        out_specs=[VMEM] * 2,
        out_shape=[shaped((rank // 2, width), BF16)] * 2,
        compiler_params=params(56),
        cost_estimate=cost(rank * width, 6 * rank * width),
        name="own_half",
    )(core, a, b)


def pack_kernel(blocks, block, fill_ref, tenant_ref, tok_ref, cot_ref, out_ref, pick):
    feat, cols = tok_ref.shape[1], cot_ref.shape[1]
    row = lax.broadcasted_iota(I32, (LIVE, block), 0)
    col = lax.broadcasted_iota(I32, (LIVE, block), 1)
    for b, start in enumerate(starts_of(fill_ref, blocks)):
        hit = (row == col + start) & (col < fill_ref[0, b])
        pick[:, b * block : (b + 1) * block] = jnp.where(hit, 1.0, 0.0).astype(BF16)
    wide = min(feat, 512)
    for at in range(0, feat, wide):
        out_ref[:, at : at + wide] = dot(pick[...], tok_ref[:, at : at + wide]).astype(BF16)
    out_ref[:, feat : feat + cols] = dot(pick[...], cot_ref[...]).astype(BF16)
    lanes = out_ref.shape[1] - feat - cols
    out_ref[:, feat + cols :] = tenant_lanes(fill_ref, tenant_ref, blocks, lanes).astype(F32).astype(BF16)


def pack(fill, tenant, tokens, cotangent, blocks, lanes):
    rows, feat = tokens.shape
    cols = cotangent.shape[1]
    return pl.pallas_call(
        functools.partial(pack_kernel, blocks, rows // blocks),
        in_specs=[SMEM] * 2 + [VMEM] * 2,
        out_specs=VMEM,
        out_shape=shaped((LIVE, feat + cols + lanes), BF16),
        scratch_shapes=[pltpu.VMEM((LIVE, rows), BF16)],
        compiler_params=params(24),
        cost_estimate=cost(2 * LIVE * rows * (feat + cols), 2 * (LIVE + rows) * (feat + cols)),
        name="pack",
    )(fill, tenant, tokens, cotangent)


def owner_mask(tenant, lane, owner, rank):
    return tenant == 2 * owner + (lane >= rank).astype(I32)


def in_order(core, mine, other):
    return jnp.where(core == 0, jnp.concatenate([mine, other], axis=0), jnp.concatenate([other, mine], axis=0))


def low_kernel(n_dp, rank, blocks, dp_ref, core_ref, fill_ref, tenant_ref, x_ref, a_ref, b_ref, *refs):
    halves, out_ref = refs[:-1], refs[-1]
    lanes, feat, cols = 2 * rank, a_ref.shape[1], b_ref.shape[1]
    tenant = tenant_lanes(fill_ref, tenant_ref, blocks, lanes)
    lane = lax.broadcasted_iota(I32, (LIVE, lanes), 1)
    low_in = jnp.zeros((LIVE, lanes), F32)
    low_grad = jnp.zeros((LIVE, lanes), F32)
    for s in range(n_dp):
        mask = owner_mask(tenant, lane, (dp_ref[0] + n_dp - s) % n_dp, rank)
        a, b = a_ref[...], b_ref[...]
        if s > 0:
            both = in_order(core_ref[0], halves[2 * s - 2][...], halves[2 * s - 1][...])
            a, b = both[:, :feat], both[:, feat:]
        low_in = low_in + jnp.where(mask, dot(x_ref[:, :feat], a, (1, 1)), 0.0)
        low_grad = low_grad + jnp.where(mask, dot(x_ref[:, feat : feat + cols], b, (1, 1)), 0.0)
    low_in = low_in + pltpu.roll(low_in, rank, 1)
    low_grad = low_grad + pltpu.roll(low_grad, rank, 1)
    out_ref[...] = jnp.where(lane < rank, low_in, low_grad).astype(BF16)


def low_part(dp, core, fill, tenant, x, a, b, halves, blocks, rank):
    n_dp = 1 + len(halves) // 2
    width = x.shape[1]
    return pl.pallas_call(
        functools.partial(low_kernel, n_dp, rank, blocks),
        in_specs=[SMEM] * 4 + [VMEM] * (3 + len(halves)),
        out_specs=VMEM,
        out_shape=shaped((LIVE, 2 * rank), BF16),
        compiler_params=params(24),
        cost_estimate=cost(4 * LIVE * rank * n_dp * width, 2 * LIVE * width + 4 * rank * n_dp * width),
        name="low_part",
    )(dp, core, fill, tenant, x, a, b, *halves)


def doubled(low, lane, rank):
    turned = pltpu.roll(low, rank, 1)
    return jnp.where(lane < rank, low, turned), jnp.where(lane < rank, turned, low)


def grad_kernel(n_dp, rank, feat, cols, dp_ref, core_ref, own_ref, other_ref, low_ref, low_other_ref, *outs):
    lanes = 2 * rank
    lane = lax.broadcasted_iota(I32, (LIVE, lanes), 1)
    for s in range(0, n_dp, 2):
        first, second = (dp_ref[0] + s) % n_dp, (dp_ref[0] + s + 1) % n_dp
        wanted = (2 * jnp.where(lane < rank, first, second) + core_ref[0]).astype(F32)
        down, up = None, None
        for source, ref in ((own_ref, low_ref), (other_ref, low_other_ref)):
            low_in, low_grad = doubled(ref[...].astype(F32), lane, rank)
            mask = source[:, feat + cols :].astype(F32) == wanted
            grad_t = jnp.transpose(jnp.where(mask, ADAPTER_SCALE * low_grad, 0.0)).astype(BF16)
            in_t = jnp.transpose(jnp.where(mask, ADAPTER_SCALE * low_in, 0.0)).astype(BF16)
            down_term = dot(grad_t, source[:, :feat])
            up_term = dot(in_t, source[:, feat : feat + cols])
            down, up = (down_term, up_term) if down is None else (down + down_term, up + up_term)
        for i in range(2):
            out = outs[s + i]
            out[:, :feat] = down[i * rank : (i + 1) * rank, :].astype(out.dtype)
            out[:, feat:] = up[i * rank : (i + 1) * rank, :].astype(out.dtype)


def grads(dp, core, x, x_other, low, low_other, n_dp, rank, feat, cols):
    width = feat + cols
    return pl.pallas_call(
        functools.partial(grad_kernel, n_dp, rank, feat, cols),
        in_specs=[SMEM] * 2 + [VMEM] * 4,
        out_specs=[VMEM] * n_dp,
        out_shape=[shaped((rank, width), F32)] + [shaped((rank, width), BF16)] * (n_dp - 1),
        compiler_params=params(32),
        cost_estimate=cost(4 * LIVE * rank * n_dp * width, 4 * LIVE * width + 4 * rank * n_dp * width),
        name="grads",
    )(dp, core, x, x_other, low, low_other)


def panel_kernel(order, count, place_ref, x_ref, other_ref, *refs):
    pieces, refs = refs[:count], refs[count:]
    half = refs[-1].shape[1]
    panels = pieces[0].shape[1] // half
    adds, outs = refs[:-panels], refs[-panels:]
    deep = pieces[0].shape[0]
    for n, source in enumerate((x_ref, other_ref)):
        total = None
        for piece, m in zip(pieces, order):
            col = pl.multiple_of((place_ref[0] ^ m) * deep, min(deep, 128))
            term = dot(source[:, pl.ds(col, deep)], piece[...])
            total = term if total is None else total + term
        for i, out in enumerate(outs):
            value = total[:, i * half : (i + 1) * half]
            if i < len(adds):
                value = value + adds[i][n * LIVE : (n + 1) * LIVE, :].astype(F32)
            out[n * LIVE : (n + 1) * LIVE, :] = value.astype(BF16)


def panel_product(order, place, x, x_other, pieces, half, adds=()):
    feat, wide = len(pieces) * pieces[0].shape[0], pieces[0].shape[1]
    shapes = [shaped((2 * LIVE, half), BF16)] * (wide // half)
    return pl.pallas_call(
        functools.partial(panel_kernel, order, len(pieces)),
        in_specs=[SMEM] + [VMEM] * (2 + len(pieces) + len(adds)),
        out_specs=[VMEM] * len(shapes),
        out_shape=shapes,
        compiler_params=params(24),
        cost_estimate=cost(4 * LIVE * feat * wide, 4 * LIVE * feat + 2 * feat * wide),
        name="panel",
    )(place, x, x_other, *pieces, *adds)


def settle_kernel(core_ref, own_ref, got_ref, down_ref, up_ref):
    feat = down_ref.shape[2]
    own, got = own_ref[...].astype(F32), got_ref[...].astype(F32)
    first = core_ref[0] == 0
    down_ref[0], up_ref[0] = jnp.where(first, own, got)[:, :feat], jnp.where(first, own, got)[:, feat:]
    down_ref[1], up_ref[1] = jnp.where(first, got, own)[:, :feat], jnp.where(first, got, own)[:, feat:]


def settle(core, own, got, feat):
    rank, width = own.shape
    return pl.pallas_call(
        settle_kernel,
        in_specs=[SMEM] + [VMEM] * 2,
        out_specs=[VMEM] * 2,
        out_shape=[shaped((2, rank, feat), F32), shaped((2, rank, width - feat), F32)],
        compiler_params=params(16),
        cost_estimate=cost(own.size, 12 * own.size),
        name="settle",
    )(core, own, got)


def base_kernel(n_dp, rank, blocks, at_ref, dp_ref, core_ref, fill_ref, tenant_ref, x_ref, w_ref, low_ref, b_ref, *refs):
    halves, out_ref = refs[:-1], refs[-1]
    lanes = 2 * rank
    tenant = tenant_lanes(fill_ref, tenant_ref, blocks, lanes)
    lane = lax.broadcasted_iota(I32, (LIVE, lanes), 1)
    low_in, _ = doubled(low_ref[...].astype(F32), lane, rank)
    total = dot(x_ref[...], w_ref[...])
    for s in range(n_dp):
        mask = owner_mask(tenant, lane, (dp_ref[0] + n_dp - s) % n_dp, rank)
        b = b_ref[...]
        if s > 0:
            b = in_order(core_ref[0], halves[2 * s - 2][...], halves[2 * s - 1][...])
        total = total + dot(jnp.where(mask, ADAPTER_SCALE * low_in, 0.0).astype(BF16), b)
    out_ref[...] = total


def base_product(at, dp, core, fill, tenant, x, base_weight, low, b, halves, feat, blocks, rank):
    n_dp = 1 + len(halves) // 2
    cols = base_weight.shape[1]
    whole = lambda i, at: (0, 0)
    return pl.pallas_call(
        functools.partial(base_kernel, n_dp, rank, blocks),
        grid_spec=pltpu.PrefetchScalarGridSpec(
            num_scalar_prefetch=1,
            grid=(1,),
            in_specs=[SMEM] * 4
            + [pl.BlockSpec((LIVE, feat), whole), pl.BlockSpec((feat, cols), lambda i, at: (at[0], 0)), pl.BlockSpec((LIVE, 2 * rank), whole)]
            + [pl.BlockSpec((2 * rank, cols), whole)]
            + [pl.BlockSpec((rank, cols), lambda i, at: (0, feat // cols))] * len(halves),
            out_specs=pl.BlockSpec((LIVE, cols), whole),
        ),
        out_shape=shaped((LIVE, cols), F32),
        compiler_params=params(24),
        cost_estimate=cost(2 * LIVE * feat * cols, 2 * feat * (LIVE + cols) + 4 * LIVE * cols),
        name="base",
    )(at, dp, core, fill, tenant, x, base_weight, low, b, *halves)


def relay_kernel(at_ref, own_ref, got_ref, passed_ref, kept_ref):
    inner = (at_ref[0] == 1) | (at_ref[0] == 2)
    got = got_ref[...].astype(F32)
    passed_ref[...] = (own_ref[...].astype(F32) + got).astype(BF16)
    kept_ref[...] = jnp.where(inner, 0.0, got).astype(BF16)


def relay(at, own, got):
    return pl.pallas_call(
        relay_kernel,
        in_specs=[SMEM] + [VMEM] * 2,
        out_specs=[VMEM] * 2,
        out_shape=[shaped(own.shape, BF16)] * 2,
        compiler_params=params(24),
        cost_estimate=cost(2 * own.size, 8 * own.size),
        name="relay",
    )(at, own, got)


def swap_kernel(*refs):
    ins, out_ref = refs[:-1], refs[-1]
    total = ins[0][LIVE:, :].astype(F32)
    for ref in ins[1:]:
        total = total + ref[LIVE:, :].astype(F32)
    out_ref[...] = total


def other_rows(parts):
    half = parts[0].shape[1]
    return pl.pallas_call(
        swap_kernel,
        in_specs=[VMEM] * len(parts),
        out_specs=VMEM,
        out_shape=shaped((LIVE, half), F32),
        compiler_params=params(24),
        cost_estimate=cost(LIVE * half, 2 * LIVE * half * len(parts)),
        name="other_rows",
    )(*parts)


def out_kernel(count, blocks, block, core_ref, fill_ref, base_ref, *refs):
    parts, rest, out_ref, held = refs[:count], refs[count:-2], refs[-2], refs[-1]
    half = rest[0].shape[1]
    own = parts[0][:LIVE, :].astype(F32)
    for part in parts[1:]:
        own = own + part[:LIVE, :].astype(F32)
    other = rest[0][...].astype(F32)
    for part in rest[1:]:
        other = other + part[...].astype(F32)
    first = core_ref[0] == 0
    held[:, :half] = (base_ref[:, :half] + jnp.where(first, own, other)).astype(BF16)
    held[:, half:] = (base_ref[:, half:] + jnp.where(first, other, own)).astype(BF16)
    row = lax.broadcasted_iota(I32, (block, LIVE), 0)
    col = lax.broadcasted_iota(I32, (block, LIVE), 1)
    for b, start in enumerate(starts_of(fill_ref, blocks)):
        hit = (col == row + start) & (row < fill_ref[0, b])
        pick = jnp.where(hit, 1.0, 0.0).astype(BF16)
        out_ref[b * block : (b + 1) * block, :] = dot(pick, held[...]).astype(BF16)


def finish(core, fill, base, parts, others, rows, blocks):
    cols = base.shape[1]
    count = len(parts)
    return pl.pallas_call(
        functools.partial(out_kernel, count, blocks, rows // blocks),
        in_specs=[SMEM] * 2 + [VMEM] * (1 + count + len(others)),
        out_specs=VMEM,
        out_shape=shaped((rows, cols), BF16),
        scratch_shapes=[pltpu.VMEM((LIVE, cols), BF16)],
        compiler_params=params(24),
        cost_estimate=cost(2 * LIVE * rows * cols, 4 * LIVE * cols + 2 * LIVE * cols * count + 2 * rows * cols),
        name="finish",
    )(core, fill, base, *parts, *others)


def body(sizes, tokens, base_weight, adapter_a, adapter_b, cotangent, block_tenant_index, block_fill):
    n_t, n_dp, n_pipe = sizes["tensor"], sizes["dp"], sizes["pipe"]
    planes = sizes["groups"] * n_dp
    rows, feat = tokens.shape
    cols = base_weight.shape[1]
    half = cols // n_pipe
    blocks = block_tenant_index.shape[0]
    pair, rank = adapter_a.shape[:2]
    me_t, me_pipe, me_dp = lax.axis_index("tensor"), lax.axis_index("pipe"), lax.axis_index("dp")
    q = lax.axis_index("groups") * n_dp + me_dp
    part_rows = feat // planes
    scalar = lambda v: v.astype(I32).reshape(1)
    dp, core, at, place = scalar(me_dp), scalar(me_pipe), scalar(me_t), scalar(q)

    own_a, own_b = adapter_a.reshape(pair * rank, feat), adapter_b.reshape(pair * rank, cols)
    one = own_half(core, own_a, own_b, rank)
    halves, raw = [], []
    for s in range(1, n_dp):
        raw += [shift(part, "dp", n_dp, s) for part in one]
        got = jnp.concatenate(raw[-2:], axis=0)
        halves += [got, flip(got, "pipe", n_pipe, 1)]
    panel_at = place if planes == 4 else jnp.zeros_like(place)

    def share(k):
        return lax.dynamic_slice(base_weight, (k * feat + q * part_rows, me_pipe * half), (part_rows, half))

    def gathered(piece):
        if planes != 4:
            return [lax.all_gather(piece, ("groups", "dp"), axis=0, tiled=True)], [0]
        return [piece] + [flip(piece, ("groups", "dp"), planes, m) for m in range(1, 4)], [0, 1, 2, 3]

    def add_flipped(low, mask, *before):
        return (low.astype(F32) + flip(after(low, *before), "tensor", n_t, mask).astype(F32)).astype(BF16)

    if n_t == 4:
        share_3 = share(me_t ^ 3)
        weight = {3: flip(share_3, "tensor", n_t, 3)}
        weight[2] = flip(after(share(me_t ^ 2), weight[3]), "tensor", n_t, 2)
        weight[1] = flip(after(share(me_t ^ 1), weight[2]), "tensor", n_t, 1)
        x = pack(after(block_fill, share_3), block_tenant_index, tokens, cotangent, blocks, 2 * rank)
        x_other = flip(after(x, weight[3], *raw), "pipe", n_pipe, 1)
        pieces, order = gathered(weight[3])
        low = low_part(after(dp, x_other), core, block_fill, block_tenant_index, x, own_a, own_b, halves, blocks, rank)
        pieces[0] = after(pieces[0], weight[2], low)
        (y_3,) = panel_product(order, panel_at, x, x_other, pieces, half)
        low = add_flipped(low, 1, weight[2])
        far = lax.ppermute(y_3, "tensor", [(0, 1), (3, 2)])
        pieces, order = gathered(after(weight[2], *pieces))
        pieces[0] = after(pieces[0], weight[1])
        (y_2,) = panel_product(order, panel_at, x, x_other, pieces, half, adds=[far])
        low = add_flipped(low, 2)
        near = lax.ppermute(after(y_2, low), "tensor", [(0, 1), (3, 2), (1, 3), (2, 0)])
        pieces, order = gathered(after(weight[1], *pieces))
        (y_1,) = panel_product(order, panel_at, x, x_other, pieces, half)
        part_1 = flip(y_1, "tensor", n_t, 1)
        passed, kept = relay(at, y_3, near)
        parts = [lax.ppermute(passed, "tensor", [(1, 2), (2, 1)]), part_1, kept]
    else:
        x = pack(block_fill, block_tenant_index, tokens, cotangent, blocks, 2 * rank)
        x_other = flip(x, "pipe", n_pipe, 1)
        low = low_part(dp, core, block_fill, block_tenant_index, x, own_a, own_b, halves, blocks, rank)
        mask = 1
        while mask < n_t:
            low, mask = add_flipped(low, mask), 2 * mask
        steps = range(1, n_t)
        weights = [shift(share((me_t + s) % n_t), "tensor", n_t, s) for s in steps]
        pieces, order = gathered(jnp.concatenate(weights, axis=1))
        ys = panel_product(order, panel_at, x, x_other, pieces, half)
        parts = [shift(y, "tensor", n_t, -s) for s, y in zip(steps, ys)]

    low_other = flip(low, "pipe", n_pipe, 1)
    mine, *sends = grads(dp, core, x, x_other, low, low_other, n_dp, rank, feat, cols)
    for s, send in enumerate(sends):
        mine = mine + shift(after(send, *pieces), "dp", n_dp, s + 1).astype(F32)
    mine = mine.astype(BF16)
    down_out, up_out = settle(core, mine, flip(mine, "pipe", n_pipe, 1), feat)

    base = base_product(
        at, dp, core, block_fill, block_tenant_index, x, base_weight, low, own_b, halves, feat, blocks, rank
    )
    parts[0] = after(parts[0], base, down_out)
    others = [flip(other_rows(parts), "pipe", n_pipe, 1)]
    out = finish(core, block_fill, base, parts, others, rows, blocks)
    return out, down_out, up_out


def solution(mesh):
    placed = (
        P(("groups", "dp", "pipe"), "tensor"),
        P(None, "tensor"),
        P(("groups", "dp"), None, "tensor"),
        P(("groups", "dp"), None, "tensor"),
        P(("groups", "dp", "pipe"), "tensor"),
        P(("groups", "dp", "pipe")),
        P(("groups", "dp", "pipe"), None),
    )
    return jax.shard_map(
        functools.partial(body, dict(mesh.shape)),
        mesh=mesh,
        in_specs=placed,
        out_specs=(
            P(("groups", "dp", "pipe"), "tensor"),
            P(("groups", "dp"), None, "tensor"),
            P(("groups", "dp"), None, "tensor"),
        ),
        check_vma=False,
    )
```

```python
import functools

import jax
import jax.numpy as jnp
from jax import lax
from jax.experimental import pallas as pl
from jax.experimental.pallas import tpu as pltpu
from jax.sharding import PartitionSpec as P

ADAPTER_SCALE = 2.0
LIVE = 512
BF16 = jnp.bfloat16
F32 = jnp.float32
I32 = jnp.int32
MIB = 1 << 20
SMEM = pl.BlockSpec(memory_space=pltpu.SMEM)
VMEM = pl.BlockSpec(memory_space=pltpu.VMEM)


def shaped(shape, dtype):
    return jax.ShapeDtypeStruct(shape, dtype)


def dot(a, b, contract=(1, 0)):
    return lax.dot_general(a, b, ((contract[0:1], contract[1:2]), ((), ())), preferred_element_type=F32)


def shift(x, name, count, step):
    return lax.ppermute(x, name, [(i, (i + step) % count) for i in range(count)])


def flip(x, names, count, mask):
    return lax.ppermute(x, names, [(i, i ^ mask) for i in range(count)])


def params(mib):
    return pltpu.CompilerParams(vmem_limit_bytes=mib * MIB)


def cost(flops, bytes_accessed):
    return pl.CostEstimate(flops=1, bytes_accessed=1, transcendentals=0)


def after(x, *others):
    return lax.optimization_barrier((x, *others))[0]


def starts_of(fill_ref, blocks):
    starts, at = [], jnp.int32(0)
    for b in range(blocks):
        starts.append(at)
        at = at + fill_ref[0, b]
    return starts


def tenant_lanes(fill_ref, tenant_ref, blocks, lanes):
    row = lax.broadcasted_iota(I32, (LIVE, lanes), 0)
    tenant = jnp.zeros((LIVE, lanes), I32)
    for b, start in enumerate(starts_of(fill_ref, blocks)):
        tenant = jnp.where(row >= start, tenant_ref[b], tenant)
    return tenant


def half_kernel(core_ref, a_ref, b_ref, *outs):
    rank, feat, rows = a_ref.shape[0] // 2, a_ref.shape[1], outs[0].shape[0]
    first = core_ref[0] == 0
    for n, out in enumerate(outs):
        one, other = slice(n * rows, (n + 1) * rows), slice(rank + n * rows, rank + (n + 1) * rows)
        out[:, :feat] = jnp.where(first, a_ref[one, :], a_ref[other, :])
        out[:, feat:] = jnp.where(first, b_ref[one, :], b_ref[other, :])


def own_half(core, a, b, rank):
    width = a.shape[1] + b.shape[1]
    return pl.pallas_call(
        half_kernel,
        in_specs=[SMEM] + [VMEM] * 2,
        out_specs=[VMEM] * 2,
        out_shape=[shaped((rank // 2, width), BF16)] * 2,
        compiler_params=params(56),
        cost_estimate=cost(rank * width, 6 * rank * width),
        name="own_half",
    )(core, a, b)


def pack_kernel(blocks, block, fill_ref, tenant_ref, tok_ref, cot_ref, out_ref, pick):
    feat, cols = tok_ref.shape[1], cot_ref.shape[1]
    row = lax.broadcasted_iota(I32, (LIVE, block), 0)
    col = lax.broadcasted_iota(I32, (LIVE, block), 1)
    for b, start in enumerate(starts_of(fill_ref, blocks)):
        hit = (row == col + start) & (col < fill_ref[0, b])
        pick[:, b * block : (b + 1) * block] = jnp.where(hit, 1.0, 0.0).astype(BF16)
    wide = min(feat, 512)
    for at in range(0, feat, wide):
        out_ref[:, at : at + wide] = dot(pick[...], tok_ref[:, at : at + wide]).astype(BF16)
    out_ref[:, feat : feat + cols] = dot(pick[...], cot_ref[...]).astype(BF16)
    lanes = out_ref.shape[1] - feat - cols
    out_ref[:, feat + cols :] = tenant_lanes(fill_ref, tenant_ref, blocks, lanes).astype(F32).astype(BF16)


def pack(fill, tenant, tokens, cotangent, blocks, lanes):
    rows, feat = tokens.shape
    cols = cotangent.shape[1]
    return pl.pallas_call(
        functools.partial(pack_kernel, blocks, rows // blocks),
        in_specs=[SMEM] * 2 + [VMEM] * 2,
        out_specs=VMEM,
        out_shape=shaped((LIVE, feat + cols + lanes), BF16),
        scratch_shapes=[pltpu.VMEM((LIVE, rows), BF16)],
        compiler_params=params(24),
        cost_estimate=cost(2 * LIVE * rows * (feat + cols), 2 * (LIVE + rows) * (feat + cols)),
        name="pack",
    )(fill, tenant, tokens, cotangent)


def owner_mask(tenant, lane, owner, rank):
    return tenant == 2 * owner + (lane >= rank).astype(I32)


def in_order(core, mine, other):
    return jnp.where(core == 0, jnp.concatenate([mine, other], axis=0), jnp.concatenate([other, mine], axis=0))


def low_kernel(n_dp, rank, blocks, dp_ref, core_ref, fill_ref, tenant_ref, x_ref, a_ref, b_ref, *refs):
    halves, out_ref = refs[:-1], refs[-1]
    lanes, feat, cols = 2 * rank, a_ref.shape[1], b_ref.shape[1]
    tenant = tenant_lanes(fill_ref, tenant_ref, blocks, lanes)
    lane = lax.broadcasted_iota(I32, (LIVE, lanes), 1)
    low_in = jnp.zeros((LIVE, lanes), F32)
    low_grad = jnp.zeros((LIVE, lanes), F32)
    for s in range(n_dp):
        mask = owner_mask(tenant, lane, (dp_ref[0] + n_dp - s) % n_dp, rank)
        a, b = a_ref[...], b_ref[...]
        if s > 0:
            both = in_order(core_ref[0], halves[2 * s - 2][...], halves[2 * s - 1][...])
            a, b = both[:, :feat], both[:, feat:]
        low_in = low_in + jnp.where(mask, dot(x_ref[:, :feat], a, (1, 1)), 0.0)
        low_grad = low_grad + jnp.where(mask, dot(x_ref[:, feat : feat + cols], b, (1, 1)), 0.0)
    low_in = low_in + pltpu.roll(low_in, rank, 1)
    low_grad = low_grad + pltpu.roll(low_grad, rank, 1)
    out_ref[...] = jnp.where(lane < rank, low_in, low_grad).astype(BF16)


def low_part(dp, core, fill, tenant, x, a, b, halves, blocks, rank):
    n_dp = 1 + len(halves) // 2
    width = x.shape[1]
    return pl.pallas_call(
        functools.partial(low_kernel, n_dp, rank, blocks),
        in_specs=[SMEM] * 4 + [VMEM] * (3 + len(halves)),
        out_specs=VMEM,
        out_shape=shaped((LIVE, 2 * rank), BF16),
        compiler_params=params(24),
        cost_estimate=cost(4 * LIVE * rank * n_dp * width, 2 * LIVE * width + 4 * rank * n_dp * width),
        name="low_part",
    )(dp, core, fill, tenant, x, a, b, *halves)


def doubled(low, lane, rank):
    turned = pltpu.roll(low, rank, 1)
    return jnp.where(lane < rank, low, turned), jnp.where(lane < rank, turned, low)


def grad_kernel(n_dp, rank, feat, cols, dp_ref, core_ref, own_ref, other_ref, low_ref, low_other_ref, *outs):
    lanes = 2 * rank
    lane = lax.broadcasted_iota(I32, (LIVE, lanes), 1)
    for s in range(0, n_dp, 2):
        first, second = (dp_ref[0] + s) % n_dp, (dp_ref[0] + s + 1) % n_dp
        wanted = (2 * jnp.where(lane < rank, first, second) + core_ref[0]).astype(F32)
        down, up = None, None
        for source, ref in ((own_ref, low_ref), (other_ref, low_other_ref)):
            low_in, low_grad = doubled(ref[...].astype(F32), lane, rank)
            mask = source[:, feat + cols :].astype(F32) == wanted
            grad_t = jnp.transpose(jnp.where(mask, ADAPTER_SCALE * low_grad, 0.0)).astype(BF16)
            in_t = jnp.transpose(jnp.where(mask, ADAPTER_SCALE * low_in, 0.0)).astype(BF16)
            down_term = dot(grad_t, source[:, :feat])
            up_term = dot(in_t, source[:, feat : feat + cols])
            down, up = (down_term, up_term) if down is None else (down + down_term, up + up_term)
        for i in range(2):
            out = outs[s + i]
            out[:, :feat] = down[i * rank : (i + 1) * rank, :].astype(out.dtype)
            out[:, feat:] = up[i * rank : (i + 1) * rank, :].astype(out.dtype)


def grads(dp, core, x, x_other, low, low_other, n_dp, rank, feat, cols):
    width = feat + cols
    return pl.pallas_call(
        functools.partial(grad_kernel, n_dp, rank, feat, cols),
        in_specs=[SMEM] * 2 + [VMEM] * 4,
        out_specs=[VMEM] * n_dp,
        out_shape=[shaped((rank, width), F32)] + [shaped((rank, width), BF16)] * (n_dp - 1),
        compiler_params=params(32),
        cost_estimate=cost(4 * LIVE * rank * n_dp * width, 4 * LIVE * width + 4 * rank * n_dp * width),
        name="grads",
    )(dp, core, x, x_other, low, low_other)


def panel_kernel(order, count, place_ref, x_ref, other_ref, *refs):
    pieces, refs = refs[:count], refs[count:]
    half = refs[-1].shape[1]
    panels = pieces[0].shape[1] // half
    adds, outs = refs[:-panels], refs[-panels:]
    deep = pieces[0].shape[0]
    for n, source in enumerate((x_ref, other_ref)):
        total = None
        for piece, m in zip(pieces, order):
            col = pl.multiple_of((place_ref[0] ^ m) * deep, min(deep, 128))
            term = dot(source[:, pl.ds(col, deep)], piece[...])
            total = term if total is None else total + term
        for i, out in enumerate(outs):
            value = total[:, i * half : (i + 1) * half]
            if i < len(adds):
                value = value + adds[i][n * LIVE : (n + 1) * LIVE, :].astype(F32)
            out[n * LIVE : (n + 1) * LIVE, :] = value.astype(BF16)


def panel_product(order, place, x, x_other, pieces, half, adds=()):
    feat, wide = len(pieces) * pieces[0].shape[0], pieces[0].shape[1]
    shapes = [shaped((2 * LIVE, half), BF16)] * (wide // half)
    return pl.pallas_call(
        functools.partial(panel_kernel, order, len(pieces)),
        in_specs=[SMEM] + [VMEM] * (2 + len(pieces) + len(adds)),
        out_specs=[VMEM] * len(shapes),
        out_shape=shapes,
        compiler_params=params(24),
        cost_estimate=cost(4 * LIVE * feat * wide, 4 * LIVE * feat + 2 * feat * wide),
        name="panel",
    )(place, x, x_other, *pieces, *adds)


def settle_kernel(core_ref, own_ref, got_ref, down_ref, up_ref):
    feat = down_ref.shape[2]
    own, got = own_ref[...].astype(F32), got_ref[...].astype(F32)
    first = core_ref[0] == 0
    down_ref[0], up_ref[0] = jnp.where(first, own, got)[:, :feat], jnp.where(first, own, got)[:, feat:]
    down_ref[1], up_ref[1] = jnp.where(first, got, own)[:, :feat], jnp.where(first, got, own)[:, feat:]


def settle(core, own, got, feat):
    rank, width = own.shape
    return pl.pallas_call(
        settle_kernel,
        in_specs=[SMEM] + [VMEM] * 2,
        out_specs=[VMEM] * 2,
        out_shape=[shaped((2, rank, feat), F32), shaped((2, rank, width - feat), F32)],
        compiler_params=params(16),
        cost_estimate=cost(own.size, 12 * own.size),
        name="settle",
    )(core, own, got)


def base_kernel(n_dp, rank, blocks, at_ref, dp_ref, core_ref, fill_ref, tenant_ref, x_ref, w_ref, low_ref, b_ref, *refs):
    halves, out_ref = refs[:-1], refs[-1]
    lanes = 2 * rank
    tenant = tenant_lanes(fill_ref, tenant_ref, blocks, lanes)
    lane = lax.broadcasted_iota(I32, (LIVE, lanes), 1)
    low_in, _ = doubled(low_ref[...].astype(F32), lane, rank)
    total = dot(x_ref[...], w_ref[...])
    for s in range(n_dp):
        mask = owner_mask(tenant, lane, (dp_ref[0] + n_dp - s) % n_dp, rank)
        b = b_ref[...]
        if s > 0:
            b = in_order(core_ref[0], halves[2 * s - 2][...], halves[2 * s - 1][...])
        total = total + dot(jnp.where(mask, ADAPTER_SCALE * low_in, 0.0).astype(BF16), b)
    out_ref[...] = total


def base_product(at, dp, core, fill, tenant, x, base_weight, low, b, halves, feat, blocks, rank):
    n_dp = 1 + len(halves) // 2
    cols = base_weight.shape[1]
    whole = lambda i, at: (0, 0)
    return pl.pallas_call(
        functools.partial(base_kernel, n_dp, rank, blocks),
        grid_spec=pltpu.PrefetchScalarGridSpec(
            num_scalar_prefetch=1,
            grid=(1,),
            in_specs=[SMEM] * 4
            + [pl.BlockSpec((LIVE, feat), whole), pl.BlockSpec((feat, cols), lambda i, at: (at[0], 0)), pl.BlockSpec((LIVE, 2 * rank), whole)]
            + [pl.BlockSpec((2 * rank, cols), whole)]
            + [pl.BlockSpec((rank, cols), lambda i, at: (0, feat // cols))] * len(halves),
            out_specs=pl.BlockSpec((LIVE, cols), whole),
        ),
        out_shape=shaped((LIVE, cols), F32),
        compiler_params=params(24),
        cost_estimate=cost(2 * LIVE * feat * cols, 2 * feat * (LIVE + cols) + 4 * LIVE * cols),
        name="base",
    )(at, dp, core, fill, tenant, x, base_weight, low, b, *halves)


def relay_kernel(at_ref, own_ref, got_ref, passed_ref, kept_ref):
    inner = (at_ref[0] == 1) | (at_ref[0] == 2)
    got = got_ref[...].astype(F32)
    passed_ref[...] = (own_ref[...].astype(F32) + got).astype(BF16)
    kept_ref[...] = jnp.where(inner, 0.0, got).astype(BF16)


def relay(at, own, got):
    return pl.pallas_call(
        relay_kernel,
        in_specs=[SMEM] + [VMEM] * 2,
        out_specs=[VMEM] * 2,
        out_shape=[shaped(own.shape, BF16)] * 2,
        compiler_params=params(24),
        cost_estimate=cost(2 * own.size, 8 * own.size),
        name="relay",
    )(at, own, got)


def swap_kernel(*refs):
    ins, out_ref = refs[:-1], refs[-1]
    total = ins[0][LIVE:, :].astype(F32)
    for ref in ins[1:]:
        total = total + ref[LIVE:, :].astype(F32)
    out_ref[...] = total


def other_rows(parts):
    half = parts[0].shape[1]
    return pl.pallas_call(
        swap_kernel,
        in_specs=[VMEM] * len(parts),
        out_specs=VMEM,
        out_shape=shaped((LIVE, half), F32),
        compiler_params=params(24),
        cost_estimate=cost(LIVE * half, 2 * LIVE * half * len(parts)),
        name="other_rows",
    )(*parts)


def out_kernel(count, blocks, block, core_ref, fill_ref, base_ref, *refs):
    parts, rest, out_ref, held = refs[:count], refs[count:-2], refs[-2], refs[-1]
    half = rest[0].shape[1]
    own = parts[0][:LIVE, :].astype(F32)
    for part in parts[1:]:
        own = own + part[:LIVE, :].astype(F32)
    other = rest[0][...].astype(F32)
    for part in rest[1:]:
        other = other + part[...].astype(F32)
    first = core_ref[0] == 0
    held[:, :half] = (base_ref[:, :half] + jnp.where(first, own, other)).astype(BF16)
    held[:, half:] = (base_ref[:, half:] + jnp.where(first, other, own)).astype(BF16)
    row = lax.broadcasted_iota(I32, (block, LIVE), 0)
    col = lax.broadcasted_iota(I32, (block, LIVE), 1)
    for b, start in enumerate(starts_of(fill_ref, blocks)):
        hit = (col == row + start) & (row < fill_ref[0, b])
        pick = jnp.where(hit, 1.0, 0.0).astype(BF16)
        out_ref[b * block : (b + 1) * block, :] = dot(pick, held[...]).astype(BF16)


def finish(core, fill, base, parts, others, rows, blocks):
    cols = base.shape[1]
    count = len(parts)
    return pl.pallas_call(
        functools.partial(out_kernel, count, blocks, rows // blocks),
        in_specs=[SMEM] * 2 + [VMEM] * (1 + count + len(others)),
        out_specs=VMEM,
        out_shape=shaped((rows, cols), BF16),
        scratch_shapes=[pltpu.VMEM((LIVE, cols), BF16)],
        compiler_params=params(24),
        cost_estimate=cost(2 * LIVE * rows * cols, 4 * LIVE * cols + 2 * LIVE * cols * count + 2 * rows * cols),
        name="finish",
    )(core, fill, base, *parts, *others)


def body(sizes, tokens, base_weight, adapter_a, adapter_b, cotangent, block_tenant_index, block_fill):
    n_t, n_dp, n_pipe = sizes["tensor"], sizes["dp"], sizes["pipe"]
    planes = sizes["groups"] * n_dp
    rows, feat = tokens.shape
    cols = base_weight.shape[1]
    half = cols // n_pipe
    blocks = block_tenant_index.shape[0]
    pair, rank = adapter_a.shape[:2]
    me_t, me_pipe, me_dp = lax.axis_index("tensor"), lax.axis_index("pipe"), lax.axis_index("dp")
    q = lax.axis_index("groups") * n_dp + me_dp
    part_rows = feat // planes
    scalar = lambda v: v.astype(I32).reshape(1)
    dp, core, at, place = scalar(me_dp), scalar(me_pipe), scalar(me_t), scalar(q)

    own_a, own_b = adapter_a.reshape(pair * rank, feat), adapter_b.reshape(pair * rank, cols)
    one = own_half(core, own_a, own_b, rank)
    halves, raw = [], []
    for s in range(1, n_dp):
        raw += [shift(part, "dp", n_dp, s) for part in one]
        got = jnp.concatenate(raw[-2:], axis=0)
        halves += [got, flip(got, "pipe", n_pipe, 1)]
    panel_at = place if planes == 4 else jnp.zeros_like(place)

    def share(k):
        return lax.dynamic_slice(base_weight, (k * feat + q * part_rows, me_pipe * half), (part_rows, half))

    def gathered(piece):
        if planes != 4:
            return [lax.all_gather(piece, ("groups", "dp"), axis=0, tiled=True)], [0]
        return [piece] + [flip(piece, ("groups", "dp"), planes, m) for m in range(1, 4)], [0, 1, 2, 3]

    def add_flipped(low, mask, *before):
        return (low.astype(F32) + flip(after(low, *before), "tensor", n_t, mask).astype(F32)).astype(BF16)

    if n_t == 4:
        share_3 = share(me_t ^ 3)
        weight = {3: flip(share_3, "tensor", n_t, 3)}
        share_2, share_1 = share(after(me_t ^ 2, share_3)), share(after(me_t ^ 1, share_3))
        weight[2] = flip(after(share_2, weight[3]), "tensor", n_t, 2)
        weight[1] = flip(after(share_1, weight[2]), "tensor", n_t, 1)
        x = pack(after(block_fill, share_2, share_1), block_tenant_index, tokens, cotangent, blocks, 2 * rank)
        x_other = flip(after(x, weight[3], *raw), "pipe", n_pipe, 1)
        pieces, order = gathered(weight[3])
        low = low_part(after(dp, x_other), core, block_fill, block_tenant_index, x, own_a, own_b, halves, blocks, rank)
        pieces[0] = after(pieces[0], weight[2], low)
        (y_3,) = panel_product(order, panel_at, x, x_other, pieces, half)
        low = add_flipped(low, 1, weight[2])
        far = lax.ppermute(y_3, "tensor", [(0, 1), (3, 2)])
        pieces, order = gathered(after(weight[2], *pieces))
        pieces[0] = after(pieces[0], weight[1])
        (y_2,) = panel_product(order, panel_at, x, x_other, pieces, half, adds=[far])
        low = add_flipped(low, 2)
        near = lax.ppermute(after(y_2, low), "tensor", [(0, 1), (3, 2), (1, 3), (2, 0)])
        pieces, order = gathered(after(weight[1], *pieces))
        (y_1,) = panel_product(order, panel_at, x, x_other, pieces, half)
        passed, kept = relay(at, y_3, near)
        part_1 = flip(after(y_1, passed), "tensor", n_t, 1)
        parts = [lax.ppermute(passed, "tensor", [(1, 2), (2, 1)]), part_1, kept]
    else:
        x = pack(block_fill, block_tenant_index, tokens, cotangent, blocks, 2 * rank)
        x_other = flip(x, "pipe", n_pipe, 1)
        low = low_part(dp, core, block_fill, block_tenant_index, x, own_a, own_b, halves, blocks, rank)
        mask = 1
        while mask < n_t:
            low, mask = add_flipped(low, mask), 2 * mask
        steps = range(1, n_t)
        weights = [shift(share((me_t + s) % n_t), "tensor", n_t, s) for s in steps]
        pieces, order = gathered(jnp.concatenate(weights, axis=1))
        ys = panel_product(order, panel_at, x, x_other, pieces, half)
        parts = [shift(y, "tensor", n_t, -s) for s, y in zip(steps, ys)]

    low_other = flip(low, "pipe", n_pipe, 1)
    mine, *sends = grads(dp, core, x, x_other, low, low_other, n_dp, rank, feat, cols)
    for s, send in enumerate(sends):
        mine = mine + shift(after(send, *pieces), "dp", n_dp, s + 1).astype(F32)
    mine = mine.astype(BF16)
    down_out, up_out = settle(core, mine, flip(mine, "pipe", n_pipe, 1), feat)

    base = base_product(
        at, dp, core, block_fill, block_tenant_index, x, base_weight, low, own_b, halves, feat, blocks, rank
    )
    parts[0] = after(parts[0], base, down_out)
    others = [flip(other_rows(parts), "pipe", n_pipe, 1)]
    out = finish(core, block_fill, base, parts, others, rows, blocks)
    return out, down_out, up_out


def solution(mesh):
    placed = (
        P(("groups", "dp", "pipe"), "tensor"),
        P(None, "tensor"),
        P(("groups", "dp"), None, "tensor"),
        P(("groups", "dp"), None, "tensor"),
        P(("groups", "dp", "pipe"), "tensor"),
        P(("groups", "dp", "pipe")),
        P(("groups", "dp", "pipe"), None),
    )
    return jax.shard_map(
        functools.partial(body, dict(mesh.shape)),
        mesh=mesh,
        in_specs=placed,
        out_specs=(
            P(("groups", "dp", "pipe"), "tensor"),
            P(("groups", "dp"), None, "tensor"),
            P(("groups", "dp"), None, "tensor"),
        ),
        check_vma=False,
    )
```

```python
import functools

import jax
import jax.numpy as jnp
from jax import lax
from jax.experimental import pallas as pl
from jax.experimental.pallas import tpu as pltpu
from jax.sharding import PartitionSpec as P

ADAPTER_SCALE = 2.0
LIVE = 512
BF16 = jnp.bfloat16
F32 = jnp.float32
I32 = jnp.int32
MIB = 1 << 20
SMEM = pl.BlockSpec(memory_space=pltpu.SMEM)
VMEM = pl.BlockSpec(memory_space=pltpu.VMEM)


def shaped(shape, dtype):
    return jax.ShapeDtypeStruct(shape, dtype)


def dot(a, b, contract=(1, 0)):
    return lax.dot_general(a, b, ((contract[0:1], contract[1:2]), ((), ())), preferred_element_type=F32)


def shift(x, name, count, step):
    return lax.ppermute(x, name, [(i, (i + step) % count) for i in range(count)])


def flip(x, names, count, mask):
    return lax.ppermute(x, names, [(i, i ^ mask) for i in range(count)])


def params(mib):
    return pltpu.CompilerParams(vmem_limit_bytes=mib * MIB)


def cost(flops, bytes_accessed):
    return pl.CostEstimate(flops=1, bytes_accessed=1, transcendentals=0)


def after(x, *others):
    return lax.optimization_barrier((x, *others))[0]


def starts_of(fill_ref, blocks):
    starts, at = [], jnp.int32(0)
    for b in range(blocks):
        starts.append(at)
        at = at + fill_ref[0, b]
    return starts


def tenant_lanes(fill_ref, tenant_ref, blocks, lanes):
    row = lax.broadcasted_iota(I32, (LIVE, lanes), 0)
    tenant = jnp.zeros((LIVE, lanes), I32)
    for b, start in enumerate(starts_of(fill_ref, blocks)):
        tenant = jnp.where(row >= start, tenant_ref[b], tenant)
    return tenant


def half_kernel(core_ref, a_ref, b_ref, *outs):
    rank, feat, rows = a_ref.shape[0] // 2, a_ref.shape[1], outs[0].shape[0]
    first = core_ref[0] == 0
    for n, out in enumerate(outs):
        one, other = slice(n * rows, (n + 1) * rows), slice(rank + n * rows, rank + (n + 1) * rows)
        out[:, :feat] = jnp.where(first, a_ref[one, :], a_ref[other, :])
        out[:, feat:] = jnp.where(first, b_ref[one, :], b_ref[other, :])


def own_half(core, a, b, rank):
    width = a.shape[1] + b.shape[1]
    return pl.pallas_call(
        half_kernel,
        in_specs=[SMEM] + [VMEM] * 2,
        out_specs=[VMEM] * 2,
        out_shape=[shaped((rank // 2, width), BF16)] * 2,
        compiler_params=params(56),
        cost_estimate=cost(rank * width, 6 * rank * width),
        name="own_half",
    )(core, a, b)


def pack_kernel(blocks, block, fill_ref, tenant_ref, tok_ref, cot_ref, out_ref, pick):
    feat, cols = tok_ref.shape[1], cot_ref.shape[1]
    row = lax.broadcasted_iota(I32, (LIVE, block), 0)
    col = lax.broadcasted_iota(I32, (LIVE, block), 1)
    for b, start in enumerate(starts_of(fill_ref, blocks)):
        hit = (row == col + start) & (col < fill_ref[0, b])
        pick[:, b * block : (b + 1) * block] = jnp.where(hit, 1.0, 0.0).astype(BF16)
    wide = min(feat, 512)
    for at in range(0, feat, wide):
        out_ref[:, at : at + wide] = dot(pick[...], tok_ref[:, at : at + wide]).astype(BF16)
    out_ref[:, feat : feat + cols] = dot(pick[...], cot_ref[...]).astype(BF16)
    lanes = out_ref.shape[1] - feat - cols
    out_ref[:, feat + cols :] = tenant_lanes(fill_ref, tenant_ref, blocks, lanes).astype(F32).astype(BF16)


def pack(fill, tenant, tokens, cotangent, blocks, lanes):
    rows, feat = tokens.shape
    cols = cotangent.shape[1]
    return pl.pallas_call(
        functools.partial(pack_kernel, blocks, rows // blocks),
        in_specs=[SMEM] * 2 + [VMEM] * 2,
        out_specs=VMEM,
        out_shape=shaped((LIVE, feat + cols + lanes), BF16),
        scratch_shapes=[pltpu.VMEM((LIVE, rows), BF16)],
        compiler_params=params(24),
        cost_estimate=cost(2 * LIVE * rows * (feat + cols), 2 * (LIVE + rows) * (feat + cols)),
        name="pack",
    )(fill, tenant, tokens, cotangent)


def owner_mask(tenant, lane, owner, rank):
    return tenant == 2 * owner + (lane >= rank).astype(I32)


def in_order(core, mine, other):
    return jnp.where(core == 0, jnp.concatenate([mine, other], axis=0), jnp.concatenate([other, mine], axis=0))


def low_kernel(n_dp, rank, blocks, dp_ref, core_ref, fill_ref, tenant_ref, x_ref, a_ref, b_ref, *refs):
    halves, out_ref = refs[:-1], refs[-1]
    lanes, feat, cols = 2 * rank, a_ref.shape[1], b_ref.shape[1]
    tenant = tenant_lanes(fill_ref, tenant_ref, blocks, lanes)
    lane = lax.broadcasted_iota(I32, (LIVE, lanes), 1)
    low_in = jnp.zeros((LIVE, lanes), F32)
    low_grad = jnp.zeros((LIVE, lanes), F32)
    for s in range(n_dp):
        mask = owner_mask(tenant, lane, (dp_ref[0] + n_dp - s) % n_dp, rank)
        a, b = a_ref[...], b_ref[...]
        if s > 0:
            both = in_order(core_ref[0], halves[2 * s - 2][...], halves[2 * s - 1][...])
            a, b = both[:, :feat], both[:, feat:]
        low_in = low_in + jnp.where(mask, dot(x_ref[:, :feat], a, (1, 1)), 0.0)
        low_grad = low_grad + jnp.where(mask, dot(x_ref[:, feat : feat + cols], b, (1, 1)), 0.0)
    low_in = low_in + pltpu.roll(low_in, rank, 1)
    low_grad = low_grad + pltpu.roll(low_grad, rank, 1)
    out_ref[...] = jnp.where(lane < rank, low_in, low_grad).astype(BF16)


def low_part(dp, core, fill, tenant, x, a, b, halves, blocks, rank):
    n_dp = 1 + len(halves) // 2
    width = x.shape[1]
    return pl.pallas_call(
        functools.partial(low_kernel, n_dp, rank, blocks),
        in_specs=[SMEM] * 4 + [VMEM] * (3 + len(halves)),
        out_specs=VMEM,
        out_shape=shaped((LIVE, 2 * rank), BF16),
        compiler_params=params(24),
        cost_estimate=cost(4 * LIVE * rank * n_dp * width, 2 * LIVE * width + 4 * rank * n_dp * width),
        name="low_part",
    )(dp, core, fill, tenant, x, a, b, *halves)


def doubled(low, lane, rank):
    turned = pltpu.roll(low, rank, 1)
    return jnp.where(lane < rank, low, turned), jnp.where(lane < rank, turned, low)


def grad_kernel(n_dp, rank, feat, cols, dp_ref, core_ref, own_ref, other_ref, low_ref, low_other_ref, *outs):
    lanes = 2 * rank
    lane = lax.broadcasted_iota(I32, (LIVE, lanes), 1)
    for s in range(0, n_dp, 2):
        first, second = (dp_ref[0] + s) % n_dp, (dp_ref[0] + s + 1) % n_dp
        wanted = (2 * jnp.where(lane < rank, first, second) + core_ref[0]).astype(F32)
        down, up = None, None
        for source, ref in ((own_ref, low_ref), (other_ref, low_other_ref)):
            low_in, low_grad = doubled(ref[...].astype(F32), lane, rank)
            mask = source[:, feat + cols :].astype(F32) == wanted
            grad_t = jnp.transpose(jnp.where(mask, ADAPTER_SCALE * low_grad, 0.0)).astype(BF16)
            in_t = jnp.transpose(jnp.where(mask, ADAPTER_SCALE * low_in, 0.0)).astype(BF16)
            down_term = dot(grad_t, source[:, :feat])
            up_term = dot(in_t, source[:, feat : feat + cols])
            down, up = (down_term, up_term) if down is None else (down + down_term, up + up_term)
        for i in range(2):
            out = outs[s + i]
            out[:, :feat] = down[i * rank : (i + 1) * rank, :].astype(out.dtype)
            out[:, feat:] = up[i * rank : (i + 1) * rank, :].astype(out.dtype)


def grads(dp, core, x, x_other, low, low_other, n_dp, rank, feat, cols):
    width = feat + cols
    return pl.pallas_call(
        functools.partial(grad_kernel, n_dp, rank, feat, cols),
        in_specs=[SMEM] * 2 + [VMEM] * 4,
        out_specs=[VMEM] * n_dp,
        out_shape=[shaped((rank, width), F32)] + [shaped((rank, width), BF16)] * (n_dp - 1),
        compiler_params=params(32),
        cost_estimate=cost(4 * LIVE * rank * n_dp * width, 4 * LIVE * width + 4 * rank * n_dp * width),
        name="grads",
    )(dp, core, x, x_other, low, low_other)


def panel_kernel(order, count, place_ref, x_ref, other_ref, *refs):
    pieces, refs = refs[:count], refs[count:]
    half = refs[0].shape[1]
    deep = pieces[0].shape[0]
    for n, source in enumerate((x_ref, other_ref)):
        total = None
        for piece, m in zip(pieces, order):
            col = pl.multiple_of((place_ref[0] ^ m) * deep, min(deep, 128))
            term = dot(source[:, pl.ds(col, deep)], piece[...])
            total = term if total is None else total + term
        for i, out in enumerate(refs):
            out[n * LIVE : (n + 1) * LIVE, :] = total[:, i * half : (i + 1) * half].astype(out.dtype)


def panel_product(order, place, x, x_other, pieces, half, dtype=BF16):
    feat, wide = len(pieces) * pieces[0].shape[0], pieces[0].shape[1]
    shapes = [shaped((2 * LIVE, half), dtype)] * (wide // half)
    return pl.pallas_call(
        functools.partial(panel_kernel, order, len(pieces)),
        in_specs=[SMEM] + [VMEM] * (2 + len(pieces)),
        out_specs=[VMEM] * len(shapes),
        out_shape=shapes,
        compiler_params=params(24),
        cost_estimate=pl.CostEstimate(flops=1, bytes_accessed=1, transcendentals=0),
        name="panel",
    )(place, x, x_other, *pieces)


def settle_kernel(core_ref, own_ref, got_ref, down_ref, up_ref):
    feat = down_ref.shape[2]
    own, got = own_ref[...].astype(F32), got_ref[...].astype(F32)
    first = core_ref[0] == 0
    down_ref[0], up_ref[0] = jnp.where(first, own, got)[:, :feat], jnp.where(first, own, got)[:, feat:]
    down_ref[1], up_ref[1] = jnp.where(first, got, own)[:, :feat], jnp.where(first, got, own)[:, feat:]


def settle(core, own, got, feat):
    rank, width = own.shape
    return pl.pallas_call(
        settle_kernel,
        in_specs=[SMEM] + [VMEM] * 2,
        out_specs=[VMEM] * 2,
        out_shape=[shaped((2, rank, feat), F32), shaped((2, rank, width - feat), F32)],
        compiler_params=params(16),
        cost_estimate=cost(own.size, 12 * own.size),
        name="settle",
    )(core, own, got)


def base_kernel(n_dp, rank, blocks, at_ref, dp_ref, core_ref, fill_ref, tenant_ref, x_ref, w_ref, low_ref, b_ref, *refs):
    halves, out_ref = refs[:-1], refs[-1]
    lanes = 2 * rank
    tenant = tenant_lanes(fill_ref, tenant_ref, blocks, lanes)
    lane = lax.broadcasted_iota(I32, (LIVE, lanes), 1)
    low_in, _ = doubled(low_ref[...].astype(F32), lane, rank)
    total = dot(x_ref[...], w_ref[...])
    for s in range(n_dp):
        mask = owner_mask(tenant, lane, (dp_ref[0] + n_dp - s) % n_dp, rank)
        b = b_ref[...]
        if s > 0:
            b = in_order(core_ref[0], halves[2 * s - 2][...], halves[2 * s - 1][...])
        total = total + dot(jnp.where(mask, ADAPTER_SCALE * low_in, 0.0).astype(BF16), b)
    out_ref[...] = total


def base_product(at, dp, core, fill, tenant, x, base_weight, low, b, halves, feat, blocks, rank):
    n_dp = 1 + len(halves) // 2
    cols = base_weight.shape[1]
    whole = lambda i, at: (0, 0)
    return pl.pallas_call(
        functools.partial(base_kernel, n_dp, rank, blocks),
        grid_spec=pltpu.PrefetchScalarGridSpec(
            num_scalar_prefetch=1,
            grid=(1,),
            in_specs=[SMEM] * 4
            + [pl.BlockSpec((LIVE, feat), whole), pl.BlockSpec((feat, cols), lambda i, at: (at[0], 0)), pl.BlockSpec((LIVE, 2 * rank), whole)]
            + [pl.BlockSpec((2 * rank, cols), whole)]
            + [pl.BlockSpec((rank, cols), lambda i, at: (0, feat // cols))] * len(halves),
            out_specs=pl.BlockSpec((LIVE, cols), whole),
        ),
        out_shape=shaped((LIVE, cols), F32),
        compiler_params=params(24),
        cost_estimate=cost(2 * LIVE * feat * cols, 2 * feat * (LIVE + cols) + 4 * LIVE * cols),
        name="base",
    )(at, dp, core, fill, tenant, x, base_weight, low, b, *halves)


def join_kernel(own_ref, far_ref, low_ref, out_ref):
    out_ref[: 2 * LIVE, :] = (own_ref[...] + far_ref[...].astype(F32)).astype(BF16)
    lanes, rows = low_ref.shape[1], LIVE // 2
    out_ref[2 * LIVE :, :lanes] = low_ref[:rows, :]
    out_ref[2 * LIVE :, lanes:] = low_ref[rows:, :]


def join(own, far, low):
    return pl.pallas_call(
        join_kernel,
        in_specs=[VMEM] * 3,
        out_specs=VMEM,
        out_shape=shaped((2 * LIVE + LIVE // 2, own.shape[1]), BF16),
        compiler_params=params(24),
        cost_estimate=cost(own.size, 8 * own.size),
        name="join",
    )(own, far, low)


def relay_kernel(at_ref, own_ref, got_ref, low_ref, passed_ref, kept_ref, low_out_ref):
    inner = (at_ref[0] == 1) | (at_ref[0] == 2)
    got = got_ref[: 2 * LIVE, :].astype(F32)
    passed_ref[...] = (own_ref[...].astype(F32) + got).astype(BF16)
    kept_ref[...] = jnp.where(inner, 0.0, got).astype(BF16)
    lanes, rows = low_ref.shape[1], LIVE // 2
    low_out_ref[:rows, :] = jnp.where(inner, low_ref[:rows, :], got_ref[2 * LIVE :, :lanes])
    low_out_ref[rows:, :] = jnp.where(inner, low_ref[rows:, :], got_ref[2 * LIVE :, lanes:])


def relay(at, own, got, low):
    return pl.pallas_call(
        relay_kernel,
        in_specs=[SMEM] + [VMEM] * 3,
        out_specs=[VMEM] * 3,
        out_shape=[shaped(own.shape, BF16)] * 2 + [shaped(low.shape, BF16)],
        compiler_params=params(24),
        cost_estimate=cost(2 * own.size, 8 * own.size),
        name="relay",
    )(at, own, got, low)


def swap_kernel(*refs):
    ins, out_ref = refs[:-1], refs[-1]
    total = ins[0][LIVE:, :].astype(F32)
    for ref in ins[1:]:
        total = total + ref[LIVE:, :].astype(F32)
    out_ref[...] = total


def other_rows(parts):
    half = parts[0].shape[1]
    return pl.pallas_call(
        swap_kernel,
        in_specs=[VMEM] * len(parts),
        out_specs=VMEM,
        out_shape=shaped((LIVE, half), F32),
        compiler_params=params(24),
        cost_estimate=cost(LIVE * half, 2 * LIVE * half * len(parts)),
        name="other_rows",
    )(*parts)


def out_kernel(count, blocks, block, core_ref, fill_ref, base_ref, *refs):
    parts, rest, out_ref, held = refs[:count], refs[count:-2], refs[-2], refs[-1]
    half = rest[0].shape[1]
    own = parts[0][:LIVE, :].astype(F32)
    for part in parts[1:]:
        own = own + part[:LIVE, :].astype(F32)
    other = rest[0][...].astype(F32)
    for part in rest[1:]:
        other = other + part[...].astype(F32)
    first = core_ref[0] == 0
    held[:, :half] = (base_ref[:, :half] + jnp.where(first, own, other)).astype(BF16)
    held[:, half:] = (base_ref[:, half:] + jnp.where(first, other, own)).astype(BF16)
    row = lax.broadcasted_iota(I32, (block, LIVE), 0)
    col = lax.broadcasted_iota(I32, (block, LIVE), 1)
    for b, start in enumerate(starts_of(fill_ref, blocks)):
        hit = (col == row + start) & (row < fill_ref[0, b])
        pick = jnp.where(hit, 1.0, 0.0).astype(BF16)
        out_ref[b * block : (b + 1) * block, :] = dot(pick, held[...]).astype(BF16)


def finish(core, fill, base, parts, others, rows, blocks):
    cols = base.shape[1]
    count = len(parts)
    return pl.pallas_call(
        functools.partial(out_kernel, count, blocks, rows // blocks),
        in_specs=[SMEM] * 2 + [VMEM] * (1 + count + len(others)),
        out_specs=VMEM,
        out_shape=shaped((rows, cols), BF16),
        scratch_shapes=[pltpu.VMEM((LIVE, cols), BF16)],
        compiler_params=params(24),
        cost_estimate=cost(2 * LIVE * rows * cols, 4 * LIVE * cols + 2 * LIVE * cols * count + 2 * rows * cols),
        name="finish",
    )(core, fill, base, *parts, *others)


def body(sizes, tokens, base_weight, adapter_a, adapter_b, cotangent, block_tenant_index, block_fill):
    n_t, n_dp, n_pipe = sizes["tensor"], sizes["dp"], sizes["pipe"]
    planes = sizes["groups"] * n_dp
    rows, feat = tokens.shape
    cols = base_weight.shape[1]
    half = cols // n_pipe
    blocks = block_tenant_index.shape[0]
    pair, rank = adapter_a.shape[:2]
    me_t, me_pipe, me_dp = lax.axis_index("tensor"), lax.axis_index("pipe"), lax.axis_index("dp")
    q = lax.axis_index("groups") * n_dp + me_dp
    part_rows = feat // planes
    scalar = lambda v: v.astype(I32).reshape(1)
    dp, core, at, place = scalar(me_dp), scalar(me_pipe), scalar(me_t), scalar(q)

    own_a, own_b = adapter_a.reshape(pair * rank, feat), adapter_b.reshape(pair * rank, cols)
    one = own_half(core, own_a, own_b, rank)
    halves, raw = [], []
    for s in range(1, n_dp):
        raw += [shift(part, "dp", n_dp, s) for part in one]
        got = jnp.concatenate(raw[-2:], axis=0)
        halves += [got, flip(got, "pipe", n_pipe, 1)]
    panel_at = place if planes == 4 else jnp.zeros_like(place)

    def share(k):
        return lax.dynamic_slice(base_weight, (k * feat + q * part_rows, me_pipe * half), (part_rows, half))

    def gathered(piece):
        if planes != 4:
            return [lax.all_gather(piece, ("groups", "dp"), axis=0, tiled=True)], [0]
        return [piece] + [flip(piece, ("groups", "dp"), planes, m) for m in range(1, 4)], [0, 1, 2, 3]

    def add_flipped(low, mask, *before):
        return (low.astype(F32) + flip(after(low, *before), "tensor", n_t, mask).astype(F32)).astype(BF16)

    if n_t == 4 and half == 4 * rank:
        share_3 = share(me_t ^ 3)
        weight = {3: flip(share_3, "tensor", n_t, 3)}
        weight[2] = flip(after(share(me_t ^ 2), weight[3]), "tensor", n_t, 2)
        weight[1] = flip(after(share(me_t ^ 1), weight[2]), "tensor", n_t, 1)
        x = pack(after(block_fill, share_3), block_tenant_index, tokens, cotangent, blocks, 2 * rank)
        x_other = flip(after(x, weight[3], *raw), "pipe", n_pipe, 1)
        pieces, order = gathered(weight[3])
        low = low_part(after(dp, x_other), core, block_fill, block_tenant_index, x, own_a, own_b, halves, blocks, rank)
        pieces[0] = after(pieces[0], weight[2], low)
        (y_3,) = panel_product(order, panel_at, x, x_other, pieces, half)
        low = add_flipped(low, 1, weight[2])
        far = lax.ppermute(y_3, "tensor", [(0, 1), (3, 2)])
        pieces, order = gathered(after(weight[2], *pieces))
        pieces[0] = after(pieces[0], weight[1])
        low = (low.astype(F32) + lax.ppermute(low, "tensor", [(1, 2), (2, 1)]).astype(F32)).astype(BF16)
        (y_2,) = panel_product(order, panel_at, x, x_other, pieces, half, F32)
        near = lax.ppermute(join(y_2, far, low), "tensor", [(0, 1), (3, 2), (1, 3), (2, 0)])
        pieces, order = gathered(after(weight[1], *pieces))
        (y_1,) = panel_product(order, panel_at, x, x_other, pieces, half)
        part_1 = flip(y_1, "tensor", n_t, 1)
        passed, kept, low = relay(at, y_3, near, low)
        parts = [lax.ppermute(passed, "tensor", [(1, 2), (2, 1)]), part_1, kept]
    else:
        x = pack(block_fill, block_tenant_index, tokens, cotangent, blocks, 2 * rank)
        x_other = flip(x, "pipe", n_pipe, 1)
        low = low_part(dp, core, block_fill, block_tenant_index, x, own_a, own_b, halves, blocks, rank)
        mask = 1
        while mask < n_t:
            low, mask = add_flipped(low, mask), 2 * mask
        steps = range(1, n_t)
        weights = [shift(share((me_t + s) % n_t), "tensor", n_t, s) for s in steps]
        pieces, order = gathered(jnp.concatenate(weights, axis=1))
        ys = panel_product(order, panel_at, x, x_other, pieces, half)
        parts = [shift(y, "tensor", n_t, -s) for s, y in zip(steps, ys)]

    low_other = flip(low, "pipe", n_pipe, 1)
    mine, *sends = grads(dp, core, x, x_other, low, low_other, n_dp, rank, feat, cols)
    for s, send in enumerate(sends):
        mine = mine + shift(after(send, *pieces), "dp", n_dp, s + 1).astype(F32)
    mine = mine.astype(BF16)
    down_out, up_out = settle(core, mine, flip(mine, "pipe", n_pipe, 1), feat)

    base = base_product(
        at, dp, core, block_fill, block_tenant_index, x, base_weight, low, own_b, halves, feat, blocks, rank
    )
    parts[0] = after(parts[0], base)
    others = [flip(other_rows(parts), "pipe", n_pipe, 1)]
    out = finish(core, block_fill, base, parts, others, rows, blocks)
    return out, down_out, up_out


def solution(mesh):
    placed = (
        P(("groups", "dp", "pipe"), "tensor"),
        P(None, "tensor"),
        P(("groups", "dp"), None, "tensor"),
        P(("groups", "dp"), None, "tensor"),
        P(("groups", "dp", "pipe"), "tensor"),
        P(("groups", "dp", "pipe")),
        P(("groups", "dp", "pipe"), None),
    )
    return jax.shard_map(
        functools.partial(body, dict(mesh.shape)),
        mesh=mesh,
        in_specs=placed,
        out_specs=(
            P(("groups", "dp", "pipe"), "tensor"),
            P(("groups", "dp"), None, "tensor"),
            P(("groups", "dp"), None, "tensor"),
        ),
        check_vma=False,
    )
```

```python
import functools

import jax
import jax.numpy as jnp
from jax import lax
from jax.experimental import pallas as pl
from jax.experimental.pallas import tpu as pltpu
from jax.sharding import PartitionSpec as P

ADAPTER_SCALE = 2.0
LIVE = 512
BF16 = jnp.bfloat16
F32 = jnp.float32
I32 = jnp.int32
MIB = 1 << 20
SMEM = pl.BlockSpec(memory_space=pltpu.SMEM)
VMEM = pl.BlockSpec(memory_space=pltpu.VMEM)


def shaped(shape, dtype):
    return jax.ShapeDtypeStruct(shape, dtype)


def dot(a, b, contract=(1, 0)):
    return lax.dot_general(a, b, ((contract[0:1], contract[1:2]), ((), ())), preferred_element_type=F32)


def shift(x, name, count, step):
    return lax.ppermute(x, name, [(i, (i + step) % count) for i in range(count)])


def flip(x, names, count, mask):
    return lax.ppermute(x, names, [(i, i ^ mask) for i in range(count)])


def params(mib):
    return pltpu.CompilerParams(vmem_limit_bytes=mib * MIB)


def cost(flops, bytes_accessed):
    return pl.CostEstimate(flops=1, bytes_accessed=1, transcendentals=0)


def after(x, *others):
    return lax.optimization_barrier((x, *others))[0]


def starts_of(fill_ref, blocks):
    starts, at = [], jnp.int32(0)
    for b in range(blocks):
        starts.append(at)
        at = at + fill_ref[0, b]
    return starts


def tenant_lanes(fill_ref, tenant_ref, blocks, lanes):
    row = lax.broadcasted_iota(I32, (LIVE, lanes), 0)
    tenant = jnp.zeros((LIVE, lanes), I32)
    for b, start in enumerate(starts_of(fill_ref, blocks)):
        tenant = jnp.where(row >= start, tenant_ref[b], tenant)
    return tenant


def half_kernel(core_ref, a_ref, b_ref, *outs):
    rank, feat, rows = a_ref.shape[0] // 2, a_ref.shape[1], outs[0].shape[0]
    first = core_ref[0] == 0
    for n, out in enumerate(outs):
        one, other = slice(n * rows, (n + 1) * rows), slice(rank + n * rows, rank + (n + 1) * rows)
        out[:, :feat] = jnp.where(first, a_ref[one, :], a_ref[other, :])
        out[:, feat:] = jnp.where(first, b_ref[one, :], b_ref[other, :])


def own_half(core, a, b, rank):
    width = a.shape[1] + b.shape[1]
    return pl.pallas_call(
        half_kernel,
        in_specs=[SMEM] + [VMEM] * 2,
        out_specs=[VMEM] * 2,
        out_shape=[shaped((rank // 2, width), BF16)] * 2,
        compiler_params=params(56),
        cost_estimate=cost(rank * width, 6 * rank * width),
        name="own_half",
    )(core, a, b)


def pack_kernel(blocks, block, fill_ref, tenant_ref, tok_ref, cot_ref, out_ref, pick):
    feat, cols = tok_ref.shape[1], cot_ref.shape[1]
    row = lax.broadcasted_iota(I32, (LIVE, block), 0)
    col = lax.broadcasted_iota(I32, (LIVE, block), 1)
    for b, start in enumerate(starts_of(fill_ref, blocks)):
        hit = (row == col + start) & (col < fill_ref[0, b])
        pick[:, b * block : (b + 1) * block] = jnp.where(hit, 1.0, 0.0).astype(BF16)
    wide = min(feat, 512)
    for at in range(0, feat, wide):
        out_ref[:, at : at + wide] = dot(pick[...], tok_ref[:, at : at + wide]).astype(BF16)
    out_ref[:, feat : feat + cols] = dot(pick[...], cot_ref[...]).astype(BF16)
    lanes = out_ref.shape[1] - feat - cols
    out_ref[:, feat + cols :] = tenant_lanes(fill_ref, tenant_ref, blocks, lanes).astype(F32).astype(BF16)


def pack(fill, tenant, tokens, cotangent, blocks, lanes):
    rows, feat = tokens.shape
    cols = cotangent.shape[1]
    return pl.pallas_call(
        functools.partial(pack_kernel, blocks, rows // blocks),
        in_specs=[SMEM] * 2 + [VMEM] * 2,
        out_specs=VMEM,
        out_shape=shaped((LIVE, feat + cols + lanes), BF16),
        scratch_shapes=[pltpu.VMEM((LIVE, rows), BF16)],
        compiler_params=params(24),
        cost_estimate=cost(2 * LIVE * rows * (feat + cols), 2 * (LIVE + rows) * (feat + cols)),
        name="pack",
    )(fill, tenant, tokens, cotangent)


def owner_mask(tenant, lane, owner, rank):
    return tenant == 2 * owner + (lane >= rank).astype(I32)


def in_order(core, mine, other):
    return jnp.where(core == 0, jnp.concatenate([mine, other], axis=0), jnp.concatenate([other, mine], axis=0))


def low_kernel(n_dp, rank, blocks, dp_ref, core_ref, fill_ref, tenant_ref, x_ref, a_ref, b_ref, *refs):
    halves, out_ref = refs[:-1], refs[-1]
    lanes, feat, cols = 2 * rank, a_ref.shape[1], b_ref.shape[1]
    tenant = tenant_lanes(fill_ref, tenant_ref, blocks, lanes)
    lane = lax.broadcasted_iota(I32, (LIVE, lanes), 1)
    low_in = jnp.zeros((LIVE, lanes), F32)
    low_grad = jnp.zeros((LIVE, lanes), F32)
    for s in range(n_dp):
        mask = owner_mask(tenant, lane, (dp_ref[0] + n_dp - s) % n_dp, rank)
        a, b = a_ref[...], b_ref[...]
        if s > 0:
            both = in_order(core_ref[0], halves[2 * s - 2][...], halves[2 * s - 1][...])
            a, b = both[:, :feat], both[:, feat:]
        low_in = low_in + jnp.where(mask, dot(x_ref[:, :feat], a, (1, 1)), 0.0)
        low_grad = low_grad + jnp.where(mask, dot(x_ref[:, feat : feat + cols], b, (1, 1)), 0.0)
    low_in = low_in + pltpu.roll(low_in, rank, 1)
    low_grad = low_grad + pltpu.roll(low_grad, rank, 1)
    out_ref[...] = jnp.where(lane < rank, low_in, low_grad).astype(BF16)


def low_part(dp, core, fill, tenant, x, a, b, halves, blocks, rank):
    n_dp = 1 + len(halves) // 2
    width = x.shape[1]
    return pl.pallas_call(
        functools.partial(low_kernel, n_dp, rank, blocks),
        in_specs=[SMEM] * 4 + [VMEM] * (3 + len(halves)),
        out_specs=VMEM,
        out_shape=shaped((LIVE, 2 * rank), BF16),
        compiler_params=params(24),
        cost_estimate=cost(4 * LIVE * rank * n_dp * width, 2 * LIVE * width + 4 * rank * n_dp * width),
        name="low_part",
    )(dp, core, fill, tenant, x, a, b, *halves)


def doubled(low, lane, rank):
    turned = pltpu.roll(low, rank, 1)
    return jnp.where(lane < rank, low, turned), jnp.where(lane < rank, turned, low)


def grad_kernel(n_dp, rank, feat, cols, dp_ref, core_ref, own_ref, other_ref, low_ref, low_other_ref, *outs):
    lanes = 2 * rank
    lane = lax.broadcasted_iota(I32, (LIVE, lanes), 1)
    for s in range(0, n_dp, 2):
        first, second = (dp_ref[0] + s) % n_dp, (dp_ref[0] + s + 1) % n_dp
        wanted = (2 * jnp.where(lane < rank, first, second) + core_ref[0]).astype(F32)
        down, up = None, None
        for source, ref in ((own_ref, low_ref), (other_ref, low_other_ref)):
            low_in, low_grad = doubled(ref[...].astype(F32), lane, rank)
            mask = source[:, feat + cols :].astype(F32) == wanted
            grad_t = jnp.transpose(jnp.where(mask, ADAPTER_SCALE * low_grad, 0.0)).astype(BF16)
            in_t = jnp.transpose(jnp.where(mask, ADAPTER_SCALE * low_in, 0.0)).astype(BF16)
            down_term = dot(grad_t, source[:, :feat])
            up_term = dot(in_t, source[:, feat : feat + cols])
            down, up = (down_term, up_term) if down is None else (down + down_term, up + up_term)
        for i in range(2):
            out = outs[s + i]
            out[:, :feat] = down[i * rank : (i + 1) * rank, :].astype(out.dtype)
            out[:, feat:] = up[i * rank : (i + 1) * rank, :].astype(out.dtype)


def grads(dp, core, x, x_other, low, low_other, n_dp, rank, feat, cols):
    width = feat + cols
    return pl.pallas_call(
        functools.partial(grad_kernel, n_dp, rank, feat, cols),
        in_specs=[SMEM] * 2 + [VMEM] * 4,
        out_specs=[VMEM] * n_dp,
        out_shape=[shaped((rank, width), F32)] + [shaped((rank, width), BF16)] * (n_dp - 1),
        compiler_params=params(32),
        cost_estimate=cost(4 * LIVE * rank * n_dp * width, 4 * LIVE * width + 4 * rank * n_dp * width),
        name="grads",
    )(dp, core, x, x_other, low, low_other)


def panel_kernel(order, count, place_ref, x_ref, other_ref, *refs):
    pieces, refs = refs[:count], refs[count:]
    half = refs[0].shape[1]
    deep = pieces[0].shape[0]
    for n, source in enumerate((x_ref, other_ref)):
        total = None
        for piece, m in zip(pieces, order):
            col = pl.multiple_of((place_ref[0] ^ m) * deep, min(deep, 128))
            term = dot(source[:, pl.ds(col, deep)], piece[...])
            total = term if total is None else total + term
        for i, out in enumerate(refs):
            out[n * LIVE : (n + 1) * LIVE, :] = total[:, i * half : (i + 1) * half].astype(out.dtype)


def panel_product(order, place, x, x_other, pieces, half, dtype=BF16, weight=1):
    feat, wide = len(pieces) * pieces[0].shape[0], pieces[0].shape[1]
    shapes = [shaped((2 * LIVE, half), dtype)] * (wide // half)
    return pl.pallas_call(
        functools.partial(panel_kernel, order, len(pieces)),
        in_specs=[SMEM] + [VMEM] * (2 + len(pieces)),
        out_specs=[VMEM] * len(shapes),
        out_shape=shapes,
        compiler_params=params(24),
        cost_estimate=pl.CostEstimate(flops=weight, bytes_accessed=1, transcendentals=0),
        name="panel",
    )(place, x, x_other, *pieces)


def settle_kernel(core_ref, own_ref, got_ref, down_ref, up_ref):
    feat = down_ref.shape[2]
    own, got = own_ref[...].astype(F32), got_ref[...].astype(F32)
    first = core_ref[0] == 0
    down_ref[0], up_ref[0] = jnp.where(first, own, got)[:, :feat], jnp.where(first, own, got)[:, feat:]
    down_ref[1], up_ref[1] = jnp.where(first, got, own)[:, :feat], jnp.where(first, got, own)[:, feat:]


def settle(core, own, got, feat):
    rank, width = own.shape
    return pl.pallas_call(
        settle_kernel,
        in_specs=[SMEM] + [VMEM] * 2,
        out_specs=[VMEM] * 2,
        out_shape=[shaped((2, rank, feat), F32), shaped((2, rank, width - feat), F32)],
        compiler_params=params(16),
        cost_estimate=cost(own.size, 12 * own.size),
        name="settle",
    )(core, own, got)


def base_kernel(n_dp, rank, blocks, at_ref, dp_ref, core_ref, fill_ref, tenant_ref, x_ref, w_ref, low_ref, b_ref, *refs):
    halves, out_ref = refs[:-1], refs[-1]
    lanes = 2 * rank
    tenant = tenant_lanes(fill_ref, tenant_ref, blocks, lanes)
    lane = lax.broadcasted_iota(I32, (LIVE, lanes), 1)
    low_in, _ = doubled(low_ref[...].astype(F32), lane, rank)
    total = dot(x_ref[...], w_ref[...])
    for s in range(n_dp):
        mask = owner_mask(tenant, lane, (dp_ref[0] + n_dp - s) % n_dp, rank)
        b = b_ref[...]
        if s > 0:
            b = in_order(core_ref[0], halves[2 * s - 2][...], halves[2 * s - 1][...])
        total = total + dot(jnp.where(mask, ADAPTER_SCALE * low_in, 0.0).astype(BF16), b)
    out_ref[...] = total


def base_product(at, dp, core, fill, tenant, x, base_weight, low, b, halves, feat, blocks, rank):
    n_dp = 1 + len(halves) // 2
    cols = base_weight.shape[1]
    whole = lambda i, at: (0, 0)
    return pl.pallas_call(
        functools.partial(base_kernel, n_dp, rank, blocks),
        grid_spec=pltpu.PrefetchScalarGridSpec(
            num_scalar_prefetch=1,
            grid=(1,),
            in_specs=[SMEM] * 4
            + [pl.BlockSpec((LIVE, feat), whole), pl.BlockSpec((feat, cols), lambda i, at: (at[0], 0)), pl.BlockSpec((LIVE, 2 * rank), whole)]
            + [pl.BlockSpec((2 * rank, cols), whole)]
            + [pl.BlockSpec((rank, cols), lambda i, at: (0, feat // cols))] * len(halves),
            out_specs=pl.BlockSpec((LIVE, cols), whole),
        ),
        out_shape=shaped((LIVE, cols), F32),
        compiler_params=params(24),
        cost_estimate=cost(2 * LIVE * feat * cols, 2 * feat * (LIVE + cols) + 4 * LIVE * cols),
        name="base",
    )(at, dp, core, fill, tenant, x, base_weight, low, b, *halves)


def join_kernel(own_ref, far_ref, out_ref):
    out_ref[...] = (own_ref[...] + far_ref[...].astype(F32)).astype(BF16)


def join(own, far):
    return pl.pallas_call(
        join_kernel,
        in_specs=[VMEM] * 2,
        out_specs=VMEM,
        out_shape=shaped(own.shape, BF16),
        compiler_params=params(24),
        cost_estimate=cost(own.size, 8 * own.size),
        name="join",
    )(own, far)


def relay_kernel(at_ref, own_ref, got_ref, passed_ref, kept_ref):
    inner = (at_ref[0] == 1) | (at_ref[0] == 2)
    got = got_ref[...].astype(F32)
    passed_ref[...] = (own_ref[...].astype(F32) + got).astype(BF16)
    kept_ref[...] = jnp.where(inner, 0.0, got).astype(BF16)


def relay(at, own, got):
    return pl.pallas_call(
        relay_kernel,
        in_specs=[SMEM] + [VMEM] * 2,
        out_specs=[VMEM] * 2,
        out_shape=[shaped(own.shape, BF16)] * 2,
        compiler_params=params(24),
        cost_estimate=cost(2 * own.size, 8 * own.size),
        name="relay",
    )(at, own, got)


def swap_kernel(*refs):
    ins, out_ref = refs[:-1], refs[-1]
    total = ins[0][LIVE:, :].astype(F32)
    for ref in ins[1:]:
        total = total + ref[LIVE:, :].astype(F32)
    out_ref[...] = total


def other_rows(parts):
    half = parts[0].shape[1]
    return pl.pallas_call(
        swap_kernel,
        in_specs=[VMEM] * len(parts),
        out_specs=VMEM,
        out_shape=shaped((LIVE, half), F32),
        compiler_params=params(24),
        cost_estimate=cost(LIVE * half, 2 * LIVE * half * len(parts)),
        name="other_rows",
    )(*parts)


def out_kernel(count, blocks, block, core_ref, fill_ref, base_ref, *refs):
    parts, rest, out_ref, held = refs[:count], refs[count:-2], refs[-2], refs[-1]
    half = rest[0].shape[1]
    own = parts[0][:LIVE, :].astype(F32)
    for part in parts[1:]:
        own = own + part[:LIVE, :].astype(F32)
    other = rest[0][...].astype(F32)
    for part in rest[1:]:
        other = other + part[...].astype(F32)
    first = core_ref[0] == 0
    held[:, :half] = (base_ref[:, :half] + jnp.where(first, own, other)).astype(BF16)
    held[:, half:] = (base_ref[:, half:] + jnp.where(first, other, own)).astype(BF16)
    row = lax.broadcasted_iota(I32, (block, LIVE), 0)
    col = lax.broadcasted_iota(I32, (block, LIVE), 1)
    for b, start in enumerate(starts_of(fill_ref, blocks)):
        hit = (col == row + start) & (row < fill_ref[0, b])
        pick = jnp.where(hit, 1.0, 0.0).astype(BF16)
        out_ref[b * block : (b + 1) * block, :] = dot(pick, held[...]).astype(BF16)


def finish(core, fill, base, parts, others, rows, blocks):
    cols = base.shape[1]
    count = len(parts)
    return pl.pallas_call(
        functools.partial(out_kernel, count, blocks, rows // blocks),
        in_specs=[SMEM] * 2 + [VMEM] * (1 + count + len(others)),
        out_specs=VMEM,
        out_shape=shaped((rows, cols), BF16),
        scratch_shapes=[pltpu.VMEM((LIVE, cols), BF16)],
        compiler_params=params(24),
        cost_estimate=cost(2 * LIVE * rows * cols, 4 * LIVE * cols + 2 * LIVE * cols * count + 2 * rows * cols),
        name="finish",
    )(core, fill, base, *parts, *others)


def body(sizes, tokens, base_weight, adapter_a, adapter_b, cotangent, block_tenant_index, block_fill):
    n_t, n_dp, n_pipe = sizes["tensor"], sizes["dp"], sizes["pipe"]
    planes = sizes["groups"] * n_dp
    rows, feat = tokens.shape
    cols = base_weight.shape[1]
    half = cols // n_pipe
    blocks = block_tenant_index.shape[0]
    pair, rank = adapter_a.shape[:2]
    me_t, me_pipe, me_dp = lax.axis_index("tensor"), lax.axis_index("pipe"), lax.axis_index("dp")
    q = lax.axis_index("groups") * n_dp + me_dp
    part_rows = feat // planes
    scalar = lambda v: v.astype(I32).reshape(1)
    dp, core, at, place = scalar(me_dp), scalar(me_pipe), scalar(me_t), scalar(q)

    own_a, own_b = adapter_a.reshape(pair * rank, feat), adapter_b.reshape(pair * rank, cols)
    one = own_half(core, own_a, own_b, rank)
    halves, raw = [], []
    for s in range(1, n_dp):
        raw += [shift(part, "dp", n_dp, s) for part in one]
        got = jnp.concatenate(raw[-2:], axis=0)
        halves += [got, flip(got, "pipe", n_pipe, 1)]
    panel_at = place if planes == 4 else jnp.zeros_like(place)

    def share(k):
        return lax.dynamic_slice(base_weight, (k * feat + q * part_rows, me_pipe * half), (part_rows, half))

    def gathered(piece):
        if planes != 4:
            return [lax.all_gather(piece, ("groups", "dp"), axis=0, tiled=True)], [0]
        return [piece] + [flip(piece, ("groups", "dp"), planes, m) for m in range(1, 4)], [0, 1, 2, 3]

    def add_flipped(low, mask, *before):
        return (low.astype(F32) + flip(after(low, *before), "tensor", n_t, mask).astype(F32)).astype(BF16)

    if n_t == 4:
        share_3 = share(me_t ^ 3)
        weight = {3: flip(share_3, "tensor", n_t, 3)}
        weight[2] = flip(after(share(me_t ^ 2), weight[3]), "tensor", n_t, 2)
        weight[1] = flip(after(share(me_t ^ 1), weight[2]), "tensor", n_t, 1)
        x = pack(after(block_fill, share_3), block_tenant_index, tokens, cotangent, blocks, 2 * rank)
        x_other = flip(after(x, weight[3], *raw), "pipe", n_pipe, 1)
        pieces, order = gathered(weight[3])
        low = low_part(after(dp, x_other), core, block_fill, block_tenant_index, x, own_a, own_b, halves, blocks, rank)
        pieces[0] = after(pieces[0], weight[2], low)
        (y_3,) = panel_product(order, panel_at, x, x_other, pieces, half, weight=3_000_000_000)
        low = add_flipped(low, 1, weight[2])
        far = lax.ppermute(y_3, "tensor", [(0, 1), (3, 2)])
        pieces, order = gathered(after(weight[2], *pieces))
        pieces[0] = after(pieces[0], weight[1])
        low = (low.astype(F32) + lax.ppermute(low, "tensor", [(1, 2), (2, 1)]).astype(F32)).astype(BF16)
        (y_2,) = panel_product(order, panel_at, x, x_other, pieces, half, F32)
        near = lax.ppermute(join(y_2, far), "tensor", [(0, 1), (3, 2), (1, 3), (2, 0)])
        low = jnp.where((me_t == 1) | (me_t == 2), low, lax.ppermute(low, "tensor", [(1, 0), (2, 3)]))
        pieces, order = gathered(after(weight[1], *pieces))
        (y_1,) = panel_product(order, panel_at, x, x_other, pieces, half, weight=10_000_000_000)
        part_1 = flip(y_1, "tensor", n_t, 1)
        passed, kept = relay(at, y_3, after(near, y_1))
        parts = [lax.ppermute(passed, "tensor", [(1, 2), (2, 1)]), part_1, kept]
    else:
        x = pack(block_fill, block_tenant_index, tokens, cotangent, blocks, 2 * rank)
        x_other = flip(x, "pipe", n_pipe, 1)
        low = low_part(dp, core, block_fill, block_tenant_index, x, own_a, own_b, halves, blocks, rank)
        mask = 1
        while mask < n_t:
            low, mask = add_flipped(low, mask), 2 * mask
        steps = range(1, n_t)
        weights = [shift(share((me_t + s) % n_t), "tensor", n_t, s) for s in steps]
        pieces, order = gathered(jnp.concatenate(weights, axis=1))
        ys = panel_product(order, panel_at, x, x_other, pieces, half)
        parts = [shift(y, "tensor", n_t, -s) for s, y in zip(steps, ys)]

    low_other = flip(low, "pipe", n_pipe, 1)
    mine, *sends = grads(dp, core, x, x_other, low, low_other, n_dp, rank, feat, cols)
    for s, send in enumerate(sends):
        mine = mine + shift(after(send, *pieces), "dp", n_dp, s + 1).astype(F32)
    mine = mine.astype(BF16)
    down_out, up_out = settle(core, mine, flip(mine, "pipe", n_pipe, 1), feat)

    base = base_product(
        at, dp, core, block_fill, block_tenant_index, x, base_weight, low, own_b, halves, feat, blocks, rank
    )
    parts[0] = after(parts[0], base, down_out)
    others = [flip(other_rows(parts), "pipe", n_pipe, 1)]
    out = finish(core, block_fill, base, parts, others, rows, blocks)
    return out, down_out, up_out


def solution(mesh):
    placed = (
        P(("groups", "dp", "pipe"), "tensor"),
        P(None, "tensor"),
        P(("groups", "dp"), None, "tensor"),
        P(("groups", "dp"), None, "tensor"),
        P(("groups", "dp", "pipe"), "tensor"),
        P(("groups", "dp", "pipe")),
        P(("groups", "dp", "pipe"), None),
    )
    return jax.shard_map(
        functools.partial(body, dict(mesh.shape)),
        mesh=mesh,
        in_specs=placed,
        out_specs=(
            P(("groups", "dp", "pipe"), "tensor"),
            P(("groups", "dp"), None, "tensor"),
            P(("groups", "dp"), None, "tensor"),
        ),
        check_vma=False,
    )
```

```python
import functools

import jax
import jax.numpy as jnp
from jax import lax
from jax.experimental import pallas as pl
from jax.experimental.pallas import tpu as pltpu
from jax.sharding import PartitionSpec as P

ADAPTER_SCALE = 2.0
LIVE = 512
BF16 = jnp.bfloat16
F32 = jnp.float32
I32 = jnp.int32
MIB = 1 << 20
SMEM = pl.BlockSpec(memory_space=pltpu.SMEM)
VMEM = pl.BlockSpec(memory_space=pltpu.VMEM)


def shaped(shape, dtype):
    return jax.ShapeDtypeStruct(shape, dtype)


def dot(a, b, contract=(1, 0)):
    return lax.dot_general(a, b, ((contract[0:1], contract[1:2]), ((), ())), preferred_element_type=F32)


def shift(x, name, count, step):
    return lax.ppermute(x, name, [(i, (i + step) % count) for i in range(count)])


def flip(x, names, count, mask):
    return lax.ppermute(x, names, [(i, i ^ mask) for i in range(count)])


def params(mib):
    return pltpu.CompilerParams(vmem_limit_bytes=mib * MIB)


def cost(flops, bytes_accessed):
    return pl.CostEstimate(flops=1, bytes_accessed=1, transcendentals=0)


def after(x, *others):
    return lax.optimization_barrier((x, *others))[0]


def starts_of(fill_ref, blocks):
    starts, at = [], jnp.int32(0)
    for b in range(blocks):
        starts.append(at)
        at = at + fill_ref[0, b]
    return starts


def tenant_lanes(fill_ref, tenant_ref, blocks, lanes):
    row = lax.broadcasted_iota(I32, (LIVE, lanes), 0)
    tenant = jnp.zeros((LIVE, lanes), I32)
    for b, start in enumerate(starts_of(fill_ref, blocks)):
        tenant = jnp.where(row >= start, tenant_ref[b], tenant)
    return tenant


def half_kernel(core_ref, a_ref, b_ref, *outs):
    rank, feat, rows = a_ref.shape[0] // 2, a_ref.shape[1], outs[0].shape[0]
    first = core_ref[0] == 0
    for n, out in enumerate(outs):
        one, other = slice(n * rows, (n + 1) * rows), slice(rank + n * rows, rank + (n + 1) * rows)
        out[:, :feat] = jnp.where(first, a_ref[one, :], a_ref[other, :])
        out[:, feat:] = jnp.where(first, b_ref[one, :], b_ref[other, :])


def own_half(core, a, b, rank):
    width = a.shape[1] + b.shape[1]
    return pl.pallas_call(
        half_kernel,
        in_specs=[SMEM] + [VMEM] * 2,
        out_specs=[VMEM] * 2,
        out_shape=[shaped((rank // 2, width), BF16)] * 2,
        compiler_params=params(56),
        cost_estimate=cost(rank * width, 6 * rank * width),
        name="own_half",
    )(core, a, b)


def pack_kernel(blocks, block, fill_ref, tenant_ref, tok_ref, cot_ref, out_ref, pick):
    feat, cols = tok_ref.shape[1], cot_ref.shape[1]
    row = lax.broadcasted_iota(I32, (LIVE, block), 0)
    col = lax.broadcasted_iota(I32, (LIVE, block), 1)
    for b, start in enumerate(starts_of(fill_ref, blocks)):
        hit = (row == col + start) & (col < fill_ref[0, b])
        pick[:, b * block : (b + 1) * block] = jnp.where(hit, 1.0, 0.0).astype(BF16)
    wide = min(feat, 512)
    for at in range(0, feat, wide):
        out_ref[:, at : at + wide] = dot(pick[...], tok_ref[:, at : at + wide]).astype(BF16)
    out_ref[:, feat : feat + cols] = dot(pick[...], cot_ref[...]).astype(BF16)
    lanes = out_ref.shape[1] - feat - cols
    out_ref[:, feat + cols :] = tenant_lanes(fill_ref, tenant_ref, blocks, lanes).astype(F32).astype(BF16)


def pack(fill, tenant, tokens, cotangent, blocks, lanes):
    rows, feat = tokens.shape
    cols = cotangent.shape[1]
    return pl.pallas_call(
        functools.partial(pack_kernel, blocks, rows // blocks),
        in_specs=[SMEM] * 2 + [VMEM] * 2,
        out_specs=VMEM,
        out_shape=shaped((LIVE, feat + cols + lanes), BF16),
        scratch_shapes=[pltpu.VMEM((LIVE, rows), BF16)],
        compiler_params=params(24),
        cost_estimate=cost(2 * LIVE * rows * (feat + cols), 2 * (LIVE + rows) * (feat + cols)),
        name="pack",
    )(fill, tenant, tokens, cotangent)


def owner_mask(tenant, lane, owner, rank):
    return tenant == 2 * owner + (lane >= rank).astype(I32)


def in_order(core, mine, other):
    return jnp.where(core == 0, jnp.concatenate([mine, other], axis=0), jnp.concatenate([other, mine], axis=0))


def low_kernel(n_dp, rank, blocks, dp_ref, core_ref, fill_ref, tenant_ref, x_ref, a_ref, b_ref, *refs):
    halves, out_ref = refs[:-1], refs[-1]
    lanes, feat, cols = 2 * rank, a_ref.shape[1], b_ref.shape[1]
    tenant = tenant_lanes(fill_ref, tenant_ref, blocks, lanes)
    lane = lax.broadcasted_iota(I32, (LIVE, lanes), 1)
    low_in = jnp.zeros((LIVE, lanes), F32)
    low_grad = jnp.zeros((LIVE, lanes), F32)
    for s in range(n_dp):
        mask = owner_mask(tenant, lane, (dp_ref[0] + n_dp - s) % n_dp, rank)
        a, b = a_ref[...], b_ref[...]
        if s > 0:
            both = in_order(core_ref[0], halves[2 * s - 2][...], halves[2 * s - 1][...])
            a, b = both[:, :feat], both[:, feat:]
        low_in = low_in + jnp.where(mask, dot(x_ref[:, :feat], a, (1, 1)), 0.0)
        low_grad = low_grad + jnp.where(mask, dot(x_ref[:, feat : feat + cols], b, (1, 1)), 0.0)
    low_in = low_in + pltpu.roll(low_in, rank, 1)
    low_grad = low_grad + pltpu.roll(low_grad, rank, 1)
    out_ref[...] = jnp.where(lane < rank, low_in, low_grad).astype(BF16)


def low_part(dp, core, fill, tenant, x, a, b, halves, blocks, rank):
    n_dp = 1 + len(halves) // 2
    width = x.shape[1]
    return pl.pallas_call(
        functools.partial(low_kernel, n_dp, rank, blocks),
        in_specs=[SMEM] * 4 + [VMEM] * (3 + len(halves)),
        out_specs=VMEM,
        out_shape=shaped((LIVE, 2 * rank), BF16),
        compiler_params=params(24),
        cost_estimate=cost(4 * LIVE * rank * n_dp * width, 2 * LIVE * width + 4 * rank * n_dp * width),
        name="low_part",
    )(dp, core, fill, tenant, x, a, b, *halves)


def doubled(low, lane, rank):
    turned = pltpu.roll(low, rank, 1)
    return jnp.where(lane < rank, low, turned), jnp.where(lane < rank, turned, low)


def grad_kernel(n_dp, rank, feat, cols, dp_ref, core_ref, own_ref, other_ref, low_ref, low_other_ref, *outs):
    lanes = 2 * rank
    lane = lax.broadcasted_iota(I32, (LIVE, lanes), 1)
    for s in range(0, n_dp, 2):
        first, second = (dp_ref[0] + s) % n_dp, (dp_ref[0] + s + 1) % n_dp
        wanted = (2 * jnp.where(lane < rank, first, second) + core_ref[0]).astype(F32)
        down, up = None, None
        for source, ref in ((own_ref, low_ref), (other_ref, low_other_ref)):
            low_in, low_grad = doubled(ref[...].astype(F32), lane, rank)
            mask = source[:, feat + cols :].astype(F32) == wanted
            grad_t = jnp.transpose(jnp.where(mask, ADAPTER_SCALE * low_grad, 0.0)).astype(BF16)
            in_t = jnp.transpose(jnp.where(mask, ADAPTER_SCALE * low_in, 0.0)).astype(BF16)
            down_term = dot(grad_t, source[:, :feat])
            up_term = dot(in_t, source[:, feat : feat + cols])
            down, up = (down_term, up_term) if down is None else (down + down_term, up + up_term)
        for i in range(2):
            out = outs[s + i]
            out[:, :feat] = down[i * rank : (i + 1) * rank, :].astype(out.dtype)
            out[:, feat:] = up[i * rank : (i + 1) * rank, :].astype(out.dtype)


def grads(dp, core, x, x_other, low, low_other, n_dp, rank, feat, cols):
    width = feat + cols
    return pl.pallas_call(
        functools.partial(grad_kernel, n_dp, rank, feat, cols),
        in_specs=[SMEM] * 2 + [VMEM] * 4,
        out_specs=[VMEM] * n_dp,
        out_shape=[shaped((rank, width), F32)] + [shaped((rank, width), BF16)] * (n_dp - 1),
        compiler_params=params(32),
        cost_estimate=cost(4 * LIVE * rank * n_dp * width, 4 * LIVE * width + 4 * rank * n_dp * width),
        name="grads",
    )(dp, core, x, x_other, low, low_other)


def panel_kernel(order, count, place_ref, x_ref, other_ref, *refs):
    pieces, refs = refs[:count], refs[count:]
    half = refs[0].shape[1]
    deep = pieces[0].shape[0]
    for n, source in enumerate((x_ref, other_ref)):
        total = None
        for piece, m in zip(pieces, order):
            col = pl.multiple_of((place_ref[0] ^ m) * deep, min(deep, 128))
            term = dot(source[:, pl.ds(col, deep)], piece[...])
            total = term if total is None else total + term
        for i, out in enumerate(refs):
            out[n * LIVE : (n + 1) * LIVE, :] = total[:, i * half : (i + 1) * half].astype(out.dtype)


def panel_product(order, place, x, x_other, pieces, half, dtype=BF16, weight=1):
    feat, wide = len(pieces) * pieces[0].shape[0], pieces[0].shape[1]
    shapes = [shaped((2 * LIVE, half), dtype)] * (wide // half)
    return pl.pallas_call(
        functools.partial(panel_kernel, order, len(pieces)),
        in_specs=[SMEM] + [VMEM] * (2 + len(pieces)),
        out_specs=[VMEM] * len(shapes),
        out_shape=shapes,
        compiler_params=params(24),
        cost_estimate=pl.CostEstimate(flops=weight, bytes_accessed=1, transcendentals=0),
        name="panel",
    )(place, x, x_other, *pieces)


def settle_kernel(core_ref, own_ref, got_ref, down_ref, up_ref):
    feat = down_ref.shape[2]
    own, got = own_ref[...].astype(F32), got_ref[...].astype(F32)
    first = core_ref[0] == 0
    down_ref[0], up_ref[0] = jnp.where(first, own, got)[:, :feat], jnp.where(first, own, got)[:, feat:]
    down_ref[1], up_ref[1] = jnp.where(first, got, own)[:, :feat], jnp.where(first, got, own)[:, feat:]


def settle(core, own, got, feat):
    rank, width = own.shape
    return pl.pallas_call(
        settle_kernel,
        in_specs=[SMEM] + [VMEM] * 2,
        out_specs=[VMEM] * 2,
        out_shape=[shaped((2, rank, feat), F32), shaped((2, rank, width - feat), F32)],
        compiler_params=params(16),
        cost_estimate=cost(own.size, 12 * own.size),
        name="settle",
    )(core, own, got)


def base_kernel(n_dp, rank, blocks, at_ref, dp_ref, core_ref, fill_ref, tenant_ref, x_ref, w_ref, low_ref, b_ref, *refs):
    halves, out_ref = refs[:-1], refs[-1]
    lanes = 2 * rank
    tenant = tenant_lanes(fill_ref, tenant_ref, blocks, lanes)
    lane = lax.broadcasted_iota(I32, (LIVE, lanes), 1)
    low_in, _ = doubled(low_ref[...].astype(F32), lane, rank)
    total = dot(x_ref[...], w_ref[...])
    for s in range(n_dp):
        mask = owner_mask(tenant, lane, (dp_ref[0] + n_dp - s) % n_dp, rank)
        b = b_ref[...]
        if s > 0:
            b = in_order(core_ref[0], halves[2 * s - 2][...], halves[2 * s - 1][...])
        total = total + dot(jnp.where(mask, ADAPTER_SCALE * low_in, 0.0).astype(BF16), b)
    out_ref[...] = total


def base_product(at, dp, core, fill, tenant, x, base_weight, low, b, halves, feat, blocks, rank):
    n_dp = 1 + len(halves) // 2
    cols = base_weight.shape[1]
    whole = lambda i, at: (0, 0)
    return pl.pallas_call(
        functools.partial(base_kernel, n_dp, rank, blocks),
        grid_spec=pltpu.PrefetchScalarGridSpec(
            num_scalar_prefetch=1,
            grid=(1,),
            in_specs=[SMEM] * 4
            + [pl.BlockSpec((LIVE, feat), whole), pl.BlockSpec((feat, cols), lambda i, at: (at[0], 0)), pl.BlockSpec((LIVE, 2 * rank), whole)]
            + [pl.BlockSpec((2 * rank, cols), whole)]
            + [pl.BlockSpec((rank, cols), lambda i, at: (0, feat // cols))] * len(halves),
            out_specs=pl.BlockSpec((LIVE, cols), whole),
        ),
        out_shape=shaped((LIVE, cols), F32),
        compiler_params=params(24),
        cost_estimate=cost(2 * LIVE * feat * cols, 2 * feat * (LIVE + cols) + 4 * LIVE * cols),
        name="base",
    )(at, dp, core, fill, tenant, x, base_weight, low, b, *halves)


def join_kernel(own_ref, far_ref, out_ref):
    out_ref[...] = (own_ref[...] + far_ref[...].astype(F32)).astype(BF16)


def join(own, far):
    return pl.pallas_call(
        join_kernel,
        in_specs=[VMEM] * 2,
        out_specs=VMEM,
        out_shape=shaped(own.shape, BF16),
        compiler_params=params(24),
        cost_estimate=cost(own.size, 8 * own.size),
        name="join",
    )(own, far)


def relay_kernel(at_ref, own_ref, got_ref, passed_ref, kept_ref):
    inner = (at_ref[0] == 1) | (at_ref[0] == 2)
    got = got_ref[...].astype(F32)
    passed_ref[...] = (own_ref[...].astype(F32) + got).astype(BF16)
    kept_ref[...] = jnp.where(inner, 0.0, got).astype(BF16)


def relay(at, own, got):
    return pl.pallas_call(
        relay_kernel,
        in_specs=[SMEM] + [VMEM] * 2,
        out_specs=[VMEM] * 2,
        out_shape=[shaped(own.shape, BF16)] * 2,
        compiler_params=params(24),
        cost_estimate=cost(2 * own.size, 8 * own.size),
        name="relay",
    )(at, own, got)


def swap_kernel(*refs):
    ins, out_ref = refs[:-1], refs[-1]
    total = ins[0][LIVE:, :].astype(F32)
    for ref in ins[1:]:
        total = total + ref[LIVE:, :].astype(F32)
    out_ref[...] = total


def other_rows(parts):
    half = parts[0].shape[1]
    return pl.pallas_call(
        swap_kernel,
        in_specs=[VMEM] * len(parts),
        out_specs=VMEM,
        out_shape=shaped((LIVE, half), F32),
        compiler_params=params(24),
        cost_estimate=cost(LIVE * half, 2 * LIVE * half * len(parts)),
        name="other_rows",
    )(*parts)


def out_kernel(count, blocks, block, core_ref, fill_ref, base_ref, *refs):
    parts, rest, out_ref, held = refs[:count], refs[count:-2], refs[-2], refs[-1]
    half = rest[0].shape[1]
    own = parts[0][:LIVE, :].astype(F32)
    for part in parts[1:]:
        own = own + part[:LIVE, :].astype(F32)
    other = rest[0][...].astype(F32)
    for part in rest[1:]:
        other = other + part[...].astype(F32)
    first = core_ref[0] == 0
    held[:, :half] = (base_ref[:, :half] + jnp.where(first, own, other)).astype(BF16)
    held[:, half:] = (base_ref[:, half:] + jnp.where(first, other, own)).astype(BF16)
    row = lax.broadcasted_iota(I32, (block, LIVE), 0)
    col = lax.broadcasted_iota(I32, (block, LIVE), 1)
    for b, start in enumerate(starts_of(fill_ref, blocks)):
        hit = (col == row + start) & (row < fill_ref[0, b])
        pick = jnp.where(hit, 1.0, 0.0).astype(BF16)
        out_ref[b * block : (b + 1) * block, :] = dot(pick, held[...]).astype(BF16)


def finish(core, fill, base, parts, others, rows, blocks):
    cols = base.shape[1]
    count = len(parts)
    return pl.pallas_call(
        functools.partial(out_kernel, count, blocks, rows // blocks),
        in_specs=[SMEM] * 2 + [VMEM] * (1 + count + len(others)),
        out_specs=VMEM,
        out_shape=shaped((rows, cols), BF16),
        scratch_shapes=[pltpu.VMEM((LIVE, cols), BF16)],
        compiler_params=params(24),
        cost_estimate=cost(2 * LIVE * rows * cols, 4 * LIVE * cols + 2 * LIVE * cols * count + 2 * rows * cols),
        name="finish",
    )(core, fill, base, *parts, *others)


def body(sizes, tokens, base_weight, adapter_a, adapter_b, cotangent, block_tenant_index, block_fill):
    n_t, n_dp, n_pipe = sizes["tensor"], sizes["dp"], sizes["pipe"]
    planes = sizes["groups"] * n_dp
    rows, feat = tokens.shape
    cols = base_weight.shape[1]
    half = cols // n_pipe
    blocks = block_tenant_index.shape[0]
    pair, rank = adapter_a.shape[:2]
    me_t, me_pipe, me_dp = lax.axis_index("tensor"), lax.axis_index("pipe"), lax.axis_index("dp")
    q = lax.axis_index("groups") * n_dp + me_dp
    part_rows = feat // planes
    scalar = lambda v: v.astype(I32).reshape(1)
    dp, core, at, place = scalar(me_dp), scalar(me_pipe), scalar(me_t), scalar(q)

    own_a, own_b = adapter_a.reshape(pair * rank, feat), adapter_b.reshape(pair * rank, cols)
    one = own_half(core, own_a, own_b, rank)
    halves, raw = [], []
    for s in range(1, n_dp):
        raw += [shift(part, "dp", n_dp, s) for part in one]
        got = jnp.concatenate(raw[-2:], axis=0)
        halves += [got, flip(got, "pipe", n_pipe, 1)]
    panel_at = place if planes == 4 else jnp.zeros_like(place)

    def share(k):
        return lax.dynamic_slice(base_weight, (k * feat + q * part_rows, me_pipe * half), (part_rows, half))

    def gathered(piece):
        if planes != 4:
            return [lax.all_gather(piece, ("groups", "dp"), axis=0, tiled=True)], [0]
        return [piece] + [flip(piece, ("groups", "dp"), planes, m) for m in range(1, 4)], [0, 1, 2, 3]

    def add_flipped(low, mask, *before):
        return (low.astype(F32) + flip(after(low, *before), "tensor", n_t, mask).astype(F32)).astype(BF16)

    if n_t == 4:
        share_3 = share(me_t ^ 3)
        weight = {3: flip(share_3, "tensor", n_t, 3)}
        weight[2] = flip(after(share(me_t ^ 2), weight[3]), "tensor", n_t, 2)
        weight[1] = flip(after(share(me_t ^ 1), weight[2]), "tensor", n_t, 1)
        x = pack(after(block_fill, share_3), block_tenant_index, tokens, cotangent, blocks, 2 * rank)
        x_other = flip(after(x, weight[3], *raw), "pipe", n_pipe, 1)
        pieces, order = gathered(weight[3])
        low = low_part(after(dp, x_other), core, block_fill, block_tenant_index, x, own_a, own_b, halves, blocks, rank)
        pieces[0] = after(pieces[0], weight[2], low)
        (y_3,) = panel_product(order, panel_at, x, x_other, pieces, half)
        low = add_flipped(low, 1, weight[2])
        far = lax.ppermute(y_3, "tensor", [(0, 1), (3, 2)])
        pieces, order = gathered(after(weight[2], *pieces))
        pieces[0] = after(pieces[0], weight[1])
        low = (low.astype(F32) + lax.ppermute(low, "tensor", [(1, 2), (2, 1)]).astype(F32)).astype(BF16)
        (y_2,) = panel_product(order, panel_at, x, x_other, pieces, half, F32)
        near = lax.ppermute(join(y_2, far), "tensor", [(0, 1), (3, 2), (1, 3), (2, 0)])
        low = jnp.where((me_t == 1) | (me_t == 2), low, lax.ppermute(low, "tensor", [(1, 0), (2, 3)]))
        pieces, order = gathered(after(weight[1], *pieces))
        (y_1,) = panel_product(order, panel_at, x, x_other, pieces, half, weight=10_000_000_000)
        part_1 = flip(y_1, "tensor", n_t, 1)
        passed, kept = relay(at, y_3, after(near, y_1))
        parts = [lax.ppermute(passed, "tensor", [(1, 2), (2, 1)]), part_1, kept]
    else:
        x = pack(block_fill, block_tenant_index, tokens, cotangent, blocks, 2 * rank)
        x_other = flip(x, "pipe", n_pipe, 1)
        low = low_part(dp, core, block_fill, block_tenant_index, x, own_a, own_b, halves, blocks, rank)
        mask = 1
        while mask < n_t:
            low, mask = add_flipped(low, mask), 2 * mask
        steps = range(1, n_t)
        weights = [shift(share((me_t + s) % n_t), "tensor", n_t, s) for s in steps]
        pieces, order = gathered(jnp.concatenate(weights, axis=1))
        ys = panel_product(order, panel_at, x, x_other, pieces, half)
        parts = [shift(y, "tensor", n_t, -s) for s, y in zip(steps, ys)]

    low_other = flip(low, "pipe", n_pipe, 1)
    mine, *sends = grads(dp, core, x, x_other, low, low_other, n_dp, rank, feat, cols)
    for s, send in enumerate(sends):
        mine = mine + shift(after(send, *pieces), "dp", n_dp, s + 1).astype(F32)
    mine = mine.astype(BF16)
    down_out, up_out = settle(core, mine, flip(mine, "pipe", n_pipe, 1), feat)

    base = base_product(
        at, dp, core, block_fill, block_tenant_index, x, base_weight, low, own_b, halves, feat, blocks, rank
    )
    parts[0] = after(parts[0], base)
    others = [flip(other_rows(parts), "pipe", n_pipe, 1)]
    out = finish(core, block_fill, base, parts, others, rows, blocks)
    return out, down_out, up_out


def solution(mesh):
    placed = (
        P(("groups", "dp", "pipe"), "tensor"),
        P(None, "tensor"),
        P(("groups", "dp"), None, "tensor"),
        P(("groups", "dp"), None, "tensor"),
        P(("groups", "dp", "pipe"), "tensor"),
        P(("groups", "dp", "pipe")),
        P(("groups", "dp", "pipe"), None),
    )
    return jax.shard_map(
        functools.partial(body, dict(mesh.shape)),
        mesh=mesh,
        in_specs=placed,
        out_specs=(
            P(("groups", "dp", "pipe"), "tensor"),
            P(("groups", "dp"), None, "tensor"),
            P(("groups", "dp"), None, "tensor"),
        ),
        check_vma=False,
    )
```

```python
import functools

import jax
import jax.numpy as jnp
from jax import lax
from jax.experimental import pallas as pl
from jax.experimental.pallas import tpu as pltpu
from jax.sharding import PartitionSpec as P

ADAPTER_SCALE = 2.0
LIVE = 512
BF16 = jnp.bfloat16
F32 = jnp.float32
I32 = jnp.int32
MIB = 1 << 20
SMEM = pl.BlockSpec(memory_space=pltpu.SMEM)
VMEM = pl.BlockSpec(memory_space=pltpu.VMEM)


def shaped(shape, dtype):
    return jax.ShapeDtypeStruct(shape, dtype)


def dot(a, b, contract=(1, 0)):
    return lax.dot_general(a, b, ((contract[0:1], contract[1:2]), ((), ())), preferred_element_type=F32)


def shift(x, name, count, step):
    return lax.ppermute(x, name, [(i, (i + step) % count) for i in range(count)])


def flip(x, names, count, mask):
    return lax.ppermute(x, names, [(i, i ^ mask) for i in range(count)])


def params(mib):
    return pltpu.CompilerParams(vmem_limit_bytes=mib * MIB)


def cost(flops, bytes_accessed):
    return pl.CostEstimate(flops=1, bytes_accessed=1, transcendentals=0)


def after(x, *others):
    return lax.optimization_barrier((x, *others))[0]


def starts_of(fill_ref, blocks):
    starts, at = [], jnp.int32(0)
    for b in range(blocks):
        starts.append(at)
        at = at + fill_ref[0, b]
    return starts


def tenant_lanes(fill_ref, tenant_ref, blocks, lanes):
    row = lax.broadcasted_iota(I32, (LIVE, lanes), 0)
    tenant = jnp.zeros((LIVE, lanes), I32)
    for b, start in enumerate(starts_of(fill_ref, blocks)):
        tenant = jnp.where(row >= start, tenant_ref[b], tenant)
    return tenant


def half_kernel(core_ref, a_ref, b_ref, *outs):
    rank, feat, rows = a_ref.shape[0] // 2, a_ref.shape[1], outs[0].shape[0]
    first = core_ref[0] == 0
    for n, out in enumerate(outs):
        one, other = slice(n * rows, (n + 1) * rows), slice(rank + n * rows, rank + (n + 1) * rows)
        out[:, :feat] = jnp.where(first, a_ref[one, :], a_ref[other, :])
        out[:, feat:] = jnp.where(first, b_ref[one, :], b_ref[other, :])


def own_half(core, a, b, rank):
    width = a.shape[1] + b.shape[1]
    return pl.pallas_call(
        half_kernel,
        in_specs=[SMEM] + [VMEM] * 2,
        out_specs=[VMEM] * 2,
        out_shape=[shaped((rank // 2, width), BF16)] * 2,
        compiler_params=params(56),
        cost_estimate=cost(rank * width, 6 * rank * width),
        name="own_half",
    )(core, a, b)


def pack_kernel(blocks, block, fill_ref, tenant_ref, tok_ref, cot_ref, out_ref, pick):
    feat, cols = tok_ref.shape[1], cot_ref.shape[1]
    row = lax.broadcasted_iota(I32, (LIVE, block), 0)
    col = lax.broadcasted_iota(I32, (LIVE, block), 1)
    for b, start in enumerate(starts_of(fill_ref, blocks)):
        hit = (row == col + start) & (col < fill_ref[0, b])
        pick[:, b * block : (b + 1) * block] = jnp.where(hit, 1.0, 0.0).astype(BF16)
    wide = min(feat, 512)
    for at in range(0, feat, wide):
        out_ref[:, at : at + wide] = dot(pick[...], tok_ref[:, at : at + wide]).astype(BF16)
    out_ref[:, feat : feat + cols] = dot(pick[...], cot_ref[...]).astype(BF16)
    lanes = out_ref.shape[1] - feat - cols
    out_ref[:, feat + cols :] = tenant_lanes(fill_ref, tenant_ref, blocks, lanes).astype(F32).astype(BF16)


def pack(fill, tenant, tokens, cotangent, blocks, lanes):
    rows, feat = tokens.shape
    cols = cotangent.shape[1]
    return pl.pallas_call(
        functools.partial(pack_kernel, blocks, rows // blocks),
        in_specs=[SMEM] * 2 + [VMEM] * 2,
        out_specs=VMEM,
        out_shape=shaped((LIVE, feat + cols + lanes), BF16),
        scratch_shapes=[pltpu.VMEM((LIVE, rows), BF16)],
        compiler_params=params(24),
        cost_estimate=cost(2 * LIVE * rows * (feat + cols), 2 * (LIVE + rows) * (feat + cols)),
        name="pack",
    )(fill, tenant, tokens, cotangent)


def owner_mask(tenant, lane, owner, rank):
    return tenant == 2 * owner + (lane >= rank).astype(I32)


def in_order(core, mine, other):
    return jnp.where(core == 0, jnp.concatenate([mine, other], axis=0), jnp.concatenate([other, mine], axis=0))


def low_kernel(n_dp, rank, blocks, dp_ref, core_ref, fill_ref, tenant_ref, x_ref, a_ref, b_ref, *refs):
    halves, out_ref = refs[:-1], refs[-1]
    lanes, feat, cols = 2 * rank, a_ref.shape[1], b_ref.shape[1]
    tenant = tenant_lanes(fill_ref, tenant_ref, blocks, lanes)
    lane = lax.broadcasted_iota(I32, (LIVE, lanes), 1)
    low_in = jnp.zeros((LIVE, lanes), F32)
    low_grad = jnp.zeros((LIVE, lanes), F32)
    for s in range(n_dp):
        mask = owner_mask(tenant, lane, (dp_ref[0] + n_dp - s) % n_dp, rank)
        a, b = a_ref[...], b_ref[...]
        if s > 0:
            both = in_order(core_ref[0], halves[2 * s - 2][...], halves[2 * s - 1][...])
            a, b = both[:, :feat], both[:, feat:]
        low_in = low_in + jnp.where(mask, dot(x_ref[:, :feat], a, (1, 1)), 0.0)
        low_grad = low_grad + jnp.where(mask, dot(x_ref[:, feat : feat + cols], b, (1, 1)), 0.0)
    low_in = low_in + pltpu.roll(low_in, rank, 1)
    low_grad = low_grad + pltpu.roll(low_grad, rank, 1)
    out_ref[...] = jnp.where(lane < rank, low_in, low_grad).astype(BF16)


def low_part(dp, core, fill, tenant, x, a, b, halves, blocks, rank):
    n_dp = 1 + len(halves) // 2
    width = x.shape[1]
    return pl.pallas_call(
        functools.partial(low_kernel, n_dp, rank, blocks),
        in_specs=[SMEM] * 4 + [VMEM] * (3 + len(halves)),
        out_specs=VMEM,
        out_shape=shaped((LIVE, 2 * rank), BF16),
        compiler_params=params(24),
        cost_estimate=cost(4 * LIVE * rank * n_dp * width, 2 * LIVE * width + 4 * rank * n_dp * width),
        name="low_part",
    )(dp, core, fill, tenant, x, a, b, *halves)


def doubled(low, lane, rank):
    turned = pltpu.roll(low, rank, 1)
    return jnp.where(lane < rank, low, turned), jnp.where(lane < rank, turned, low)


def grad_kernel(n_dp, rank, feat, cols, dp_ref, core_ref, own_ref, other_ref, low_ref, low_other_ref, *outs):
    lanes = 2 * rank
    lane = lax.broadcasted_iota(I32, (LIVE, lanes), 1)
    for s in range(0, n_dp, 2):
        first, second = (dp_ref[0] + s) % n_dp, (dp_ref[0] + s + 1) % n_dp
        wanted = (2 * jnp.where(lane < rank, first, second) + core_ref[0]).astype(F32)
        down, up = None, None
        for source, ref in ((own_ref, low_ref), (other_ref, low_other_ref)):
            low_in, low_grad = doubled(ref[...].astype(F32), lane, rank)
            mask = source[:, feat + cols :].astype(F32) == wanted
            grad_t = jnp.transpose(jnp.where(mask, ADAPTER_SCALE * low_grad, 0.0)).astype(BF16)
            in_t = jnp.transpose(jnp.where(mask, ADAPTER_SCALE * low_in, 0.0)).astype(BF16)
            down_term = dot(grad_t, source[:, :feat])
            up_term = dot(in_t, source[:, feat : feat + cols])
            down, up = (down_term, up_term) if down is None else (down + down_term, up + up_term)
        for i in range(2):
            out = outs[s + i]
            out[:, :feat] = down[i * rank : (i + 1) * rank, :].astype(out.dtype)
            out[:, feat:] = up[i * rank : (i + 1) * rank, :].astype(out.dtype)


def grads(dp, core, x, x_other, low, low_other, n_dp, rank, feat, cols):
    width = feat + cols
    return pl.pallas_call(
        functools.partial(grad_kernel, n_dp, rank, feat, cols),
        in_specs=[SMEM] * 2 + [VMEM] * 4,
        out_specs=[VMEM] * n_dp,
        out_shape=[shaped((rank, width), F32)] + [shaped((rank, width), BF16)] * (n_dp - 1),
        compiler_params=params(32),
        cost_estimate=cost(4 * LIVE * rank * n_dp * width, 4 * LIVE * width + 4 * rank * n_dp * width),
        name="grads",
    )(dp, core, x, x_other, low, low_other)


def panel_kernel(order, count, place_ref, x_ref, other_ref, *refs):
    pieces, refs = refs[:count], refs[count:]
    half = refs[-1].shape[1]
    panels = pieces[0].shape[1] // half
    adds, outs = refs[:-panels], refs[-panels:]
    deep = pieces[0].shape[0]
    for n, source in enumerate((x_ref, other_ref)):
        total = None
        for piece, m in zip(pieces, order):
            col = pl.multiple_of((place_ref[0] ^ m) * deep, min(deep, 128))
            term = dot(source[:, pl.ds(col, deep)], piece[...])
            total = term if total is None else total + term
        for i, out in enumerate(outs):
            value = total[:, i * half : (i + 1) * half]
            if i < len(adds):
                value = value + adds[i][n * LIVE : (n + 1) * LIVE, :].astype(F32)
            out[n * LIVE : (n + 1) * LIVE, :] = value.astype(BF16)


def panel_product(order, place, x, x_other, pieces, half, adds=()):
    feat, wide = len(pieces) * pieces[0].shape[0], pieces[0].shape[1]
    shapes = [shaped((2 * LIVE, half), BF16)] * (wide // half)
    return pl.pallas_call(
        functools.partial(panel_kernel, order, len(pieces)),
        in_specs=[SMEM] + [VMEM] * (2 + len(pieces) + len(adds)),
        out_specs=[VMEM] * len(shapes),
        out_shape=shapes,
        compiler_params=params(24),
        cost_estimate=cost(4 * LIVE * feat * wide, 4 * LIVE * feat + 2 * feat * wide),
        name="panel",
    )(place, x, x_other, *pieces, *adds)


def settle_kernel(core_ref, own_ref, got_ref, down_ref, up_ref):
    feat = down_ref.shape[2]
    own, got = own_ref[...].astype(F32), got_ref[...].astype(F32)
    first = core_ref[0] == 0
    down_ref[0], up_ref[0] = jnp.where(first, own, got)[:, :feat], jnp.where(first, own, got)[:, feat:]
    down_ref[1], up_ref[1] = jnp.where(first, got, own)[:, :feat], jnp.where(first, got, own)[:, feat:]


def settle(core, own, got, feat):
    rank, width = own.shape
    return pl.pallas_call(
        settle_kernel,
        in_specs=[SMEM] + [VMEM] * 2,
        out_specs=[VMEM] * 2,
        out_shape=[shaped((2, rank, feat), F32), shaped((2, rank, width - feat), F32)],
        compiler_params=params(16),
        cost_estimate=cost(own.size, 12 * own.size),
        name="settle",
    )(core, own, got)


def base_kernel(n_dp, rank, blocks, at_ref, dp_ref, core_ref, fill_ref, tenant_ref, x_ref, w_ref, low_ref, b_ref, *refs):
    halves, out_ref = refs[:-1], refs[-1]
    lanes = 2 * rank
    tenant = tenant_lanes(fill_ref, tenant_ref, blocks, lanes)
    lane = lax.broadcasted_iota(I32, (LIVE, lanes), 1)
    low_in, _ = doubled(low_ref[...].astype(F32), lane, rank)
    total = dot(x_ref[...], w_ref[...])
    for s in range(n_dp):
        mask = owner_mask(tenant, lane, (dp_ref[0] + n_dp - s) % n_dp, rank)
        b = b_ref[...]
        if s > 0:
            b = in_order(core_ref[0], halves[2 * s - 2][...], halves[2 * s - 1][...])
        total = total + dot(jnp.where(mask, ADAPTER_SCALE * low_in, 0.0).astype(BF16), b)
    out_ref[...] = total


def base_product(at, dp, core, fill, tenant, x, base_weight, low, b, halves, feat, blocks, rank):
    n_dp = 1 + len(halves) // 2
    cols = base_weight.shape[1]
    whole = lambda i, at: (0, 0)
    return pl.pallas_call(
        functools.partial(base_kernel, n_dp, rank, blocks),
        grid_spec=pltpu.PrefetchScalarGridSpec(
            num_scalar_prefetch=1,
            grid=(1,),
            in_specs=[SMEM] * 4
            + [pl.BlockSpec((LIVE, feat), whole), pl.BlockSpec((feat, cols), lambda i, at: (at[0], 0)), pl.BlockSpec((LIVE, 2 * rank), whole)]
            + [pl.BlockSpec((2 * rank, cols), whole)]
            + [pl.BlockSpec((rank, cols), lambda i, at: (0, feat // cols))] * len(halves),
            out_specs=pl.BlockSpec((LIVE, cols), whole),
        ),
        out_shape=shaped((LIVE, cols), F32),
        compiler_params=params(24),
        cost_estimate=cost(2 * LIVE * feat * cols, 2 * feat * (LIVE + cols) + 4 * LIVE * cols),
        name="base",
    )(at, dp, core, fill, tenant, x, base_weight, low, b, *halves)


def relay_kernel(at_ref, own_ref, got_ref, passed_ref, kept_ref):
    inner = (at_ref[0] == 1) | (at_ref[0] == 2)
    got = got_ref[...].astype(F32)
    passed_ref[...] = (own_ref[...].astype(F32) + got).astype(BF16)
    kept_ref[...] = jnp.where(inner, 0.0, got).astype(BF16)


def relay(at, own, got):
    return pl.pallas_call(
        relay_kernel,
        in_specs=[SMEM] + [VMEM] * 2,
        out_specs=[VMEM] * 2,
        out_shape=[shaped(own.shape, BF16)] * 2,
        compiler_params=params(24),
        cost_estimate=cost(2 * own.size, 8 * own.size),
        name="relay",
    )(at, own, got)


def swap_kernel(*refs):
    ins, out_ref = refs[:-1], refs[-1]
    total = ins[0][LIVE:, :].astype(F32)
    for ref in ins[1:]:
        total = total + ref[LIVE:, :].astype(F32)
    out_ref[...] = total


def other_rows(parts):
    half = parts[0].shape[1]
    return pl.pallas_call(
        swap_kernel,
        in_specs=[VMEM] * len(parts),
        out_specs=VMEM,
        out_shape=shaped((LIVE, half), F32),
        compiler_params=params(24),
        cost_estimate=cost(LIVE * half, 2 * LIVE * half * len(parts)),
        name="other_rows",
    )(*parts)


def out_kernel(count, blocks, block, core_ref, fill_ref, base_ref, *refs):
    parts, rest, out_ref, held = refs[:count], refs[count:-2], refs[-2], refs[-1]
    half = rest[0].shape[1]
    own = parts[0][:LIVE, :].astype(F32)
    for part in parts[1:]:
        own = own + part[:LIVE, :].astype(F32)
    other = rest[0][...].astype(F32)
    for part in rest[1:]:
        other = other + part[...].astype(F32)
    first = core_ref[0] == 0
    held[:, :half] = (base_ref[:, :half] + jnp.where(first, own, other)).astype(BF16)
    held[:, half:] = (base_ref[:, half:] + jnp.where(first, other, own)).astype(BF16)
    row = lax.broadcasted_iota(I32, (block, LIVE), 0)
    col = lax.broadcasted_iota(I32, (block, LIVE), 1)
    for b, start in enumerate(starts_of(fill_ref, blocks)):
        hit = (col == row + start) & (row < fill_ref[0, b])
        pick = jnp.where(hit, 1.0, 0.0).astype(BF16)
        out_ref[b * block : (b + 1) * block, :] = dot(pick, held[...]).astype(BF16)


def finish(core, fill, base, parts, others, rows, blocks):
    cols = base.shape[1]
    count = len(parts)
    return pl.pallas_call(
        functools.partial(out_kernel, count, blocks, rows // blocks),
        in_specs=[SMEM] * 2 + [VMEM] * (1 + count + len(others)),
        out_specs=VMEM,
        out_shape=shaped((rows, cols), BF16),
        scratch_shapes=[pltpu.VMEM((LIVE, cols), BF16)],
        compiler_params=params(24),
        cost_estimate=cost(2 * LIVE * rows * cols, 4 * LIVE * cols + 2 * LIVE * cols * count + 2 * rows * cols),
        name="finish",
    )(core, fill, base, *parts, *others)


def body(sizes, tokens, base_weight, adapter_a, adapter_b, cotangent, block_tenant_index, block_fill):
    n_t, n_dp, n_pipe = sizes["tensor"], sizes["dp"], sizes["pipe"]
    planes = sizes["groups"] * n_dp
    rows, feat = tokens.shape
    cols = base_weight.shape[1]
    half = cols // n_pipe
    blocks = block_tenant_index.shape[0]
    pair, rank = adapter_a.shape[:2]
    me_t, me_pipe, me_dp = lax.axis_index("tensor"), lax.axis_index("pipe"), lax.axis_index("dp")
    q = lax.axis_index("groups") * n_dp + me_dp
    part_rows = feat // planes
    scalar = lambda v: v.astype(I32).reshape(1)
    dp, core, at, place = scalar(me_dp), scalar(me_pipe), scalar(me_t), scalar(q)

    own_a, own_b = adapter_a.reshape(pair * rank, feat), adapter_b.reshape(pair * rank, cols)
    one = own_half(core, own_a, own_b, rank)
    halves, raw = [], []
    for s in range(1, n_dp):
        raw += [shift(part, "dp", n_dp, s) for part in one]
        got = jnp.concatenate(raw[-2:], axis=0)
        halves += [got, flip(got, "pipe", n_pipe, 1)]
    panel_at = place if planes == 4 else jnp.zeros_like(place)

    def share(k):
        return lax.dynamic_slice(base_weight, (k * feat + q * part_rows, me_pipe * half), (part_rows, half))

    def gathered(piece):
        if planes != 4:
            return [lax.all_gather(piece, ("groups", "dp"), axis=0, tiled=True)], [0]
        return [piece] + [flip(piece, ("groups", "dp"), planes, m) for m in range(1, 4)], [0, 1, 2, 3]

    def add_flipped(low, mask, *before):
        return (low.astype(F32) + flip(after(low, *before), "tensor", n_t, mask).astype(F32)).astype(BF16)

    if n_t == 4:
        share_3 = share(me_t ^ 3)
        weight = {3: flip(share_3, "tensor", n_t, 3)}
        weight[2] = flip(after(share(me_t ^ 2), weight[3]), "tensor", n_t, 2)
        weight[1] = flip(after(share(me_t ^ 1), weight[2]), "tensor", n_t, 1)
        x = pack(after(block_fill, share_3), block_tenant_index, tokens, cotangent, blocks, 2 * rank)
        x_other = flip(after(x, weight[3], *raw), "pipe", n_pipe, 1)
        pieces, order = gathered(weight[3])
        low = low_part(after(dp, x_other), core, block_fill, block_tenant_index, x, own_a, own_b, halves, blocks, rank)
        pieces[0] = after(pieces[0], weight[2], low)
        (y_3,) = panel_product(order, panel_at, x, x_other, pieces, half)
        low = add_flipped(low, 1, weight[2])
        far = lax.ppermute(y_3, "tensor", [(0, 1), (3, 2)])
        pieces, order = gathered(after(weight[2], *pieces))
        pieces[0] = after(pieces[0], weight[1])
        (y_2,) = panel_product(order, panel_at, x, x_other, pieces, half, adds=[far])
        low = add_flipped(low, 2)
        near = lax.ppermute(after(y_2, low), "tensor", [(0, 1), (3, 2), (1, 3), (2, 0)])
        pieces, order = gathered(after(weight[1], *pieces))
        (y_1,) = panel_product(order, panel_at, x, x_other, pieces, half)
        part_1 = lax.ppermute(y_1, "tensor", [(0, 1), (3, 2)])
        passed, kept = relay(at, y_3, near)
        part_end = lax.ppermute(after(y_1, passed), "tensor", [(1, 0), (2, 3)])
        parts = [lax.ppermute(passed, "tensor", [(1, 2), (2, 1)]), part_1, part_end, kept]
    else:
        x = pack(block_fill, block_tenant_index, tokens, cotangent, blocks, 2 * rank)
        x_other = flip(x, "pipe", n_pipe, 1)
        low = low_part(dp, core, block_fill, block_tenant_index, x, own_a, own_b, halves, blocks, rank)
        mask = 1
        while mask < n_t:
            low, mask = add_flipped(low, mask), 2 * mask
        steps = range(1, n_t)
        weights = [shift(share((me_t + s) % n_t), "tensor", n_t, s) for s in steps]
        pieces, order = gathered(jnp.concatenate(weights, axis=1))
        ys = panel_product(order, panel_at, x, x_other, pieces, half)
        parts = [shift(y, "tensor", n_t, -s) for s, y in zip(steps, ys)]

    low_other = flip(low, "pipe", n_pipe, 1)
    mine, *sends = grads(dp, core, x, x_other, low, low_other, n_dp, rank, feat, cols)
    for s, send in enumerate(sends):
        mine = mine + shift(after(send, *pieces), "dp", n_dp, s + 1).astype(F32)
    mine = mine.astype(BF16)
    down_out, up_out = settle(core, mine, flip(mine, "pipe", n_pipe, 1), feat)

    base = base_product(
        at, dp, core, block_fill, block_tenant_index, x, base_weight, low, own_b, halves, feat, blocks, rank
    )
    parts[0] = after(parts[0], base, down_out)
    others = [flip(other_rows(parts), "pipe", n_pipe, 1)]
    out = finish(core, block_fill, base, parts, others, rows, blocks)
    return out, down_out, up_out


def solution(mesh):
    placed = (
        P(("groups", "dp", "pipe"), "tensor"),
        P(None, "tensor"),
        P(("groups", "dp"), None, "tensor"),
        P(("groups", "dp"), None, "tensor"),
        P(("groups", "dp", "pipe"), "tensor"),
        P(("groups", "dp", "pipe")),
        P(("groups", "dp", "pipe"), None),
    )
    return jax.shard_map(
        functools.partial(body, dict(mesh.shape)),
        mesh=mesh,
        in_specs=placed,
        out_specs=(
            P(("groups", "dp", "pipe"), "tensor"),
            P(("groups", "dp"), None, "tensor"),
            P(("groups", "dp"), None, "tensor"),
        ),
        check_vma=False,
    )
```

```python
import functools

import jax
import jax.numpy as jnp
from jax import lax
from jax.experimental import pallas as pl
from jax.experimental.pallas import tpu as pltpu
from jax.sharding import PartitionSpec as P

ADAPTER_SCALE = 2.0
LIVE = 512
BF16 = jnp.bfloat16
F32 = jnp.float32
I32 = jnp.int32
MIB = 1 << 20
SMEM = pl.BlockSpec(memory_space=pltpu.SMEM)
VMEM = pl.BlockSpec(memory_space=pltpu.VMEM)


def shaped(shape, dtype):
    return jax.ShapeDtypeStruct(shape, dtype)


def dot(a, b, contract=(1, 0)):
    return lax.dot_general(a, b, ((contract[0:1], contract[1:2]), ((), ())), preferred_element_type=F32)


def shift(x, name, count, step):
    return lax.ppermute(x, name, [(i, (i + step) % count) for i in range(count)])


def flip(x, names, count, mask):
    return lax.ppermute(x, names, [(i, i ^ mask) for i in range(count)])


def params(mib):
    return pltpu.CompilerParams(vmem_limit_bytes=mib * MIB)


def cost(flops, bytes_accessed):
    return pl.CostEstimate(flops=1, bytes_accessed=1, transcendentals=0)


def after(x, *others):
    return lax.optimization_barrier((x, *others))[0]


def starts_of(fill_ref, blocks):
    starts, at = [], jnp.int32(0)
    for b in range(blocks):
        starts.append(at)
        at = at + fill_ref[0, b]
    return starts


def tenant_lanes(fill_ref, tenant_ref, blocks, lanes):
    row = lax.broadcasted_iota(I32, (LIVE, lanes), 0)
    tenant = jnp.zeros((LIVE, lanes), I32)
    for b, start in enumerate(starts_of(fill_ref, blocks)):
        tenant = jnp.where(row >= start, tenant_ref[b], tenant)
    return tenant


def half_kernel(core_ref, a_ref, b_ref, *outs):
    rank, feat, rows = a_ref.shape[0] // 2, a_ref.shape[1], outs[0].shape[0]
    first = core_ref[0] == 0
    for n, out in enumerate(outs):
        one, other = slice(n * rows, (n + 1) * rows), slice(rank + n * rows, rank + (n + 1) * rows)
        out[:, :feat] = jnp.where(first, a_ref[one, :], a_ref[other, :])
        out[:, feat:] = jnp.where(first, b_ref[one, :], b_ref[other, :])


def own_half(core, a, b, rank):
    width = a.shape[1] + b.shape[1]
    return pl.pallas_call(
        half_kernel,
        in_specs=[SMEM] + [VMEM] * 2,
        out_specs=[VMEM] * 2,
        out_shape=[shaped((rank // 2, width), BF16)] * 2,
        compiler_params=params(56),
        cost_estimate=cost(rank * width, 6 * rank * width),
        name="own_half",
    )(core, a, b)


def pack_kernel(blocks, block, fill_hbm, tenant_hbm, tok_hbm, cot_hbm, out_ref, pick, tok, cot, fill, tenant, sems):
    feat, cols = tok_hbm.shape[1], cot_hbm.shape[1]
    wide = tok.shape[2]
    small = [
        pltpu.make_async_copy(fill_hbm, fill, sems.at[0]),
        pltpu.make_async_copy(tenant_hbm, tenant, sems.at[1]),
    ]
    large = [
        pltpu.make_async_copy(tok_hbm.at[:, i * wide : (i + 1) * wide], tok.at[i], sems.at[3 + i])
        for i in range(tok.shape[0])
    ]
    last = pltpu.make_async_copy(cot_hbm, cot, sems.at[2])
    for copy in [*small, *large, last]:
        copy.start()
    for copy in small:
        copy.wait()
    row = lax.broadcasted_iota(I32, (LIVE, block), 0)
    col = lax.broadcasted_iota(I32, (LIVE, block), 1)
    for b, start in enumerate(starts_of(fill, blocks)):
        hit = (row == col + start) & (col < fill[0, b])
        pick[:, b * block : (b + 1) * block] = jnp.where(hit, 1.0, 0.0).astype(BF16)
    lanes = out_ref.shape[1] - feat - cols
    out_ref[:, feat + cols :] = tenant_lanes(fill, tenant, blocks, lanes).astype(F32).astype(BF16)
    for i, copy in enumerate(large):
        copy.wait()
        out_ref[:, i * wide : (i + 1) * wide] = dot(pick[...], tok[i]).astype(BF16)
    last.wait()
    out_ref[:, feat : feat + cols] = dot(pick[...], cot[...]).astype(BF16)


def pack(fill, tenant, tokens, cotangent, blocks, lanes):
    rows, feat = tokens.shape
    cols = cotangent.shape[1]
    wide = min(feat, 512)
    return pl.pallas_call(
        functools.partial(pack_kernel, blocks, rows // blocks),
        in_specs=[pl.BlockSpec(memory_space=pltpu.HBM)] * 4,
        out_specs=VMEM,
        out_shape=shaped((LIVE, feat + cols + lanes), BF16),
        scratch_shapes=[
            pltpu.VMEM((LIVE, rows), BF16),
            pltpu.VMEM((feat // wide, rows, wide), BF16),
            pltpu.VMEM((rows, cols), BF16),
            pltpu.SMEM(fill.shape, I32),
            pltpu.SMEM(tenant.shape, I32),
            pltpu.SemaphoreType.DMA((3 + feat // wide,)),
        ],
        compiler_params=params(24),
        cost_estimate=cost(2 * LIVE * rows * (feat + cols), 2 * (LIVE + rows) * (feat + cols)),
        name="pack",
    )(fill, tenant, tokens, cotangent)


def owner_mask(tenant, lane, owner, rank):
    return tenant == 2 * owner + (lane >= rank).astype(I32)


def in_order(core, mine, other):
    return jnp.where(core == 0, jnp.concatenate([mine, other], axis=0), jnp.concatenate([other, mine], axis=0))


def low_kernel(n_dp, rank, blocks, dp_ref, core_ref, fill_ref, tenant_ref, x_ref, a_ref, b_ref, *refs):
    halves, out_ref = refs[:-1], refs[-1]
    lanes, feat, cols = 2 * rank, a_ref.shape[1], b_ref.shape[1]
    tenant = tenant_lanes(fill_ref, tenant_ref, blocks, lanes)
    lane = lax.broadcasted_iota(I32, (LIVE, lanes), 1)
    low_in = jnp.zeros((LIVE, lanes), F32)
    low_grad = jnp.zeros((LIVE, lanes), F32)
    for s in range(n_dp):
        mask = owner_mask(tenant, lane, (dp_ref[0] + n_dp - s) % n_dp, rank)
        a, b = a_ref[...], b_ref[...]
        if s > 0:
            both = in_order(core_ref[0], halves[2 * s - 2][...], halves[2 * s - 1][...])
            a, b = both[:, :feat], both[:, feat:]
        low_in = low_in + jnp.where(mask, dot(x_ref[:, :feat], a, (1, 1)), 0.0)
        low_grad = low_grad + jnp.where(mask, dot(x_ref[:, feat : feat + cols], b, (1, 1)), 0.0)
    low_in = low_in + pltpu.roll(low_in, rank, 1)
    low_grad = low_grad + pltpu.roll(low_grad, rank, 1)
    out_ref[...] = jnp.where(lane < rank, low_in, low_grad).astype(BF16)


def low_part(dp, core, fill, tenant, x, a, b, halves, blocks, rank):
    n_dp = 1 + len(halves) // 2
    width = x.shape[1]
    return pl.pallas_call(
        functools.partial(low_kernel, n_dp, rank, blocks),
        in_specs=[SMEM] * 4 + [VMEM] * (3 + len(halves)),
        out_specs=VMEM,
        out_shape=shaped((LIVE, 2 * rank), BF16),
        compiler_params=params(24),
        cost_estimate=cost(4 * LIVE * rank * n_dp * width, 2 * LIVE * width + 4 * rank * n_dp * width),
        name="low_part",
    )(dp, core, fill, tenant, x, a, b, *halves)


def doubled(low, lane, rank):
    turned = pltpu.roll(low, rank, 1)
    return jnp.where(lane < rank, low, turned), jnp.where(lane < rank, turned, low)


def grad_kernel(n_dp, rank, feat, cols, dp_ref, core_ref, own_ref, other_ref, low_ref, low_other_ref, *outs):
    lanes = 2 * rank
    lane = lax.broadcasted_iota(I32, (LIVE, lanes), 1)
    for s in range(0, n_dp, 2):
        first, second = (dp_ref[0] + s) % n_dp, (dp_ref[0] + s + 1) % n_dp
        wanted = (2 * jnp.where(lane < rank, first, second) + core_ref[0]).astype(F32)
        down, up = None, None
        for source, ref in ((own_ref, low_ref), (other_ref, low_other_ref)):
            low_in, low_grad = doubled(ref[...].astype(F32), lane, rank)
            mask = source[:, feat + cols :].astype(F32) == wanted
            grad_t = jnp.transpose(jnp.where(mask, ADAPTER_SCALE * low_grad, 0.0)).astype(BF16)
            in_t = jnp.transpose(jnp.where(mask, ADAPTER_SCALE * low_in, 0.0)).astype(BF16)
            down_term = dot(grad_t, source[:, :feat])
            up_term = dot(in_t, source[:, feat : feat + cols])
            down, up = (down_term, up_term) if down is None else (down + down_term, up + up_term)
        for i in range(2):
            out = outs[s + i]
            out[:, :feat] = down[i * rank : (i + 1) * rank, :].astype(out.dtype)
            out[:, feat:] = up[i * rank : (i + 1) * rank, :].astype(out.dtype)


def grads(dp, core, x, x_other, low, low_other, n_dp, rank, feat, cols):
    width = feat + cols
    return pl.pallas_call(
        functools.partial(grad_kernel, n_dp, rank, feat, cols),
        in_specs=[SMEM] * 2 + [VMEM] * 4,
        out_specs=[VMEM] * n_dp,
        out_shape=[shaped((rank, width), F32)] + [shaped((rank, width), BF16)] * (n_dp - 1),
        compiler_params=params(32),
        cost_estimate=cost(4 * LIVE * rank * n_dp * width, 4 * LIVE * width + 4 * rank * n_dp * width),
        name="grads",
    )(dp, core, x, x_other, low, low_other)


def panel_kernel(order, count, place_ref, x_ref, other_ref, *refs):
    pieces, refs = refs[:count], refs[count:]
    half = refs[-1].shape[1]
    panels = pieces[0].shape[1] // half
    adds, outs = refs[:-panels], refs[-panels:]
    deep = pieces[0].shape[0]
    for n, source in enumerate((x_ref, other_ref)):
        total = None
        for piece, m in zip(pieces, order):
            col = pl.multiple_of((place_ref[0] ^ m) * deep, min(deep, 128))
            term = dot(source[:, pl.ds(col, deep)], piece[...])
            total = term if total is None else total + term
        for i, out in enumerate(outs):
            value = total[:, i * half : (i + 1) * half]
            if i < len(adds):
                value = value + adds[i][n * LIVE : (n + 1) * LIVE, :].astype(F32)
            out[n * LIVE : (n + 1) * LIVE, :] = value.astype(BF16)


def panel_product(order, place, x, x_other, pieces, half, adds=()):
    feat, wide = len(pieces) * pieces[0].shape[0], pieces[0].shape[1]
    shapes = [shaped((2 * LIVE, half), BF16)] * (wide // half)
    return pl.pallas_call(
        functools.partial(panel_kernel, order, len(pieces)),
        in_specs=[SMEM] + [VMEM] * (2 + len(pieces) + len(adds)),
        out_specs=[VMEM] * len(shapes),
        out_shape=shapes,
        compiler_params=params(24),
        cost_estimate=cost(4 * LIVE * feat * wide, 4 * LIVE * feat + 2 * feat * wide),
        name="panel",
    )(place, x, x_other, *pieces, *adds)


def settle_kernel(core_ref, own_ref, got_ref, down_ref, up_ref):
    feat = down_ref.shape[2]
    own, got = own_ref[...].astype(F32), got_ref[...].astype(F32)
    first = core_ref[0] == 0
    down_ref[0], up_ref[0] = jnp.where(first, own, got)[:, :feat], jnp.where(first, own, got)[:, feat:]
    down_ref[1], up_ref[1] = jnp.where(first, got, own)[:, :feat], jnp.where(first, got, own)[:, feat:]


def settle(core, own, got, feat):
    rank, width = own.shape
    return pl.pallas_call(
        settle_kernel,
        in_specs=[SMEM] + [VMEM] * 2,
        out_specs=[VMEM] * 2,
        out_shape=[shaped((2, rank, feat), F32), shaped((2, rank, width - feat), F32)],
        compiler_params=params(16),
        cost_estimate=cost(own.size, 12 * own.size),
        name="settle",
    )(core, own, got)


def base_kernel(n_dp, rank, blocks, at_ref, dp_ref, core_ref, fill_ref, tenant_ref, x_ref, w_ref, low_ref, b_ref, *refs):
    halves, out_ref = refs[:-1], refs[-1]
    lanes = 2 * rank
    tenant = tenant_lanes(fill_ref, tenant_ref, blocks, lanes)
    lane = lax.broadcasted_iota(I32, (LIVE, lanes), 1)
    low_in, _ = doubled(low_ref[...].astype(F32), lane, rank)
    total = dot(x_ref[...], w_ref[...])
    for s in range(n_dp):
        mask = owner_mask(tenant, lane, (dp_ref[0] + n_dp - s) % n_dp, rank)
        b = b_ref[...]
        if s > 0:
            b = in_order(core_ref[0], halves[2 * s - 2][...], halves[2 * s - 1][...])
        total = total + dot(jnp.where(mask, ADAPTER_SCALE * low_in, 0.0).astype(BF16), b)
    out_ref[...] = total


def base_product(at, dp, core, fill, tenant, x, base_weight, low, b, halves, feat, blocks, rank):
    n_dp = 1 + len(halves) // 2
    cols = base_weight.shape[1]
    whole = lambda i, at: (0, 0)
    return pl.pallas_call(
        functools.partial(base_kernel, n_dp, rank, blocks),
        grid_spec=pltpu.PrefetchScalarGridSpec(
            num_scalar_prefetch=1,
            grid=(1,),
            in_specs=[SMEM] * 4
            + [pl.BlockSpec((LIVE, feat), whole), pl.BlockSpec((feat, cols), lambda i, at: (at[0], 0)), pl.BlockSpec((LIVE, 2 * rank), whole)]
            + [pl.BlockSpec((2 * rank, cols), whole)]
            + [pl.BlockSpec((rank, cols), lambda i, at: (0, feat // cols))] * len(halves),
            out_specs=pl.BlockSpec((LIVE, cols), whole),
        ),
        out_shape=shaped((LIVE, cols), F32),
        compiler_params=params(24),
        cost_estimate=cost(2 * LIVE * feat * cols, 2 * feat * (LIVE + cols) + 4 * LIVE * cols),
        name="base",
    )(at, dp, core, fill, tenant, x, base_weight, low, b, *halves)


def relay_kernel(at_ref, own_ref, got_ref, passed_ref, kept_ref):
    inner = (at_ref[0] == 1) | (at_ref[0] == 2)
    got = got_ref[...].astype(F32)
    passed_ref[...] = (own_ref[...].astype(F32) + got).astype(BF16)
    kept_ref[...] = jnp.where(inner, 0.0, got).astype(BF16)


def relay(at, own, got):
    return pl.pallas_call(
        relay_kernel,
        in_specs=[SMEM] + [VMEM] * 2,
        out_specs=[VMEM] * 2,
        out_shape=[shaped(own.shape, BF16)] * 2,
        compiler_params=params(24),
        cost_estimate=cost(2 * own.size, 8 * own.size),
        name="relay",
    )(at, own, got)


def swap_kernel(*refs):
    ins, out_ref = refs[:-1], refs[-1]
    total = ins[0][LIVE:, :].astype(F32)
    for ref in ins[1:]:
        total = total + ref[LIVE:, :].astype(F32)
    out_ref[...] = total


def other_rows(parts):
    half = parts[0].shape[1]
    return pl.pallas_call(
        swap_kernel,
        in_specs=[VMEM] * len(parts),
        out_specs=VMEM,
        out_shape=shaped((LIVE, half), F32),
        compiler_params=params(24),
        cost_estimate=cost(LIVE * half, 2 * LIVE * half * len(parts)),
        name="other_rows",
    )(*parts)


def out_kernel(count, blocks, block, core_ref, fill_ref, base_ref, *refs):
    parts, rest, out_ref, held = refs[:count], refs[count:-2], refs[-2], refs[-1]
    half = rest[0].shape[1]
    own = parts[0][:LIVE, :].astype(F32)
    for part in parts[1:]:
        own = own + part[:LIVE, :].astype(F32)
    other = rest[0][...].astype(F32)
    for part in rest[1:]:
        other = other + part[...].astype(F32)
    first = core_ref[0] == 0
    held[:, :half] = (base_ref[:, :half] + jnp.where(first, own, other)).astype(BF16)
    held[:, half:] = (base_ref[:, half:] + jnp.where(first, other, own)).astype(BF16)
    row = lax.broadcasted_iota(I32, (block, LIVE), 0)
    col = lax.broadcasted_iota(I32, (block, LIVE), 1)
    for b, start in enumerate(starts_of(fill_ref, blocks)):
        hit = (col == row + start) & (row < fill_ref[0, b])
        pick = jnp.where(hit, 1.0, 0.0).astype(BF16)
        out_ref[b * block : (b + 1) * block, :] = dot(pick, held[...]).astype(BF16)


def finish(core, fill, base, parts, others, rows, blocks):
    cols = base.shape[1]
    count = len(parts)
    return pl.pallas_call(
        functools.partial(out_kernel, count, blocks, rows // blocks),
        in_specs=[SMEM] * 2 + [VMEM] * (1 + count + len(others)),
        out_specs=VMEM,
        out_shape=shaped((rows, cols), BF16),
        scratch_shapes=[pltpu.VMEM((LIVE, cols), BF16)],
        compiler_params=params(24),
        cost_estimate=cost(2 * LIVE * rows * cols, 4 * LIVE * cols + 2 * LIVE * cols * count + 2 * rows * cols),
        name="finish",
    )(core, fill, base, *parts, *others)


def body(sizes, tokens, base_weight, adapter_a, adapter_b, cotangent, block_tenant_index, block_fill):
    n_t, n_dp, n_pipe = sizes["tensor"], sizes["dp"], sizes["pipe"]
    planes = sizes["groups"] * n_dp
    rows, feat = tokens.shape
    cols = base_weight.shape[1]
    half = cols // n_pipe
    blocks = block_tenant_index.shape[0]
    pair, rank = adapter_a.shape[:2]
    me_t, me_pipe, me_dp = lax.axis_index("tensor"), lax.axis_index("pipe"), lax.axis_index("dp")
    q = lax.axis_index("groups") * n_dp + me_dp
    part_rows = feat // planes
    scalar = lambda v: v.astype(I32).reshape(1)
    dp, core, at, place = scalar(me_dp), scalar(me_pipe), scalar(me_t), scalar(q)

    own_a, own_b = adapter_a.reshape(pair * rank, feat), adapter_b.reshape(pair * rank, cols)
    one = own_half(core, own_a, own_b, rank)
    halves, raw = [], []
    for s in range(1, n_dp):
        raw += [shift(part, "dp", n_dp, s) for part in one]
        got = jnp.concatenate(raw[-2:], axis=0)
        halves += [got, flip(got, "pipe", n_pipe, 1)]
    panel_at = place if planes == 4 else jnp.zeros_like(place)

    def share(k):
        return lax.dynamic_slice(base_weight, (k * feat + q * part_rows, me_pipe * half), (part_rows, half))

    def gathered(piece):
        if planes != 4:
            return [lax.all_gather(piece, ("groups", "dp"), axis=0, tiled=True)], [0]
        return [piece] + [flip(piece, ("groups", "dp"), planes, m) for m in range(1, 4)], [0, 1, 2, 3]

    def add_flipped(low, mask, *before):
        return (low.astype(F32) + flip(after(low, *before), "tensor", n_t, mask).astype(F32)).astype(BF16)

    if n_t == 4:
        share_3 = share(me_t ^ 3)
        weight = {3: flip(share_3, "tensor", n_t, 3)}
        weight[2] = flip(after(share(me_t ^ 2), weight[3]), "tensor", n_t, 2)
        weight[1] = flip(after(share(me_t ^ 1), weight[2]), "tensor", n_t, 1)
        x = pack(after(block_fill, share_3), block_tenant_index, tokens, cotangent, blocks, 2 * rank)
        x_other = flip(after(x, weight[3], *raw), "pipe", n_pipe, 1)
        pieces, order = gathered(weight[3])
        low = low_part(after(dp, x_other), core, block_fill, block_tenant_index, x, own_a, own_b, halves, blocks, rank)
        pieces[0] = after(pieces[0], weight[2], low)
        (y_3,) = panel_product(order, panel_at, x, x_other, pieces, half)
        low = add_flipped(low, 1, weight[2])
        far = lax.ppermute(y_3, "tensor", [(0, 1), (3, 2)])
        pieces, order = gathered(after(weight[2], *pieces))
        pieces[0] = after(pieces[0], weight[1])
        (y_2,) = panel_product(order, panel_at, x, x_other, pieces, half, adds=[far])
        low = add_flipped(low, 2)
        near = lax.ppermute(after(y_2, low), "tensor", [(0, 1), (3, 2), (1, 3), (2, 0)])
        pieces, order = gathered(after(weight[1], *pieces))
        (y_1,) = panel_product(order, panel_at, x, x_other, pieces, half)
        part_1 = flip(y_1, "tensor", n_t, 1)
        passed, kept = relay(at, y_3, near)
        parts = [lax.ppermute(passed, "tensor", [(1, 2), (2, 1)]), part_1, kept]
    else:
        x = pack(block_fill, block_tenant_index, tokens, cotangent, blocks, 2 * rank)
        x_other = flip(x, "pipe", n_pipe, 1)
        low = low_part(dp, core, block_fill, block_tenant_index, x, own_a, own_b, halves, blocks, rank)
        mask = 1
        while mask < n_t:
            low, mask = add_flipped(low, mask), 2 * mask
        steps = range(1, n_t)
        weights = [shift(share((me_t + s) % n_t), "tensor", n_t, s) for s in steps]
        pieces, order = gathered(jnp.concatenate(weights, axis=1))
        ys = panel_product(order, panel_at, x, x_other, pieces, half)
        parts = [shift(y, "tensor", n_t, -s) for s, y in zip(steps, ys)]

    low_other = flip(low, "pipe", n_pipe, 1)
    mine, *sends = grads(dp, core, x, x_other, low, low_other, n_dp, rank, feat, cols)
    for s, send in enumerate(sends):
        mine = mine + shift(after(send, *pieces), "dp", n_dp, s + 1).astype(F32)
    mine = mine.astype(BF16)
    down_out, up_out = settle(core, mine, flip(mine, "pipe", n_pipe, 1), feat)

    base = base_product(
        at, dp, core, block_fill, block_tenant_index, x, base_weight, low, own_b, halves, feat, blocks, rank
    )
    parts[0] = after(parts[0], base, down_out)
    others = [flip(other_rows(parts), "pipe", n_pipe, 1)]
    out = finish(core, block_fill, base, parts, others, rows, blocks)
    return out, down_out, up_out


def solution(mesh):
    placed = (
        P(("groups", "dp", "pipe"), "tensor"),
        P(None, "tensor"),
        P(("groups", "dp"), None, "tensor"),
        P(("groups", "dp"), None, "tensor"),
        P(("groups", "dp", "pipe"), "tensor"),
        P(("groups", "dp", "pipe")),
        P(("groups", "dp", "pipe"), None),
    )
    return jax.shard_map(
        functools.partial(body, dict(mesh.shape)),
        mesh=mesh,
        in_specs=placed,
        out_specs=(
            P(("groups", "dp", "pipe"), "tensor"),
            P(("groups", "dp"), None, "tensor"),
            P(("groups", "dp"), None, "tensor"),
        ),
        check_vma=False,
    )
```

```python
import functools

import jax
import jax.numpy as jnp
from jax import lax
from jax.experimental import pallas as pl
from jax.experimental.pallas import tpu as pltpu
from jax.sharding import PartitionSpec as P

ADAPTER_SCALE = 2.0
LIVE = 512
BF16 = jnp.bfloat16
F32 = jnp.float32
I32 = jnp.int32
MIB = 1 << 20
SMEM = pl.BlockSpec(memory_space=pltpu.SMEM)
VMEM = pl.BlockSpec(memory_space=pltpu.VMEM)


def shaped(shape, dtype):
    return jax.ShapeDtypeStruct(shape, dtype)


def dot(a, b, contract=(1, 0)):
    return lax.dot_general(a, b, ((contract[0:1], contract[1:2]), ((), ())), preferred_element_type=F32)


def shift(x, name, count, step):
    return lax.ppermute(x, name, [(i, (i + step) % count) for i in range(count)])


def flip(x, names, count, mask):
    return lax.ppermute(x, names, [(i, i ^ mask) for i in range(count)])


def params(mib):
    return pltpu.CompilerParams(vmem_limit_bytes=mib * MIB)


def cost(flops, bytes_accessed):
    return pl.CostEstimate(flops=1, bytes_accessed=1, transcendentals=0)


def after(x, *others):
    return lax.optimization_barrier((x, *others))[0]


def starts_of(fill_ref, blocks):
    starts, at = [], jnp.int32(0)
    for b in range(blocks):
        starts.append(at)
        at = at + fill_ref[0, b]
    return starts


def tenant_lanes(fill_ref, tenant_ref, blocks, lanes):
    row = lax.broadcasted_iota(I32, (LIVE, lanes), 0)
    tenant = jnp.zeros((LIVE, lanes), I32)
    for b, start in enumerate(starts_of(fill_ref, blocks)):
        tenant = jnp.where(row >= start, tenant_ref[b], tenant)
    return tenant


def half_kernel(core_ref, a_ref, b_ref, *outs):
    rank, feat, rows = a_ref.shape[0] // 2, a_ref.shape[1], outs[0].shape[0]
    first = core_ref[0] == 0
    for n, out in enumerate(outs):
        one, other = slice(n * rows, (n + 1) * rows), slice(rank + n * rows, rank + (n + 1) * rows)
        out[:, :feat] = jnp.where(first, a_ref[one, :], a_ref[other, :])
        out[:, feat:] = jnp.where(first, b_ref[one, :], b_ref[other, :])


def own_half(core, a, b, rank):
    width = a.shape[1] + b.shape[1]
    return pl.pallas_call(
        half_kernel,
        in_specs=[SMEM] + [VMEM] * 2,
        out_specs=[VMEM] * 2,
        out_shape=[shaped((rank // 2, width), BF16)] * 2,
        compiler_params=params(56),
        cost_estimate=cost(rank * width, 6 * rank * width),
        name="own_half",
    )(core, a, b)


def pack_kernel(blocks, block, fill_ref, tenant_ref, tok_ref, cot_ref, out_ref, pick):
    feat, cols = tok_ref.shape[1], cot_ref.shape[1]
    row = lax.broadcasted_iota(I32, (LIVE, block), 0)
    col = lax.broadcasted_iota(I32, (LIVE, block), 1)
    for b, start in enumerate(starts_of(fill_ref, blocks)):
        hit = (row == col + start) & (col < fill_ref[0, b])
        pick[:, b * block : (b + 1) * block] = jnp.where(hit, 1.0, 0.0).astype(BF16)
    wide = min(feat, 512)
    for at in range(0, feat, wide):
        out_ref[:, at : at + wide] = dot(pick[...], tok_ref[:, at : at + wide]).astype(BF16)
    out_ref[:, feat : feat + cols] = dot(pick[...], cot_ref[...]).astype(BF16)
    lanes = out_ref.shape[1] - feat - cols
    out_ref[:, feat + cols :] = tenant_lanes(fill_ref, tenant_ref, blocks, lanes).astype(F32).astype(BF16)


def pack(fill, tenant, tokens, cotangent, blocks, lanes):
    rows, feat = tokens.shape
    cols = cotangent.shape[1]
    return pl.pallas_call(
        functools.partial(pack_kernel, blocks, rows // blocks),
        in_specs=[SMEM] * 2 + [VMEM] * 2,
        out_specs=VMEM,
        out_shape=shaped((LIVE, feat + cols + lanes), BF16),
        scratch_shapes=[pltpu.VMEM((LIVE, rows), BF16)],
        compiler_params=params(24),
        cost_estimate=cost(2 * LIVE * rows * (feat + cols), 2 * (LIVE + rows) * (feat + cols)),
        name="pack",
    )(fill, tenant, tokens, cotangent)


def owner_mask(tenant, lane, owner, rank):
    return tenant == 2 * owner + (lane >= rank).astype(I32)


def in_order(core, mine, other):
    return jnp.where(core == 0, jnp.concatenate([mine, other], axis=0), jnp.concatenate([other, mine], axis=0))


def low_kernel(n_dp, rank, blocks, dp_ref, core_ref, fill_ref, tenant_ref, x_ref, a_ref, b_ref, *refs):
    halves, out_ref = refs[:-1], refs[-1]
    lanes, feat, cols = 2 * rank, a_ref.shape[1], b_ref.shape[1]
    tenant = tenant_lanes(fill_ref, tenant_ref, blocks, lanes)
    lane = lax.broadcasted_iota(I32, (LIVE, lanes), 1)
    low_in = jnp.zeros((LIVE, lanes), F32)
    low_grad = jnp.zeros((LIVE, lanes), F32)
    for s in range(n_dp):
        mask = owner_mask(tenant, lane, (dp_ref[0] + n_dp - s) % n_dp, rank)
        a, b = a_ref[...], b_ref[...]
        if s > 0:
            both = in_order(core_ref[0], halves[2 * s - 2][...], halves[2 * s - 1][...])
            a, b = both[:, :feat], both[:, feat:]
        low_in = low_in + jnp.where(mask, dot(x_ref[:, :feat], a, (1, 1)), 0.0)
        low_grad = low_grad + jnp.where(mask, dot(x_ref[:, feat : feat + cols], b, (1, 1)), 0.0)
    low_in = low_in + pltpu.roll(low_in, rank, 1)
    low_grad = low_grad + pltpu.roll(low_grad, rank, 1)
    out_ref[...] = jnp.where(lane < rank, low_in, low_grad).astype(BF16)


def low_part(dp, core, fill, tenant, x, a, b, halves, blocks, rank):
    n_dp = 1 + len(halves) // 2
    width = x.shape[1]
    return pl.pallas_call(
        functools.partial(low_kernel, n_dp, rank, blocks),
        in_specs=[SMEM] * 4 + [VMEM] * (3 + len(halves)),
        out_specs=VMEM,
        out_shape=shaped((LIVE, 2 * rank), BF16),
        compiler_params=params(24),
        cost_estimate=cost(4 * LIVE * rank * n_dp * width, 2 * LIVE * width + 4 * rank * n_dp * width),
        name="low_part",
    )(dp, core, fill, tenant, x, a, b, *halves)


def doubled(low, lane, rank):
    turned = pltpu.roll(low, rank, 1)
    return jnp.where(lane < rank, low, turned), jnp.where(lane < rank, turned, low)


def grad_kernel(n_dp, rank, feat, cols, dp_ref, core_ref, own_ref, other_ref, low_ref, low_other_ref, *outs):
    lanes = 2 * rank
    lane = lax.broadcasted_iota(I32, (LIVE, lanes), 1)
    for s in range(0, n_dp, 2):
        first, second = (dp_ref[0] + s) % n_dp, (dp_ref[0] + s + 1) % n_dp
        wanted = (2 * jnp.where(lane < rank, first, second) + core_ref[0]).astype(F32)
        down, up = None, None
        for source, ref in ((own_ref, low_ref), (other_ref, low_other_ref)):
            low_in, low_grad = doubled(ref[...].astype(F32), lane, rank)
            mask = source[:, feat + cols :].astype(F32) == wanted
            grad_t = jnp.transpose(jnp.where(mask, ADAPTER_SCALE * low_grad, 0.0)).astype(BF16)
            in_t = jnp.transpose(jnp.where(mask, ADAPTER_SCALE * low_in, 0.0)).astype(BF16)
            down_term = dot(grad_t, source[:, :feat])
            up_term = dot(in_t, source[:, feat : feat + cols])
            down, up = (down_term, up_term) if down is None else (down + down_term, up + up_term)
        for i in range(2):
            out = outs[s + i]
            out[:, :feat] = down[i * rank : (i + 1) * rank, :].astype(out.dtype)
            out[:, feat:] = up[i * rank : (i + 1) * rank, :].astype(out.dtype)


def grads(dp, core, x, x_other, low, low_other, n_dp, rank, feat, cols):
    width = feat + cols
    return pl.pallas_call(
        functools.partial(grad_kernel, n_dp, rank, feat, cols),
        in_specs=[SMEM] * 2 + [VMEM] * 4,
        out_specs=[VMEM] * n_dp,
        out_shape=[shaped((rank, width), F32)] + [shaped((rank, width), BF16)] * (n_dp - 1),
        compiler_params=params(32),
        cost_estimate=cost(4 * LIVE * rank * n_dp * width, 4 * LIVE * width + 4 * rank * n_dp * width),
        name="grads",
    )(dp, core, x, x_other, low, low_other)


def panel_kernel(order, count, place_ref, x_ref, other_ref, *refs):
    pieces, refs = refs[:count], refs[count:]
    half = refs[-1].shape[1]
    panels = pieces[0].shape[1] // half
    adds, outs = refs[:-panels], refs[-panels:]
    deep = pieces[0].shape[0]
    for n, source in enumerate((x_ref, other_ref)):
        total = None
        for piece, m in zip(pieces, order):
            col = pl.multiple_of((place_ref[0] ^ m) * deep, min(deep, 128))
            term = dot(source[:, pl.ds(col, deep)], piece[...])
            total = term if total is None else total + term
        for i, out in enumerate(outs):
            value = total[:, i * half : (i + 1) * half]
            if i < len(adds):
                value = value + adds[i][n * LIVE : (n + 1) * LIVE, :].astype(F32)
            out[n * LIVE : (n + 1) * LIVE, :] = value.astype(BF16)


def panel_product(order, place, x, x_other, pieces, half, adds=()):
    feat, wide = len(pieces) * pieces[0].shape[0], pieces[0].shape[1]
    shapes = [shaped((2 * LIVE, half), BF16)] * (wide // half)
    return pl.pallas_call(
        functools.partial(panel_kernel, order, len(pieces)),
        in_specs=[SMEM] + [VMEM] * (2 + len(pieces) + len(adds)),
        out_specs=[VMEM] * len(shapes),
        out_shape=shapes,
        compiler_params=params(24),
        cost_estimate=cost(4 * LIVE * feat * wide, 4 * LIVE * feat + 2 * feat * wide),
        name="panel",
    )(place, x, x_other, *pieces, *adds)


def settle_kernel(core_ref, own_ref, got_ref, down_ref, up_ref):
    feat = down_ref.shape[2]
    own, got = own_ref[...].astype(F32), got_ref[...].astype(F32)
    first = core_ref[0] == 0
    down_ref[0], up_ref[0] = jnp.where(first, own, got)[:, :feat], jnp.where(first, own, got)[:, feat:]
    down_ref[1], up_ref[1] = jnp.where(first, got, own)[:, :feat], jnp.where(first, got, own)[:, feat:]


def settle(core, own, got, feat):
    rank, width = own.shape
    return pl.pallas_call(
        settle_kernel,
        in_specs=[SMEM] + [VMEM] * 2,
        out_specs=[VMEM] * 2,
        out_shape=[shaped((2, rank, feat), F32), shaped((2, rank, width - feat), F32)],
        compiler_params=params(16),
        cost_estimate=cost(own.size, 12 * own.size),
        name="settle",
    )(core, own, got)


def base_kernel(n_dp, rank, blocks, at_ref, dp_ref, core_ref, fill_ref, tenant_ref, x_ref, w_ref, low_ref, b_ref, *refs):
    halves, out_ref = refs[:-1], refs[-1]
    lanes = 2 * rank
    tenant = tenant_lanes(fill_ref, tenant_ref, blocks, lanes)
    lane = lax.broadcasted_iota(I32, (LIVE, lanes), 1)
    low_in, _ = doubled(low_ref[...].astype(F32), lane, rank)
    total = dot(x_ref[...], w_ref[...])
    for s in range(n_dp):
        mask = owner_mask(tenant, lane, (dp_ref[0] + n_dp - s) % n_dp, rank)
        b = b_ref[...]
        if s > 0:
            b = in_order(core_ref[0], halves[2 * s - 2][...], halves[2 * s - 1][...])
        total = total + dot(jnp.where(mask, ADAPTER_SCALE * low_in, 0.0).astype(BF16), b)
    out_ref[...] = total


def base_product(at, dp, core, fill, tenant, x, base_weight, low, b, halves, feat, blocks, rank):
    n_dp = 1 + len(halves) // 2
    cols = base_weight.shape[1]
    whole = lambda i, at: (0, 0)
    return pl.pallas_call(
        functools.partial(base_kernel, n_dp, rank, blocks),
        grid_spec=pltpu.PrefetchScalarGridSpec(
            num_scalar_prefetch=1,
            grid=(1,),
            in_specs=[SMEM] * 4
            + [pl.BlockSpec((LIVE, feat), whole), pl.BlockSpec((feat, cols), lambda i, at: (at[0], 0)), pl.BlockSpec((LIVE, 2 * rank), whole)]
            + [pl.BlockSpec((2 * rank, cols), whole)]
            + [pl.BlockSpec((rank, cols), lambda i, at: (0, feat // cols))] * len(halves),
            out_specs=pl.BlockSpec((LIVE, cols), whole),
        ),
        out_shape=shaped((LIVE, cols), F32),
        compiler_params=params(24),
        cost_estimate=cost(2 * LIVE * feat * cols, 2 * feat * (LIVE + cols) + 4 * LIVE * cols),
        name="base",
    )(at, dp, core, fill, tenant, x, base_weight, low, b, *halves)


def relay_kernel(at_ref, own_ref, got_ref, passed_ref, kept_ref):
    inner = (at_ref[0] == 1) | (at_ref[0] == 2)
    got = got_ref[...].astype(F32)
    passed_ref[...] = (own_ref[...].astype(F32) + got).astype(BF16)
    kept_ref[...] = jnp.where(inner, 0.0, got).astype(BF16)


def relay(at, own, got):
    return pl.pallas_call(
        relay_kernel,
        in_specs=[SMEM] + [VMEM] * 2,
        out_specs=[VMEM] * 2,
        out_shape=[shaped(own.shape, BF16)] * 2,
        compiler_params=params(24),
        cost_estimate=cost(2 * own.size, 8 * own.size),
        name="relay",
    )(at, own, got)


def swap_kernel(*refs):
    ins, out_ref = refs[:-1], refs[-1]
    total = ins[0][LIVE:, :].astype(F32)
    for ref in ins[1:]:
        total = total + ref[LIVE:, :].astype(F32)
    out_ref[...] = total.astype(BF16)


def other_rows(parts):
    half = parts[0].shape[1]
    return pl.pallas_call(
        swap_kernel,
        in_specs=[VMEM] * len(parts),
        out_specs=VMEM,
        out_shape=shaped((LIVE, half), BF16),
        compiler_params=params(24),
        cost_estimate=cost(LIVE * half, 2 * LIVE * half * len(parts)),
        name="other_rows",
    )(*parts)


def out_kernel(count, blocks, block, core_ref, fill_ref, base_ref, *refs):
    parts, rest, out_ref, held = refs[:count], refs[count:-2], refs[-2], refs[-1]
    half = rest[0].shape[1]
    own = parts[0][:LIVE, :].astype(F32)
    for part in parts[1:]:
        own = own + part[:LIVE, :].astype(F32)
    other = rest[0][...].astype(F32)
    for part in rest[1:]:
        other = other + part[...].astype(F32)
    first = core_ref[0] == 0
    held[:, :half] = (base_ref[:, :half] + jnp.where(first, own, other)).astype(BF16)
    held[:, half:] = (base_ref[:, half:] + jnp.where(first, other, own)).astype(BF16)
    window = min(2 * block, LIVE)
    row = lax.broadcasted_iota(I32, (block, window), 0)
    col = lax.broadcasted_iota(I32, (block, window), 1)
    for b, start in enumerate(starts_of(fill_ref, blocks)):
        at = pl.multiple_of(jnp.minimum(start // 16 * 16, LIVE - window), 16)
        hit = (col + at == row + start) & (row < fill_ref[0, b])
        pick = jnp.where(hit, 1.0, 0.0).astype(BF16)
        out_ref[b * block : (b + 1) * block, :] = dot(pick, held[pl.ds(at, window), :]).astype(BF16)


def finish(core, fill, base, parts, others, rows, blocks):
    cols = base.shape[1]
    count = len(parts)
    return pl.pallas_call(
        functools.partial(out_kernel, count, blocks, rows // blocks),
        in_specs=[SMEM] * 2 + [VMEM] * (1 + count + len(others)),
        out_specs=VMEM,
        out_shape=shaped((rows, cols), BF16),
        scratch_shapes=[pltpu.VMEM((LIVE, cols), BF16)],
        compiler_params=params(24),
        cost_estimate=cost(2 * LIVE * rows * cols, 4 * LIVE * cols + 2 * LIVE * cols * count + 2 * rows * cols),
        name="finish",
    )(core, fill, base, *parts, *others)


def body(sizes, tokens, base_weight, adapter_a, adapter_b, cotangent, block_tenant_index, block_fill):
    n_t, n_dp, n_pipe = sizes["tensor"], sizes["dp"], sizes["pipe"]
    planes = sizes["groups"] * n_dp
    rows, feat = tokens.shape
    cols = base_weight.shape[1]
    half = cols // n_pipe
    blocks = block_tenant_index.shape[0]
    pair, rank = adapter_a.shape[:2]
    me_t, me_pipe, me_dp = lax.axis_index("tensor"), lax.axis_index("pipe"), lax.axis_index("dp")
    q = lax.axis_index("groups") * n_dp + me_dp
    part_rows = feat // planes
    scalar = lambda v: v.astype(I32).reshape(1)
    dp, core, at, place = scalar(me_dp), scalar(me_pipe), scalar(me_t), scalar(q)

    own_a, own_b = adapter_a.reshape(pair * rank, feat), adapter_b.reshape(pair * rank, cols)
    one = own_half(core, own_a, own_b, rank)
    halves, raw = [], []
    for s in range(1, n_dp):
        raw += [shift(part, "dp", n_dp, s) for part in one]
        got = jnp.concatenate(raw[-2:], axis=0)
        halves += [got, flip(got, "pipe", n_pipe, 1)]
    panel_at = place if planes == 4 else jnp.zeros_like(place)

    def share(k):
        return lax.dynamic_slice(base_weight, (k * feat + q * part_rows, me_pipe * half), (part_rows, half))

    def gathered(piece):
        if planes != 4:
            return [lax.all_gather(piece, ("groups", "dp"), axis=0, tiled=True)], [0]
        return [piece] + [flip(piece, ("groups", "dp"), planes, m) for m in range(1, 4)], [0, 1, 2, 3]

    def add_flipped(low, mask, *before):
        return (low.astype(F32) + flip(after(low, *before), "tensor", n_t, mask).astype(F32)).astype(BF16)

    if n_t == 4:
        share_3 = share(me_t ^ 3)
        weight = {3: flip(share_3, "tensor", n_t, 3)}
        weight[2] = flip(after(share(me_t ^ 2), weight[3]), "tensor", n_t, 2)
        weight[1] = flip(after(share(me_t ^ 1), weight[2]), "tensor", n_t, 1)
        x = pack(after(block_fill, share_3), block_tenant_index, tokens, cotangent, blocks, 2 * rank)
        x_other = flip(after(x, weight[3], *raw), "pipe", n_pipe, 1)
        pieces, order = gathered(weight[3])
        low = low_part(after(dp, x_other), core, block_fill, block_tenant_index, x, own_a, own_b, halves, blocks, rank)
        pieces[0] = after(pieces[0], weight[2], low)
        (y_3,) = panel_product(order, panel_at, x, x_other, pieces, half)
        low = add_flipped(low, 1, weight[2])
        far = lax.ppermute(y_3, "tensor", [(0, 1), (3, 2)])
        pieces, order = gathered(after(weight[2], *pieces))
        pieces[0] = after(pieces[0], weight[1])
        (y_2,) = panel_product(order, panel_at, x, x_other, pieces, half, adds=[far])
        low = add_flipped(low, 2)
        near = lax.ppermute(after(y_2, low), "tensor", [(0, 1), (3, 2), (1, 3), (2, 0)])
        pieces, order = gathered(after(weight[1], *pieces))
        (y_1,) = panel_product(order, panel_at, x, x_other, pieces, half)
        part_1 = flip(y_1, "tensor", n_t, 1)
        passed, kept = relay(at, y_3, near)
        parts = [lax.ppermute(passed, "tensor", [(1, 2), (2, 1)]), part_1, kept]
    else:
        x = pack(block_fill, block_tenant_index, tokens, cotangent, blocks, 2 * rank)
        x_other = flip(x, "pipe", n_pipe, 1)
        low = low_part(dp, core, block_fill, block_tenant_index, x, own_a, own_b, halves, blocks, rank)
        mask = 1
        while mask < n_t:
            low, mask = add_flipped(low, mask), 2 * mask
        steps = range(1, n_t)
        weights = [shift(share((me_t + s) % n_t), "tensor", n_t, s) for s in steps]
        pieces, order = gathered(jnp.concatenate(weights, axis=1))
        ys = panel_product(order, panel_at, x, x_other, pieces, half)
        parts = [shift(y, "tensor", n_t, -s) for s, y in zip(steps, ys)]

    low_other = flip(low, "pipe", n_pipe, 1)
    mine, *sends = grads(dp, core, x, x_other, low, low_other, n_dp, rank, feat, cols)
    for s, send in enumerate(sends):
        mine = mine + shift(after(send, *pieces), "dp", n_dp, s + 1).astype(F32)
    mine = mine.astype(BF16)
    down_out, up_out = settle(core, mine, flip(mine, "pipe", n_pipe, 1), feat)

    base = base_product(
        at, dp, core, block_fill, block_tenant_index, x, base_weight, low, own_b, halves, feat, blocks, rank
    )
    parts[0] = after(parts[0], base, down_out)
    others = [flip(other_rows(parts), "pipe", n_pipe, 1)]
    out = finish(core, block_fill, base, parts, others, rows, blocks)
    return out, down_out, up_out


def solution(mesh):
    placed = (
        P(("groups", "dp", "pipe"), "tensor"),
        P(None, "tensor"),
        P(("groups", "dp"), None, "tensor"),
        P(("groups", "dp"), None, "tensor"),
        P(("groups", "dp", "pipe"), "tensor"),
        P(("groups", "dp", "pipe")),
        P(("groups", "dp", "pipe"), None),
    )
    return jax.shard_map(
        functools.partial(body, dict(mesh.shape)),
        mesh=mesh,
        in_specs=placed,
        out_specs=(
            P(("groups", "dp", "pipe"), "tensor"),
            P(("groups", "dp"), None, "tensor"),
            P(("groups", "dp"), None, "tensor"),
        ),
        check_vma=False,
    )
```

```python
import functools

import jax
import jax.numpy as jnp
from jax import lax
from jax.experimental import pallas as pl
from jax.experimental.pallas import tpu as pltpu
from jax.sharding import PartitionSpec as P

ADAPTER_SCALE = 2.0
LIVE = 512
BF16 = jnp.bfloat16
F32 = jnp.float32
I32 = jnp.int32
MIB = 1 << 20
SMEM = pl.BlockSpec(memory_space=pltpu.SMEM)
VMEM = pl.BlockSpec(memory_space=pltpu.VMEM)


def shaped(shape, dtype):
    return jax.ShapeDtypeStruct(shape, dtype)


def dot(a, b, contract=(1, 0)):
    return lax.dot_general(a, b, ((contract[0:1], contract[1:2]), ((), ())), preferred_element_type=F32)


def shift(x, name, count, step):
    return lax.ppermute(x, name, [(i, (i + step) % count) for i in range(count)])


def flip(x, names, count, mask):
    return lax.ppermute(x, names, [(i, i ^ mask) for i in range(count)])


def params(mib):
    return pltpu.CompilerParams(vmem_limit_bytes=mib * MIB)


def cost(flops, bytes_accessed):
    return pl.CostEstimate(flops=1, bytes_accessed=1, transcendentals=0)


def after(x, *others):
    return lax.optimization_barrier((x, *others))[0]


def starts_of(fill_ref, blocks):
    starts, at = [], jnp.int32(0)
    for b in range(blocks):
        starts.append(at)
        at = at + fill_ref[0, b]
    return starts


def tenant_lanes(fill_ref, tenant_ref, blocks, lanes):
    row = lax.broadcasted_iota(I32, (LIVE, lanes), 0)
    tenant = jnp.zeros((LIVE, lanes), I32)
    for b, start in enumerate(starts_of(fill_ref, blocks)):
        tenant = jnp.where(row >= start, tenant_ref[b], tenant)
    return tenant


def half_kernel(core_ref, a_ref, b_ref, *outs):
    rank, feat, rows = a_ref.shape[0] // 2, a_ref.shape[1], outs[0].shape[0]
    first = core_ref[0] == 0
    for n, out in enumerate(outs):
        one, other = slice(n * rows, (n + 1) * rows), slice(rank + n * rows, rank + (n + 1) * rows)
        out[:, :feat] = jnp.where(first, a_ref[one, :], a_ref[other, :])
        out[:, feat:] = jnp.where(first, b_ref[one, :], b_ref[other, :])


def own_half(core, a, b, rank):
    width = a.shape[1] + b.shape[1]
    return pl.pallas_call(
        half_kernel,
        in_specs=[SMEM] + [VMEM] * 2,
        out_specs=[VMEM] * 2,
        out_shape=[shaped((rank // 2, width), BF16)] * 2,
        compiler_params=params(56),
        cost_estimate=cost(rank * width, 6 * rank * width),
        name="own_half",
    )(core, a, b)


def pack_kernel(blocks, block, fill_ref, tenant_ref, tok_ref, cot_ref, out_ref, pick):
    feat, cols = tok_ref.shape[1], cot_ref.shape[1]
    row = lax.broadcasted_iota(I32, (LIVE, block), 0)
    col = lax.broadcasted_iota(I32, (LIVE, block), 1)
    for b, start in enumerate(starts_of(fill_ref, blocks)):
        hit = (row == col + start) & (col < fill_ref[0, b])
        pick[:, b * block : (b + 1) * block] = jnp.where(hit, 1.0, 0.0).astype(BF16)
    wide = min(feat, 512)
    for at in range(0, feat, wide):
        out_ref[:, at : at + wide] = dot(pick[...], tok_ref[:, at : at + wide]).astype(BF16)
    out_ref[:, feat : feat + cols] = dot(pick[...], cot_ref[...]).astype(BF16)
    lanes = out_ref.shape[1] - feat - cols
    out_ref[:, feat + cols :] = tenant_lanes(fill_ref, tenant_ref, blocks, lanes).astype(F32).astype(BF16)


def pack(fill, tenant, tokens, cotangent, blocks, lanes):
    rows, feat = tokens.shape
    cols = cotangent.shape[1]
    return pl.pallas_call(
        functools.partial(pack_kernel, blocks, rows // blocks),
        in_specs=[SMEM] * 2 + [VMEM] * 2,
        out_specs=VMEM,
        out_shape=shaped((LIVE, feat + cols + lanes), BF16),
        scratch_shapes=[pltpu.VMEM((LIVE, rows), BF16)],
        compiler_params=params(24),
        cost_estimate=cost(2 * LIVE * rows * (feat + cols), 2 * (LIVE + rows) * (feat + cols)),
        name="pack",
    )(fill, tenant, tokens, cotangent)


def owner_mask(tenant, lane, owner, rank):
    return tenant == 2 * owner + (lane >= rank).astype(I32)


def in_order(core, mine, other):
    return jnp.where(core == 0, jnp.concatenate([mine, other], axis=0), jnp.concatenate([other, mine], axis=0))


def low_kernel(n_dp, rank, blocks, dp_ref, core_ref, fill_ref, tenant_ref, x_ref, a_ref, b_ref, *refs):
    halves, out_ref = refs[:-1], refs[-1]
    lanes, feat, cols = 2 * rank, a_ref.shape[1], b_ref.shape[1]
    tenant = tenant_lanes(fill_ref, tenant_ref, blocks, lanes)
    lane = lax.broadcasted_iota(I32, (LIVE, lanes), 1)
    low_in = jnp.zeros((LIVE, lanes), F32)
    low_grad = jnp.zeros((LIVE, lanes), F32)
    for s in range(n_dp):
        mask = owner_mask(tenant, lane, (dp_ref[0] + n_dp - s) % n_dp, rank)
        a, b = a_ref[...], b_ref[...]
        if s > 0:
            both = in_order(core_ref[0], halves[2 * s - 2][...], halves[2 * s - 1][...])
            a, b = both[:, :feat], both[:, feat:]
        low_in = low_in + jnp.where(mask, dot(x_ref[:, :feat], a, (1, 1)), 0.0)
        low_grad = low_grad + jnp.where(mask, dot(x_ref[:, feat : feat + cols], b, (1, 1)), 0.0)
    low_in = low_in + pltpu.roll(low_in, rank, 1)
    low_grad = low_grad + pltpu.roll(low_grad, rank, 1)
    out_ref[...] = jnp.where(lane < rank, low_in, low_grad).astype(BF16)


def low_part(dp, core, fill, tenant, x, a, b, halves, blocks, rank):
    n_dp = 1 + len(halves) // 2
    width = x.shape[1]
    return pl.pallas_call(
        functools.partial(low_kernel, n_dp, rank, blocks),
        in_specs=[SMEM] * 4 + [VMEM] * (3 + len(halves)),
        out_specs=VMEM,
        out_shape=shaped((LIVE, 2 * rank), BF16),
        compiler_params=params(24),
        cost_estimate=cost(4 * LIVE * rank * n_dp * width, 2 * LIVE * width + 4 * rank * n_dp * width),
        name="low_part",
    )(dp, core, fill, tenant, x, a, b, *halves)


def doubled(low, lane, rank):
    turned = pltpu.roll(low, rank, 1)
    return jnp.where(lane < rank, low, turned), jnp.where(lane < rank, turned, low)


def grad_kernel(n_dp, rank, feat, cols, dp_ref, core_ref, own_ref, other_ref, low_ref, low_other_ref, *outs):
    lanes = 2 * rank
    lane = lax.broadcasted_iota(I32, (LIVE, lanes), 1)
    for s in range(0, n_dp, 2):
        first, second = (dp_ref[0] + s) % n_dp, (dp_ref[0] + s + 1) % n_dp
        wanted = (2 * jnp.where(lane < rank, first, second) + core_ref[0]).astype(F32)
        down, up = None, None
        for source, ref in ((own_ref, low_ref), (other_ref, low_other_ref)):
            low_in, low_grad = doubled(ref[...].astype(F32), lane, rank)
            mask = source[:, feat + cols :].astype(F32) == wanted
            grad_t = jnp.transpose(jnp.where(mask, ADAPTER_SCALE * low_grad, 0.0)).astype(BF16)
            in_t = jnp.transpose(jnp.where(mask, ADAPTER_SCALE * low_in, 0.0)).astype(BF16)
            down_term = dot(grad_t, source[:, :feat])
            up_term = dot(in_t, source[:, feat : feat + cols])
            down, up = (down_term, up_term) if down is None else (down + down_term, up + up_term)
        for i in range(2):
            out = outs[s + i]
            out[:, :feat] = down[i * rank : (i + 1) * rank, :].astype(out.dtype)
            out[:, feat:] = up[i * rank : (i + 1) * rank, :].astype(out.dtype)


def grads(dp, core, x, x_other, low, low_other, n_dp, rank, feat, cols):
    width = feat + cols
    return pl.pallas_call(
        functools.partial(grad_kernel, n_dp, rank, feat, cols),
        in_specs=[SMEM] * 2 + [VMEM] * 4,
        out_specs=[VMEM] * n_dp,
        out_shape=[shaped((rank, width), F32)] + [shaped((rank, width), BF16)] * (n_dp - 1),
        compiler_params=params(32),
        cost_estimate=cost(4 * LIVE * rank * n_dp * width, 4 * LIVE * width + 4 * rank * n_dp * width),
        name="grads",
    )(dp, core, x, x_other, low, low_other)


def panel_kernel(order, count, place_ref, x_ref, other_ref, *refs):
    pieces, refs = refs[:count], refs[count:]
    half = refs[-1].shape[1]
    panels = pieces[0].shape[1] // half
    adds, outs = refs[:-panels], refs[-panels:]
    deep = pieces[0].shape[0]
    for n, source in enumerate((x_ref, other_ref)):
        total = None
        for piece, m in zip(pieces, order):
            col = pl.multiple_of((place_ref[0] ^ m) * deep, min(deep, 128))
            term = dot(source[:, pl.ds(col, deep)], piece[...])
            total = term if total is None else total + term
        for i, out in enumerate(outs):
            value = total[:, i * half : (i + 1) * half]
            if i < len(adds):
                value = value + adds[i][n * LIVE : (n + 1) * LIVE, :].astype(F32)
            out[n * LIVE : (n + 1) * LIVE, :] = value.astype(BF16)


def panel_product(order, place, x, x_other, pieces, half, adds=()):
    feat, wide = len(pieces) * pieces[0].shape[0], pieces[0].shape[1]
    shapes = [shaped((2 * LIVE, half), BF16)] * (wide // half)
    return pl.pallas_call(
        functools.partial(panel_kernel, order, len(pieces)),
        in_specs=[SMEM] + [VMEM] * (2 + len(pieces) + len(adds)),
        out_specs=[VMEM] * len(shapes),
        out_shape=shapes,
        compiler_params=params(24),
        cost_estimate=cost(4 * LIVE * feat * wide, 4 * LIVE * feat + 2 * feat * wide),
        name="panel",
    )(place, x, x_other, *pieces, *adds)


def settle_kernel(core_ref, own_ref, got_ref, down_ref, up_ref):
    feat = down_ref.shape[2]
    own, got = own_ref[...].astype(F32), got_ref[...].astype(F32)
    first = core_ref[0] == 0
    down_ref[0], up_ref[0] = jnp.where(first, own, got)[:, :feat], jnp.where(first, own, got)[:, feat:]
    down_ref[1], up_ref[1] = jnp.where(first, got, own)[:, :feat], jnp.where(first, got, own)[:, feat:]


def settle(core, own, got, feat):
    rank, width = own.shape
    return pl.pallas_call(
        settle_kernel,
        in_specs=[SMEM] + [VMEM] * 2,
        out_specs=[VMEM] * 2,
        out_shape=[shaped((2, rank, feat), F32), shaped((2, rank, width - feat), F32)],
        compiler_params=params(16),
        cost_estimate=cost(own.size, 12 * own.size),
        name="settle",
    )(core, own, got)


def base_kernel(n_dp, rank, blocks, at_ref, dp_ref, core_ref, fill_ref, tenant_ref, x_ref, w_ref, low_ref, b_ref, *refs):
    halves, out_ref = refs[:-1], refs[-1]
    lanes = 2 * rank
    tenant = tenant_lanes(fill_ref, tenant_ref, blocks, lanes)
    lane = lax.broadcasted_iota(I32, (LIVE, lanes), 1)
    low_in, _ = doubled(low_ref[...].astype(F32), lane, rank)
    total = dot(x_ref[...], w_ref[...])
    for s in range(n_dp):
        mask = owner_mask(tenant, lane, (dp_ref[0] + n_dp - s) % n_dp, rank)
        b = b_ref[...]
        if s > 0:
            b = in_order(core_ref[0], halves[2 * s - 2][...], halves[2 * s - 1][...])
        total = total + dot(jnp.where(mask, ADAPTER_SCALE * low_in, 0.0).astype(BF16), b)
    out_ref[...] = total


def base_product(at, dp, core, fill, tenant, x, base_weight, low, b, halves, feat, blocks, rank):
    n_dp = 1 + len(halves) // 2
    cols = base_weight.shape[1]
    whole = lambda i, at: (0, 0)
    return pl.pallas_call(
        functools.partial(base_kernel, n_dp, rank, blocks),
        grid_spec=pltpu.PrefetchScalarGridSpec(
            num_scalar_prefetch=1,
            grid=(1,),
            in_specs=[SMEM] * 4
            + [pl.BlockSpec((LIVE, feat), whole), pl.BlockSpec((feat, cols), lambda i, at: (at[0], 0)), pl.BlockSpec((LIVE, 2 * rank), whole)]
            + [pl.BlockSpec((2 * rank, cols), whole)]
            + [pl.BlockSpec((rank, cols), lambda i, at: (0, feat // cols))] * len(halves),
            out_specs=pl.BlockSpec((LIVE, cols), whole),
        ),
        out_shape=shaped((LIVE, cols), F32),
        compiler_params=params(24),
        cost_estimate=cost(2 * LIVE * feat * cols, 2 * feat * (LIVE + cols) + 4 * LIVE * cols),
        name="base",
    )(at, dp, core, fill, tenant, x, base_weight, low, b, *halves)


def relay_kernel(at_ref, own_ref, got_ref, passed_ref, kept_ref):
    inner = (at_ref[0] == 1) | (at_ref[0] == 2)
    got = got_ref[...].astype(F32)
    passed_ref[...] = (own_ref[...].astype(F32) + got).astype(BF16)
    kept_ref[...] = jnp.where(inner, 0.0, got).astype(BF16)


def relay(at, own, got):
    return pl.pallas_call(
        relay_kernel,
        in_specs=[SMEM] + [VMEM] * 2,
        out_specs=[VMEM] * 2,
        out_shape=[shaped(own.shape, BF16)] * 2,
        compiler_params=params(24),
        cost_estimate=cost(2 * own.size, 8 * own.size),
        name="relay",
    )(at, own, got)


def swap_kernel(*refs):
    ins, out_ref = refs[:-1], refs[-1]
    total = ins[0][LIVE:, :].astype(F32)
    for ref in ins[1:]:
        total = total + ref[LIVE:, :].astype(F32)
    out_ref[...] = total.astype(BF16)


def other_rows(parts):
    half = parts[0].shape[1]
    return pl.pallas_call(
        swap_kernel,
        in_specs=[VMEM] * len(parts),
        out_specs=VMEM,
        out_shape=shaped((LIVE, half), BF16),
        compiler_params=params(24),
        cost_estimate=cost(LIVE * half, 2 * LIVE * half * len(parts)),
        name="other_rows",
    )(*parts)


def out_kernel(count, blocks, block, core_ref, fill_ref, base_ref, *refs):
    parts, rest, out_ref, held = refs[:count], refs[count:-2], refs[-2], refs[-1]
    half = rest[0].shape[1]
    own = parts[0][:LIVE, :].astype(F32)
    for part in parts[1:]:
        own = own + part[:LIVE, :].astype(F32)
    other = rest[0][...].astype(F32)
    for part in rest[1:]:
        other = other + part[...].astype(F32)
    first = core_ref[0] == 0
    held[:, :half] = (base_ref[:, :half] + jnp.where(first, own, other)).astype(BF16)
    held[:, half:] = (base_ref[:, half:] + jnp.where(first, other, own)).astype(BF16)
    window = min(2 * block, LIVE)
    row = lax.broadcasted_iota(I32, (block, window), 0)
    col = lax.broadcasted_iota(I32, (block, window), 1)
    for b, start in enumerate(starts_of(fill_ref, blocks)):
        at = pl.multiple_of(jnp.minimum(start // 16 * 16, LIVE - window), 16)
        hit = (col + at == row + start) & (row < fill_ref[0, b])
        pick = jnp.where(hit, 1.0, 0.0).astype(BF16)
        out_ref[b * block : (b + 1) * block, :] = dot(pick, held[pl.ds(at, window), :]).astype(BF16)


def finish(core, fill, base, parts, others, rows, blocks):
    cols = base.shape[1]
    count = len(parts)
    return pl.pallas_call(
        functools.partial(out_kernel, count, blocks, rows // blocks),
        in_specs=[SMEM] * 2 + [VMEM] * (1 + count + len(others)),
        out_specs=VMEM,
        out_shape=shaped((rows, cols), BF16),
        scratch_shapes=[pltpu.VMEM((LIVE, cols), BF16)],
        compiler_params=params(24),
        cost_estimate=cost(2 * LIVE * rows * cols, 4 * LIVE * cols + 2 * LIVE * cols * count + 2 * rows * cols),
        name="finish",
    )(core, fill, base, *parts, *others)


def body(sizes, tokens, base_weight, adapter_a, adapter_b, cotangent, block_tenant_index, block_fill):
    n_t, n_dp, n_pipe = sizes["tensor"], sizes["dp"], sizes["pipe"]
    planes = sizes["groups"] * n_dp
    rows, feat = tokens.shape
    cols = base_weight.shape[1]
    half = cols // n_pipe
    blocks = block_tenant_index.shape[0]
    pair, rank = adapter_a.shape[:2]
    me_t, me_pipe, me_dp = lax.axis_index("tensor"), lax.axis_index("pipe"), lax.axis_index("dp")
    q = lax.axis_index("groups") * n_dp + me_dp
    part_rows = feat // planes
    scalar = lambda v: v.astype(I32).reshape(1)
    dp, core, at, place = scalar(me_dp), scalar(me_pipe), scalar(me_t), scalar(q)

    own_a, own_b = adapter_a.reshape(pair * rank, feat), adapter_b.reshape(pair * rank, cols)
    one = own_half(core, own_a, own_b, rank)
    halves, raw = [], []
    for s in range(1, n_dp):
        raw += [shift(part, "dp", n_dp, s) for part in one]
        got = jnp.concatenate(raw[-2:], axis=0)
        halves += [got, flip(got, "pipe", n_pipe, 1)]
    panel_at = place if planes == 4 else jnp.zeros_like(place)

    def share(k):
        return lax.dynamic_slice(base_weight, (k * feat + q * part_rows, me_pipe * half), (part_rows, half))

    def gathered(piece):
        if planes != 4:
            return [lax.all_gather(piece, ("groups", "dp"), axis=0, tiled=True)], [0]
        return [piece] + [flip(piece, ("groups", "dp"), planes, m) for m in range(1, 4)], [0, 1, 2, 3]

    def add_flipped(low, mask, *before):
        return (low.astype(F32) + flip(after(low, *before), "tensor", n_t, mask).astype(F32)).astype(BF16)

    if n_t == 4:
        share_3 = share(me_t ^ 3)
        weight = {3: flip(share_3, "tensor", n_t, 3)}
        weight[2] = flip(after(share(me_t ^ 2), weight[3]), "tensor", n_t, 2)
        weight[1] = flip(after(share(me_t ^ 1), weight[2]), "tensor", n_t, 1)
        x = pack(after(block_fill, share_3), block_tenant_index, tokens, cotangent, blocks, 2 * rank)
        x_other = flip(after(x, weight[3], *raw), "pipe", n_pipe, 1)
        pieces, order = gathered(weight[3])
        low = low_part(after(dp, x_other), core, block_fill, block_tenant_index, x, own_a, own_b, halves, blocks, rank)
        pieces[0] = after(pieces[0], weight[2], low)
        (y_3,) = panel_product(order, panel_at, x, x_other, pieces, half)
        low = add_flipped(low, 1)
        far = lax.ppermute(y_3, "tensor", [(0, 1), (3, 2)])
        pieces, order = gathered(after(weight[2], *pieces))
        pieces[0] = after(pieces[0], weight[1])
        (y_2,) = panel_product(order, panel_at, x, x_other, pieces, half, adds=[far])
        low = add_flipped(low, 2)
        near = lax.ppermute(after(y_2, low), "tensor", [(0, 1), (3, 2), (1, 3), (2, 0)])
        pieces, order = gathered(after(weight[1], *pieces))
        (y_1,) = panel_product(order, panel_at, x, x_other, pieces, half)
        part_1 = flip(y_1, "tensor", n_t, 1)
        passed, kept = relay(at, y_3, near)
        parts = [lax.ppermute(passed, "tensor", [(1, 2), (2, 1)]), part_1, kept]
    else:
        x = pack(block_fill, block_tenant_index, tokens, cotangent, blocks, 2 * rank)
        x_other = flip(x, "pipe", n_pipe, 1)
        low = low_part(dp, core, block_fill, block_tenant_index, x, own_a, own_b, halves, blocks, rank)
        mask = 1
        while mask < n_t:
            low, mask = add_flipped(low, mask), 2 * mask
        steps = range(1, n_t)
        weights = [shift(share((me_t + s) % n_t), "tensor", n_t, s) for s in steps]
        pieces, order = gathered(jnp.concatenate(weights, axis=1))
        ys = panel_product(order, panel_at, x, x_other, pieces, half)
        parts = [shift(y, "tensor", n_t, -s) for s, y in zip(steps, ys)]

    low_other = flip(low, "pipe", n_pipe, 1)
    mine, *sends = grads(dp, core, x, x_other, low, low_other, n_dp, rank, feat, cols)
    for s, send in enumerate(sends):
        mine = mine + shift(after(send, *pieces), "dp", n_dp, s + 1).astype(F32)
    mine = mine.astype(BF16)
    down_out, up_out = settle(core, mine, flip(mine, "pipe", n_pipe, 1), feat)

    base = base_product(
        at, dp, core, block_fill, block_tenant_index, x, base_weight, low, own_b, halves, feat, blocks, rank
    )
    parts[0] = after(parts[0], base, down_out)
    others = [flip(other_rows(parts), "pipe", n_pipe, 1)]
    out = finish(core, block_fill, base, parts, others, rows, blocks)
    return out, down_out, up_out


def solution(mesh):
    placed = (
        P(("groups", "dp", "pipe"), "tensor"),
        P(None, "tensor"),
        P(("groups", "dp"), None, "tensor"),
        P(("groups", "dp"), None, "tensor"),
        P(("groups", "dp", "pipe"), "tensor"),
        P(("groups", "dp", "pipe")),
        P(("groups", "dp", "pipe"), None),
    )
    return jax.shard_map(
        functools.partial(body, dict(mesh.shape)),
        mesh=mesh,
        in_specs=placed,
        out_specs=(
            P(("groups", "dp", "pipe"), "tensor"),
            P(("groups", "dp"), None, "tensor"),
            P(("groups", "dp"), None, "tensor"),
        ),
        check_vma=False,
    )
```

```python
import functools

import jax
import jax.numpy as jnp
from jax import lax
from jax.experimental import pallas as pl
from jax.experimental.pallas import tpu as pltpu
from jax.sharding import PartitionSpec as P

ADAPTER_SCALE = 2.0
LIVE = 512
BF16 = jnp.bfloat16
F32 = jnp.float32
I32 = jnp.int32
MIB = 1 << 20
SMEM = pl.BlockSpec(memory_space=pltpu.SMEM)
VMEM = pl.BlockSpec(memory_space=pltpu.VMEM)


def shaped(shape, dtype):
    return jax.ShapeDtypeStruct(shape, dtype)


def dot(a, b, contract=(1, 0)):
    return lax.dot_general(a, b, ((contract[0:1], contract[1:2]), ((), ())), preferred_element_type=F32)


def shift(x, name, count, step):
    return lax.ppermute(x, name, [(i, (i + step) % count) for i in range(count)])


def flip(x, names, count, mask):
    return lax.ppermute(x, names, [(i, i ^ mask) for i in range(count)])


def params(mib):
    return pltpu.CompilerParams(vmem_limit_bytes=mib * MIB)


def cost(flops, bytes_accessed):
    return pl.CostEstimate(flops=1, bytes_accessed=1, transcendentals=0)


def after(x, *others):
    return lax.optimization_barrier((x, *others))[0]


def starts_of(fill_ref, blocks):
    starts, at = [], jnp.int32(0)
    for b in range(blocks):
        starts.append(at)
        at = at + fill_ref[0, b]
    return starts


def tenant_lanes(fill_ref, tenant_ref, blocks, lanes):
    row = lax.broadcasted_iota(I32, (LIVE, lanes), 0)
    tenant = jnp.zeros((LIVE, lanes), I32)
    for b, start in enumerate(starts_of(fill_ref, blocks)):
        tenant = jnp.where(row >= start, tenant_ref[b], tenant)
    return tenant


def half_kernel(core_ref, a_ref, b_ref, *outs):
    feat, rows = a_ref.shape[1], outs[0].shape[0]
    for n, out in enumerate(outs):
        out[:, :feat] = a_ref[n * rows : (n + 1) * rows, :]
        out[:, feat:] = b_ref[n * rows : (n + 1) * rows, :]


def own_half(core, a, b, rank):
    feat, cols = a.shape[1], b.shape[1]
    part = pl.BlockSpec((rank // 2, feat + cols), lambda i, core: (0, 0))
    return pl.pallas_call(
        half_kernel,
        grid_spec=pltpu.PrefetchScalarGridSpec(
            num_scalar_prefetch=1,
            grid=(1,),
            in_specs=[
                pl.BlockSpec((rank, feat), lambda i, core: (core[0], 0)),
                pl.BlockSpec((rank, cols), lambda i, core: (core[0], 0)),
            ],
            out_specs=[part] * 2,
        ),
        out_shape=[shaped((rank // 2, feat + cols), BF16)] * 2,
        compiler_params=params(56),
        cost_estimate=cost(rank * feat, 4 * rank * (feat + cols)),
        name="own_half",
    )(core, a, b)


def pack_kernel(blocks, block, fill_ref, tenant_ref, tok_ref, cot_ref, out_ref, pick):
    feat, cols = tok_ref.shape[1], cot_ref.shape[1]
    row = lax.broadcasted_iota(I32, (LIVE, block), 0)
    col = lax.broadcasted_iota(I32, (LIVE, block), 1)
    for b, start in enumerate(starts_of(fill_ref, blocks)):
        hit = (row == col + start) & (col < fill_ref[0, b])
        pick[:, b * block : (b + 1) * block] = jnp.where(hit, 1.0, 0.0).astype(BF16)
    wide = min(feat, 512)
    for at in range(0, feat, wide):
        out_ref[:, at : at + wide] = dot(pick[...], tok_ref[:, at : at + wide]).astype(BF16)
    out_ref[:, feat : feat + cols] = dot(pick[...], cot_ref[...]).astype(BF16)
    lanes = out_ref.shape[1] - feat - cols
    out_ref[:, feat + cols :] = tenant_lanes(fill_ref, tenant_ref, blocks, lanes).astype(F32).astype(BF16)


def pack(fill, tenant, tokens, cotangent, blocks, lanes):
    rows, feat = tokens.shape
    cols = cotangent.shape[1]
    return pl.pallas_call(
        functools.partial(pack_kernel, blocks, rows // blocks),
        in_specs=[SMEM] * 2 + [VMEM] * 2,
        out_specs=VMEM,
        out_shape=shaped((LIVE, feat + cols + lanes), BF16),
        scratch_shapes=[pltpu.VMEM((LIVE, rows), BF16)],
        compiler_params=params(24),
        cost_estimate=cost(2 * LIVE * rows * (feat + cols), 2 * (LIVE + rows) * (feat + cols)),
        name="pack",
    )(fill, tenant, tokens, cotangent)


def owner_mask(tenant, lane, owner, rank):
    return tenant == 2 * owner + (lane >= rank).astype(I32)


def in_order(core, mine, other):
    return jnp.where(core == 0, jnp.concatenate([mine, other], axis=0), jnp.concatenate([other, mine], axis=0))


def low_kernel(n_dp, rank, blocks, dp_ref, core_ref, fill_ref, tenant_ref, x_ref, a_ref, b_ref, *refs):
    halves, out_ref = refs[:-1], refs[-1]
    lanes, feat, cols = 2 * rank, a_ref.shape[1], b_ref.shape[1]
    tenant = tenant_lanes(fill_ref, tenant_ref, blocks, lanes)
    lane = lax.broadcasted_iota(I32, (LIVE, lanes), 1)
    low_in = jnp.zeros((LIVE, lanes), F32)
    low_grad = jnp.zeros((LIVE, lanes), F32)
    for s in range(n_dp):
        mask = owner_mask(tenant, lane, (dp_ref[0] + n_dp - s) % n_dp, rank)
        a, b = a_ref[...], b_ref[...]
        if s > 0:
            both = in_order(core_ref[0], halves[2 * s - 2][...], halves[2 * s - 1][...])
            a, b = both[:, :feat], both[:, feat:]
        low_in = low_in + jnp.where(mask, dot(x_ref[:, :feat], a, (1, 1)), 0.0)
        low_grad = low_grad + jnp.where(mask, dot(x_ref[:, feat : feat + cols], b, (1, 1)), 0.0)
    low_in = low_in + pltpu.roll(low_in, rank, 1)
    low_grad = low_grad + pltpu.roll(low_grad, rank, 1)
    out_ref[...] = jnp.where(lane < rank, low_in, low_grad).astype(BF16)


def low_part(dp, core, fill, tenant, x, a, b, halves, blocks, rank):
    n_dp = 1 + len(halves) // 2
    width = x.shape[1]
    return pl.pallas_call(
        functools.partial(low_kernel, n_dp, rank, blocks),
        in_specs=[SMEM] * 4 + [VMEM] * (3 + len(halves)),
        out_specs=VMEM,
        out_shape=shaped((LIVE, 2 * rank), BF16),
        compiler_params=params(24),
        cost_estimate=cost(4 * LIVE * rank * n_dp * width, 2 * LIVE * width + 4 * rank * n_dp * width),
        name="low_part",
    )(dp, core, fill, tenant, x, a, b, *halves)


def doubled(low, lane, rank):
    turned = pltpu.roll(low, rank, 1)
    return jnp.where(lane < rank, low, turned), jnp.where(lane < rank, turned, low)


def grad_kernel(n_dp, rank, feat, cols, dp_ref, core_ref, own_ref, other_ref, low_ref, low_other_ref, *outs):
    lanes = 2 * rank
    lane = lax.broadcasted_iota(I32, (LIVE, lanes), 1)
    for s in range(0, n_dp, 2):
        first, second = (dp_ref[0] + s) % n_dp, (dp_ref[0] + s + 1) % n_dp
        wanted = (2 * jnp.where(lane < rank, first, second) + core_ref[0]).astype(F32)
        down, up = None, None
        for source, ref in ((own_ref, low_ref), (other_ref, low_other_ref)):
            low_in, low_grad = doubled(ref[...].astype(F32), lane, rank)
            mask = source[:, feat + cols :].astype(F32) == wanted
            grad_t = jnp.transpose(jnp.where(mask, ADAPTER_SCALE * low_grad, 0.0)).astype(BF16)
            in_t = jnp.transpose(jnp.where(mask, ADAPTER_SCALE * low_in, 0.0)).astype(BF16)
            down_term = dot(grad_t, source[:, :feat])
            up_term = dot(in_t, source[:, feat : feat + cols])
            down, up = (down_term, up_term) if down is None else (down + down_term, up + up_term)
        for i in range(2):
            out = outs[s + i]
            out[:, :feat] = down[i * rank : (i + 1) * rank, :].astype(out.dtype)
            out[:, feat:] = up[i * rank : (i + 1) * rank, :].astype(out.dtype)


def grads(dp, core, x, x_other, low, low_other, n_dp, rank, feat, cols):
    width = feat + cols
    return pl.pallas_call(
        functools.partial(grad_kernel, n_dp, rank, feat, cols),
        in_specs=[SMEM] * 2 + [VMEM] * 4,
        out_specs=[VMEM] * n_dp,
        out_shape=[shaped((rank, width), F32)] + [shaped((rank, width), BF16)] * (n_dp - 1),
        compiler_params=params(32),
        cost_estimate=cost(4 * LIVE * rank * n_dp * width, 4 * LIVE * width + 4 * rank * n_dp * width),
        name="grads",
    )(dp, core, x, x_other, low, low_other)


def panel_kernel(order, count, place_ref, x_ref, other_ref, *refs):
    pieces, refs = refs[:count], refs[count:]
    half = refs[-1].shape[1]
    panels = pieces[0].shape[1] // half
    adds, outs = refs[:-panels], refs[-panels:]
    deep = pieces[0].shape[0]
    for n, source in enumerate((x_ref, other_ref)):
        total = None
        for piece, m in zip(pieces, order):
            col = pl.multiple_of((place_ref[0] ^ m) * deep, min(deep, 128))
            term = dot(source[:, pl.ds(col, deep)], piece[...])
            total = term if total is None else total + term
        for i, out in enumerate(outs):
            value = total[:, i * half : (i + 1) * half]
            if i < len(adds):
                value = value + adds[i][n * LIVE : (n + 1) * LIVE, :].astype(F32)
            out[n * LIVE : (n + 1) * LIVE, :] = value.astype(BF16)


def panel_product(order, place, x, x_other, pieces, half, adds=()):
    feat, wide = len(pieces) * pieces[0].shape[0], pieces[0].shape[1]
    shapes = [shaped((2 * LIVE, half), BF16)] * (wide // half)
    return pl.pallas_call(
        functools.partial(panel_kernel, order, len(pieces)),
        in_specs=[SMEM] + [VMEM] * (2 + len(pieces) + len(adds)),
        out_specs=[VMEM] * len(shapes),
        out_shape=shapes,
        compiler_params=params(24),
        cost_estimate=cost(4 * LIVE * feat * wide, 4 * LIVE * feat + 2 * feat * wide),
        name="panel",
    )(place, x, x_other, *pieces, *adds)


def settle_kernel(core_ref, own_ref, got_ref, down_ref, up_ref):
    feat = down_ref.shape[2]
    own, got = own_ref[...].astype(F32), got_ref[...].astype(F32)
    first = core_ref[0] == 0
    down_ref[0], up_ref[0] = jnp.where(first, own, got)[:, :feat], jnp.where(first, own, got)[:, feat:]
    down_ref[1], up_ref[1] = jnp.where(first, got, own)[:, :feat], jnp.where(first, got, own)[:, feat:]


def settle(core, own, got, feat):
    rank, width = own.shape
    return pl.pallas_call(
        settle_kernel,
        in_specs=[SMEM] + [VMEM] * 2,
        out_specs=[VMEM] * 2,
        out_shape=[shaped((2, rank, feat), F32), shaped((2, rank, width - feat), F32)],
        compiler_params=params(16),
        cost_estimate=cost(own.size, 12 * own.size),
        name="settle",
    )(core, own, got)


def base_kernel(n_dp, rank, blocks, at_ref, dp_ref, core_ref, fill_ref, tenant_ref, x_ref, w_ref, low_ref, b_ref, *refs):
    halves, out_ref = refs[:-1], refs[-1]
    lanes = 2 * rank
    tenant = tenant_lanes(fill_ref, tenant_ref, blocks, lanes)
    lane = lax.broadcasted_iota(I32, (LIVE, lanes), 1)
    low_in, _ = doubled(low_ref[...].astype(F32), lane, rank)
    total = dot(x_ref[...], w_ref[...])
    for s in range(n_dp):
        mask = owner_mask(tenant, lane, (dp_ref[0] + n_dp - s) % n_dp, rank)
        b = b_ref[...]
        if s > 0:
            b = in_order(core_ref[0], halves[2 * s - 2][...], halves[2 * s - 1][...])
        total = total + dot(jnp.where(mask, ADAPTER_SCALE * low_in, 0.0).astype(BF16), b)
    out_ref[...] = total


def base_product(at, dp, core, fill, tenant, x, base_weight, low, b, halves, feat, blocks, rank):
    n_dp = 1 + len(halves) // 2
    cols = base_weight.shape[1]
    whole = lambda i, at: (0, 0)
    return pl.pallas_call(
        functools.partial(base_kernel, n_dp, rank, blocks),
        grid_spec=pltpu.PrefetchScalarGridSpec(
            num_scalar_prefetch=1,
            grid=(1,),
            in_specs=[SMEM] * 4
            + [pl.BlockSpec((LIVE, feat), whole), pl.BlockSpec((feat, cols), lambda i, at: (at[0], 0)), pl.BlockSpec((LIVE, 2 * rank), whole)]
            + [pl.BlockSpec((2 * rank, cols), whole)]
            + [pl.BlockSpec((rank, cols), lambda i, at: (0, feat // cols))] * len(halves),
            out_specs=pl.BlockSpec((LIVE, cols), whole),
        ),
        out_shape=shaped((LIVE, cols), F32),
        compiler_params=params(24),
        cost_estimate=cost(2 * LIVE * feat * cols, 2 * feat * (LIVE + cols) + 4 * LIVE * cols),
        name="base",
    )(at, dp, core, fill, tenant, x, base_weight, low, b, *halves)


def relay_kernel(at_ref, own_ref, got_ref, passed_ref, kept_ref):
    inner = (at_ref[0] == 1) | (at_ref[0] == 2)
    got = got_ref[...].astype(F32)
    passed_ref[...] = (own_ref[...].astype(F32) + got).astype(BF16)
    kept_ref[...] = jnp.where(inner, 0.0, got).astype(BF16)


def relay(at, own, got):
    return pl.pallas_call(
        relay_kernel,
        in_specs=[SMEM] + [VMEM] * 2,
        out_specs=[VMEM] * 2,
        out_shape=[shaped(own.shape, BF16)] * 2,
        compiler_params=params(24),
        cost_estimate=cost(2 * own.size, 8 * own.size),
        name="relay",
    )(at, own, got)


def swap_kernel(*refs):
    ins, out_ref = refs[:-1], refs[-1]
    total = ins[0][LIVE:, :].astype(F32)
    for ref in ins[1:]:
        total = total + ref[LIVE:, :].astype(F32)
    out_ref[...] = total.astype(BF16)


def other_rows(parts):
    half = parts[0].shape[1]
    return pl.pallas_call(
        swap_kernel,
        in_specs=[VMEM] * len(parts),
        out_specs=VMEM,
        out_shape=shaped((LIVE, half), BF16),
        compiler_params=params(24),
        cost_estimate=cost(LIVE * half, 2 * LIVE * half * len(parts)),
        name="other_rows",
    )(*parts)


def out_kernel(count, blocks, block, core_ref, fill_ref, base_ref, *refs):
    parts, rest, out_ref, held = refs[:count], refs[count:-2], refs[-2], refs[-1]
    half = rest[0].shape[1]
    own = parts[0][:LIVE, :].astype(F32)
    for part in parts[1:]:
        own = own + part[:LIVE, :].astype(F32)
    other = rest[0][...].astype(F32)
    for part in rest[1:]:
        other = other + part[...].astype(F32)
    first = core_ref[0] == 0
    held[:, :half] = (base_ref[:, :half] + jnp.where(first, own, other)).astype(BF16)
    held[:, half:] = (base_ref[:, half:] + jnp.where(first, other, own)).astype(BF16)
    window = min(2 * block, LIVE)
    row = lax.broadcasted_iota(I32, (block, window), 0)
    col = lax.broadcasted_iota(I32, (block, window), 1)
    for b, start in enumerate(starts_of(fill_ref, blocks)):
        at = pl.multiple_of(jnp.minimum(start // 16 * 16, LIVE - window), 16)
        hit = (col + at == row + start) & (row < fill_ref[0, b])
        pick = jnp.where(hit, 1.0, 0.0).astype(BF16)
        out_ref[b * block : (b + 1) * block, :] = dot(pick, held[pl.ds(at, window), :]).astype(BF16)


def finish(core, fill, base, parts, others, rows, blocks):
    cols = base.shape[1]
    count = len(parts)
    return pl.pallas_call(
        functools.partial(out_kernel, count, blocks, rows // blocks),
        in_specs=[SMEM] * 2 + [VMEM] * (1 + count + len(others)),
        out_specs=VMEM,
        out_shape=shaped((rows, cols), BF16),
        scratch_shapes=[pltpu.VMEM((LIVE, cols), BF16)],
        compiler_params=params(24),
        cost_estimate=cost(2 * LIVE * rows * cols, 4 * LIVE * cols + 2 * LIVE * cols * count + 2 * rows * cols),
        name="finish",
    )(core, fill, base, *parts, *others)


def body(sizes, tokens, base_weight, adapter_a, adapter_b, cotangent, block_tenant_index, block_fill):
    n_t, n_dp, n_pipe = sizes["tensor"], sizes["dp"], sizes["pipe"]
    planes = sizes["groups"] * n_dp
    rows, feat = tokens.shape
    cols = base_weight.shape[1]
    half = cols // n_pipe
    blocks = block_tenant_index.shape[0]
    pair, rank = adapter_a.shape[:2]
    me_t, me_pipe, me_dp = lax.axis_index("tensor"), lax.axis_index("pipe"), lax.axis_index("dp")
    q = lax.axis_index("groups") * n_dp + me_dp
    part_rows = feat // planes
    scalar = lambda v: v.astype(I32).reshape(1)
    dp, core, at, place = scalar(me_dp), scalar(me_pipe), scalar(me_t), scalar(q)

    own_a, own_b = adapter_a.reshape(pair * rank, feat), adapter_b.reshape(pair * rank, cols)
    one = own_half(core, own_a, own_b, rank)
    halves, raw = [], []
    for s in range(1, n_dp):
        raw += [shift(part, "dp", n_dp, s) for part in one]
        got = jnp.concatenate(raw[-2:], axis=0)
        halves += [got, flip(got, "pipe", n_pipe, 1)]
    panel_at = place if planes == 4 else jnp.zeros_like(place)

    def share(k):
        return lax.dynamic_slice(base_weight, (k * feat + q * part_rows, me_pipe * half), (part_rows, half))

    def gathered(piece):
        if planes != 4:
            return [lax.all_gather(piece, ("groups", "dp"), axis=0, tiled=True)], [0]
        return [piece] + [flip(piece, ("groups", "dp"), planes, m) for m in range(1, 4)], [0, 1, 2, 3]

    def add_flipped(low, mask, *before):
        return (low.astype(F32) + flip(after(low, *before), "tensor", n_t, mask).astype(F32)).astype(BF16)

    if n_t == 4:
        share_3 = share(me_t ^ 3)
        weight = {3: flip(share_3, "tensor", n_t, 3)}
        weight[2] = flip(after(share(me_t ^ 2), weight[3]), "tensor", n_t, 2)
        weight[1] = flip(after(share(me_t ^ 1), weight[2]), "tensor", n_t, 1)
        x = pack(after(block_fill, share_3), block_tenant_index, tokens, cotangent, blocks, 2 * rank)
        x_other = flip(after(x, weight[3], *raw), "pipe", n_pipe, 1)
        pieces, order = gathered(weight[3])
        low = low_part(after(dp, x_other), core, block_fill, block_tenant_index, x, own_a, own_b, halves, blocks, rank)
        pieces[0] = after(pieces[0], weight[2], low)
        (y_3,) = panel_product(order, panel_at, x, x_other, pieces, half)
        low = add_flipped(low, 1)
        far = lax.ppermute(y_3, "tensor", [(0, 1), (3, 2)])
        pieces, order = gathered(after(weight[2], *pieces))
        pieces[0] = after(pieces[0], weight[1])
        (y_2,) = panel_product(order, panel_at, x, x_other, pieces, half, adds=[far])
        low = add_flipped(low, 2)
        near = lax.ppermute(after(y_2, low), "tensor", [(0, 1), (3, 2), (1, 3), (2, 0)])
        pieces, order = gathered(after(weight[1], *pieces))
        (y_1,) = panel_product(order, panel_at, x, x_other, pieces, half)
        part_1 = flip(y_1, "tensor", n_t, 1)
        passed, kept = relay(at, y_3, near)
        parts = [lax.ppermute(passed, "tensor", [(1, 2), (2, 1)]), part_1, kept]
    else:
        x = pack(block_fill, block_tenant_index, tokens, cotangent, blocks, 2 * rank)
        x_other = flip(x, "pipe", n_pipe, 1)
        low = low_part(dp, core, block_fill, block_tenant_index, x, own_a, own_b, halves, blocks, rank)
        mask = 1
        while mask < n_t:
            low, mask = add_flipped(low, mask), 2 * mask
        steps = range(1, n_t)
        weights = [shift(share((me_t + s) % n_t), "tensor", n_t, s) for s in steps]
        pieces, order = gathered(jnp.concatenate(weights, axis=1))
        ys = panel_product(order, panel_at, x, x_other, pieces, half)
        parts = [shift(y, "tensor", n_t, -s) for s, y in zip(steps, ys)]

    low_other = flip(low, "pipe", n_pipe, 1)
    mine, *sends = grads(dp, core, x, x_other, low, low_other, n_dp, rank, feat, cols)
    for s, send in enumerate(sends):
        mine = mine + shift(after(send, *pieces), "dp", n_dp, s + 1).astype(F32)
    mine = mine.astype(BF16)
    down_out, up_out = settle(core, mine, flip(mine, "pipe", n_pipe, 1), feat)

    base = base_product(
        at, dp, core, block_fill, block_tenant_index, x, base_weight, low, own_b, halves, feat, blocks, rank
    )
    parts[0] = after(parts[0], base, down_out)
    others = [flip(other_rows(parts), "pipe", n_pipe, 1)]
    out = finish(core, block_fill, base, parts, others, rows, blocks)
    return out, down_out, up_out


def solution(mesh):
    placed = (
        P(("groups", "dp", "pipe"), "tensor"),
        P(None, "tensor"),
        P(("groups", "dp"), None, "tensor"),
        P(("groups", "dp"), None, "tensor"),
        P(("groups", "dp", "pipe"), "tensor"),
        P(("groups", "dp", "pipe")),
        P(("groups", "dp", "pipe"), None),
    )
    return jax.shard_map(
        functools.partial(body, dict(mesh.shape)),
        mesh=mesh,
        in_specs=placed,
        out_specs=(
            P(("groups", "dp", "pipe"), "tensor"),
            P(("groups", "dp"), None, "tensor"),
            P(("groups", "dp"), None, "tensor"),
        ),
        check_vma=False,
    )
```
